32 devices in a mesh: ctx: 8 (over z, y), kv: 4 (over x, core).
Axes of the slice: x: 2, y: 2, z: 4, core: 2. Of those that a mesh axis runs over, the one named last changes fastest.
Arguments:
- query: bfloat16 [2, 1024, 8192], P(None, 'ctx', 'kv')
- kv_rows: bfloat16 [2, 1024, 2048], P(None, 'ctx', 'kv')
- keep: int32 [2, 8, 8, 512], P(None, 'ctx', 'kv'), may hold values from 0 to 639, as said below
- dest: int32 [8192, 1], P('ctx'), may hold values from 0 to 31; in each aligned block of 1024 rows (0 to 1023, 1024 to 2047, ...) at most 64 rows name the same one
- offsets: int32 [2], replicated, may hold values from 0 to 6, as said below
Outputs:
- attention: bfloat16 [2, 1024, 8192], P(None, 'ctx', 'kv')
- row_scores: float32 [2, 8, 5120], P(None, 'kv', 'ctx')
- owner_cache: bfloat16 [16384, 2048], P(('ctx', 'kv'))
The draws below stay inside these ranges and needn't reach their ends.
Inputs may be any that keep to these rules, and one draw needn't show every extreme that they name: `keep`: each list holds 512 distinct indices in increasing order; an index below 512 names a cache slot, an index k of 512 or more names span row k - 512. `dest`: among the 1024 rows of one context shard no owner is named more than 64 times; owner o is the device at position o in the ctx-major order of ctx and kv. `offsets`: one prompt starts at the first shard and another prompt at the second-to-last shard.
All inputs are finite; a program needn't handle non-finite values.
Results may differ from the reference program's by a relative error of at most 0.0049.
Values may be sent and summed in bfloat16 or wider, within the bound.
No kernel may reach another device: no remote copies, remote signals or barrier semaphores. Data moves between devices by JAX's collectives and lax.ppermute only.
A program may use at most 192 MiB of HBM per device.

```python
import math
import jax
import jax.numpy as jnp
import numpy as np
from jax import lax

Q_HEADS = 64
KV_HEADS = 8
HEAD = 128
PROMPTS = 2
CH = 128
KEPT_ROWS = 512
TOKENS = 1024
OWNERS = 32
CAP = 64


def draw_query(key, part):
    shape = (PROMPTS, TOKENS, Q_HEADS * HEAD)
    own = jax.random.fold_in(key, 11)
    return jnp.clip(jax.random.normal(own, shape, jnp.float32), -6.0, 6.0).astype(jnp.bfloat16)


def draw_kv_rows(key, part):
    shape = (PROMPTS, TOKENS, KV_HEADS, 2 * HEAD)
    own = jax.random.fold_in(key, 21)
    base = jnp.clip(jax.random.normal(own, shape, jnp.float32), -6.0, 6.0)
    return base.reshape(PROMPTS, TOKENS, KV_HEADS * 2 * HEAD).astype(jnp.bfloat16)


def draw_keep(key, part):
    total_count = KEPT_ROWS + CH
    shards = TOKENS // CH
    unscaled_scores = jax.random.randint(jax.random.fold_in(key, 31), (PROMPTS, shards, KV_HEADS, total_count), 0, 4096)
    row_index = jnp.arange(total_count, dtype=jnp.int32)
    score_boost = jnp.where(row_index < KEPT_ROWS, 2048, 0)
    attention_scores = (unscaled_scores + score_boost) * total_count + row_index
    chosen = lax.top_k(attention_scores, KEPT_ROWS)[1]
    return jnp.sort(chosen, axis=-1).astype(jnp.int32)


def draw_offsets(key, part):
    shards = TOKENS // CH
    drawn = jax.random.randint(jax.random.fold_in(key, 41), (PROMPTS,), 0, shards - 1)
    order = jax.random.permutation(jax.random.fold_in(key, 42), PROMPTS)
    prompt_ids = jnp.arange(PROMPTS, dtype=jnp.int32)
    earliest = prompt_ids == order[0]
    latest = prompt_ids == order[1]
    result = jnp.where(earliest, 0, jnp.where(latest, shards - 2, drawn))
    return result.astype(jnp.int32)


def shared_out(stream_key, own, number, rows, count, top, reach, skew):
    ranking = jax.random.permutation(stream_key, count)
    heavy_load, usual = portions_of(count, rows * top, reach, skew, True), portions_of(count, rows * top, reach, skew, False)
    places = jnp.arange(count)

    def named(tallies, turn):
        used = int((tallies > 0).sum())
        fixed = max(1, used // 4)
        shifted = fixed + (places - fixed + turn * (used - fixed)) % max(1, count - fixed)
        return jnp.zeros((count,), jnp.int32).at[ranking[jnp.where(places < fixed, places, shifted)]].set(jnp.asarray(tallies, jnp.int32))

    tallies = jnp.where(number % 4 == 0, named(heavy_load, number // 4), named(usual, number - number // 4 - 1))
    mixed = jax.random.permutation(jax.random.fold_in(own, 3), count)
    source_of, receiver = mixed[0:count // 2 * 2:2], mixed[1:count // 2 * 2:2]
    slack = jnp.minimum(tallies[source_of] - 1, reach - tallies[receiver]) // 2
    slack = jnp.where((source_of == ranking[0]) | (receiver == ranking[0]) | (tallies[receiver] == 0), 0, jnp.maximum(slack, 0))
    shifted = jax.random.randint(jax.random.fold_in(own, 4), (count // 2,), 0, 1 << 20) % (slack + 1)
    tallies = tallies.at[source_of].add(-shifted).at[receiver].add(shifted)
    items = jnp.searchsorted(jnp.cumsum(tallies), jnp.arange(rows * top), side="right").astype(jnp.int32)
    listing = items.reshape(top, rows).T
    listing = listing[jax.random.permutation(jax.random.fold_in(own, 1), rows)]
    turn = jax.random.randint(jax.random.fold_in(own, 2), (rows, 1), 0, top)
    return jnp.take_along_axis(listing, (jnp.arange(top)[None, :] + turn) % top, axis=1)


def portions_of(number_of, total, bound, lean, full):
    portions = [(1 << 20) // math.isqrt(grade ** lean) + 1 for grade in range(1, number_of + 1)]
    largest = bound if full else min(bound, max(-(-total // number_of), total * portions[0] // sum(portions)))
    least = 1 if total - largest >= number_of - 1 else 0
    given, rest = [largest] + [least] * (number_of - 1), total - largest - least * (number_of - 1)
    while rest > 0:
        movable = [i for i in range(1, number_of) if given[i] < largest] or [i for i in range(1, number_of) if given[i] < bound]
        whole, remaining = sum([portions[i] for i in movable]), rest
        for i in movable:
            addition = min(bound - given[i], max(1, remaining * portions[i] // whole), rest)
            given[i] = given[i] + addition
            rest = rest - addition
    return np.array(given)


def setup_inputs(seed: int = 0) -> dict:
    arg_keys = jax.random.split(jax.random.key(seed), 6)
    query = draw_query(jax.random.fold_in(arg_keys[5], 71), 0)
    kv_rows = draw_kv_rows(jax.random.fold_in(arg_keys[5], 71), 0)
    keep = draw_keep(jax.random.fold_in(arg_keys[5], 71), 0)
    dest_keys = jax.random.split(jax.random.fold_in(arg_keys[3], 1), (TOKENS // CH * PROMPTS * KEPT_ROWS) // (PROMPTS * KEPT_ROWS))
    dest_turns = jax.random.permutation(jax.random.fold_in(arg_keys[3], 3), (TOKENS // CH * PROMPTS * KEPT_ROWS) // (PROMPTS * KEPT_ROWS))
    dest = jax.vmap(lambda own, number: shared_out(jax.random.fold_in(arg_keys[3], 2), own, number, PROMPTS * KEPT_ROWS, OWNERS, 1, CAP, 1))(dest_keys, dest_turns).reshape((TOKENS // CH * PROMPTS * KEPT_ROWS, 1))
    offsets = draw_offsets(jax.random.fold_in(arg_keys[5], 71), 0)
    return {"query": query, "kv_rows": kv_rows, "keep": keep, "dest": dest, "offsets": offsets}


def reference(query, kv_rows, keep, dest, offsets):
    group = Q_HEADS // KV_HEADS
    shards = TOKENS // CH
    width = 2 * HEAD
    qsix = query.reshape(PROMPTS, shards, CH, KV_HEADS, group, HEAD)
    kvfive = kv_rows.reshape(PROMPTS, shards, CH, KV_HEADS, width)
    scale = 1.0 / math.sqrt(HEAD)
    causal = jnp.arange(CH)[None, :] <= jnp.arange(CH)[:, None]
    highest = lax.Precision.HIGHEST

    def shard(carry, row_index):
        cache, valid = carry
        queries = lax.dynamic_index_in_dim(qsix, row_index, 1, keepdims=False).astype(jnp.float32)
        span_kv = lax.dynamic_index_in_dim(kvfive, row_index, 1, keepdims=False)
        rows_all = jnp.concatenate([cache, span_kv], axis=1)
        keys = rows_all[..., :HEAD].astype(jnp.float32)
        values = rows_all[..., HEAD:].astype(jnp.float32)
        attention_scores = jnp.einsum('pqhgd,pkhd->phgqk', queries, keys, precision=highest) * scale
        seen = jnp.broadcast_to(valid[:, :, None, :], (PROMPTS, KV_HEADS, CH, KEPT_ROWS))
        near = jnp.broadcast_to(causal[None, None], (PROMPTS, KV_HEADS, CH, CH))
        allowed = jnp.concatenate([seen, near], axis=3)[:, :, None]
        attention_scores = jnp.where(allowed, attention_scores, -1e+30)
        peak = lax.optimization_barrier(jnp.max(attention_scores, axis=-1, keepdims=True))
        expo = jnp.where(allowed, jnp.exp(attention_scores - peak), 0.0)
        weights = expo / lax.optimization_barrier(jnp.sum(expo, axis=-1, keepdims=True))
        rounded = lax.optimization_barrier(weights.astype(jnp.bfloat16)).astype(jnp.float32)
        mixed = jnp.einsum('phgqk,pkhd->pqhgd', rounded, values, precision=highest)
        flag = (row_index >= offsets).astype(jnp.float32)
        mixed = (mixed * flag[:, None, None, None, None]).astype(jnp.bfloat16)
        mass = lax.optimization_barrier(jnp.sum(weights, axis=(2, 3))) * flag[:, None, None]
        keep_now = lax.dynamic_index_in_dim(keep, row_index, 1, keepdims=False)
        picked = jnp.take_along_axis(rows_all, jnp.transpose(keep_now, (0, 2, 1))[..., None], axis=1)
        valid_all = jnp.concatenate([valid, jnp.ones((PROMPTS, KV_HEADS, CH), dtype=bool)], axis=2)
        new_valid = jnp.take_along_axis(valid_all, keep_now, axis=2)
        living = flag > 0.5
        cache = jnp.where(living[:, None, None, None], picked, cache)
        valid = jnp.where(living[:, None, None], new_valid, valid)
        return ((cache, valid), (mixed, mass, cache))
    start = (jnp.zeros((PROMPTS, KEPT_ROWS, KV_HEADS, width), jnp.bfloat16), jnp.zeros((PROMPTS, KV_HEADS, KEPT_ROWS), dtype=bool))
    _, (mixed, mass, caches) = lax.scan(shard, start, jnp.arange(shards, dtype=jnp.int32))
    attention = jnp.transpose(mixed, (1, 0, 2, 3, 4, 5)).reshape(PROMPTS, TOKENS, Q_HEADS * HEAD)
    row_scores = jnp.transpose(mass, (1, 2, 0, 3)).reshape(PROMPTS, KV_HEADS, shards * (KEPT_ROWS + CH))
    rows = caches.reshape(shards, PROMPTS * KEPT_ROWS, KV_HEADS * width)
    owning_shards = dest.reshape(shards, PROMPTS * KEPT_ROWS)
    onehot = (owning_shards[..., None] == jnp.arange(OWNERS, dtype=jnp.int32)).astype(jnp.int32)
    rank = lax.optimization_barrier(jnp.sum((jnp.cumsum(onehot, axis=1) - 1) * onehot, axis=2))
    source = jnp.arange(shards, dtype=jnp.int32)[:, None]
    flat = (owning_shards * shards + source) * CAP + rank
    owner_cache = jnp.zeros((OWNERS * shards * CAP, KV_HEADS * width), jnp.bfloat16)
    owner_cache = owner_cache.at[flat.reshape(-1)].set(rows.reshape(-1, KV_HEADS * width))
    return (attention, row_scores, owner_cache)
```

```python
import functools
import math

import jax
import jax.numpy as jnp
from jax import lax
from jax.experimental import pallas as pl
from jax.experimental.pallas import tpu as pltpu
from jax.sharding import PartitionSpec as P

HEAD = 128
WIDTH = 2 * HEAD
LANES = 128
VMEM_BYTES = 56 * 1024 * 1024


def look_up(state, keep, fresh):
    tiles = state.shape[1] // LANES
    parts = []
    for tile in range(tiles):
        wanted = keep[:, tile * LANES : (tile + 1) * LANES]
        high = wanted >> 7
        low = wanted & 127
        found = jnp.where(high >= tiles, fresh + wanted - state.shape[1], 0)
        for source in range(tiles):
            held = state[:, source * LANES : (source + 1) * LANES]
            moved = jnp.take_along_axis(held, low, axis=1, mode="promise_in_bounds")
            found = jnp.where(high == source, moved, found)
        parts.append(found)
    return jnp.concatenate(parts, axis=1)


def split(state):
    both = jnp.concatenate([state >> 7, state & 127], axis=0)
    return both.astype(jnp.float32).astype(jnp.bfloat16)


def index_kernel(
    where_ref, keep_early_ref, keep_late_ref, dest_ref, slot_ref, row_ref, column_ref, coded
):
    shards, heads, cache = keep_early_ref.shape
    cap = slot_ref.shape[0] // shards
    span = LANES
    early, mine, me = where_ref[0], where_ref[1], where_ref[2]
    empty = jnp.minimum(keep_early_ref[0], 0)

    def follow(shard, carry):
        state, own = carry
        own = jnp.where(shard == mine, state, own)
        state = look_up(state, keep_early_ref[shard], shard * span + 1)
        coded[shard] = split(state)
        return state, own

    _, own_early = lax.fori_loop(0, shards, follow, (empty, empty), unroll=shards <= 8)
    base = shards * span + 1
    late_first = look_up(empty, keep_late_ref[0], base)
    late_second = look_up(late_first, keep_late_ref[1], base + span)
    own_late = jnp.where(mine == shards - 1, late_first, 0)
    for index, own in enumerate((own_early, own_late)):
        row_ref[index] = own
        column_ref[index] = jnp.transpose(own.astype(jnp.float32)).astype(jnp.int32)

    named = (dest_ref[...] == me).astype(jnp.float32)
    chunks = named.shape[1] // LANES
    upper = (
        lax.broadcasted_iota(jnp.int32, (LANES, LANES), 0)
        <= lax.broadcasted_iota(jnp.int32, (LANES, LANES), 1)
    ).astype(jnp.float32).astype(jnp.bfloat16)
    total = jnp.zeros((shards, 1), jnp.float32)
    ranks = []
    for chunk in range(chunks):
        part = named[:, chunk * LANES : (chunk + 1) * LANES]
        upto = jnp.dot(part.astype(jnp.bfloat16), upper, preferred_element_type=jnp.float32)
        ranks.append(jnp.where(part > 0, upto + total, 0.0))
        total = total + upto[:, LANES - 1 :]
    low_half = jnp.concatenate(ranks[: chunks // 2], axis=1)
    high_half = jnp.concatenate(ranks[chunks // 2 :], axis=1)
    rank_early = jnp.where(early == 0, low_half, high_half)
    rank_late = jnp.where(early == 0, high_half, low_half)
    place = lax.broadcasted_iota(jnp.int32, (cap, cache), 0).astype(jnp.float32) + 1.0
    contract = (((1,), (1,)), ((), ()))
    for shard in range(shards):
        pick = (rank_early[shard : shard + 1] == place).astype(jnp.float32).astype(jnp.bfloat16)
        found = lax.dot_general(pick, coded[shard], contract, preferred_element_type=jnp.float32)
        if shard >= shards - 2:
            state = late_first if shard == shards - 2 else late_second
            pick = (rank_late[shard : shard + 1] == place).astype(jnp.float32).astype(jnp.bfloat16)
            found += lax.dot_general(
                pick, split(state), contract, preferred_element_type=jnp.float32
            )
        tokens = found[:, :heads] * 128.0 + found[:, heads:]
        slot_ref[shard * cap : (shard + 1) * cap, :] = tokens.astype(jnp.int32)


def column_of(table, head):
    lane = lax.broadcasted_iota(jnp.int32, table.shape, 1)
    return jnp.sum(
        jnp.where(lane == head, table, 0).astype(jnp.float32), axis=1, keepdims=True
    ).astype(jnp.int32)


def picked(column, first, tokens):
    number = lax.broadcasted_iota(jnp.int32, (column.shape[0], tokens.shape[0]), 1) + first
    table = (column == number).astype(jnp.float32).astype(jnp.bfloat16)
    return jnp.dot(table, tokens, preferred_element_type=jnp.float32)


def attend(q_ref, prompt, keys, values, seen, out_ref, score_ref, head):
    span = q_ref.shape[1]
    cache = seen.shape[1]
    group = q_ref.shape[2] // HEAD
    causal = lax.broadcasted_iota(jnp.int32, (span, span), 1) <= lax.broadcasted_iota(
        jnp.int32, (span, span), 0
    )
    bias = jnp.concatenate(
        [
            jnp.broadcast_to(jnp.where(seen > 0, 0.0, -1e30), (span, cache)),
            jnp.where(causal, 0.0, -1e30),
        ],
        axis=1,
    )
    scale = math.log2(math.e) / math.sqrt(HEAD)
    mass = jnp.zeros((1, cache + span), jnp.float32)
    for member in range(group):
        query = q_ref[prompt, :, member * HEAD : (member + 1) * HEAD]
        scores = lax.dot_general(
            query, keys, (((1,), (1,)), ((), ())), preferred_element_type=jnp.float32
        )
        scores = scores + bias
        peak = jnp.max(scores, axis=1, keepdims=True)
        expo = jnp.exp2((scores - peak) * scale)
        weights = expo * (1.0 / jnp.sum(expo, axis=1, keepdims=True))
        mass = mass + jnp.sum(weights, axis=0, keepdims=True)
        mixed = jnp.dot(weights.astype(jnp.bfloat16), values, preferred_element_type=jnp.float32)
        out_ref[prompt, :, member * HEAD : (member + 1) * HEAD] = mixed.astype(jnp.bfloat16)
    score_ref[prompt, pl.ds(head, 1), :] = mass


def attention_kernel(
    where_ref, q_ref, span_ref, early_ref, late_ref, row_ref, column_ref, out_ref, score_ref
):
    early, mine, column, shards = where_ref[0], where_ref[1], where_ref[3], early_ref.shape[0]
    span = q_ref.shape[1]
    late = 1 - early
    local_head = pl.program_id(0)
    head = column * pl.num_programs(0) + local_head

    def run(which, prompt, tokens, first):
        chosen = column_of(column_ref[which], head)
        cached = picked(chosen, first, tokens).astype(jnp.bfloat16)
        rows = jnp.concatenate([cached, span_ref[prompt]], axis=0)
        seen = row_ref[which, pl.ds(head, 1), :]
        attend(
            q_ref, prompt, rows[:, :HEAD], rows[:, HEAD:], seen, out_ref, score_ref, local_head
        )

    run(0, early, early_ref[:, 0].reshape(shards * span, WIDTH), 1)

    @pl.when(mine >= shards - 2)
    def _():
        run(1, late, late_ref[0, 0], shards * span + 1)

    @pl.when(mine < shards - 2)
    def _():
        out_ref[late] = jnp.zeros(out_ref.shape[1:], out_ref.dtype)
        score_ref[late, pl.ds(local_head, 1), :] = jnp.zeros((1, score_ref.shape[2]), jnp.float32)


def owner_kernel(slot_ref, early_ref, late_ref, out_ref):
    shards, _, span, width = early_ref.shape
    rows = out_ref.shape[0]
    chosen = column_of(slot_ref[...], pl.program_id(0))
    bands = 4
    band = rows // bands
    reach = shards * span // bands
    tokens = early_ref[:, 0].reshape(shards * span, width)
    for index in range(bands):
        part = chosen[index * band : (index + 1) * band]
        found = picked(part, 1, tokens[: (index + 1) * reach])
        if index == bands - 1:
            found += picked(part, shards * span + 1, late_ref[:, 0].reshape(2 * span, width))
        out_ref[index * band : (index + 1) * band, :] = found.astype(jnp.bfloat16)


def local(query, kv_rows, keep, dest, offsets):
    prompts, span, qwidth = query.shape
    shards, columns = lax.axis_size("ctx"), lax.axis_size("kv")
    width = kv_rows.shape[2]
    heads_dev = width // WIDTH
    heads = heads_dev * columns
    cache = keep.shape[3]
    owners = shards * columns
    cap = 2 * prompts * cache // owners
    mine, column = lax.axis_index("ctx"), lax.axis_index("kv")
    early = jnp.where(offsets[0] < offsets[1], 0, 1).astype(jnp.int32)
    facts = jnp.stack([early, mine, mine * columns + column, column]).astype(jnp.int32)

    swap = early == 1
    ordered_kv = jnp.where(swap, kv_rows[::-1], kv_rows)
    ordered_keep = jnp.where(swap, keep[::-1, 0], keep[:, 0])
    digits = jnp.stack([ordered_keep >> 7, ordered_keep & 127], axis=1)
    share = dest.shape[0] // columns
    own_dest = lax.dynamic_slice_in_dim(dest[:, 0], column * share, share)
    facts_rows = jnp.concatenate([digits.reshape(-1), own_dest]).astype(jnp.bfloat16)
    used = facts_rows.shape[0]
    room = 16 * width
    facts_rows = jnp.concatenate([facts_rows, jnp.zeros((room - used,), jnp.bfloat16)])
    payload = jnp.concatenate(
        [ordered_kv.reshape(prompts * span, width), facts_rows.reshape(16, width)], axis=0
    )
    whole = lax.all_gather(payload, ("ctx", "kv")).reshape(
        shards, columns, prompts * span + 16, width
    )

    told = whole[:, :, prompts * span :, :].reshape(shards, columns, room).astype(jnp.int32)
    kept = told[:, :, : prompts * 2 * heads_dev * cache].reshape(
        shards, columns, prompts, 2, heads_dev, cache
    )
    kept = kept[:, :, :, 0] * 128 + kept[:, :, :, 1]
    kept = jnp.transpose(kept, (2, 0, 1, 3, 4)).reshape(prompts, shards, heads, cache)
    whole_dest = told[:, :, used - share : used].reshape(shards, columns * share)

    vmem = pl.BlockSpec(memory_space=pltpu.VMEM)
    smem = pl.BlockSpec(memory_space=pltpu.SMEM)
    params = pltpu.CompilerParams(vmem_limit_bytes=VMEM_BYTES)
    slots, rows, cols = pl.pallas_call(
        index_kernel,
        out_shape=(
            jax.ShapeDtypeStruct((shards * cap, heads), jnp.int32),
            jax.ShapeDtypeStruct((2, heads, cache), jnp.int32),
            jax.ShapeDtypeStruct((2, cache, heads), jnp.int32),
        ),
        in_specs=[smem, vmem, vmem, vmem],
        out_specs=(vmem, vmem, vmem),
        scratch_shapes=[pltpu.VMEM((shards, 2 * heads, cache), jnp.bfloat16)],
        compiler_params=params,
    )(facts, kept[0], kept[1, shards - 2 :], whole_dest)

    group_width = qwidth // heads_dev
    attention, row_scores = pl.pallas_call(
        attention_kernel,
        grid_spec=pltpu.PrefetchScalarGridSpec(
            num_scalar_prefetch=1,
            grid=(heads_dev,),
            in_specs=[
                pl.BlockSpec((prompts, span, group_width), lambda h, w: (0, 0, h)),
                pl.BlockSpec((prompts, span, WIDTH), lambda h, w: (0, 0, h)),
                pl.BlockSpec((shards, 1, span, WIDTH), lambda h, w: (0, w[3], 0, h)),
                pl.BlockSpec((1, 1, span, WIDTH), lambda h, w: (shards - 2, w[3], 1, h)),
                pl.BlockSpec((2, heads, cache), lambda h, w: (0, 0, 0)),
                pl.BlockSpec((2, cache, heads), lambda h, w: (0, 0, 0)),
            ],
            out_specs=(
                pl.BlockSpec((prompts, span, group_width), lambda h, w: (0, 0, h)),
                pl.BlockSpec((prompts, heads_dev, cache + span), lambda h, w: (0, 0, 0)),
            ),
        ),
        out_shape=(
            jax.ShapeDtypeStruct((prompts, span, qwidth), jnp.bfloat16),
            jax.ShapeDtypeStruct((prompts, heads_dev, cache + span), jnp.float32),
        ),
        compiler_params=params,
    )(facts, query, kv_rows, whole, whole, rows, cols)

    owner_cache = pl.pallas_call(
        owner_kernel,
        grid=(heads,),
        in_specs=[
            pl.BlockSpec((shards * cap, heads), lambda g: (0, 0)),
            pl.BlockSpec(
                (shards, 1, span, WIDTH), lambda g: (0, g // heads_dev, 0, g % heads_dev)
            ),
            pl.BlockSpec(
                (2, 1, span, WIDTH),
                lambda g: (shards // 2 - 1, g // heads_dev, 1, g % heads_dev),
            ),
        ],
        out_specs=pl.BlockSpec((shards * cap, WIDTH), lambda g: (0, g)),
        out_shape=jax.ShapeDtypeStruct((shards * cap, heads * WIDTH), jnp.bfloat16),
        compiler_params=params,
    )(slots, whole, whole)
    return (attention, row_scores, owner_cache)


def solution(mesh):
    placed = (
        P(None, "ctx", "kv"),
        P(None, "ctx", "kv"),
        P(None, "ctx", "kv", None),
        P("ctx", None),
        P(),
    )
    return jax.shard_map(
        local,
        mesh=mesh,
        in_specs=placed,
        out_specs=(P(None, "ctx", "kv"), P(None, "kv", "ctx"), P(("ctx", "kv"), None)),
        check_vma=False,
    )
```

```python
import functools
import math

import jax
import jax.numpy as jnp
from jax import lax
from jax.experimental import pallas as pl
from jax.experimental.pallas import tpu as pltpu
from jax.sharding import PartitionSpec as P

HEAD = 128
WIDTH = 2 * HEAD
LANES = 128
VMEM_BYTES = 40 * 1024 * 1024


def look_up(state, keep, fresh):
    tiles = state.shape[1] // LANES
    parts = []
    for tile in range(tiles):
        wanted = keep[:, tile * LANES : (tile + 1) * LANES]
        high = wanted >> 7
        low = wanted & 127
        found = jnp.where(high >= tiles, fresh + wanted - state.shape[1], 0)
        for source in range(tiles):
            held = state[:, source * LANES : (source + 1) * LANES]
            moved = jnp.take_along_axis(held, low, axis=1, mode="promise_in_bounds")
            found = jnp.where(high == source, moved, found)
        parts.append(found)
    return jnp.concatenate(parts, axis=1)


def split(state):
    both = jnp.concatenate([state >> 7, state & 127], axis=0)
    return both.astype(jnp.float32).astype(jnp.bfloat16)


def index_kernel(
    where_ref, keep_early_ref, keep_late_ref, dest_ref, slot_ref, row_ref, column_ref, coded
):
    shards, heads, cache = keep_early_ref.shape
    owners = slot_ref.shape[0]
    cap = slot_ref.shape[1] // shards
    span = LANES
    early, mine = where_ref[0], where_ref[1]
    empty = jnp.minimum(keep_early_ref[0], 0)

    def follow(shard, carry):
        state, own = carry
        own = jnp.where(shard == mine, state, own)
        state = look_up(state, keep_early_ref[shard], shard * span + 1)
        coded[shard] = split(state)
        return state, own

    _, own_early = lax.fori_loop(0, shards, follow, (empty, empty), unroll=shards <= 8)
    base = shards * span + 1
    late_first = look_up(empty, keep_late_ref[0], base)
    late_second = look_up(late_first, keep_late_ref[1], base + span)
    own_late = jnp.where(mine == shards - 1, late_first, 0)
    for index, own in enumerate((own_early, own_late)):
        row_ref[index] = own
        column_ref[index] = jnp.transpose(own.astype(jnp.float32)).astype(jnp.int32)

    chunks = dest_ref.shape[1] // LANES
    upper = (
        lax.broadcasted_iota(jnp.int32, (LANES, LANES), 0)
        <= lax.broadcasted_iota(jnp.int32, (LANES, LANES), 1)
    ).astype(jnp.float32).astype(jnp.bfloat16)
    place = lax.broadcasted_iota(jnp.int32, (cap, cache), 0).astype(jnp.float32) + 1.0
    contract = (((1,), (1,)), ((), ()))
    for owner in range(owners):
        named = (dest_ref[...] == where_ref[2] ^ owner).astype(jnp.float32)
        total = jnp.zeros((shards, 1), jnp.float32)
        ranks = []
        for chunk in range(chunks):
            part = named[:, chunk * LANES : (chunk + 1) * LANES]
            upto = jnp.dot(part.astype(jnp.bfloat16), upper, preferred_element_type=jnp.float32)
            ranks.append(jnp.where(part > 0, upto + total, 0.0))
            total = total + upto[:, LANES - 1 :]
        low_half = jnp.concatenate(ranks[: chunks // 2], axis=1)
        high_half = jnp.concatenate(ranks[chunks // 2 :], axis=1)
        rank_early = jnp.where(early == 0, low_half, high_half)
        rank_late = jnp.where(early == 0, high_half, low_half)
        for shard in range(shards):
            pick = (rank_early[shard : shard + 1] == place).astype(jnp.float32)
            found = lax.dot_general(
                pick.astype(jnp.bfloat16),
                coded[shard],
                contract,
                preferred_element_type=jnp.float32,
            )
            if shard >= shards - 2:
                state = late_first if shard == shards - 2 else late_second
                pick = (rank_late[shard : shard + 1] == place).astype(jnp.float32)
                found += lax.dot_general(
                    pick.astype(jnp.bfloat16),
                    split(state),
                    contract,
                    preferred_element_type=jnp.float32,
                )
            tokens = found[:, :heads] * 128.0 + found[:, heads:]
            slot_ref[owner, shard * cap : (shard + 1) * cap, :] = tokens.astype(jnp.int32)


def column_of(table, head):
    lane = lax.broadcasted_iota(jnp.int32, table.shape, 1)
    return jnp.sum(
        jnp.where(lane == head, table, 0).astype(jnp.float32), axis=1, keepdims=True
    ).astype(jnp.int32)


def picked(column, first, tokens):
    number = lax.broadcasted_iota(jnp.int32, (column.shape[0], tokens.shape[0]), 1) + first
    table = (column == number).astype(jnp.float32).astype(jnp.bfloat16)
    return jnp.dot(table, tokens, preferred_element_type=jnp.float32)


def attend(q_ref, prompt, keys, values, seen, out_ref, score_ref, head):
    span = q_ref.shape[1]
    cache = seen.shape[1]
    group = q_ref.shape[2] // HEAD
    causal = lax.broadcasted_iota(jnp.int32, (span, span), 1) <= lax.broadcasted_iota(
        jnp.int32, (span, span), 0
    )
    bias = jnp.concatenate(
        [
            jnp.broadcast_to(jnp.where(seen > 0, 0.0, -1e30), (span, cache)),
            jnp.where(causal, 0.0, -1e30),
        ],
        axis=1,
    )
    scale = math.log2(math.e) / math.sqrt(HEAD)
    mass = jnp.zeros((1, cache + span), jnp.float32)
    for member in range(group):
        query = q_ref[prompt, :, member * HEAD : (member + 1) * HEAD]
        scores = lax.dot_general(
            query, keys, (((1,), (1,)), ((), ())), preferred_element_type=jnp.float32
        )
        scores = scores + bias
        peak = jnp.max(scores, axis=1, keepdims=True)
        expo = jnp.exp2((scores - peak) * scale)
        weights = expo * (1.0 / jnp.sum(expo, axis=1, keepdims=True))
        mass = mass + jnp.sum(weights, axis=0, keepdims=True)
        mixed = jnp.dot(weights.astype(jnp.bfloat16), values, preferred_element_type=jnp.float32)
        out_ref[prompt, :, member * HEAD : (member + 1) * HEAD] = mixed.astype(jnp.bfloat16)
    score_ref[prompt, pl.ds(head, 1), :] = mass


def gather_early(facts_ref, refs, tokens_ref):
    if len(refs) == 1:
        tokens_ref[...] = refs[0][...].reshape(tokens_ref.shape)
        return
    span = refs[0].shape[0]
    shards = len(refs)
    mine = facts_ref[1]
    turns = shards // 2
    for index, ref in enumerate(refs):
        turn, flip = index % turns, index // turns
        place = lax.rem(mine - 2 * turn + shards, shards)
        if flip:
            place = place + 1 - 2 * lax.rem(mine, 2)
        tokens_ref[pl.ds(pl.multiple_of(place * span, span), span), :] = ref[...]


def gather_late(facts_ref, refs, tokens_ref):
    if len(refs) == 1:
        tokens_ref[...] = refs[0][...].reshape(tokens_ref.shape)
        return
    span = refs[0].shape[0]
    side = lax.rem(facts_ref[1], 2)
    for flip, ref in enumerate(refs):
        place = side + flip - 2 * side * flip
        tokens_ref[pl.ds(pl.multiple_of(place * span, span), span), :] = ref[...]


def attention_kernel(pieces, facts_ref, q_ref, span_ref, row_ref, column_ref, *rest):
    early_refs, late_refs = rest[:pieces], rest[pieces : -4]
    out_ref, score_ref, early_tokens, late_tokens = rest[-4:]
    early, mine, column = facts_ref[0], facts_ref[1], facts_ref[3]
    span = q_ref.shape[1]
    shards = early_tokens.shape[0] // span
    late = 1 - early
    local_head = pl.program_id(0)
    head = column * pl.num_programs(0) + local_head

    def run(which, prompt, tokens, first):
        chosen = column_of(column_ref[which], head)
        cached = picked(chosen, first, tokens).astype(jnp.bfloat16)
        rows = jnp.concatenate([cached, span_ref[prompt]], axis=0)
        seen = row_ref[which, pl.ds(head, 1), :]
        attend(
            q_ref, prompt, rows[:, :HEAD], rows[:, HEAD:], seen, out_ref, score_ref, local_head
        )

    gather_early(facts_ref, early_refs, early_tokens)
    run(0, early, early_tokens[...], 1)

    @pl.when(mine >= shards - 2)
    def _():
        gather_late(facts_ref, late_refs, late_tokens)
        run(1, late, late_tokens[...], shards * span + 1)

    @pl.when(mine < shards - 2)
    def _():
        out_ref[late] = jnp.zeros(out_ref.shape[1:], out_ref.dtype)
        score_ref[late, pl.ds(local_head, 1), :] = jnp.zeros((1, score_ref.shape[2]), jnp.float32)


def owner_kernel(pieces, facts_ref, slot_ref, *rest):
    early_refs, late_refs = rest[:pieces], rest[pieces : -3]
    out_ref, early_tokens, late_tokens = rest[-3:]
    gather_early(facts_ref, early_refs, early_tokens)
    gather_late(facts_ref, late_refs, late_tokens)
    owners, rows = slot_ref.shape[0], slot_ref.shape[1]
    reach = early_tokens.shape[0]
    bands = 4
    band = rows // bands
    for owner in range(owners):
        chosen = column_of(slot_ref[owner], facts_ref[4] + pl.program_id(0))
        for index in range(bands):
            part = chosen[index * band : (index + 1) * band]
            found = picked(part, 1, early_tokens[: (index + 1) * reach // bands])
            if index == bands - 1:
                found += picked(part, reach + 1, late_tokens[...])
            out_ref[owner, index * band : (index + 1) * band, :] = found.astype(jnp.bfloat16)


def assemble_kernel(facts_ref, *refs):
    out_ref = refs[-1]
    for index, ref in enumerate(refs[:-1]):

        @pl.when(pl.program_id(0) == index)
        def _(ref=ref):
            out_ref[...] = ref[...]


def send(value, axis, pairs):
    return lax.ppermute(value, axis, pairs)


def spread_by_permutes(early_kv, late_kv, shards, columns):
    count = shards * columns
    rounds = shards // 2
    both = ("ctx", "kv")

    def across_y(value):
        return send(value, "ctx", [(i, i ^ 1) for i in range(shards)])

    def across_x(value):
        return send(value, "kv", [(i, i ^ 2) for i in range(columns)])

    def across_both(value):
        return send(value, both, [(i, i ^ columns ^ 2) for i in range(count)])

    level = lax.axis_index("ctx") // 2
    first = send(late_kv, "ctx", [(6, 2), (7, 3)])
    pieces = [early_kv]
    for turn in range(1, rounds):
        pieces.append(send(early_kv, "ctx", [(i, (i + 2 * turn) % shards) for i in range(shards)]))
    relay = jnp.where(level == 3, late_kv, first)
    second = send(relay, "ctx", [(6, 4), (7, 5), (2, 0), (3, 1)])
    late = jnp.where(level % 2 == 1, relay, second)
    own_early = pieces + [across_y(piece) for piece in pieces]
    own_late = [late, across_y(late)]
    other_early = [across_x(piece) for piece in pieces] + [across_both(piece) for piece in pieces]
    other_late = [across_x(late), across_both(late)]
    return (own_early, own_late), (other_early, other_late)


def local(query, kv_rows, keep, dest, offsets):
    prompts, span, qwidth = query.shape
    shards, columns = lax.axis_size("ctx"), lax.axis_size("kv")
    width = kv_rows.shape[2]
    heads_dev = width // WIDTH
    heads = heads_dev * columns
    cache = keep.shape[3]
    owners = shards * columns
    cap = 2 * prompts * cache // owners
    mine, column = lax.axis_index("ctx"), lax.axis_index("kv")
    early = jnp.where(offsets[0] < offsets[1], 0, 1).astype(jnp.int32)
    swap = early == 1
    in_planes = shards == 8 and columns == 4

    ordered_keep = jnp.where(swap, keep[::-1, 0], keep[:, 0])
    digits = jnp.stack([ordered_keep >> 7, ordered_keep & 127], axis=1)
    share = dest.shape[0] // columns
    own_dest = lax.dynamic_slice_in_dim(dest[:, 0], column * share, share)
    notes = jnp.concatenate([digits.reshape(-1), own_dest]).astype(jnp.bfloat16)
    used = notes.shape[0]
    room = 16 * width
    notes = jnp.concatenate([notes, jnp.zeros((room - used,), jnp.bfloat16)])
    told = lax.all_gather(notes.reshape(16, width), ("ctx", "kv"))
    told = told.reshape(shards, columns, room).astype(jnp.int32)
    kept = told[:, :, : prompts * 2 * heads_dev * cache].reshape(
        shards, columns, prompts, 2, heads_dev, cache
    )
    kept = kept[:, :, :, 0] * 128 + kept[:, :, :, 1]
    kept = jnp.transpose(kept, (2, 0, 1, 3, 4)).reshape(prompts, shards, heads, cache)
    whole_dest = told[:, :, used - share : used].reshape(shards, columns * share)

    early_kv = jnp.where(swap, kv_rows[1], kv_rows[0])
    late_kv = jnp.where(swap, kv_rows[0], kv_rows[1])
    if in_planes:
        own, other = spread_by_permutes(early_kv, late_kv, shards, columns)
        pieces = shards
        served = 2
    else:
        whole = lax.all_gather(
            jnp.concatenate([early_kv, late_kv], axis=0), ("ctx", "kv")
        ).reshape(shards, columns, prompts * span, width)
        pieces = 1
        served = 1

    def facts(first_head):
        return jnp.stack([early, mine, mine * columns + column, column, first_head]).astype(
            jnp.int32
        )

    vmem = pl.BlockSpec(memory_space=pltpu.VMEM)
    smem = pl.BlockSpec(memory_space=pltpu.SMEM)
    params = pltpu.CompilerParams(vmem_limit_bytes=VMEM_BYTES)
    own_facts = facts(column * heads_dev)
    slots, rows, cols = pl.pallas_call(
        index_kernel,
        out_shape=(
            jax.ShapeDtypeStruct((served, shards * cap, heads), jnp.int32),
            jax.ShapeDtypeStruct((2, heads, cache), jnp.int32),
            jax.ShapeDtypeStruct((2, cache, heads), jnp.int32),
        ),
        in_specs=[smem, vmem, vmem, vmem],
        out_specs=(vmem, vmem, vmem),
        scratch_shapes=[pltpu.VMEM((shards, 2 * heads, cache), jnp.bfloat16)],
        compiler_params=params,
        cost_estimate=pl.CostEstimate(flops=10**8, bytes_accessed=10**7, transcendentals=0),
    )(own_facts, kept[0], kept[1, shards - 2 :], whole_dest)

    scratch = [
        pltpu.VMEM((shards * span, WIDTH), jnp.bfloat16),
        pltpu.VMEM((2 * span, WIDTH), jnp.bfloat16),
    ]
    if in_planes:
        own_specs = [pl.BlockSpec((span, WIDTH), lambda h, w: (0, h))] * (pieces + 2)
        own_arrays = own[0] + own[1]
    else:
        own_specs = [
            pl.BlockSpec((shards, 1, span, WIDTH), lambda h, w: (0, w[3], 0, h)),
            pl.BlockSpec((2, 1, span, WIDTH), lambda h, w: (shards // 2 - 1, w[3], 1, h)),
        ]
        own_arrays = [whole, whole]
    group_width = qwidth // heads_dev
    attention, row_scores = pl.pallas_call(
        functools.partial(attention_kernel, pieces),
        grid_spec=pltpu.PrefetchScalarGridSpec(
            num_scalar_prefetch=1,
            grid=(heads_dev,),
            in_specs=[
                pl.BlockSpec((prompts, span, group_width), lambda h, w: (0, 0, h)),
                pl.BlockSpec((prompts, span, WIDTH), lambda h, w: (0, 0, h)),
                pl.BlockSpec((2, heads, cache), lambda h, w: (0, 0, 0)),
                pl.BlockSpec((2, cache, heads), lambda h, w: (0, 0, 0)),
            ]
            + own_specs,
            out_specs=(
                pl.BlockSpec((prompts, span, group_width), lambda h, w: (0, 0, h)),
                pl.BlockSpec((prompts, heads_dev, cache + span), lambda h, w: (0, 0, 0)),
            ),
            scratch_shapes=scratch,
        ),
        out_shape=(
            jax.ShapeDtypeStruct((prompts, span, qwidth), jnp.bfloat16),
            jax.ShapeDtypeStruct((prompts, heads_dev, cache + span), jnp.float32),
        ),
        compiler_params=params,
        cost_estimate=pl.CostEstimate(flops=10**10, bytes_accessed=10**7, transcendentals=10**6),
    )(own_facts, query, kv_rows, rows, cols, *own_arrays)

    def place_rows(which, count, specs, arrays):
        return pl.pallas_call(
            functools.partial(owner_kernel, pieces),
            grid_spec=pltpu.PrefetchScalarGridSpec(
                num_scalar_prefetch=1,
                grid=(count,),
                in_specs=[
                    pl.BlockSpec((served, shards * cap, heads), lambda g, w: (0, 0, 0))
                ]
                + specs,
                out_specs=pl.BlockSpec((served, shards * cap, WIDTH), lambda g, w: (0, 0, g)),
                scratch_shapes=scratch,
            ),
            out_shape=jax.ShapeDtypeStruct((served, shards * cap, count * WIDTH), jnp.bfloat16),
            compiler_params=params,
            cost_estimate=pl.CostEstimate(
                flops=10**10, bytes_accessed=10**7, transcendentals=0
            ),
        )(which, slots, *arrays)

    if not in_planes:
        specs = [
            pl.BlockSpec(
                (shards, 1, span, WIDTH), lambda g, w: (0, g // heads_dev, 0, g % heads_dev)
            ),
            pl.BlockSpec(
                (2, 1, span, WIDTH),
                lambda g, w: (shards // 2 - 1, g // heads_dev, 1, g % heads_dev),
            ),
        ]
        return (attention, row_scores, place_rows(facts(0), heads, specs, [whole, whole])[0])

    near = place_rows(own_facts, heads_dev, own_specs, own_arrays)
    far = place_rows(facts((column ^ 2) * heads_dev), heads_dev, own_specs, other[0] + other[1])
    siblings = [(i, i ^ 1) for i in range(columns)]
    blocks = [near[0], send(near[1], "kv", siblings), far[0], send(far[1], "kv", siblings)]
    owner_cache = pl.pallas_call(
        assemble_kernel,
        grid_spec=pltpu.PrefetchScalarGridSpec(
            num_scalar_prefetch=1,
            grid=(columns,),
            in_specs=[pl.BlockSpec((shards * cap, width), lambda g, w: (0, 0))] * columns,
            out_specs=pl.BlockSpec((shards * cap, width), lambda g, w: (0, w[3] ^ g)),
        ),
        out_shape=jax.ShapeDtypeStruct((shards * cap, columns * width), jnp.bfloat16),
        compiler_params=params,
        cost_estimate=pl.CostEstimate(flops=0, bytes_accessed=10**7, transcendentals=0),
    )(own_facts, *blocks)
    return (attention, row_scores, owner_cache)


def solution(mesh):
    placed = (
        P(None, "ctx", "kv"),
        P(None, "ctx", "kv"),
        P(None, "ctx", "kv", None),
        P("ctx", None),
        P(),
    )
    return jax.shard_map(
        local,
        mesh=mesh,
        in_specs=placed,
        out_specs=(P(None, "ctx", "kv"), P(None, "kv", "ctx"), P(("ctx", "kv"), None)),
        check_vma=False,
    )
```

```python
import functools
import math

import jax
import jax.numpy as jnp
from jax import lax
from jax.experimental import pallas as pl
from jax.experimental.pallas import tpu as pltpu
from jax.sharding import PartitionSpec as P

HEAD = 128
WIDTH = 2 * HEAD
LANES = 128
VMEM_BYTES = 56 * 1024 * 1024
PLANE_BYTES = 28 * 1024 * 1024
NOTES = 16


def look_up(state, keep, fresh):
    tiles = state.shape[1] // LANES
    parts = []
    for tile in range(tiles):
        wanted = keep[:, tile * LANES : (tile + 1) * LANES]
        high = wanted >> 7
        low = wanted & 127
        found = jnp.where(high >= tiles, fresh + wanted - state.shape[1], 0)
        for source in range(tiles):
            held = state[:, source * LANES : (source + 1) * LANES]
            moved = jnp.take_along_axis(held, low, axis=1, mode="promise_in_bounds")
            found = jnp.where(high == source, moved, found)
        parts.append(found)
    return jnp.concatenate(parts, axis=1)


def split(state):
    both = jnp.concatenate([state >> 7, state & 127], axis=0)
    return both.astype(jnp.float32).astype(jnp.bfloat16)


def index_kernel(
    where_ref, keep_early_ref, keep_late_ref, dest_ref, slot_ref, row_ref, column_ref, coded
):
    shards, heads, cache = keep_early_ref.shape
    cap = slot_ref.shape[0] // shards
    span = LANES
    early, mine, me = where_ref[0], where_ref[1], where_ref[2]
    empty = jnp.minimum(keep_early_ref[0], 0)

    def follow(shard, carry):
        state, own = carry
        own = jnp.where(shard == mine, state, own)
        state = look_up(state, keep_early_ref[shard], shard * span + 1)
        coded[shard] = split(state)
        return state, own

    _, own_early = lax.fori_loop(0, shards, follow, (empty, empty), unroll=shards <= 8)
    base = shards * span + 1
    late_first = look_up(empty, keep_late_ref[0], base)
    late_second = look_up(late_first, keep_late_ref[1], base + span)
    own_late = jnp.where(mine == shards - 1, late_first, 0)
    for index, own in enumerate((own_early, own_late)):
        row_ref[index] = own
        column_ref[index] = jnp.transpose(own.astype(jnp.float32)).astype(jnp.int32)

    named = (dest_ref[...] == me).astype(jnp.float32)
    chunks = named.shape[1] // LANES
    upper = (
        lax.broadcasted_iota(jnp.int32, (LANES, LANES), 0)
        <= lax.broadcasted_iota(jnp.int32, (LANES, LANES), 1)
    ).astype(jnp.float32).astype(jnp.bfloat16)
    total = jnp.zeros((shards, 1), jnp.float32)
    ranks = []
    for chunk in range(chunks):
        part = named[:, chunk * LANES : (chunk + 1) * LANES]
        upto = jnp.dot(part.astype(jnp.bfloat16), upper, preferred_element_type=jnp.float32)
        ranks.append(jnp.where(part > 0, upto + total, 0.0))
        total = total + upto[:, LANES - 1 :]
    low_half = jnp.concatenate(ranks[: chunks // 2], axis=1)
    high_half = jnp.concatenate(ranks[chunks // 2 :], axis=1)
    rank_early = jnp.where(early == 0, low_half, high_half)
    rank_late = jnp.where(early == 0, high_half, low_half)
    place = lax.broadcasted_iota(jnp.int32, (cap, cache), 0).astype(jnp.float32) + 1.0
    contract = (((1,), (1,)), ((), ()))
    for shard in range(shards):
        pick = (rank_early[shard : shard + 1] == place).astype(jnp.float32).astype(jnp.bfloat16)
        found = lax.dot_general(pick, coded[shard], contract, preferred_element_type=jnp.float32)
        if shard >= shards - 2:
            state = late_first if shard == shards - 2 else late_second
            pick = (rank_late[shard : shard + 1] == place).astype(jnp.float32).astype(jnp.bfloat16)
            found += lax.dot_general(
                pick, split(state), contract, preferred_element_type=jnp.float32
            )
        tokens = found[:, :heads] * 128.0 + found[:, heads:]
        slot_ref[shard * cap : (shard + 1) * cap, :] = tokens.astype(jnp.int32)


def column_of(table, head):
    lane = lax.broadcasted_iota(jnp.int32, table.shape, 1)
    return jnp.sum(
        jnp.where(lane == head, table, 0).astype(jnp.float32), axis=1, keepdims=True
    ).astype(jnp.int32)


def picked(column, first, tokens):
    number = lax.broadcasted_iota(jnp.int32, (column.shape[0], tokens.shape[0]), 1) + first
    table = (column == number).astype(jnp.float32).astype(jnp.bfloat16)
    return jnp.dot(table, tokens, preferred_element_type=jnp.float32)


def attend(q_ref, prompt, keys, values, seen, out_ref, score_ref, head):
    span = q_ref.shape[1]
    cache = seen.shape[1]
    group = q_ref.shape[2] // HEAD
    causal = lax.broadcasted_iota(jnp.int32, (span, span), 1) <= lax.broadcasted_iota(
        jnp.int32, (span, span), 0
    )
    bias = jnp.concatenate(
        [
            jnp.broadcast_to(jnp.where(seen > 0, 0.0, -1e30), (span, cache)),
            jnp.where(causal, 0.0, -1e30),
        ],
        axis=1,
    )
    scale = math.log2(math.e) / math.sqrt(HEAD)
    mass = jnp.zeros((1, cache + span), jnp.float32)
    for member in range(group):
        query = q_ref[prompt, :, member * HEAD : (member + 1) * HEAD]
        scores = lax.dot_general(
            query, keys, (((1,), (1,)), ((), ())), preferred_element_type=jnp.float32
        )
        scores = scores + bias
        peak = jnp.max(scores, axis=1, keepdims=True)
        expo = jnp.exp2((scores - peak) * scale)
        weights = expo * (1.0 / jnp.sum(expo, axis=1, keepdims=True))
        mass = mass + jnp.sum(weights, axis=0, keepdims=True)
        mixed = jnp.dot(weights.astype(jnp.bfloat16), values, preferred_element_type=jnp.float32)
        out_ref[prompt, :, member * HEAD : (member + 1) * HEAD] = mixed.astype(jnp.bfloat16)
    score_ref[prompt, pl.ds(head, 1), :] = mass


def attention_kernel(
    where_ref, q_ref, span_ref, early_ref, late_ref, row_ref, column_ref, out_ref, score_ref
):
    early, mine, column, shards = where_ref[0], where_ref[1], where_ref[3], early_ref.shape[0]
    span = q_ref.shape[1]
    late = 1 - early
    local_head = pl.program_id(0)
    head = column * pl.num_programs(0) + local_head

    def run(which, prompt, tokens, first):
        chosen = column_of(column_ref[which], head)
        cached = picked(chosen, first, tokens).astype(jnp.bfloat16)
        rows = jnp.concatenate([cached, span_ref[prompt]], axis=0)
        seen = row_ref[which, pl.ds(head, 1), :]
        attend(
            q_ref, prompt, rows[:, :HEAD], rows[:, HEAD:], seen, out_ref, score_ref, local_head
        )

    run(0, early, early_ref[:, 0].reshape(shards * span, WIDTH), 1)

    @pl.when(mine >= shards - 2)
    def _():
        run(1, late, late_ref[0, 0], shards * span + 1)

    @pl.when(mine < shards - 2)
    def _():
        out_ref[late] = jnp.zeros(out_ref.shape[1:], out_ref.dtype)
        score_ref[late, pl.ds(local_head, 1), :] = jnp.zeros((1, score_ref.shape[2]), jnp.float32)


def owner_kernel(slot_ref, early_ref, late_ref, out_ref):
    shards, _, span, width = early_ref.shape
    rows = out_ref.shape[0]
    chosen = column_of(slot_ref[...], pl.program_id(0))
    bands = 4
    band = rows // bands
    reach = shards * span // bands
    tokens = early_ref[:, 0].reshape(shards * span, width)
    for index in range(bands):
        part = chosen[index * band : (index + 1) * band]
        found = picked(part, 1, tokens[: (index + 1) * reach])
        if index == bands - 1:
            found += picked(part, shards * span + 1, late_ref[:, 0].reshape(2 * span, width))
        out_ref[index * band : (index + 1) * band, :] = found.astype(jnp.bfloat16)


def local(query, kv_rows, keep, dest, offsets):
    prompts, span, qwidth = query.shape
    shards, columns = lax.axis_size("ctx"), lax.axis_size("kv")
    width = kv_rows.shape[2]
    heads_dev = width // WIDTH
    heads = heads_dev * columns
    cache = keep.shape[3]
    owners = shards * columns
    cap = 2 * prompts * cache // owners
    mine, column = lax.axis_index("ctx"), lax.axis_index("kv")
    early = jnp.where(offsets[0] < offsets[1], 0, 1).astype(jnp.int32)
    facts = jnp.stack([early, mine, mine * columns + column, column]).astype(jnp.int32)

    swap = early == 1
    ordered_kv = jnp.where(swap, kv_rows[::-1], kv_rows)
    ordered_keep = jnp.where(swap, keep[::-1, 0], keep[:, 0])
    digits = jnp.stack([ordered_keep >> 7, ordered_keep & 127], axis=1)
    share = dest.shape[0] // columns
    own_dest = lax.dynamic_slice_in_dim(dest[:, 0], column * share, share)
    facts_rows = jnp.concatenate([digits.reshape(-1), own_dest]).astype(jnp.bfloat16)
    used = facts_rows.shape[0]
    room = 16 * width
    facts_rows = jnp.concatenate([facts_rows, jnp.zeros((room - used,), jnp.bfloat16)])
    payload = jnp.concatenate(
        [ordered_kv.reshape(prompts * span, width), facts_rows.reshape(16, width)], axis=0
    )
    whole = lax.all_gather(payload, ("ctx", "kv")).reshape(
        shards, columns, prompts * span + 16, width
    )

    told = whole[:, :, prompts * span :, :].reshape(shards, columns, room).astype(jnp.int32)
    kept = told[:, :, : prompts * 2 * heads_dev * cache].reshape(
        shards, columns, prompts, 2, heads_dev, cache
    )
    kept = kept[:, :, :, 0] * 128 + kept[:, :, :, 1]
    kept = jnp.transpose(kept, (2, 0, 1, 3, 4)).reshape(prompts, shards, heads, cache)
    whole_dest = told[:, :, used - share : used].reshape(shards, columns * share)

    vmem = pl.BlockSpec(memory_space=pltpu.VMEM)
    smem = pl.BlockSpec(memory_space=pltpu.SMEM)
    params = pltpu.CompilerParams(vmem_limit_bytes=VMEM_BYTES)
    slots, rows, cols = pl.pallas_call(
        index_kernel,
        out_shape=(
            jax.ShapeDtypeStruct((shards * cap, heads), jnp.int32),
            jax.ShapeDtypeStruct((2, heads, cache), jnp.int32),
            jax.ShapeDtypeStruct((2, cache, heads), jnp.int32),
        ),
        in_specs=[smem, vmem, vmem, vmem],
        out_specs=(vmem, vmem, vmem),
        scratch_shapes=[pltpu.VMEM((shards, 2 * heads, cache), jnp.bfloat16)],
        compiler_params=params,
    )(facts, kept[0], kept[1, shards - 2 :], whole_dest)

    group_width = qwidth // heads_dev
    attention, row_scores = pl.pallas_call(
        attention_kernel,
        grid_spec=pltpu.PrefetchScalarGridSpec(
            num_scalar_prefetch=1,
            grid=(heads_dev,),
            in_specs=[
                pl.BlockSpec((prompts, span, group_width), lambda h, w: (0, 0, h)),
                pl.BlockSpec((prompts, span, WIDTH), lambda h, w: (0, 0, h)),
                pl.BlockSpec((shards, 1, span, WIDTH), lambda h, w: (0, w[3], 0, h)),
                pl.BlockSpec((1, 1, span, WIDTH), lambda h, w: (shards - 2, w[3], 1, h)),
                pl.BlockSpec((2, heads, cache), lambda h, w: (0, 0, 0)),
                pl.BlockSpec((2, cache, heads), lambda h, w: (0, 0, 0)),
            ],
            out_specs=(
                pl.BlockSpec((prompts, span, group_width), lambda h, w: (0, 0, h)),
                pl.BlockSpec((prompts, heads_dev, cache + span), lambda h, w: (0, 0, 0)),
            ),
        ),
        out_shape=(
            jax.ShapeDtypeStruct((prompts, span, qwidth), jnp.bfloat16),
            jax.ShapeDtypeStruct((prompts, heads_dev, cache + span), jnp.float32),
        ),
        compiler_params=params,
    )(facts, query, kv_rows, whole, whole, rows, cols)

    owner_cache = pl.pallas_call(
        owner_kernel,
        grid=(heads,),
        in_specs=[
            pl.BlockSpec((shards * cap, heads), lambda g: (0, 0)),
            pl.BlockSpec(
                (shards, 1, span, WIDTH), lambda g: (0, g // heads_dev, 0, g % heads_dev)
            ),
            pl.BlockSpec(
                (2, 1, span, WIDTH),
                lambda g: (shards // 2 - 1, g // heads_dev, 1, g % heads_dev),
            ),
        ],
        out_specs=pl.BlockSpec((shards * cap, WIDTH), lambda g: (0, g)),
        out_shape=jax.ShapeDtypeStruct((shards * cap, heads * WIDTH), jnp.bfloat16),
        compiler_params=params,
    )(slots, whole, whole)
    return (attention, row_scores, owner_cache)


def assemble_kernel(facts_ref, *refs):
    out_ref = refs[-1]
    for index, ref in enumerate(refs[:-1]):

        @pl.when(pl.program_id(0) == index)
        def _(ref=ref):
            out_ref[...] = ref[...]


def dot(a, b, dims=((1,), (0,))):
    return lax.dot_general(a, b, (dims, ((), ())), preferred_element_type=jnp.float32)


def marks(table):
    return table.astype(jnp.float32).astype(jnp.bfloat16)


def prepare_kernel(offsets_ref, kv_ref, keep_ref, dest_ref, early_ref, late_ref):
    span, width = kv_ref.shape[1], kv_ref.shape[2]
    first = offsets_ref[0] < offsets_ref[1]
    early = jnp.where(first, 0, 1)
    for which, ref in ((early, early_ref), (1 - early, late_ref)):
        ref[:span, :] = kv_ref[which]
        keep = keep_ref[which]
        rows = jnp.concatenate(
            [
                (keep >> 7).astype(jnp.float32),
                (keep & 127).astype(jnp.float32),
                dest_ref[...].astype(jnp.float32),
                jnp.zeros((NOTES - 3 * keep.shape[0], width), jnp.float32),
            ],
            axis=0,
        )
        ref[span:, :] = rows.astype(jnp.bfloat16)


def read_notes(ref, base, heads):
    rows = ref[base : base + NOTES, :].astype(jnp.float32).astype(jnp.int32)
    return rows[:heads] * 128 + rows[heads : 2 * heads], rows[2 * heads : 3 * heads]


def sort_pieces(facts_ref, early, late, tokens, late_tokens, keeps, dests):
    mine = facts_ref[1]
    shards = len(early)
    heads = keeps.shape[1] // 4
    span = late_tokens.shape[0] // 2
    side = lax.rem(mine, 2)
    keeps[...] = jnp.zeros(keeps.shape, jnp.int32)
    for ref, base, turn, flip in early:
        place = lax.rem(mine - 2 * turn + shards, shards)
        if flip:
            place = place + 1 - 2 * side
        tokens[pl.ds(pl.multiple_of(place * span, span), span), :] = ref[base : base + span, :]
        keep, dest = read_notes(ref, base + span, heads)
        keeps[place, :heads, :] = keep
        dests[place, :, :] = dest
    for ref, base, flip in late:
        place = side + flip - 2 * side * flip
        late_tokens[pl.ds(pl.multiple_of(place * span, span), span), :] = ref[
            base : base + span, :
        ]
        keep, _ = read_notes(ref, base + span, heads)
        keeps[shards - 2 + place, heads : 2 * heads, :] = keep


def follow_lists(facts_ref, keeps, coded, span):
    shards, rows, cache = keeps.shape
    heads = rows // 4
    row = lax.broadcasted_iota(jnp.int32, (rows, cache), 0)
    is_early = row < heads
    state = jnp.minimum(keeps[0], 0)
    own = state
    for shard in range(shards):
        own = jnp.where(facts_ref[1] == shard, state, own)
        late_first = (shards + shard - (shards - 2)) * span + 1
        fresh = jnp.where(is_early[:, :LANES], shard * span + 1, late_first)
        state = look_up(state, keeps[shard], fresh)
        if shard < shards - 2:
            state = jnp.where(is_early, state, 0)
        coded[shard] = split(state)
    return own


def find_slots(facts_ref, dests, coded, owner, slots):
    shards, halves, cache = dests.shape
    heads = coded.shape[1] // 8
    cap = slots.shape[0] // shards
    early = facts_ref[0]
    upper = marks(
        lax.broadcasted_iota(jnp.int32, (LANES, LANES), 0)
        <= lax.broadcasted_iota(jnp.int32, (LANES, LANES), 1)
    )
    place = lax.broadcasted_iota(jnp.int32, (cap, cache), 0).astype(jnp.float32) + 1.0
    total = jnp.zeros((shards, 1), jnp.float32)
    ranks = []
    for half in range(halves):
        named = (dests[:, half, :] == owner).astype(jnp.float32)
        parts = []
        for chunk in range(cache // LANES):
            part = named[:, chunk * LANES : (chunk + 1) * LANES]
            upto = dot(part.astype(jnp.bfloat16), upper)
            parts.append(jnp.where(part > 0, upto + total, 0.0))
            total = total + upto[:, LANES - 1 :]
        ranks.append(jnp.concatenate(parts, axis=1))
    rank_early = jnp.where(early == 0, ranks[0], ranks[1])
    rank_late = jnp.where(early == 0, ranks[1], ranks[0])
    across = ((1,), (1,))
    for shard in range(shards):
        found = dot(marks(rank_early[shard : shard + 1] == place), coded[shard], across)
        tokens = found[:, :heads] * 128.0 + found[:, 4 * heads : 5 * heads]
        if shard >= shards - 2:
            found = dot(marks(rank_late[shard : shard + 1] == place), coded[shard], across)
            tokens += found[:, heads : 2 * heads] * 128.0 + found[:, 5 * heads : 6 * heads]
        slots[shard * cap : (shard + 1) * cap, :] = tokens.astype(jnp.int32)


def place_rows(slots, tokens, late_tokens, out_ref):
    rows, heads = slots.shape
    reach = tokens.shape[0]
    bands = 4
    band = rows // bands
    for head in range(heads):
        lanes = slice(head * WIDTH, (head + 1) * WIDTH)
        for index in range(bands):
            part = slots[index * band : (index + 1) * band, head : head + 1]
            found = picked(part, 1, tokens[: (index + 1) * reach // bands, lanes])
            if index == bands - 1:
                found += picked(part, reach + 1, late_tokens[:, lanes])
            out_ref[index * band : (index + 1) * band, lanes] = found.astype(jnp.bfloat16)


def attend_columns(q_ref, prompt, head, rows, seen, out_ref, score_ref):
    span = q_ref.shape[1]
    total = rows.shape[0]
    cache = total - span
    group = q_ref.shape[2] // (score_ref.shape[1] * HEAD)
    keys, values = rows[:, :HEAD], rows[:, HEAD:]
    flat = jnp.transpose(values.astype(jnp.float32)).astype(jnp.bfloat16)
    lane = lax.broadcasted_iota(jnp.int32, (total, HEAD), 1)
    hidden = jnp.where(seen > 0, 0.0, -1e30)
    hidden = jnp.concatenate([hidden, jnp.zeros((span, 1), jnp.float32)], axis=0)
    hidden = jnp.where(lane == 0, hidden, 0.0).astype(jnp.bfloat16)
    keys = jnp.concatenate([keys, hidden], axis=1)
    ones = jnp.ones((2 * span, HEAD), jnp.bfloat16)
    causal = lax.broadcasted_iota(jnp.int32, (span, 2 * span), 0) <= lax.rem(
        lax.broadcasted_iota(jnp.int32, (span, 2 * span), 1), span
    )
    bias = jnp.where(causal, 0.0, -1e30)
    scale = math.log2(math.e) / math.sqrt(HEAD)
    mass = None
    for pair in range(group // 2):
        first = (head * group + 2 * pair) * HEAD
        query = jnp.concatenate(
            [
                q_ref[prompt, :, first : first + HEAD],
                q_ref[prompt, :, first + HEAD : first + 2 * HEAD],
            ],
            axis=0,
        )
        scores = dot(keys, jnp.concatenate([query, ones], axis=1), ((1,), (1,)))
        near = scores[cache:] + bias
        scores = jnp.concatenate([scores[:cache], near], axis=0) * scale
        peak = jnp.max(scores, axis=0, keepdims=True)
        expo = jnp.exp2(scores - peak)
        weights = expo * (1.0 / jnp.sum(expo, axis=0, keepdims=True))
        both = weights[:, :span] + weights[:, span:]
        mass = both if mass is None else mass + both
        mixed = jnp.transpose(dot(flat, weights.astype(jnp.bfloat16)))
        for member in range(2):
            lanes = slice(first + member * HEAD, first + (member + 1) * HEAD)
            out_ref[prompt, :, lanes] = mixed[member * span : (member + 1) * span].astype(
                jnp.bfloat16
            )
    score_ref[prompt, head : head + 1, :] = jnp.sum(jnp.transpose(mass), axis=0, keepdims=True)


def named_pieces(refs):
    step = refs[0].shape[0]
    early, late = [], []
    for flip in range(2):
        alone, beside, beyond = refs[3 * flip : 3 * flip + 3]
        early += [(alone, 0, 0, flip), (beside, 0, 1, flip), (beside, step, 3, flip)]
        early += [(beyond, 0, 2, flip)]
        late += [(beyond, step, flip)]
    return early, late


def own_kernel(facts_ref, q_ref, span_ref, *rest):
    refs, rest = rest[:6], rest[6:]
    out_ref, score_ref, mine_ref, other_ref = rest[:4]
    tokens, late_tokens, keeps, dests, coded, slots = rest[4:]
    span = q_ref.shape[1]
    shards, heads = keeps.shape[0], score_ref.shape[1]
    cache = keeps.shape[2]
    early, mine = facts_ref[0], facts_ref[1]
    sort_pieces(facts_ref, *named_pieces(refs), tokens, late_tokens, keeps, dests)
    own = follow_lists(facts_ref, keeps, coded, span)
    own = jnp.transpose(own.astype(jnp.float32)).astype(jnp.int32)
    for flip, ref in ((1, other_ref), (0, mine_ref)):
        find_slots(facts_ref, dests, coded, facts_ref[2] ^ flip, slots)
        place_rows(slots, tokens, late_tokens, ref)

    def run(which, prompt, source, first):
        for head in range(heads):
            lanes = slice(head * WIDTH, (head + 1) * WIDTH)
            column = own[:, which * heads + head : which * heads + head + 1]
            cached = picked(column, first, source[:, lanes]).astype(jnp.bfloat16)
            rows = jnp.concatenate([cached, span_ref[prompt, :, lanes]], axis=0)
            attend_columns(q_ref, prompt, head, rows, column, out_ref, score_ref)

    run(0, early, tokens, 1)
    late = 1 - early

    @pl.when(mine >= shards - 2)
    def _():
        run(1, late, late_tokens, shards * span + 1)

    @pl.when(mine < shards - 2)
    def _():
        out_ref[late] = jnp.zeros(out_ref.shape[1:], out_ref.dtype)
        score_ref[late] = jnp.zeros((heads, cache + span), jnp.float32)


def other_kernel(facts_ref, *rest):
    refs, rest = rest[:6], rest[6:]
    mine_ref, other_ref, tokens, late_tokens, keeps, dests, coded, slots = rest
    span = late_tokens.shape[0] // 2
    sort_pieces(facts_ref, *named_pieces(refs), tokens, late_tokens, keeps, dests)
    follow_lists(facts_ref, keeps, coded, span)
    for flip, ref in ((1, other_ref), (0, mine_ref)):
        find_slots(facts_ref, dests, coded, facts_ref[2] ^ flip, slots)
        place_rows(slots, tokens, late_tokens, ref)


def send(value, axis, pairs):
    return lax.ppermute(value, axis, pairs)


def spread(early_piece, late_piece, shards, columns):
    both = ("ctx", "kv")

    def along_z(turn):
        return send(early_piece, "ctx", [(i, (i + 2 * turn) % shards) for i in range(shards)])

    def across_y(value):
        return send(value, "ctx", [(i, i ^ 1) for i in range(shards)])

    def across_x(value):
        return send(value, "kv", [(i, i ^ 2) for i in range(columns)])

    def across_both(value):
        return send(value, both, [(i, i ^ columns ^ 2) for i in range(shards * columns)])

    level = lax.axis_index("ctx") // 2
    below, above = along_z(1), along_z(3)
    first = send(late_piece, "ctx", [(6, 2), (7, 3)])
    relay = jnp.where(level == 3, late_piece, first)
    second = send(relay, "ctx", [(6, 4), (7, 5), (2, 0), (3, 1)])
    late = jnp.where(level % 2 == 1, relay, second)
    groups = [
        early_piece,
        jnp.concatenate([below, above], axis=0),
        jnp.concatenate([along_z(2), late], axis=0),
    ]
    own = groups + [across_y(value) for value in groups]
    other = [across_x(value) for value in groups] + [across_both(value) for value in groups]
    return own, other


def local_in_planes(query, kv_rows, keep, dest, offsets):
    prompts, span, qwidth = query.shape
    shards, columns = lax.axis_size("ctx"), lax.axis_size("kv")
    width = kv_rows.shape[2]
    heads = width // WIDTH
    cache = keep.shape[3]
    rows = 2 * prompts * cache // columns
    mine, column = lax.axis_index("ctx"), lax.axis_index("kv")
    early = jnp.where(offsets[0] < offsets[1], 0, 1)
    facts = jnp.stack([early, mine, mine * columns + column, column]).astype(jnp.int32)
    vmem = pl.BlockSpec(memory_space=pltpu.VMEM)
    smem = pl.BlockSpec(memory_space=pltpu.SMEM)
    params = pltpu.CompilerParams(vmem_limit_bytes=PLANE_BYTES)
    piece = jax.ShapeDtypeStruct((span + NOTES, width), jnp.bfloat16)
    early_piece, late_piece = pl.pallas_call(
        prepare_kernel,
        out_shape=(piece, piece),
        in_specs=[smem, vmem, vmem, vmem],
        out_specs=(vmem, vmem),
        compiler_params=params,
    )(offsets, kv_rows, keep[:, 0], dest.reshape(prompts, cache))
    own, other = spread(early_piece, late_piece, shards, columns)

    scratch = [
        pltpu.VMEM((shards * span, width), jnp.bfloat16),
        pltpu.VMEM((2 * span, width), jnp.bfloat16),
        pltpu.VMEM((shards, 4 * heads, cache), jnp.int32),
        pltpu.VMEM((shards, prompts, cache), jnp.int32),
        pltpu.VMEM((shards, 8 * heads, cache), jnp.bfloat16),
        pltpu.VMEM((rows, heads), jnp.int32),
    ]
    block = jax.ShapeDtypeStruct((rows, width), jnp.bfloat16)
    attention, row_scores, near, near_sent = pl.pallas_call(
        own_kernel,
        out_shape=(
            jax.ShapeDtypeStruct((prompts, span, qwidth), jnp.bfloat16),
            jax.ShapeDtypeStruct((prompts, heads, cache + span), jnp.float32),
            block,
            block,
        ),
        in_specs=[smem] + [vmem] * 8,
        out_specs=(vmem,) * 4,
        scratch_shapes=scratch,
        compiler_params=params,
        cost_estimate=pl.CostEstimate(
            flops=10**10, bytes_accessed=10**7, transcendentals=5 * 10**6
        ),
    )(facts, query, kv_rows, *own)
    far, far_sent = pl.pallas_call(
        other_kernel,
        out_shape=(block, block),
        in_specs=[smem] + [vmem] * 6,
        out_specs=(vmem,) * 2,
        scratch_shapes=scratch,
        compiler_params=params,
        cost_estimate=pl.CostEstimate(flops=3 * 10**9, bytes_accessed=10**7, transcendentals=0),
    )(facts, *other)
    siblings = [(i, i ^ 1) for i in range(columns)]
    blocks = [near, send(near_sent, "kv", siblings), far, send(far_sent, "kv", siblings)]
    owner_cache = pl.pallas_call(
        assemble_kernel,
        grid_spec=pltpu.PrefetchScalarGridSpec(
            num_scalar_prefetch=1,
            grid=(columns,),
            in_specs=[pl.BlockSpec((rows, width), lambda g, w: (0, 0))] * columns,
            out_specs=pl.BlockSpec((rows, width), lambda g, w: (0, w[3] ^ g)),
        ),
        out_shape=jax.ShapeDtypeStruct((rows, columns * width), jnp.bfloat16),
        compiler_params=params,
        cost_estimate=pl.CostEstimate(flops=0, bytes_accessed=4 * 10**6, transcendentals=0),
    )(facts, *blocks)
    return (attention, row_scores, owner_cache)


def solution(mesh):
    placed = (
        P(None, "ctx", "kv"),
        P(None, "ctx", "kv"),
        P(None, "ctx", "kv", None),
        P("ctx", None),
        P(),
    )
    in_planes = mesh.shape["ctx"] == 8 and mesh.shape["kv"] == 4
    return jax.shard_map(
        local_in_planes if in_planes else local,
        mesh=mesh,
        in_specs=placed,
        out_specs=(P(None, "ctx", "kv"), P(None, "kv", "ctx"), P(("ctx", "kv"), None)),
        check_vma=False,
    )
```

```python
import functools
import math

import jax
import jax.numpy as jnp
from jax import lax
from jax.experimental import pallas as pl
from jax.experimental.pallas import tpu as pltpu
from jax.sharding import PartitionSpec as P

HEAD = 128
WIDTH = 2 * HEAD
LANES = 128
VMEM_BYTES = 56 * 1024 * 1024
PLANE_BYTES = 28 * 1024 * 1024
NOTES = 16


def look_up(state, keep, fresh):
    tiles = state.shape[1] // LANES
    parts = []
    for tile in range(tiles):
        wanted = keep[:, tile * LANES : (tile + 1) * LANES]
        high = wanted >> 7
        low = wanted & 127
        found = jnp.where(high >= tiles, fresh + wanted - state.shape[1], 0)
        for source in range(tiles):
            held = state[:, source * LANES : (source + 1) * LANES]
            moved = jnp.take_along_axis(held, low, axis=1, mode="promise_in_bounds")
            found = jnp.where(high == source, moved, found)
        parts.append(found)
    return jnp.concatenate(parts, axis=1)


def split(state):
    both = jnp.concatenate([state >> 7, state & 127], axis=0)
    return both.astype(jnp.float32).astype(jnp.bfloat16)


def index_kernel(
    where_ref, keep_early_ref, keep_late_ref, dest_ref, slot_ref, row_ref, column_ref, coded
):
    shards, heads, cache = keep_early_ref.shape
    cap = slot_ref.shape[0] // shards
    span = LANES
    early, mine, me = where_ref[0], where_ref[1], where_ref[2]
    empty = jnp.minimum(keep_early_ref[0], 0)

    def follow(shard, carry):
        state, own = carry
        own = jnp.where(shard == mine, state, own)
        state = look_up(state, keep_early_ref[shard], shard * span + 1)
        coded[shard] = split(state)
        return state, own

    _, own_early = lax.fori_loop(0, shards, follow, (empty, empty), unroll=shards <= 8)
    base = shards * span + 1
    late_first = look_up(empty, keep_late_ref[0], base)
    late_second = look_up(late_first, keep_late_ref[1], base + span)
    own_late = jnp.where(mine == shards - 1, late_first, 0)
    for index, own in enumerate((own_early, own_late)):
        row_ref[index] = own
        column_ref[index] = jnp.transpose(own.astype(jnp.float32)).astype(jnp.int32)

    named = (dest_ref[...] == me).astype(jnp.float32)
    chunks = named.shape[1] // LANES
    upper = (
        lax.broadcasted_iota(jnp.int32, (LANES, LANES), 0)
        <= lax.broadcasted_iota(jnp.int32, (LANES, LANES), 1)
    ).astype(jnp.float32).astype(jnp.bfloat16)
    total = jnp.zeros((shards, 1), jnp.float32)
    ranks = []
    for chunk in range(chunks):
        part = named[:, chunk * LANES : (chunk + 1) * LANES]
        upto = jnp.dot(part.astype(jnp.bfloat16), upper, preferred_element_type=jnp.float32)
        ranks.append(jnp.where(part > 0, upto + total, 0.0))
        total = total + upto[:, LANES - 1 :]
    low_half = jnp.concatenate(ranks[: chunks // 2], axis=1)
    high_half = jnp.concatenate(ranks[chunks // 2 :], axis=1)
    rank_early = jnp.where(early == 0, low_half, high_half)
    rank_late = jnp.where(early == 0, high_half, low_half)
    place = lax.broadcasted_iota(jnp.int32, (cap, cache), 0).astype(jnp.float32) + 1.0
    contract = (((1,), (1,)), ((), ()))
    for shard in range(shards):
        pick = (rank_early[shard : shard + 1] == place).astype(jnp.float32).astype(jnp.bfloat16)
        found = lax.dot_general(pick, coded[shard], contract, preferred_element_type=jnp.float32)
        if shard >= shards - 2:
            state = late_first if shard == shards - 2 else late_second
            pick = (rank_late[shard : shard + 1] == place).astype(jnp.float32).astype(jnp.bfloat16)
            found += lax.dot_general(
                pick, split(state), contract, preferred_element_type=jnp.float32
            )
        tokens = found[:, :heads] * 128.0 + found[:, heads:]
        slot_ref[shard * cap : (shard + 1) * cap, :] = tokens.astype(jnp.int32)


def column_of(table, head):
    lane = lax.broadcasted_iota(jnp.int32, table.shape, 1)
    return jnp.sum(
        jnp.where(lane == head, table, 0).astype(jnp.float32), axis=1, keepdims=True
    ).astype(jnp.int32)


def picked(column, first, tokens):
    number = lax.broadcasted_iota(jnp.int32, (column.shape[0], tokens.shape[0]), 1) + first
    table = (column == number).astype(jnp.float32).astype(jnp.bfloat16)
    return jnp.dot(table, tokens, preferred_element_type=jnp.float32)


def attend(q_ref, prompt, keys, values, seen, out_ref, score_ref, head):
    span = q_ref.shape[1]
    cache = seen.shape[1]
    group = q_ref.shape[2] // HEAD
    causal = lax.broadcasted_iota(jnp.int32, (span, span), 1) <= lax.broadcasted_iota(
        jnp.int32, (span, span), 0
    )
    bias = jnp.concatenate(
        [
            jnp.broadcast_to(jnp.where(seen > 0, 0.0, -1e30), (span, cache)),
            jnp.where(causal, 0.0, -1e30),
        ],
        axis=1,
    )
    scale = math.log2(math.e) / math.sqrt(HEAD)
    mass = jnp.zeros((1, cache + span), jnp.float32)
    for member in range(group):
        query = q_ref[prompt, :, member * HEAD : (member + 1) * HEAD]
        scores = lax.dot_general(
            query, keys, (((1,), (1,)), ((), ())), preferred_element_type=jnp.float32
        )
        scores = scores + bias
        peak = jnp.max(scores, axis=1, keepdims=True)
        expo = jnp.exp2((scores - peak) * scale)
        weights = expo * (1.0 / jnp.sum(expo, axis=1, keepdims=True))
        mass = mass + jnp.sum(weights, axis=0, keepdims=True)
        mixed = jnp.dot(weights.astype(jnp.bfloat16), values, preferred_element_type=jnp.float32)
        out_ref[prompt, :, member * HEAD : (member + 1) * HEAD] = mixed.astype(jnp.bfloat16)
    score_ref[prompt, pl.ds(head, 1), :] = mass


def attention_kernel(
    where_ref, q_ref, span_ref, early_ref, late_ref, row_ref, column_ref, out_ref, score_ref
):
    early, mine, column, shards = where_ref[0], where_ref[1], where_ref[3], early_ref.shape[0]
    span = q_ref.shape[1]
    late = 1 - early
    local_head = pl.program_id(0)
    head = column * pl.num_programs(0) + local_head

    def run(which, prompt, tokens, first):
        chosen = column_of(column_ref[which], head)
        cached = picked(chosen, first, tokens).astype(jnp.bfloat16)
        rows = jnp.concatenate([cached, span_ref[prompt]], axis=0)
        seen = row_ref[which, pl.ds(head, 1), :]
        attend(
            q_ref, prompt, rows[:, :HEAD], rows[:, HEAD:], seen, out_ref, score_ref, local_head
        )

    run(0, early, early_ref[:, 0].reshape(shards * span, WIDTH), 1)

    @pl.when(mine >= shards - 2)
    def _():
        run(1, late, late_ref[0, 0], shards * span + 1)

    @pl.when(mine < shards - 2)
    def _():
        out_ref[late] = jnp.zeros(out_ref.shape[1:], out_ref.dtype)
        score_ref[late, pl.ds(local_head, 1), :] = jnp.zeros((1, score_ref.shape[2]), jnp.float32)


def owner_kernel(slot_ref, early_ref, late_ref, out_ref):
    shards, _, span, width = early_ref.shape
    rows = out_ref.shape[0]
    chosen = column_of(slot_ref[...], pl.program_id(0))
    bands = 4
    band = rows // bands
    reach = shards * span // bands
    tokens = early_ref[:, 0].reshape(shards * span, width)
    for index in range(bands):
        part = chosen[index * band : (index + 1) * band]
        found = picked(part, 1, tokens[: (index + 1) * reach])
        if index == bands - 1:
            found += picked(part, shards * span + 1, late_ref[:, 0].reshape(2 * span, width))
        out_ref[index * band : (index + 1) * band, :] = found.astype(jnp.bfloat16)


def local(query, kv_rows, keep, dest, offsets):
    prompts, span, qwidth = query.shape
    shards, columns = lax.axis_size("ctx"), lax.axis_size("kv")
    width = kv_rows.shape[2]
    heads_dev = width // WIDTH
    heads = heads_dev * columns
    cache = keep.shape[3]
    owners = shards * columns
    cap = 2 * prompts * cache // owners
    mine, column = lax.axis_index("ctx"), lax.axis_index("kv")
    early = jnp.where(offsets[0] < offsets[1], 0, 1).astype(jnp.int32)
    facts = jnp.stack([early, mine, mine * columns + column, column]).astype(jnp.int32)

    swap = early == 1
    ordered_kv = jnp.where(swap, kv_rows[::-1], kv_rows)
    ordered_keep = jnp.where(swap, keep[::-1, 0], keep[:, 0])
    digits = jnp.stack([ordered_keep >> 7, ordered_keep & 127], axis=1)
    share = dest.shape[0] // columns
    own_dest = lax.dynamic_slice_in_dim(dest[:, 0], column * share, share)
    facts_rows = jnp.concatenate([digits.reshape(-1), own_dest]).astype(jnp.bfloat16)
    used = facts_rows.shape[0]
    room = 16 * width
    facts_rows = jnp.concatenate([facts_rows, jnp.zeros((room - used,), jnp.bfloat16)])
    payload = jnp.concatenate(
        [ordered_kv.reshape(prompts * span, width), facts_rows.reshape(16, width)], axis=0
    )
    whole = lax.all_gather(payload, ("ctx", "kv")).reshape(
        shards, columns, prompts * span + 16, width
    )

    told = whole[:, :, prompts * span :, :].reshape(shards, columns, room).astype(jnp.int32)
    kept = told[:, :, : prompts * 2 * heads_dev * cache].reshape(
        shards, columns, prompts, 2, heads_dev, cache
    )
    kept = kept[:, :, :, 0] * 128 + kept[:, :, :, 1]
    kept = jnp.transpose(kept, (2, 0, 1, 3, 4)).reshape(prompts, shards, heads, cache)
    whole_dest = told[:, :, used - share : used].reshape(shards, columns * share)

    vmem = pl.BlockSpec(memory_space=pltpu.VMEM)
    smem = pl.BlockSpec(memory_space=pltpu.SMEM)
    params = pltpu.CompilerParams(vmem_limit_bytes=VMEM_BYTES)
    slots, rows, cols = pl.pallas_call(
        index_kernel,
        out_shape=(
            jax.ShapeDtypeStruct((shards * cap, heads), jnp.int32),
            jax.ShapeDtypeStruct((2, heads, cache), jnp.int32),
            jax.ShapeDtypeStruct((2, cache, heads), jnp.int32),
        ),
        in_specs=[smem, vmem, vmem, vmem],
        out_specs=(vmem, vmem, vmem),
        scratch_shapes=[pltpu.VMEM((shards, 2 * heads, cache), jnp.bfloat16)],
        compiler_params=params,
    )(facts, kept[0], kept[1, shards - 2 :], whole_dest)

    group_width = qwidth // heads_dev
    attention, row_scores = pl.pallas_call(
        attention_kernel,
        grid_spec=pltpu.PrefetchScalarGridSpec(
            num_scalar_prefetch=1,
            grid=(heads_dev,),
            in_specs=[
                pl.BlockSpec((prompts, span, group_width), lambda h, w: (0, 0, h)),
                pl.BlockSpec((prompts, span, WIDTH), lambda h, w: (0, 0, h)),
                pl.BlockSpec((shards, 1, span, WIDTH), lambda h, w: (0, w[3], 0, h)),
                pl.BlockSpec((1, 1, span, WIDTH), lambda h, w: (shards - 2, w[3], 1, h)),
                pl.BlockSpec((2, heads, cache), lambda h, w: (0, 0, 0)),
                pl.BlockSpec((2, cache, heads), lambda h, w: (0, 0, 0)),
            ],
            out_specs=(
                pl.BlockSpec((prompts, span, group_width), lambda h, w: (0, 0, h)),
                pl.BlockSpec((prompts, heads_dev, cache + span), lambda h, w: (0, 0, 0)),
            ),
        ),
        out_shape=(
            jax.ShapeDtypeStruct((prompts, span, qwidth), jnp.bfloat16),
            jax.ShapeDtypeStruct((prompts, heads_dev, cache + span), jnp.float32),
        ),
        compiler_params=params,
    )(facts, query, kv_rows, whole, whole, rows, cols)

    owner_cache = pl.pallas_call(
        owner_kernel,
        grid=(heads,),
        in_specs=[
            pl.BlockSpec((shards * cap, heads), lambda g: (0, 0)),
            pl.BlockSpec(
                (shards, 1, span, WIDTH), lambda g: (0, g // heads_dev, 0, g % heads_dev)
            ),
            pl.BlockSpec(
                (2, 1, span, WIDTH),
                lambda g: (shards // 2 - 1, g // heads_dev, 1, g % heads_dev),
            ),
        ],
        out_specs=pl.BlockSpec((shards * cap, WIDTH), lambda g: (0, g)),
        out_shape=jax.ShapeDtypeStruct((shards * cap, heads * WIDTH), jnp.bfloat16),
        compiler_params=params,
    )(slots, whole, whole)
    return (attention, row_scores, owner_cache)


def assemble_kernel(facts_ref, *refs):
    out_ref = refs[-1]
    for index, ref in enumerate(refs[:-1]):

        @pl.when(pl.program_id(0) == index)
        def _(ref=ref):
            out_ref[...] = ref[...]


def dot(a, b, dims=((1,), (0,))):
    return lax.dot_general(a, b, (dims, ((), ())), preferred_element_type=jnp.float32)


def marks(table):
    return table.astype(jnp.float32).astype(jnp.bfloat16)


def prepare_kernel(facts_ref, kv_ref, keep_ref, dest_ref, both_ref, early_ref):
    span, width = kv_ref.shape[1], kv_ref.shape[2]
    step = early_ref.shape[0]
    early = facts_ref[0]
    targets = ((early, both_ref, 0), (early, early_ref, 0), (1 - early, both_ref, step))
    for which, ref, base in targets:
        ref[base : base + span, :] = kv_ref[which]
        keep = keep_ref[which]
        rows = jnp.concatenate(
            [
                (keep >> 7).astype(jnp.float32),
                (keep & 127).astype(jnp.float32),
                dest_ref[...].astype(jnp.float32),
                jnp.zeros((NOTES - 3 * keep.shape[0], width), jnp.float32),
            ],
            axis=0,
        )
        ref[base + span : base + step, :] = rows.astype(jnp.bfloat16)


def join_first_kernel(below_ref, above_ref, both_ref, *rest):
    out_ref, on_ref = rest[-2:]
    step = both_ref.shape[0] // 2
    out_ref[:step, :] = below_ref[:step, :]
    out_ref[step:, :] = above_ref[:step, :]
    on_ref[...] = both_ref[...]


def join_second_kernel(facts_ref, beyond_ref, below_ref, above_ref, both_ref, *rest):
    out_ref = rest[-1]
    step = both_ref.shape[0] // 2
    level = facts_ref[1] // 2
    out_ref[:step, :] = beyond_ref[:step, :]
    for index, ref in enumerate((below_ref, beyond_ref, above_ref, both_ref)):

        @pl.when(level == index)
        def _(ref=ref):
            out_ref[step:, :] = ref[step:, :]


def read_notes(ref, base, heads):
    rows = ref[base : base + NOTES, :].astype(jnp.float32).astype(jnp.int32)
    return rows[:heads] * 128 + rows[heads : 2 * heads], rows[2 * heads : 3 * heads]


def sort_pieces(facts_ref, early, late, tokens, late_tokens, keeps, dests):
    mine = facts_ref[1]
    shards = len(early)
    heads = keeps.shape[1] // 4
    span = late_tokens.shape[0] // 2
    side = lax.rem(mine, 2)
    keeps[...] = jnp.zeros(keeps.shape, jnp.int32)
    for ref, base, turn, flip in early:
        place = lax.rem(mine - 2 * turn + shards, shards)
        if flip:
            place = place + 1 - 2 * side
        tokens[pl.ds(pl.multiple_of(place * span, span), span), :] = ref[base : base + span, :]
        keep, dest = read_notes(ref, base + span, heads)
        keeps[place, :heads, :] = keep
        dests[place, :, :] = dest
    for ref, base, flip in late:
        place = side + flip - 2 * side * flip
        late_tokens[pl.ds(pl.multiple_of(place * span, span), span), :] = ref[
            base : base + span, :
        ]
        keep, _ = read_notes(ref, base + span, heads)
        keeps[shards - 2 + place, heads : 2 * heads, :] = keep


def follow_lists(facts_ref, keeps, coded, span):
    shards, rows, cache = keeps.shape
    heads = rows // 4
    row = lax.broadcasted_iota(jnp.int32, (rows, cache), 0)
    is_early = row < heads
    state = jnp.minimum(keeps[0], 0)
    own = state
    for shard in range(shards):
        own = jnp.where(facts_ref[1] == shard, state, own)
        late_first = (shards + shard - (shards - 2)) * span + 1
        fresh = jnp.where(is_early[:, :LANES], shard * span + 1, late_first)
        state = look_up(state, keeps[shard], fresh)
        if shard < shards - 2:
            state = jnp.where(is_early, state, 0)
        coded[shard] = split(state)
    return own


def find_slots(facts_ref, dests, coded, owner, slots):
    shards, halves, cache = dests.shape
    heads = coded.shape[1] // 8
    cap = slots.shape[0] // shards
    early = facts_ref[0]
    upper = marks(
        lax.broadcasted_iota(jnp.int32, (LANES, LANES), 0)
        <= lax.broadcasted_iota(jnp.int32, (LANES, LANES), 1)
    )
    place = lax.broadcasted_iota(jnp.int32, (cap, cache), 0).astype(jnp.float32) + 1.0
    total = jnp.zeros((shards, 1), jnp.float32)
    ranks = []
    for half in range(halves):
        named = (dests[:, half, :] == owner).astype(jnp.float32)
        parts = []
        for chunk in range(cache // LANES):
            part = named[:, chunk * LANES : (chunk + 1) * LANES]
            upto = dot(part.astype(jnp.bfloat16), upper)
            parts.append(jnp.where(part > 0, upto + total, 0.0))
            total = total + upto[:, LANES - 1 :]
        ranks.append(jnp.concatenate(parts, axis=1))
    rank_early = jnp.where(early == 0, ranks[0], ranks[1])
    rank_late = jnp.where(early == 0, ranks[1], ranks[0])
    across = ((1,), (1,))
    for shard in range(shards):
        found = dot(marks(rank_early[shard : shard + 1] == place), coded[shard], across)
        tokens = found[:, :heads] * 128.0 + found[:, 4 * heads : 5 * heads]
        if shard >= shards - 2:
            found = dot(marks(rank_late[shard : shard + 1] == place), coded[shard], across)
            tokens += found[:, heads : 2 * heads] * 128.0 + found[:, 5 * heads : 6 * heads]
        slots[shard * cap : (shard + 1) * cap, :] = tokens.astype(jnp.int32)


def place_rows(slots, tokens, late_tokens, out_ref):
    rows, heads = slots.shape
    reach = tokens.shape[0]
    bands = 4
    band = rows // bands
    for head in range(heads):
        lanes = slice(head * WIDTH, (head + 1) * WIDTH)
        for index in range(bands):
            part = slots[index * band : (index + 1) * band, head : head + 1]
            found = picked(part, 1, tokens[: (index + 1) * reach // bands, lanes])
            if index == bands - 1:
                found += picked(part, reach + 1, late_tokens[:, lanes])
            out_ref[index * band : (index + 1) * band, lanes] = found.astype(jnp.bfloat16)


def attend_columns(q_ref, head, rows, seen, out_ref, score_ref):
    span = q_ref.shape[1]
    total = rows.shape[0]
    cache = total - span
    group = q_ref.shape[2] // (score_ref.shape[1] * HEAD)
    keys, values = rows[:, :HEAD], rows[:, HEAD:]
    flat = jnp.transpose(values.astype(jnp.float32)).astype(jnp.bfloat16)
    lane = lax.broadcasted_iota(jnp.int32, (total, HEAD), 1)
    hidden = jnp.where(seen > 0, 0.0, -1e30)
    hidden = jnp.concatenate([hidden, jnp.zeros((span, 1), jnp.float32)], axis=0)
    hidden = jnp.where(lane == 0, hidden, 0.0).astype(jnp.bfloat16)
    keys = jnp.concatenate([keys, hidden], axis=1)
    ones = jnp.ones((2 * span, HEAD), jnp.bfloat16)
    causal = lax.broadcasted_iota(jnp.int32, (span, 2 * span), 0) <= lax.rem(
        lax.broadcasted_iota(jnp.int32, (span, 2 * span), 1), span
    )
    bias = jnp.where(causal, 0.0, -1e30)
    scale = math.log2(math.e) / math.sqrt(HEAD)
    mass = None
    for pair in range(group // 2):
        first = (head * group + 2 * pair) * HEAD
        query = jnp.concatenate(
            [
                q_ref[0, :, first : first + HEAD],
                q_ref[0, :, first + HEAD : first + 2 * HEAD],
            ],
            axis=0,
        )
        scores = dot(keys, jnp.concatenate([query, ones], axis=1), ((1,), (1,)))
        near = scores[cache:] + bias
        scores = jnp.concatenate([scores[:cache], near], axis=0) * scale
        peak = jnp.max(scores, axis=0, keepdims=True)
        expo = jnp.exp2(scores - peak)
        weights = expo * (1.0 / jnp.sum(expo, axis=0, keepdims=True))
        both = weights[:, :span] + weights[:, span:]
        mass = both if mass is None else mass + both
        mixed = jnp.transpose(dot(flat, weights.astype(jnp.bfloat16)))
        for member in range(2):
            lanes = slice(first + member * HEAD, first + (member + 1) * HEAD)
            out_ref[0, :, lanes] = mixed[member * span : (member + 1) * span].astype(
                jnp.bfloat16
            )
    score_ref[0, head : head + 1, :] = jnp.sum(jnp.transpose(mass), axis=0, keepdims=True)


def named_pieces(refs):
    step = refs[1].shape[0] // 2
    early, late = [], []
    for flip in range(2):
        alone, beside, beyond = refs[3 * flip : 3 * flip + 3]
        early += [(alone, 0, 0, flip), (beside, 0, 1, flip), (beside, step, 3, flip)]
        early += [(beyond, 0, 2, flip)]
        late += [(beyond, step, flip)]
    return early, late


def late_kernel(facts_ref, q_ref, both_ref, beside_ref, out_ref, score_ref):
    mine, shards = facts_ref[1], facts_ref[5]
    heads, cache = score_ref.shape[1], score_ref.shape[2] - q_ref.shape[1]
    span = q_ref.shape[1]
    step = both_ref.shape[0] // 2

    @pl.when(mine >= shards - 2)
    def _():
        keep, _ = read_notes(beside_ref, step + span, heads)
        state = jnp.where(keep >= cache, keep - cache + 1, 0)
        state = jnp.where(mine == shards - 1, state, 0).astype(jnp.float32)
        state = jnp.concatenate([state, jnp.zeros((8 - heads, cache), jnp.float32)], axis=0)
        columns = jnp.transpose(state).astype(jnp.int32)
        for head in range(heads):
            lanes = slice(head * WIDTH, (head + 1) * WIDTH)
            column = columns[:, head : head + 1]
            cached = picked(column, 1, beside_ref[step : step + span, lanes])
            rows = jnp.concatenate(
                [cached.astype(jnp.bfloat16), both_ref[step : step + span, lanes]], axis=0
            )
            attend_columns(q_ref, head, rows, column, out_ref, score_ref)

    @pl.when(mine < shards - 2)
    def _():
        out_ref[...] = jnp.zeros(out_ref.shape, out_ref.dtype)
        score_ref[...] = jnp.zeros(score_ref.shape, jnp.float32)


def own_kernel(facts_ref, q_ref, *rest):
    refs, rest = rest[:6], rest[8:]
    out_ref, score_ref, mine_ref, other_ref = rest[:4]
    tokens, late_tokens, keeps, dests, coded, slots = rest[4:]
    span = q_ref.shape[1]
    heads = score_ref.shape[1]
    sort_pieces(facts_ref, *named_pieces(refs), tokens, late_tokens, keeps, dests)
    own = follow_lists(facts_ref, keeps, coded, span)
    own = jnp.transpose(own.astype(jnp.float32)).astype(jnp.int32)
    for flip, ref in ((1, other_ref), (0, mine_ref)):
        find_slots(facts_ref, dests, coded, facts_ref[2] ^ flip, slots)
        place_rows(slots, tokens, late_tokens, ref)
    for head in range(heads):
        lanes = slice(head * WIDTH, (head + 1) * WIDTH)
        column = own[:, head : head + 1]
        cached = picked(column, 1, tokens[:, lanes]).astype(jnp.bfloat16)
        rows = jnp.concatenate([cached, refs[0][:span, lanes]], axis=0)
        attend_columns(q_ref, head, rows, column, out_ref, score_ref)


def other_kernel(facts_ref, *rest):
    refs, rest = rest[:6], rest[6:]
    mine_ref, other_ref, tokens, late_tokens, keeps, dests, coded, slots = rest
    span = late_tokens.shape[0] // 2
    sort_pieces(facts_ref, *named_pieces(refs), tokens, late_tokens, keeps, dests)
    follow_lists(facts_ref, keeps, coded, span)
    for flip, ref in ((1, other_ref), (0, mine_ref)):
        find_slots(facts_ref, dests, coded, facts_ref[2] ^ flip, slots)
        place_rows(slots, tokens, late_tokens, ref)


def send(value, axis, pairs):
    return lax.ppermute(value, axis, pairs)


def local_in_planes(query, kv_rows, keep, dest, offsets):
    prompts, span, qwidth = query.shape
    shards, columns = lax.axis_size("ctx"), lax.axis_size("kv")
    width = kv_rows.shape[2]
    heads = width // WIDTH
    cache = keep.shape[3]
    rows = 2 * prompts * cache // columns
    mine, column = lax.axis_index("ctx"), lax.axis_index("kv")
    early = jnp.where(offsets[0] < offsets[1], 0, 1)
    facts = jnp.stack(
        [early, mine, mine * columns + column, column, 1 - early, shards]
    ).astype(jnp.int32)
    vmem = pl.BlockSpec(memory_space=pltpu.VMEM)
    smem = pl.BlockSpec(memory_space=pltpu.SMEM)
    anywhere = pl.BlockSpec(memory_space=pl.ANY)
    params = pltpu.CompilerParams(vmem_limit_bytes=PLANE_BYTES)

    def cost(flops, moved):
        return pl.CostEstimate(flops=flops, bytes_accessed=moved, transcendentals=0)

    def along_z(value, turn):
        return send(value, "ctx", [(i, (i + 2 * turn) % shards) for i in range(shards)])

    def across_y(value):
        return send(value, "ctx", [(i, i ^ 1) for i in range(shards)])

    def across_x(value):
        return send(value, "kv", [(i, i ^ 2) for i in range(columns)])

    def across_both(value):
        pairs = [(i, i ^ columns ^ 2) for i in range(shards * columns)]
        return send(value, ("ctx", "kv"), pairs)

    def across_core(value):
        return send(value, "kv", [(i, i ^ 1) for i in range(columns)])

    step = span + NOTES
    one = jax.ShapeDtypeStruct((step, width), jnp.bfloat16)
    two = jax.ShapeDtypeStruct((2 * step, width), jnp.bfloat16)
    both, early_piece = pl.pallas_call(
        prepare_kernel,
        out_shape=(two, one),
        in_specs=[smem, vmem, vmem, vmem],
        out_specs=(vmem, vmem),
        compiler_params=params,
    )(facts, kv_rows, keep[:, 0], dest.reshape(prompts, cache))

    below, above = along_z(both, 1), along_z(both, 3)
    y_own, x_own, d_own = across_y(both), across_x(early_piece), across_both(early_piece)
    beside, going = pl.pallas_call(
        join_first_kernel,
        out_shape=(two, two),
        in_specs=[vmem] * 3 + [anywhere] * 3,
        out_specs=(vmem, vmem),
        compiler_params=params,
        cost_estimate=cost(0, 10**6),
    )(below, above, both, y_own, x_own, d_own)
    beyond = along_z(going, 2)
    y_beside, x_beside, d_beside = across_y(beside), across_x(beside), across_both(beside)

    attention_shape = jax.ShapeDtypeStruct((prompts, span, qwidth), jnp.bfloat16)
    score_shape = jax.ShapeDtypeStruct((prompts, heads, cache + span), jnp.float32)

    def prompt_specs(where):
        return (
            pl.BlockSpec((1, span, qwidth), lambda i, w: (w[where], 0, 0)),
            pl.BlockSpec((1, heads, cache + span), lambda i, w: (w[where], 0, 0)),
        )

    attention, row_scores = pl.pallas_call(
        late_kernel,
        grid_spec=pltpu.PrefetchScalarGridSpec(
            num_scalar_prefetch=1,
            grid=(1,),
            in_specs=[prompt_specs(4)[0], vmem, vmem],
            out_specs=prompt_specs(4),
        ),
        out_shape=(attention_shape, score_shape),
        compiler_params=params,
        cost_estimate=cost(5 * 10**9, 10**7),
    )(facts, query, both, y_own)

    far_end = pl.pallas_call(
        join_second_kernel,
        out_shape=two,
        in_specs=[smem] + [vmem] * 4 + [anywhere] * 4,
        out_specs=vmem,
        compiler_params=params,
        cost_estimate=cost(0, 10**6),
    )(facts, beyond, below, above, both, y_beside, x_beside, d_beside, row_scores)
    y_end, x_end, d_end = across_y(far_end), across_x(far_end), across_both(far_end)
    own = [both, beside, far_end, y_own, y_beside, y_end]
    other = [x_own, x_beside, x_end, d_own, d_beside, d_end]

    scratch = [
        pltpu.VMEM((shards * span, width), jnp.bfloat16),
        pltpu.VMEM((2 * span, width), jnp.bfloat16),
        pltpu.VMEM((shards, 4 * heads, cache), jnp.int32),
        pltpu.VMEM((shards, prompts, cache), jnp.int32),
        pltpu.VMEM((shards, 8 * heads, cache), jnp.bfloat16),
        pltpu.VMEM((rows, heads), jnp.int32),
    ]
    block = jax.ShapeDtypeStruct((rows, width), jnp.bfloat16)
    attention, row_scores, near, near_sent = pl.pallas_call(
        own_kernel,
        grid_spec=pltpu.PrefetchScalarGridSpec(
            num_scalar_prefetch=1,
            grid=(1,),
            in_specs=[prompt_specs(0)[0]] + [vmem] * 6 + [anywhere] * 2,
            out_specs=prompt_specs(0) + (vmem, vmem),
            scratch_shapes=scratch,
        ),
        out_shape=(attention_shape, score_shape, block, block),
        input_output_aliases={8: 0, 9: 1},
        compiler_params=params,
        cost_estimate=cost(10**10, 10**7),
    )(facts, query, *own, attention, row_scores)
    far, far_sent = pl.pallas_call(
        other_kernel,
        out_shape=(block, block),
        in_specs=[smem] + [vmem] * 6,
        out_specs=(vmem,) * 2,
        scratch_shapes=scratch,
        compiler_params=params,
        cost_estimate=cost(3 * 10**9, 10**7),
    )(facts, *other)
    blocks = [near, across_core(near_sent), far, across_core(far_sent)]
    owner_cache = pl.pallas_call(
        assemble_kernel,
        grid_spec=pltpu.PrefetchScalarGridSpec(
            num_scalar_prefetch=1,
            grid=(columns,),
            in_specs=[pl.BlockSpec((rows, width), lambda g, w: (0, 0))] * columns,
            out_specs=pl.BlockSpec((rows, width), lambda g, w: (0, w[3] ^ g)),
        ),
        out_shape=jax.ShapeDtypeStruct((rows, columns * width), jnp.bfloat16),
        compiler_params=params,
        cost_estimate=cost(0, 4 * 10**6),
    )(facts, *blocks)
    return (attention, row_scores, owner_cache)


def solution(mesh):
    placed = (
        P(None, "ctx", "kv"),
        P(None, "ctx", "kv"),
        P(None, "ctx", "kv", None),
        P("ctx", None),
        P(),
    )
    in_planes = mesh.shape["ctx"] == 8 and mesh.shape["kv"] == 4
    return jax.shard_map(
        local_in_planes if in_planes else local,
        mesh=mesh,
        in_specs=placed,
        out_specs=(P(None, "ctx", "kv"), P(None, "kv", "ctx"), P(("ctx", "kv"), None)),
        check_vma=False,
    )
```

```python
import functools
import math

import jax
import jax.numpy as jnp
from jax import lax
from jax.experimental import pallas as pl
from jax.experimental.pallas import tpu as pltpu
from jax.sharding import PartitionSpec as P

HEAD = 128
WIDTH = 2 * HEAD
LANES = 128
VMEM_BYTES = 56 * 1024 * 1024
PLANE_BYTES = 28 * 1024 * 1024
NOTES = 16
BANDS = 4


def look_up(state, keep, fresh):
    tiles = state.shape[1] // LANES
    parts = []
    for tile in range(tiles):
        wanted = keep[:, tile * LANES : (tile + 1) * LANES]
        high = wanted >> 7
        low = wanted & 127
        found = jnp.where(high >= tiles, fresh + wanted - state.shape[1], 0)
        for source in range(tiles):
            held = state[:, source * LANES : (source + 1) * LANES]
            moved = jnp.take_along_axis(held, low, axis=1, mode="promise_in_bounds")
            found = jnp.where(high == source, moved, found)
        parts.append(found)
    return jnp.concatenate(parts, axis=1)


def split(state):
    both = jnp.concatenate([state >> 7, state & 127], axis=0)
    return both.astype(jnp.float32).astype(jnp.bfloat16)


def index_kernel(
    where_ref, keep_early_ref, keep_late_ref, dest_ref, slot_ref, row_ref, column_ref, coded
):
    shards, heads, cache = keep_early_ref.shape
    cap = slot_ref.shape[0] // shards
    span = LANES
    early, mine, me = where_ref[0], where_ref[1], where_ref[2]
    empty = jnp.minimum(keep_early_ref[0], 0)

    def follow(shard, carry):
        state, own = carry
        own = jnp.where(shard == mine, state, own)
        state = look_up(state, keep_early_ref[shard], shard * span + 1)
        coded[shard] = split(state)
        return state, own

    _, own_early = lax.fori_loop(0, shards, follow, (empty, empty), unroll=shards <= 8)
    base = shards * span + 1
    late_first = look_up(empty, keep_late_ref[0], base)
    late_second = look_up(late_first, keep_late_ref[1], base + span)
    own_late = jnp.where(mine == shards - 1, late_first, 0)
    for index, own in enumerate((own_early, own_late)):
        row_ref[index] = own
        column_ref[index] = jnp.transpose(own.astype(jnp.float32)).astype(jnp.int32)

    named = (dest_ref[...] == me).astype(jnp.float32)
    chunks = named.shape[1] // LANES
    upper = (
        lax.broadcasted_iota(jnp.int32, (LANES, LANES), 0)
        <= lax.broadcasted_iota(jnp.int32, (LANES, LANES), 1)
    ).astype(jnp.float32).astype(jnp.bfloat16)
    total = jnp.zeros((shards, 1), jnp.float32)
    ranks = []
    for chunk in range(chunks):
        part = named[:, chunk * LANES : (chunk + 1) * LANES]
        upto = jnp.dot(part.astype(jnp.bfloat16), upper, preferred_element_type=jnp.float32)
        ranks.append(jnp.where(part > 0, upto + total, 0.0))
        total = total + upto[:, LANES - 1 :]
    low_half = jnp.concatenate(ranks[: chunks // 2], axis=1)
    high_half = jnp.concatenate(ranks[chunks // 2 :], axis=1)
    rank_early = jnp.where(early == 0, low_half, high_half)
    rank_late = jnp.where(early == 0, high_half, low_half)
    place = lax.broadcasted_iota(jnp.int32, (cap, cache), 0).astype(jnp.float32) + 1.0
    contract = (((1,), (1,)), ((), ()))
    for shard in range(shards):
        pick = (rank_early[shard : shard + 1] == place).astype(jnp.float32).astype(jnp.bfloat16)
        found = lax.dot_general(pick, coded[shard], contract, preferred_element_type=jnp.float32)
        if shard >= shards - 2:
            state = late_first if shard == shards - 2 else late_second
            pick = (rank_late[shard : shard + 1] == place).astype(jnp.float32).astype(jnp.bfloat16)
            found += lax.dot_general(
                pick, split(state), contract, preferred_element_type=jnp.float32
            )
        tokens = found[:, :heads] * 128.0 + found[:, heads:]
        slot_ref[shard * cap : (shard + 1) * cap, :] = tokens.astype(jnp.int32)


def column_of(table, head):
    lane = lax.broadcasted_iota(jnp.int32, table.shape, 1)
    return jnp.sum(
        jnp.where(lane == head, table, 0).astype(jnp.float32), axis=1, keepdims=True
    ).astype(jnp.int32)


def picked(column, first, tokens):
    number = lax.broadcasted_iota(jnp.int32, (column.shape[0], tokens.shape[0]), 1) + first
    table = (column == number).astype(jnp.float32).astype(jnp.bfloat16)
    return jnp.dot(table, tokens, preferred_element_type=jnp.float32)


def attend(q_ref, prompt, keys, values, seen, out_ref, score_ref, head):
    span = q_ref.shape[1]
    cache = seen.shape[1]
    group = q_ref.shape[2] // HEAD
    causal = lax.broadcasted_iota(jnp.int32, (span, span), 1) <= lax.broadcasted_iota(
        jnp.int32, (span, span), 0
    )
    bias = jnp.concatenate(
        [
            jnp.broadcast_to(jnp.where(seen > 0, 0.0, -1e30), (span, cache)),
            jnp.where(causal, 0.0, -1e30),
        ],
        axis=1,
    )
    scale = math.log2(math.e) / math.sqrt(HEAD)
    mass = jnp.zeros((1, cache + span), jnp.float32)
    for member in range(group):
        query = q_ref[prompt, :, member * HEAD : (member + 1) * HEAD]
        scores = lax.dot_general(
            query, keys, (((1,), (1,)), ((), ())), preferred_element_type=jnp.float32
        )
        scores = scores + bias
        peak = jnp.max(scores, axis=1, keepdims=True)
        expo = jnp.exp2((scores - peak) * scale)
        weights = expo * (1.0 / jnp.sum(expo, axis=1, keepdims=True))
        mass = mass + jnp.sum(weights, axis=0, keepdims=True)
        mixed = jnp.dot(weights.astype(jnp.bfloat16), values, preferred_element_type=jnp.float32)
        out_ref[prompt, :, member * HEAD : (member + 1) * HEAD] = mixed.astype(jnp.bfloat16)
    score_ref[prompt, pl.ds(head, 1), :] = mass


def attention_kernel(
    where_ref, q_ref, span_ref, early_ref, late_ref, row_ref, column_ref, out_ref, score_ref
):
    early, mine, column, shards = where_ref[0], where_ref[1], where_ref[3], early_ref.shape[0]
    span = q_ref.shape[1]
    late = 1 - early
    local_head = pl.program_id(0)
    head = column * pl.num_programs(0) + local_head

    def run(which, prompt, tokens, first):
        chosen = column_of(column_ref[which], head)
        cached = picked(chosen, first, tokens).astype(jnp.bfloat16)
        rows = jnp.concatenate([cached, span_ref[prompt]], axis=0)
        seen = row_ref[which, pl.ds(head, 1), :]
        attend(
            q_ref, prompt, rows[:, :HEAD], rows[:, HEAD:], seen, out_ref, score_ref, local_head
        )

    run(0, early, early_ref[:, 0].reshape(shards * span, WIDTH), 1)

    @pl.when(mine >= shards - 2)
    def _():
        run(1, late, late_ref[0, 0], shards * span + 1)

    @pl.when(mine < shards - 2)
    def _():
        out_ref[late] = jnp.zeros(out_ref.shape[1:], out_ref.dtype)
        score_ref[late, pl.ds(local_head, 1), :] = jnp.zeros((1, score_ref.shape[2]), jnp.float32)


def owner_kernel(slot_ref, early_ref, late_ref, out_ref):
    shards, _, span, width = early_ref.shape
    rows = out_ref.shape[0]
    chosen = column_of(slot_ref[...], pl.program_id(0))
    bands = 4
    band = rows // bands
    reach = shards * span // bands
    tokens = early_ref[:, 0].reshape(shards * span, width)
    for index in range(bands):
        part = chosen[index * band : (index + 1) * band]
        found = picked(part, 1, tokens[: (index + 1) * reach])
        if index == bands - 1:
            found += picked(part, shards * span + 1, late_ref[:, 0].reshape(2 * span, width))
        out_ref[index * band : (index + 1) * band, :] = found.astype(jnp.bfloat16)


def local(query, kv_rows, keep, dest, offsets):
    prompts, span, qwidth = query.shape
    shards, columns = lax.axis_size("ctx"), lax.axis_size("kv")
    width = kv_rows.shape[2]
    heads_dev = width // WIDTH
    heads = heads_dev * columns
    cache = keep.shape[3]
    owners = shards * columns
    cap = 2 * prompts * cache // owners
    mine, column = lax.axis_index("ctx"), lax.axis_index("kv")
    early = jnp.where(offsets[0] < offsets[1], 0, 1).astype(jnp.int32)
    facts = jnp.stack([early, mine, mine * columns + column, column]).astype(jnp.int32)

    swap = early == 1
    ordered_kv = jnp.where(swap, kv_rows[::-1], kv_rows)
    ordered_keep = jnp.where(swap, keep[::-1, 0], keep[:, 0])
    digits = jnp.stack([ordered_keep >> 7, ordered_keep & 127], axis=1)
    share = dest.shape[0] // columns
    own_dest = lax.dynamic_slice_in_dim(dest[:, 0], column * share, share)
    facts_rows = jnp.concatenate([digits.reshape(-1), own_dest]).astype(jnp.bfloat16)
    used = facts_rows.shape[0]
    room = 16 * width
    facts_rows = jnp.concatenate([facts_rows, jnp.zeros((room - used,), jnp.bfloat16)])
    payload = jnp.concatenate(
        [ordered_kv.reshape(prompts * span, width), facts_rows.reshape(16, width)], axis=0
    )
    whole = lax.all_gather(payload, ("ctx", "kv")).reshape(
        shards, columns, prompts * span + 16, width
    )

    told = whole[:, :, prompts * span :, :].reshape(shards, columns, room).astype(jnp.int32)
    kept = told[:, :, : prompts * 2 * heads_dev * cache].reshape(
        shards, columns, prompts, 2, heads_dev, cache
    )
    kept = kept[:, :, :, 0] * 128 + kept[:, :, :, 1]
    kept = jnp.transpose(kept, (2, 0, 1, 3, 4)).reshape(prompts, shards, heads, cache)
    whole_dest = told[:, :, used - share : used].reshape(shards, columns * share)

    vmem = pl.BlockSpec(memory_space=pltpu.VMEM)
    smem = pl.BlockSpec(memory_space=pltpu.SMEM)
    params = pltpu.CompilerParams(vmem_limit_bytes=VMEM_BYTES)
    slots, rows, cols = pl.pallas_call(
        index_kernel,
        out_shape=(
            jax.ShapeDtypeStruct((shards * cap, heads), jnp.int32),
            jax.ShapeDtypeStruct((2, heads, cache), jnp.int32),
            jax.ShapeDtypeStruct((2, cache, heads), jnp.int32),
        ),
        in_specs=[smem, vmem, vmem, vmem],
        out_specs=(vmem, vmem, vmem),
        scratch_shapes=[pltpu.VMEM((shards, 2 * heads, cache), jnp.bfloat16)],
        compiler_params=params,
    )(facts, kept[0], kept[1, shards - 2 :], whole_dest)

    group_width = qwidth // heads_dev
    attention, row_scores = pl.pallas_call(
        attention_kernel,
        grid_spec=pltpu.PrefetchScalarGridSpec(
            num_scalar_prefetch=1,
            grid=(heads_dev,),
            in_specs=[
                pl.BlockSpec((prompts, span, group_width), lambda h, w: (0, 0, h)),
                pl.BlockSpec((prompts, span, WIDTH), lambda h, w: (0, 0, h)),
                pl.BlockSpec((shards, 1, span, WIDTH), lambda h, w: (0, w[3], 0, h)),
                pl.BlockSpec((1, 1, span, WIDTH), lambda h, w: (shards - 2, w[3], 1, h)),
                pl.BlockSpec((2, heads, cache), lambda h, w: (0, 0, 0)),
                pl.BlockSpec((2, cache, heads), lambda h, w: (0, 0, 0)),
            ],
            out_specs=(
                pl.BlockSpec((prompts, span, group_width), lambda h, w: (0, 0, h)),
                pl.BlockSpec((prompts, heads_dev, cache + span), lambda h, w: (0, 0, 0)),
            ),
        ),
        out_shape=(
            jax.ShapeDtypeStruct((prompts, span, qwidth), jnp.bfloat16),
            jax.ShapeDtypeStruct((prompts, heads_dev, cache + span), jnp.float32),
        ),
        compiler_params=params,
    )(facts, query, kv_rows, whole, whole, rows, cols)

    owner_cache = pl.pallas_call(
        owner_kernel,
        grid=(heads,),
        in_specs=[
            pl.BlockSpec((shards * cap, heads), lambda g: (0, 0)),
            pl.BlockSpec(
                (shards, 1, span, WIDTH), lambda g: (0, g // heads_dev, 0, g % heads_dev)
            ),
            pl.BlockSpec(
                (2, 1, span, WIDTH),
                lambda g: (shards // 2 - 1, g // heads_dev, 1, g % heads_dev),
            ),
        ],
        out_specs=pl.BlockSpec((shards * cap, WIDTH), lambda g: (0, g)),
        out_shape=jax.ShapeDtypeStruct((shards * cap, heads * WIDTH), jnp.bfloat16),
        compiler_params=params,
    )(slots, whole, whole)
    return (attention, row_scores, owner_cache)


def dot(a, b, dims=((1,), (0,))):
    return lax.dot_general(a, b, (dims, ((), ())), preferred_element_type=jnp.float32)


def marks(table):
    return table.astype(jnp.float32).astype(jnp.bfloat16)


def early_of(offsets_ref):
    return jnp.where(offsets_ref[0] < offsets_ref[1], 0, 1)


def prepare_kernel(
    offsets_ref, kv_ref, keep_ref, dest_ref, both_ref, single_ref, keep, dest, sems
):
    span = kv_ref.shape[1]
    heads, cache = keep_ref.shape[2], keep_ref.shape[3]
    early = early_of(offsets_ref)
    copies = [
        (keep_ref, keep),
        (dest_ref, dest),
        (kv_ref.at[early], single_ref.at[:span]),
        (kv_ref.at[early], both_ref.at[:span]),
        (kv_ref.at[1 - early], both_ref.at[span : 2 * span]),
    ]
    copies = [
        pltpu.make_async_copy(source, target, sems.at[index])
        for index, (source, target) in enumerate(copies)
    ]
    for copy in copies:
        copy.start()
    for copy in copies[:2]:
        copy.wait()
    lane = lax.broadcasted_iota(jnp.int32, (heads, cache), 1)
    rows = [
        keep[early, 0] - lane,
        dest[:, :cache],
        dest[:, cache:],
        keep[1 - early, 0] - lane,
        jnp.zeros((NOTES - 2 * heads - 2, cache), jnp.int32),
    ]
    rows = jnp.concatenate([row.astype(jnp.float32) for row in rows], axis=0)
    rows = rows.astype(jnp.bfloat16)
    single_ref[span:, :] = rows
    both_ref[2 * span :, :] = rows
    for copy in copies[2:]:
        copy.wait()


def two_notes(first, first_row, second, second_row):
    half = NOTES // 2
    return jnp.concatenate(
        [
            first[first_row : first_row + NOTES, :].astype(jnp.float32)[:half],
            second[second_row : second_row + NOTES, :].astype(jnp.float32)[:half],
        ],
        axis=0,
    ).astype(jnp.bfloat16)


def join_first_kernel(
    below, above, both, y_own, x_own, d_own, beside_ref, going_ref, relay_ref
):
    span = relay_ref.shape[0]
    beside_ref[:span, :] = below[:span, :]
    beside_ref[span : 2 * span, :] = above[:span, :]
    beside_ref[2 * span :, :] = two_notes(below, 2 * span, above, span)
    going_ref[:span, :] = both[:span, :]
    going_ref[span : 2 * span, :] = y_own[:span, :]
    going_ref[2 * span : 2 * span + NOTES, :] = two_notes(both, 2 * span, y_own, 2 * span)
    going_ref[2 * span + NOTES :, :] = two_notes(x_own, span, d_own, span)
    level = lax.axis_index("ctx") // 2

    @pl.when(level == 0)
    def _():
        relay_ref[...] = below[span : 2 * span, :]

    @pl.when(level > 0)
    def _():
        relay_ref[...] = both[span : 2 * span, :]


def join_second_kernel(beyond, relay, relayed, *rest):
    out_ref, late_ref = rest[-2:]
    span = relay.shape[0]
    level = lax.axis_index("ctx") // 2
    out_ref[: 2 * span, :] = beyond[: 2 * span, :]
    for ref, chosen in ((relay, (level == 0) | (level == 3)), (relayed, (level == 1) | (level == 2))):

        @pl.when(chosen)
        def _(ref=ref):
            out_ref[2 * span :, :] = ref[...]
            late_ref[...] = ref[...]


def place_of(turn, flip, shards):
    mine = lax.axis_index("ctx")
    place = lax.rem(mine - 2 * turn + shards, shards)
    return place + 1 - 2 * lax.rem(mine, 2) if flip else place


def sort_tokens(pieces, tokens, span):
    shards = tokens.shape[0] // span
    for ref, base, turn, flip in pieces:
        place = place_of(turn, flip, shards)
        tokens[pl.ds(pl.multiple_of(place * span, span), span), :] = ref[base : base + span, :]


def sort_late(pieces, late_tokens):
    span = late_tokens.shape[0] // 2
    side = lax.rem(lax.axis_index("ctx"), 2)
    for flip, ref_base in enumerate(pieces):
        ref, base = ref_base
        place = side + flip - 2 * side * flip
        late_tokens[pl.ds(pl.multiple_of(place * span, span), span), :] = ref[
            base : base + span, :
        ]


def read_notes(ref, base, part, heads):
    half = NOTES // 2
    rows = ref[base : base + NOTES, :].astype(jnp.float32).astype(jnp.int32)
    rows = rows[part * half : (part + 1) * half]
    lane = lax.broadcasted_iota(jnp.int32, (heads, rows.shape[1]), 1)
    return rows[:heads] + lane, rows[heads + 2 : 2 * heads + 2] + lane, rows[heads : heads + 2]


def sort_notes(notes, keeps, dests):
    shards, heads = keeps.shape[0], keeps.shape[1] // 4
    for ref, base, part, turn, flip in notes:
        place = place_of(turn, flip, shards)
        early, late, dest = read_notes(ref, base, part, heads)
        keeps[place, :heads, :] = early
        keeps[place, heads : 2 * heads, :] = late
        dests[place, :, :] = dest


def follow_lists(keeps, coded, span):
    shards, rows, cache = keeps.shape
    heads = rows // 4
    row = lax.broadcasted_iota(jnp.int32, (rows, cache), 0)
    is_early = row < heads
    state = jnp.where(row < 0, keeps[0], 0)
    own = state
    mine = lax.axis_index("ctx")
    for shard in range(shards):
        own = jnp.where(mine == shard, state, own)
        late_first = (shards + shard - (shards - 2)) * span + 1
        fresh = jnp.where(is_early[:, :LANES], shard * span + 1, late_first)
        state = look_up(state, keeps[shard], fresh)
        if shard < shards - 2:
            state = jnp.where(is_early, state, 0)
        coded[shard] = split(state)
    return own


def find_slots(early, dests, coded, owner, slots):
    shards, halves, cache = dests.shape
    heads = coded.shape[1] // 8
    cap = slots.shape[0] // shards
    upper = marks(
        lax.broadcasted_iota(jnp.int32, (LANES, LANES), 0)
        <= lax.broadcasted_iota(jnp.int32, (LANES, LANES), 1)
    )
    place = lax.broadcasted_iota(jnp.int32, (cap, cache), 0).astype(jnp.float32) + 1.0
    total = jnp.zeros((shards, 1), jnp.float32)
    ranks = []
    for half in range(halves):
        named = (dests[:, half, :] == owner).astype(jnp.float32)
        parts = []
        for chunk in range(cache // LANES):
            part = named[:, chunk * LANES : (chunk + 1) * LANES]
            upto = dot(part.astype(jnp.bfloat16), upper)
            parts.append(jnp.where(part > 0, upto + total, 0.0))
            total = total + upto[:, LANES - 1 :]
        ranks.append(jnp.concatenate(parts, axis=1))
    rank_early = jnp.where(early == 0, ranks[0], ranks[1])
    rank_late = jnp.where(early == 0, ranks[1], ranks[0])
    across = ((1,), (1,))
    for shard in range(shards):
        found = dot(marks(rank_early[shard : shard + 1] == place), coded[shard], across)
        tokens = found[:, :heads] * 128.0 + found[:, 4 * heads : 5 * heads]
        if shard >= shards - 2:
            found = dot(marks(rank_late[shard : shard + 1] == place), coded[shard], across)
            tokens += found[:, heads : 2 * heads] * 128.0 + found[:, 5 * heads : 6 * heads]
        slots[shard * cap : (shard + 1) * cap, :] = tokens.astype(jnp.int32)


def place_bands(slots, tokens, out_ref, bands, total_bands):
    rows, heads = slots.shape
    reach = tokens.shape[0]
    band = rows // total_bands
    for head in range(heads):
        lanes = slice(head * WIDTH, (head + 1) * WIDTH)
        for order, index in enumerate(bands):
            part = slots[index * band : (index + 1) * band, head : head + 1]
            found = picked(part, 1, tokens[: (index + 1) * reach // total_bands, lanes])
            out_ref[order * band : (order + 1) * band, lanes] = found.astype(jnp.bfloat16)


def add_late(slots, first, late_tokens, out_ref, base):
    band, heads = slots.shape
    for head in range(heads):
        lanes = slice(head * WIDTH, (head + 1) * WIDTH)
        found = picked(slots[:, head : head + 1], first, late_tokens[:, lanes])
        out_ref[base : base + band, lanes] += found.astype(jnp.bfloat16)


def attend_columns(q_ref, head, rows, seen, out_ref, score_ref):
    span = q_ref.shape[1]
    total = rows.shape[0]
    cache = total - span
    group = q_ref.shape[2] // (score_ref.shape[1] * HEAD)
    keys, values = rows[:, :HEAD], rows[:, HEAD:]
    flat = jnp.transpose(values.astype(jnp.float32)).astype(jnp.bfloat16)
    lane = lax.broadcasted_iota(jnp.int32, (total, HEAD), 1)
    hidden = jnp.where(seen > 0, 0.0, -1e30)
    hidden = jnp.concatenate([hidden, jnp.zeros((span, 1), jnp.float32)], axis=0)
    hidden = jnp.where(lane == 0, hidden, 0.0).astype(jnp.bfloat16)
    keys = jnp.concatenate([keys, hidden], axis=1)
    ones = jnp.ones((2 * span, HEAD), jnp.bfloat16)
    causal = lax.broadcasted_iota(jnp.int32, (span, 2 * span), 0) <= lax.rem(
        lax.broadcasted_iota(jnp.int32, (span, 2 * span), 1), span
    )
    bias = jnp.where(causal, 0.0, -1e30)
    scale = math.log2(math.e) / math.sqrt(HEAD)
    mass = None
    for pair in range(group // 2):
        first = (head * group + 2 * pair) * HEAD
        query = jnp.concatenate(
            [
                q_ref[0, :, first : first + HEAD],
                q_ref[0, :, first + HEAD : first + 2 * HEAD],
            ],
            axis=0,
        )
        scores = dot(keys, jnp.concatenate([query, ones], axis=1), ((1,), (1,)))
        near = scores[cache:] + bias
        scores = jnp.concatenate([scores[:cache], near], axis=0) * scale
        peak = jnp.max(scores, axis=0, keepdims=True)
        expo = jnp.exp2(scores - peak)
        weights = expo * (1.0 / jnp.sum(expo, axis=0, keepdims=True))
        both = weights[:, :span] + weights[:, span:]
        mass = both if mass is None else mass + both
        mixed = jnp.transpose(dot(flat, weights.astype(jnp.bfloat16)))
        for member in range(2):
            lanes = slice(first + member * HEAD, first + (member + 1) * HEAD)
            out_ref[0, :, lanes] = mixed[member * span : (member + 1) * span].astype(
                jnp.bfloat16
            )
    score_ref[0, head : head + 1, :] = jnp.sum(jnp.transpose(mass), axis=0, keepdims=True)


def late_kernel(offsets_ref, q_ref, both_ref, beside_ref, out_ref, score_ref):
    mine, shards = lax.axis_index("ctx"), lax.axis_size("ctx")
    heads, cache = score_ref.shape[1], score_ref.shape[2] - q_ref.shape[1]
    span = q_ref.shape[1]

    @pl.when(mine >= shards - 2)
    def _():
        _, keep, _ = read_notes(beside_ref, 2 * span, 0, heads)
        state = jnp.where(keep >= cache, keep - cache + 1, 0)
        state = jnp.where(mine == shards - 1, state, 0).astype(jnp.float32)
        state = jnp.concatenate([state, jnp.zeros((8 - heads, cache), jnp.float32)], axis=0)
        columns = jnp.transpose(state).astype(jnp.int32)
        for head in range(heads):
            lanes = slice(head * WIDTH, (head + 1) * WIDTH)
            column = columns[:, head : head + 1]
            cached = picked(column, 1, beside_ref[span : 2 * span, lanes])
            rows = jnp.concatenate(
                [cached.astype(jnp.bfloat16), both_ref[span : 2 * span, lanes]], axis=0
            )
            attend_columns(q_ref, head, rows, column, out_ref, score_ref)

    @pl.when(mine < shards - 2)
    def _():
        out_ref[...] = jnp.zeros(out_ref.shape, out_ref.dtype)
        score_ref[...] = jnp.zeros(score_ref.shape, jnp.float32)


def output_part(cache_ref, row, rows, column):
    width = cache_ref.shape[1] // lax.axis_size("kv")
    return cache_ref.at[
        pl.ds(row, rows), pl.ds(pl.multiple_of(column * width, width), width)
    ]


def early_kernel(offsets_ref, q_ref, *rest):
    both, beside, beyond, y_own, y_beside, x_own, x_beside, d_own, d_beside = rest[:9]
    out_ref, score_ref, cache_ref, top_sent, low_ref, slots_ref = rest[11:17]
    tokens, top, sem = rest[17:20]
    tables = (rest[20:23], rest[23:26])
    span = q_ref.shape[1]
    heads = score_ref.shape[1]
    early = early_of(offsets_ref)
    column = lax.axis_index("kv")
    me = lax.axis_index("ctx") * lax.axis_size("kv") + column

    def fill_slots(which, notes):
        keeps, dests, coded = tables[which]
        sort_notes(notes, keeps, dests)
        own = follow_lists(keeps, coded, span)
        for flip in range(2):
            find_slots(early, dests, coded, me ^ flip, slots_ref.at[which, flip])
        return own

    at = 2 * span
    own = fill_slots(
        0,
        [
            (both, at, 0, 0, 0),
            (beside, at, 0, 1, 0),
            (beside, at, 1, 3, 0),
            (beyond, at, 0, 2, 0),
            (beyond, at, 1, 2, 1),
            (y_own, at, 0, 0, 1),
            (y_beside, at, 0, 1, 1),
            (y_beside, at, 1, 3, 1),
        ],
    )
    own = jnp.transpose(own.astype(jnp.float32)).astype(jnp.int32)
    pieces = [(both, 0, 0, 0), (beside, 0, 1, 0), (beside, span, 3, 0), (beyond, 0, 2, 0)]
    pieces += [(beyond, span, 2, 1), (y_own, 0, 0, 1), (y_beside, 0, 1, 1), (y_beside, span, 3, 1)]
    sort_tokens(pieces, tokens, span)
    bands = tuple(range(BANDS - 1))
    place_bands(slots_ref.at[0, 0], tokens, top, bands, BANDS)
    copy = pltpu.make_async_copy(top, output_part(cache_ref, 0, top.shape[0], column), sem)
    copy.start()
    place_bands(slots_ref.at[0, 1], tokens, top_sent, bands, BANDS)
    for flip in range(2):
        place_bands(slots_ref.at[0, flip], tokens, low_ref.at[flip], (BANDS - 1,), BANDS)
    for head in range(heads):
        lanes = slice(head * WIDTH, (head + 1) * WIDTH)
        chosen = own[:, head : head + 1]
        cached = picked(chosen, 1, tokens[:, lanes]).astype(jnp.bfloat16)
        rows = jnp.concatenate([cached, both[:span, lanes]], axis=0)
        attend_columns(q_ref, head, rows, chosen, out_ref, score_ref)
    fill_slots(
        1,
        [
            (x_own, span, 0, 0, 0),
            (d_own, span, 0, 0, 1),
            (x_beside, at, 0, 1, 0),
            (x_beside, at, 1, 3, 0),
            (d_beside, at, 0, 1, 1),
            (d_beside, at, 1, 3, 1),
            (beyond, at + NOTES, 0, 2, 0),
            (beyond, at + NOTES, 1, 2, 1),
        ],
    )
    copy.wait()


def far_rows(flip, refs, far_ref, low, tokens, near_late, far_late):
    x_own, x_beside, x_end, d_own, d_beside, d_late, late, y_late, low_ref, slots_ref = refs
    span = late.shape[0]
    rows = slots_ref.shape[2]
    band = rows // BANDS
    first = tokens.shape[0] + 1
    last = pl.ds(rows - band, band)
    sort_late([(late, 0), (y_late, 0)], near_late)
    sort_late([(x_end, 2 * span), (d_late, 0)], far_late)
    low[...] = low_ref[flip]
    add_late(slots_ref.at[0, flip, last], first, near_late, low, 0)
    pieces = [(x_own, 0, 0, 0), (x_beside, 0, 1, 0), (x_beside, span, 3, 0), (x_end, 0, 2, 0)]
    pieces += [(x_end, span, 2, 1), (d_own, 0, 0, 1), (d_beside, 0, 1, 1), (d_beside, span, 3, 1)]
    sort_tokens(pieces, tokens, span)
    place_bands(slots_ref.at[1, flip], tokens, far_ref, tuple(range(BANDS)), BANDS)
    add_late(slots_ref.at[1, flip, last], first, far_late, far_ref, rows - band)


def far_sent_kernel(*refs):
    sent_ref = refs[10]
    rows = refs[9].shape[2]
    far_rows(1, refs[:10], sent_ref.at[:rows], sent_ref.at[rows:], *refs[11:])


def far_kept_kernel(*refs):
    top_ref = refs[10]
    cache_ref, far, low, tokens, near_late, far_late, sems = refs[12:]
    column = lax.axis_index("kv")
    upper = top_ref.shape[0]
    received = pltpu.make_async_copy(
        top_ref, output_part(cache_ref, 0, upper, column ^ 1), sems.at[0]
    )
    received.start()
    far_rows(0, refs[:10], far, low, tokens, near_late, far_late)
    copies = [
        pltpu.make_async_copy(
            far, output_part(cache_ref, 0, far.shape[0], column ^ 2), sems.at[1]
        ),
        pltpu.make_async_copy(
            low, output_part(cache_ref, upper, low.shape[0], column), sems.at[2]
        ),
    ]
    for copy in copies:
        copy.start()
    for copy in copies + [received]:
        copy.wait()


def last_kernel(sent_ref, _, cache_ref, sems):
    column = lax.axis_index("kv")
    rows = cache_ref.shape[0]
    band = sent_ref.shape[0] - rows
    copies = [
        pltpu.make_async_copy(
            sent_ref.at[:rows], output_part(cache_ref, 0, rows, column ^ 3), sems.at[0]
        ),
        pltpu.make_async_copy(
            sent_ref.at[rows:], output_part(cache_ref, rows - band, band, column ^ 1), sems.at[1]
        ),
    ]
    for copy in copies:
        copy.start()
    for copy in copies:
        copy.wait()


def send(value, axis, pairs):
    return lax.ppermute(value, axis, pairs)


def local_in_planes(query, kv_rows, keep, dest, offsets):
    prompts, span, qwidth = query.shape
    shards, columns = lax.axis_size("ctx"), lax.axis_size("kv")
    width = kv_rows.shape[2]
    heads = width // WIDTH
    cache = keep.shape[3]
    rows = 2 * prompts * cache // columns
    band = rows // BANDS
    vmem = pl.BlockSpec(memory_space=pltpu.VMEM)
    smem = pl.BlockSpec(memory_space=pltpu.SMEM)
    anywhere = pl.BlockSpec(memory_space=pl.ANY)
    params = pltpu.CompilerParams(vmem_limit_bytes=PLANE_BYTES)

    def cost(flops, moved):
        return pl.CostEstimate(flops=flops, bytes_accessed=moved, transcendentals=0)

    def piece(count):
        return jax.ShapeDtypeStruct((count, width), jnp.bfloat16)

    def along_z(value, turn):
        return send(value, "ctx", [(i, (i + 2 * turn) % shards) for i in range(shards)])

    def across_y(value):
        return send(value, "ctx", [(i, i ^ 1) for i in range(shards)])

    def across_x(value):
        return send(value, "kv", [(i, i ^ 2) for i in range(columns)])

    def across_both(value):
        pairs = [(i, i ^ columns ^ 2) for i in range(shards * columns)]
        return send(value, ("ctx", "kv"), pairs)

    def across_core(value):
        return send(value, "kv", [(i, i ^ 1) for i in range(columns)])

    both, single = pl.pallas_call(
        prepare_kernel,
        out_shape=(piece(2 * span + NOTES), piece(span + NOTES)),
        in_specs=[smem] + [anywhere] * 3,
        out_specs=(vmem, vmem),
        scratch_shapes=[
            pltpu.VMEM(keep.shape, jnp.int32),
            pltpu.VMEM((1, prompts * cache), jnp.int32),
            pltpu.SemaphoreType.DMA((5,)),
        ],
        compiler_params=params,
    )(offsets, kv_rows, keep, jnp.transpose(dest))

    below, above = along_z(both, 1), along_z(single, 3)
    y_own, x_own, d_own = across_y(both), across_x(single), across_both(single)
    beside, going, relay = pl.pallas_call(
        join_first_kernel,
        out_shape=(piece(2 * span + NOTES), piece(2 * span + 2 * NOTES), piece(span)),
        in_specs=[vmem] * 6,
        out_specs=(vmem,) * 3,
        compiler_params=params,
        cost_estimate=cost(0, 10**6),
    )(below, above, both, y_own, x_own, d_own)
    beyond = along_z(going, 2)
    relayed = send(relay, "ctx", [(0, 2), (1, 3), (6, 4), (7, 5)])
    y_beside, x_beside, d_beside = across_y(beside), across_x(beside), across_both(beside)

    attention_shape = jax.ShapeDtypeStruct((prompts, span, qwidth), jnp.bfloat16)
    score_shape = jax.ShapeDtypeStruct((prompts, heads, cache + span), jnp.float32)

    def prompt_specs(late):
        def block(_, offsets_ref):
            early = early_of(offsets_ref)
            return (1 - early if late else early, 0, 0)

        return (
            pl.BlockSpec((1, span, qwidth), block),
            pl.BlockSpec((1, heads, cache + span), block),
        )

    attention, row_scores = pl.pallas_call(
        late_kernel,
        grid_spec=pltpu.PrefetchScalarGridSpec(
            num_scalar_prefetch=1,
            grid=(1,),
            in_specs=[prompt_specs(True)[0], vmem, vmem],
            out_specs=prompt_specs(True),
        ),
        out_shape=(attention_shape, score_shape),
        compiler_params=params,
        cost_estimate=cost(5 * 10**9, 10**7),
    )(offsets, query, both, y_own)

    end, late = pl.pallas_call(
        join_second_kernel,
        out_shape=(piece(3 * span), piece(span)),
        in_specs=[vmem] * 3 + [anywhere] * 4,
        out_specs=(vmem, vmem),
        compiler_params=params,
        cost_estimate=cost(0, 10**6),
    )(beyond, relay, relayed, y_beside, x_beside, d_beside, row_scores)
    x_end, y_late, d_late = across_x(end), across_y(late), across_both(late)

    tokens = pltpu.VMEM((shards * span, width), jnp.bfloat16)
    late_tokens = pltpu.VMEM((2 * span, width), jnp.bfloat16)
    cache_shape = jax.ShapeDtypeStruct((rows, columns * width), jnp.bfloat16)
    attention, row_scores, owner_cache, top_sent, low, slots = pl.pallas_call(
        early_kernel,
        grid_spec=pltpu.PrefetchScalarGridSpec(
            num_scalar_prefetch=1,
            grid=(1,),
            in_specs=[prompt_specs(False)[0]] + [vmem] * 9 + [anywhere] * 2,
            out_specs=prompt_specs(False) + (anywhere, vmem, vmem, vmem),
            scratch_shapes=[
                tokens,
                pltpu.VMEM((rows - band, width), jnp.bfloat16),
                pltpu.SemaphoreType.DMA,
            ]
            + 2
            * [
                pltpu.VMEM((shards, 4 * heads, cache), jnp.int32),
                pltpu.VMEM((shards, prompts, cache), jnp.int32),
                pltpu.VMEM((shards, 8 * heads, cache), jnp.bfloat16),
            ],
        ),
        out_shape=(
            attention_shape,
            score_shape,
            cache_shape,
            piece(rows - band),
            jax.ShapeDtypeStruct((2, band, width), jnp.bfloat16),
            jax.ShapeDtypeStruct((2, 2, rows, heads), jnp.int32),
        ),
        input_output_aliases={11: 0, 12: 1},
        compiler_params=params,
        cost_estimate=cost(10**10, 10**7),
    )(
        offsets,
        query,
        both,
        beside,
        beyond,
        y_own,
        y_beside,
        x_own,
        x_beside,
        d_own,
        d_beside,
        attention,
        row_scores,
    )
    top = across_core(top_sent)
    far = (x_own, x_beside, x_end, d_own, d_beside, d_late, late, y_late, low, slots)
    sent = pl.pallas_call(
        far_sent_kernel,
        out_shape=piece(rows + band),
        in_specs=[vmem] * 10,
        out_specs=vmem,
        scratch_shapes=[tokens, late_tokens, late_tokens],
        compiler_params=params,
        cost_estimate=cost(2 * 10**9, 4 * 10**6),
    )(*far)
    received = across_core(sent)
    owner_cache = pl.pallas_call(
        far_kept_kernel,
        out_shape=cache_shape,
        in_specs=[vmem] * 10 + [anywhere] * 2,
        out_specs=anywhere,
        scratch_shapes=[
            pltpu.VMEM((rows, width), jnp.bfloat16),
            pltpu.VMEM((band, width), jnp.bfloat16),
            tokens,
            late_tokens,
            late_tokens,
            pltpu.SemaphoreType.DMA((3,)),
        ],
        input_output_aliases={11: 0},
        compiler_params=params,
        cost_estimate=cost(2 * 10**9, 4 * 10**6),
    )(*far, top, owner_cache)
    owner_cache = pl.pallas_call(
        last_kernel,
        out_shape=cache_shape,
        in_specs=[anywhere] * 2,
        out_specs=anywhere,
        scratch_shapes=[pltpu.SemaphoreType.DMA((2,))],
        input_output_aliases={1: 0},
        compiler_params=params,
        cost_estimate=cost(0, 10**6),
    )(received, owner_cache)
    return (attention, row_scores, owner_cache)


def solution(mesh):
    placed = (
        P(None, "ctx", "kv"),
        P(None, "ctx", "kv"),
        P(None, "ctx", "kv", None),
        P("ctx", None),
        P(),
    )
    in_planes = mesh.shape["ctx"] == 8 and mesh.shape["kv"] == 4
    return jax.shard_map(
        local_in_planes if in_planes else local,
        mesh=mesh,
        in_specs=placed,
        out_specs=(P(None, "ctx", "kv"), P(None, "kv", "ctx"), P(("ctx", "kv"), None)),
        check_vma=False,
    )
```

```python
import functools
import math

import jax
import jax.numpy as jnp
from jax import lax
from jax.experimental import pallas as pl
from jax.experimental.pallas import tpu as pltpu
from jax.sharding import PartitionSpec as P

HEAD = 128
WIDTH = 2 * HEAD
LANES = 128
VMEM_BYTES = 56 * 1024 * 1024
PLANE_BYTES = 28 * 1024 * 1024
NOTES = 16
BANDS = 4


def look_up(state, keep, fresh):
    tiles = state.shape[1] // LANES
    parts = []
    for tile in range(tiles):
        wanted = keep[:, tile * LANES : (tile + 1) * LANES]
        high = wanted >> 7
        low = wanted & 127
        found = jnp.where(high >= tiles, fresh + wanted - state.shape[1], 0)
        for source in range(tiles):
            held = state[:, source * LANES : (source + 1) * LANES]
            moved = jnp.take_along_axis(held, low, axis=1, mode="promise_in_bounds")
            found = jnp.where(high == source, moved, found)
        parts.append(found)
    return jnp.concatenate(parts, axis=1)


def split(state):
    both = jnp.concatenate([state >> 7, state & 127], axis=0)
    return both.astype(jnp.float32).astype(jnp.bfloat16)


def index_kernel(
    where_ref, keep_early_ref, keep_late_ref, dest_ref, slot_ref, row_ref, column_ref, coded
):
    shards, heads, cache = keep_early_ref.shape
    cap = slot_ref.shape[0] // shards
    span = LANES
    early, mine, me = where_ref[0], where_ref[1], where_ref[2]
    empty = jnp.minimum(keep_early_ref[0], 0)

    def follow(shard, carry):
        state, own = carry
        own = jnp.where(shard == mine, state, own)
        state = look_up(state, keep_early_ref[shard], shard * span + 1)
        coded[shard] = split(state)
        return state, own

    _, own_early = lax.fori_loop(0, shards, follow, (empty, empty), unroll=shards <= 8)
    base = shards * span + 1
    late_first = look_up(empty, keep_late_ref[0], base)
    late_second = look_up(late_first, keep_late_ref[1], base + span)
    own_late = jnp.where(mine == shards - 1, late_first, 0)
    for index, own in enumerate((own_early, own_late)):
        row_ref[index] = own
        column_ref[index] = jnp.transpose(own.astype(jnp.float32)).astype(jnp.int32)

    named = (dest_ref[...] == me).astype(jnp.float32)
    chunks = named.shape[1] // LANES
    upper = (
        lax.broadcasted_iota(jnp.int32, (LANES, LANES), 0)
        <= lax.broadcasted_iota(jnp.int32, (LANES, LANES), 1)
    ).astype(jnp.float32).astype(jnp.bfloat16)
    total = jnp.zeros((shards, 1), jnp.float32)
    ranks = []
    for chunk in range(chunks):
        part = named[:, chunk * LANES : (chunk + 1) * LANES]
        upto = jnp.dot(part.astype(jnp.bfloat16), upper, preferred_element_type=jnp.float32)
        ranks.append(jnp.where(part > 0, upto + total, 0.0))
        total = total + upto[:, LANES - 1 :]
    low_half = jnp.concatenate(ranks[: chunks // 2], axis=1)
    high_half = jnp.concatenate(ranks[chunks // 2 :], axis=1)
    rank_early = jnp.where(early == 0, low_half, high_half)
    rank_late = jnp.where(early == 0, high_half, low_half)
    place = lax.broadcasted_iota(jnp.int32, (cap, cache), 0).astype(jnp.float32) + 1.0
    contract = (((1,), (1,)), ((), ()))
    for shard in range(shards):
        pick = (rank_early[shard : shard + 1] == place).astype(jnp.float32).astype(jnp.bfloat16)
        found = lax.dot_general(pick, coded[shard], contract, preferred_element_type=jnp.float32)
        if shard >= shards - 2:
            state = late_first if shard == shards - 2 else late_second
            pick = (rank_late[shard : shard + 1] == place).astype(jnp.float32).astype(jnp.bfloat16)
            found += lax.dot_general(
                pick, split(state), contract, preferred_element_type=jnp.float32
            )
        tokens = found[:, :heads] * 128.0 + found[:, heads:]
        slot_ref[shard * cap : (shard + 1) * cap, :] = tokens.astype(jnp.int32)


def column_of(table, head):
    lane = lax.broadcasted_iota(jnp.int32, table.shape, 1)
    return jnp.sum(
        jnp.where(lane == head, table, 0).astype(jnp.float32), axis=1, keepdims=True
    ).astype(jnp.int32)


def picked(column, first, tokens):
    number = lax.broadcasted_iota(jnp.int32, (column.shape[0], tokens.shape[0]), 1) + first
    table = (column == number).astype(jnp.float32).astype(jnp.bfloat16)
    return jnp.dot(table, tokens, preferred_element_type=jnp.float32)


def attend(q_ref, prompt, keys, values, seen, out_ref, score_ref, head):
    span = q_ref.shape[1]
    cache = seen.shape[1]
    group = q_ref.shape[2] // HEAD
    causal = lax.broadcasted_iota(jnp.int32, (span, span), 1) <= lax.broadcasted_iota(
        jnp.int32, (span, span), 0
    )
    bias = jnp.concatenate(
        [
            jnp.broadcast_to(jnp.where(seen > 0, 0.0, -1e30), (span, cache)),
            jnp.where(causal, 0.0, -1e30),
        ],
        axis=1,
    )
    scale = math.log2(math.e) / math.sqrt(HEAD)
    mass = jnp.zeros((1, cache + span), jnp.float32)
    for member in range(group):
        query = q_ref[prompt, :, member * HEAD : (member + 1) * HEAD]
        scores = lax.dot_general(
            query, keys, (((1,), (1,)), ((), ())), preferred_element_type=jnp.float32
        )
        scores = scores + bias
        peak = jnp.max(scores, axis=1, keepdims=True)
        expo = jnp.exp2((scores - peak) * scale)
        weights = expo * (1.0 / jnp.sum(expo, axis=1, keepdims=True))
        mass = mass + jnp.sum(weights, axis=0, keepdims=True)
        mixed = jnp.dot(weights.astype(jnp.bfloat16), values, preferred_element_type=jnp.float32)
        out_ref[prompt, :, member * HEAD : (member + 1) * HEAD] = mixed.astype(jnp.bfloat16)
    score_ref[prompt, pl.ds(head, 1), :] = mass


def attention_kernel(
    where_ref, q_ref, span_ref, early_ref, late_ref, row_ref, column_ref, out_ref, score_ref
):
    early, mine, column, shards = where_ref[0], where_ref[1], where_ref[3], early_ref.shape[0]
    span = q_ref.shape[1]
    late = 1 - early
    local_head = pl.program_id(0)
    head = column * pl.num_programs(0) + local_head

    def run(which, prompt, tokens, first):
        chosen = column_of(column_ref[which], head)
        cached = picked(chosen, first, tokens).astype(jnp.bfloat16)
        rows = jnp.concatenate([cached, span_ref[prompt]], axis=0)
        seen = row_ref[which, pl.ds(head, 1), :]
        attend(
            q_ref, prompt, rows[:, :HEAD], rows[:, HEAD:], seen, out_ref, score_ref, local_head
        )

    run(0, early, early_ref[:, 0].reshape(shards * span, WIDTH), 1)

    @pl.when(mine >= shards - 2)
    def _():
        run(1, late, late_ref[0, 0], shards * span + 1)

    @pl.when(mine < shards - 2)
    def _():
        out_ref[late] = jnp.zeros(out_ref.shape[1:], out_ref.dtype)
        score_ref[late, pl.ds(local_head, 1), :] = jnp.zeros((1, score_ref.shape[2]), jnp.float32)


def owner_kernel(slot_ref, early_ref, late_ref, out_ref):
    shards, _, span, width = early_ref.shape
    rows = out_ref.shape[0]
    chosen = column_of(slot_ref[...], pl.program_id(0))
    bands = 4
    band = rows // bands
    reach = shards * span // bands
    tokens = early_ref[:, 0].reshape(shards * span, width)
    for index in range(bands):
        part = chosen[index * band : (index + 1) * band]
        found = picked(part, 1, tokens[: (index + 1) * reach])
        if index == bands - 1:
            found += picked(part, shards * span + 1, late_ref[:, 0].reshape(2 * span, width))
        out_ref[index * band : (index + 1) * band, :] = found.astype(jnp.bfloat16)


def local(query, kv_rows, keep, dest, offsets):
    prompts, span, qwidth = query.shape
    shards, columns = lax.axis_size("ctx"), lax.axis_size("kv")
    width = kv_rows.shape[2]
    heads_dev = width // WIDTH
    heads = heads_dev * columns
    cache = keep.shape[3]
    owners = shards * columns
    cap = 2 * prompts * cache // owners
    mine, column = lax.axis_index("ctx"), lax.axis_index("kv")
    early = jnp.where(offsets[0] < offsets[1], 0, 1).astype(jnp.int32)
    facts = jnp.stack([early, mine, mine * columns + column, column]).astype(jnp.int32)

    swap = early == 1
    ordered_kv = jnp.where(swap, kv_rows[::-1], kv_rows)
    ordered_keep = jnp.where(swap, keep[::-1, 0], keep[:, 0])
    digits = jnp.stack([ordered_keep >> 7, ordered_keep & 127], axis=1)
    share = dest.shape[0] // columns
    own_dest = lax.dynamic_slice_in_dim(dest[:, 0], column * share, share)
    facts_rows = jnp.concatenate([digits.reshape(-1), own_dest]).astype(jnp.bfloat16)
    used = facts_rows.shape[0]
    room = 16 * width
    facts_rows = jnp.concatenate([facts_rows, jnp.zeros((room - used,), jnp.bfloat16)])
    payload = jnp.concatenate(
        [ordered_kv.reshape(prompts * span, width), facts_rows.reshape(16, width)], axis=0
    )
    whole = lax.all_gather(payload, ("ctx", "kv")).reshape(
        shards, columns, prompts * span + 16, width
    )

    told = whole[:, :, prompts * span :, :].reshape(shards, columns, room).astype(jnp.int32)
    kept = told[:, :, : prompts * 2 * heads_dev * cache].reshape(
        shards, columns, prompts, 2, heads_dev, cache
    )
    kept = kept[:, :, :, 0] * 128 + kept[:, :, :, 1]
    kept = jnp.transpose(kept, (2, 0, 1, 3, 4)).reshape(prompts, shards, heads, cache)
    whole_dest = told[:, :, used - share : used].reshape(shards, columns * share)

    vmem = pl.BlockSpec(memory_space=pltpu.VMEM)
    smem = pl.BlockSpec(memory_space=pltpu.SMEM)
    params = pltpu.CompilerParams(vmem_limit_bytes=VMEM_BYTES)
    slots, rows, cols = pl.pallas_call(
        index_kernel,
        out_shape=(
            jax.ShapeDtypeStruct((shards * cap, heads), jnp.int32),
            jax.ShapeDtypeStruct((2, heads, cache), jnp.int32),
            jax.ShapeDtypeStruct((2, cache, heads), jnp.int32),
        ),
        in_specs=[smem, vmem, vmem, vmem],
        out_specs=(vmem, vmem, vmem),
        scratch_shapes=[pltpu.VMEM((shards, 2 * heads, cache), jnp.bfloat16)],
        compiler_params=params,
    )(facts, kept[0], kept[1, shards - 2 :], whole_dest)

    group_width = qwidth // heads_dev
    attention, row_scores = pl.pallas_call(
        attention_kernel,
        grid_spec=pltpu.PrefetchScalarGridSpec(
            num_scalar_prefetch=1,
            grid=(heads_dev,),
            in_specs=[
                pl.BlockSpec((prompts, span, group_width), lambda h, w: (0, 0, h)),
                pl.BlockSpec((prompts, span, WIDTH), lambda h, w: (0, 0, h)),
                pl.BlockSpec((shards, 1, span, WIDTH), lambda h, w: (0, w[3], 0, h)),
                pl.BlockSpec((1, 1, span, WIDTH), lambda h, w: (shards - 2, w[3], 1, h)),
                pl.BlockSpec((2, heads, cache), lambda h, w: (0, 0, 0)),
                pl.BlockSpec((2, cache, heads), lambda h, w: (0, 0, 0)),
            ],
            out_specs=(
                pl.BlockSpec((prompts, span, group_width), lambda h, w: (0, 0, h)),
                pl.BlockSpec((prompts, heads_dev, cache + span), lambda h, w: (0, 0, 0)),
            ),
        ),
        out_shape=(
            jax.ShapeDtypeStruct((prompts, span, qwidth), jnp.bfloat16),
            jax.ShapeDtypeStruct((prompts, heads_dev, cache + span), jnp.float32),
        ),
        compiler_params=params,
    )(facts, query, kv_rows, whole, whole, rows, cols)

    owner_cache = pl.pallas_call(
        owner_kernel,
        grid=(heads,),
        in_specs=[
            pl.BlockSpec((shards * cap, heads), lambda g: (0, 0)),
            pl.BlockSpec(
                (shards, 1, span, WIDTH), lambda g: (0, g // heads_dev, 0, g % heads_dev)
            ),
            pl.BlockSpec(
                (2, 1, span, WIDTH),
                lambda g: (shards // 2 - 1, g // heads_dev, 1, g % heads_dev),
            ),
        ],
        out_specs=pl.BlockSpec((shards * cap, WIDTH), lambda g: (0, g)),
        out_shape=jax.ShapeDtypeStruct((shards * cap, heads * WIDTH), jnp.bfloat16),
        compiler_params=params,
    )(slots, whole, whole)
    return (attention, row_scores, owner_cache)


def dot(a, b, dims=((1,), (0,))):
    return lax.dot_general(a, b, (dims, ((), ())), preferred_element_type=jnp.float32)


def marks(table):
    return table.astype(jnp.float32).astype(jnp.bfloat16)


def early_of(offsets_ref):
    return jnp.where(offsets_ref[0] < offsets_ref[1], 0, 1)


def prepare_kernel(
    offsets_ref, kv_ref, keep_ref, dest_ref, both_ref, single_ref, keep, dest, sems
):
    span = kv_ref.shape[1]
    heads, cache = keep_ref.shape[2], keep_ref.shape[3]
    early = early_of(offsets_ref)
    copies = [
        (keep_ref, keep),
        (dest_ref, dest),
        (kv_ref.at[early], single_ref.at[:span]),
        (kv_ref.at[early], both_ref.at[:span]),
        (kv_ref.at[1 - early], both_ref.at[span : 2 * span]),
    ]
    copies = [
        pltpu.make_async_copy(source, target, sems.at[index])
        for index, (source, target) in enumerate(copies)
    ]
    for copy in copies:
        copy.start()
    for copy in copies[:2]:
        copy.wait()
    lane = lax.broadcasted_iota(jnp.int32, (heads, cache), 1)
    rows = [
        keep[early, 0] - lane,
        dest[:, :cache],
        dest[:, cache:],
        keep[1 - early, 0] - lane,
        jnp.zeros((NOTES - 2 * heads - 2, cache), jnp.int32),
    ]
    rows = jnp.concatenate([row.astype(jnp.float32) for row in rows], axis=0)
    rows = rows.astype(jnp.bfloat16)
    single_ref[span:, :] = rows
    both_ref[2 * span :, :] = rows
    for copy in copies[2:]:
        copy.wait()


def two_notes(first, first_row, second, second_row):
    half = NOTES // 2
    return jnp.concatenate(
        [
            first[first_row : first_row + NOTES, :].astype(jnp.float32)[:half],
            second[second_row : second_row + NOTES, :].astype(jnp.float32)[:half],
        ],
        axis=0,
    ).astype(jnp.bfloat16)


def going_kernel(both, y_own, x_own, d_own, going_ref):
    span = both.shape[0] // 2 - NOTES // 2
    going_ref[:span, :] = both[:span, :]
    going_ref[span : 2 * span, :] = y_own[:span, :]
    going_ref[2 * span : 2 * span + NOTES, :] = two_notes(both, 2 * span, y_own, 2 * span)
    going_ref[2 * span + NOTES :, :] = two_notes(x_own, span, d_own, span)


def beside_kernel(below, above, both, _, beside_ref, relay_ref):
    span = relay_ref.shape[0]
    beside_ref[:span, :] = below[:span, :]
    beside_ref[span : 2 * span, :] = above[:span, :]
    beside_ref[2 * span :, :] = two_notes(below, 2 * span, above, span)
    level = lax.axis_index("ctx") // 2

    @pl.when(level == 0)
    def _():
        relay_ref[...] = below[span : 2 * span, :]

    @pl.when(level > 0)
    def _():
        relay_ref[...] = both[span : 2 * span, :]


def join_second_kernel(beyond, relay, relayed, *rest):
    out_ref, late_ref = rest[-2:]
    span = relay.shape[0]
    level = lax.axis_index("ctx") // 2
    out_ref[: 2 * span, :] = beyond[: 2 * span, :]
    for ref, chosen in ((relay, (level == 0) | (level == 3)), (relayed, (level == 1) | (level == 2))):

        @pl.when(chosen)
        def _(ref=ref):
            out_ref[2 * span :, :] = ref[...]
            late_ref[...] = ref[...]


def place_of(turn, flip, shards):
    mine = lax.axis_index("ctx")
    place = lax.rem(mine - 2 * turn + shards, shards)
    return place + 1 - 2 * lax.rem(mine, 2) if flip else place


def sort_tokens(pieces, tokens, span):
    shards = tokens.shape[0] // span
    for ref, base, turn, flip in pieces:
        place = place_of(turn, flip, shards)
        tokens[pl.ds(pl.multiple_of(place * span, span), span), :] = ref[base : base + span, :]


def sort_late(pieces, late_tokens):
    span = late_tokens.shape[0] // 2
    side = lax.rem(lax.axis_index("ctx"), 2)
    for flip, ref_base in enumerate(pieces):
        ref, base = ref_base
        place = side + flip - 2 * side * flip
        late_tokens[pl.ds(pl.multiple_of(place * span, span), span), :] = ref[
            base : base + span, :
        ]


def read_notes(ref, base, part, heads):
    half = NOTES // 2
    rows = ref[base : base + NOTES, :].astype(jnp.float32).astype(jnp.int32)
    rows = rows[part * half : (part + 1) * half]
    lane = lax.broadcasted_iota(jnp.int32, (heads, rows.shape[1]), 1)
    return rows[:heads] + lane, rows[heads + 2 : 2 * heads + 2] + lane, rows[heads : heads + 2]


def sort_notes(notes, keeps, dests):
    shards, heads = keeps.shape[0], keeps.shape[1] // 4
    for ref, base, part, turn, flip in notes:
        place = place_of(turn, flip, shards)
        early, late, dest = read_notes(ref, base, part, heads)
        keeps[place, :heads, :] = early
        keeps[place, heads : 2 * heads, :] = late
        dests[place, :, :] = dest


def follow_lists(keeps, coded, span):
    shards, rows, cache = keeps.shape
    heads = rows // 4
    row = lax.broadcasted_iota(jnp.int32, (rows, cache), 0)
    is_early = row < heads
    state = jnp.where(row < 0, keeps[0], 0)
    own = state
    mine = lax.axis_index("ctx")
    for shard in range(shards):
        own = jnp.where(mine == shard, state, own)
        late_first = (shards + shard - (shards - 2)) * span + 1
        fresh = jnp.where(is_early[:, :LANES], shard * span + 1, late_first)
        state = look_up(state, keeps[shard], fresh)
        if shard < shards - 2:
            state = jnp.where(is_early, state, 0)
        coded[shard] = split(state)
    return own


def find_slots(early, dests, coded, owner, slots):
    shards, halves, cache = dests.shape
    heads = coded.shape[1] // 8
    cap = slots.shape[0] // shards
    upper = marks(
        lax.broadcasted_iota(jnp.int32, (LANES, LANES), 0)
        <= lax.broadcasted_iota(jnp.int32, (LANES, LANES), 1)
    )
    place = lax.broadcasted_iota(jnp.int32, (cap, cache), 0).astype(jnp.float32) + 1.0
    total = jnp.zeros((shards, 1), jnp.float32)
    ranks = []
    for half in range(halves):
        named = (dests[:, half, :] == owner).astype(jnp.float32)
        parts = []
        for chunk in range(cache // LANES):
            part = named[:, chunk * LANES : (chunk + 1) * LANES]
            upto = dot(part.astype(jnp.bfloat16), upper)
            parts.append(jnp.where(part > 0, upto + total, 0.0))
            total = total + upto[:, LANES - 1 :]
        ranks.append(jnp.concatenate(parts, axis=1))
    rank_early = jnp.where(early == 0, ranks[0], ranks[1])
    rank_late = jnp.where(early == 0, ranks[1], ranks[0])
    across = ((1,), (1,))
    for shard in range(shards):
        found = dot(marks(rank_early[shard : shard + 1] == place), coded[shard], across)
        tokens = found[:, :heads] * 128.0 + found[:, 4 * heads : 5 * heads]
        if shard >= shards - 2:
            found = dot(marks(rank_late[shard : shard + 1] == place), coded[shard], across)
            tokens += found[:, heads : 2 * heads] * 128.0 + found[:, 5 * heads : 6 * heads]
        slots[shard * cap : (shard + 1) * cap, :] = tokens.astype(jnp.int32)


def place_bands(slots, tokens, out_ref, bands, total_bands):
    rows, heads = slots.shape
    reach = tokens.shape[0]
    band = rows // total_bands
    for head in range(heads):
        lanes = slice(head * WIDTH, (head + 1) * WIDTH)
        for order, index in enumerate(bands):
            part = slots[index * band : (index + 1) * band, head : head + 1]
            found = picked(part, 1, tokens[: (index + 1) * reach // total_bands, lanes])
            out_ref[order * band : (order + 1) * band, lanes] = found.astype(jnp.bfloat16)


def add_late(slots, first, late_tokens, out_ref, base):
    band, heads = slots.shape
    for head in range(heads):
        lanes = slice(head * WIDTH, (head + 1) * WIDTH)
        found = picked(slots[:, head : head + 1], first, late_tokens[:, lanes])
        out_ref[base : base + band, lanes] += found.astype(jnp.bfloat16)


def attend_columns(q_ref, head, rows, seen, out_ref, score_ref):
    span = q_ref.shape[1]
    total = rows.shape[0]
    cache = total - span
    group = q_ref.shape[2] // (score_ref.shape[1] * HEAD)
    keys, values = rows[:, :HEAD], rows[:, HEAD:]
    flat = jnp.transpose(values.astype(jnp.float32)).astype(jnp.bfloat16)
    lane = lax.broadcasted_iota(jnp.int32, (total, HEAD), 1)
    hidden = jnp.where(seen > 0, 0.0, -1e30)
    hidden = jnp.concatenate([hidden, jnp.zeros((span, 1), jnp.float32)], axis=0)
    hidden = jnp.where(lane == 0, hidden, 0.0).astype(jnp.bfloat16)
    keys = jnp.concatenate([keys, hidden], axis=1)
    ones = jnp.ones((2 * span, HEAD), jnp.bfloat16)
    causal = lax.broadcasted_iota(jnp.int32, (span, 2 * span), 0) <= lax.rem(
        lax.broadcasted_iota(jnp.int32, (span, 2 * span), 1), span
    )
    bias = jnp.where(causal, 0.0, -1e30)
    scale = math.log2(math.e) / math.sqrt(HEAD)
    mass = None
    for pair in range(group // 2):
        first = (head * group + 2 * pair) * HEAD
        query = jnp.concatenate(
            [
                q_ref[0, :, first : first + HEAD],
                q_ref[0, :, first + HEAD : first + 2 * HEAD],
            ],
            axis=0,
        )
        scores = dot(keys, jnp.concatenate([query, ones], axis=1), ((1,), (1,)))
        near = scores[cache:] + bias
        scores = jnp.concatenate([scores[:cache], near], axis=0) * scale
        peak = jnp.max(scores, axis=0, keepdims=True)
        expo = jnp.exp2(scores - peak)
        weights = expo * (1.0 / jnp.sum(expo, axis=0, keepdims=True))
        both = weights[:, :span] + weights[:, span:]
        mass = both if mass is None else mass + both
        mixed = jnp.transpose(dot(flat, weights.astype(jnp.bfloat16)))
        for member in range(2):
            lanes = slice(first + member * HEAD, first + (member + 1) * HEAD)
            out_ref[0, :, lanes] = mixed[member * span : (member + 1) * span].astype(
                jnp.bfloat16
            )
    score_ref[0, head : head + 1, :] = jnp.sum(jnp.transpose(mass), axis=0, keepdims=True)


def late_kernel(offsets_ref, q_ref, both_ref, beside_ref, out_ref, score_ref, done_ref):
    mine, shards = lax.axis_index("ctx"), lax.axis_size("ctx")
    heads, cache = score_ref.shape[1], score_ref.shape[2] - q_ref.shape[1]
    span = q_ref.shape[1]
    done_ref[...] = jnp.zeros(done_ref.shape, jnp.float32)

    @pl.when(mine >= shards - 2)
    def _():
        _, keep, _ = read_notes(beside_ref, 2 * span, 0, heads)
        state = jnp.where(keep >= cache, keep - cache + 1, 0)
        state = jnp.where(mine == shards - 1, state, 0).astype(jnp.float32)
        state = jnp.concatenate([state, jnp.zeros((8 - heads, cache), jnp.float32)], axis=0)
        columns = jnp.transpose(state).astype(jnp.int32)
        for head in range(heads):
            lanes = slice(head * WIDTH, (head + 1) * WIDTH)
            column = columns[:, head : head + 1]
            cached = picked(column, 1, beside_ref[span : 2 * span, lanes])
            rows = jnp.concatenate(
                [cached.astype(jnp.bfloat16), both_ref[span : 2 * span, lanes]], axis=0
            )
            attend_columns(q_ref, head, rows, column, out_ref, score_ref)

    @pl.when(mine < shards - 2)
    def _():
        out_ref[...] = jnp.zeros(out_ref.shape, out_ref.dtype)
        score_ref[...] = jnp.zeros(score_ref.shape, jnp.float32)


def output_part(cache_ref, row, rows, column):
    width = cache_ref.shape[1] // lax.axis_size("kv")
    return cache_ref.at[
        pl.ds(row, rows), pl.ds(pl.multiple_of(column * width, width), width)
    ]


def near_kernel(offsets_ref, *rest):
    both, beside, beyond, y_own, y_beside, x_own, x_beside, d_own, d_beside = rest[:9]
    cache_ref, tokens, own_ref, top_sent, low_ref, slots_ref = rest[9:15]
    top, sem = rest[15:17]
    tables = (rest[17:20], rest[20:23])
    span = both.shape[0] // 2 - NOTES // 2
    early = early_of(offsets_ref)
    column = lax.axis_index("kv")
    me = lax.axis_index("ctx") * lax.axis_size("kv") + column

    def fill_slots(which, notes):
        keeps, dests, coded = tables[which]
        sort_notes(notes, keeps, dests)
        own = follow_lists(keeps, coded, span)
        for flip in range(2):
            find_slots(early, dests, coded, me ^ flip, slots_ref.at[which, flip])
        return own

    at = 2 * span
    own = fill_slots(
        0,
        [
            (both, at, 0, 0, 0),
            (beside, at, 0, 1, 0),
            (beside, at, 1, 3, 0),
            (beyond, at, 0, 2, 0),
            (beyond, at, 1, 2, 1),
            (y_own, at, 0, 0, 1),
            (y_beside, at, 0, 1, 1),
            (y_beside, at, 1, 3, 1),
        ],
    )
    own_ref[...] = jnp.transpose(own.astype(jnp.float32)).astype(jnp.int32)
    pieces = [(both, 0, 0, 0), (beside, 0, 1, 0), (beside, span, 3, 0), (beyond, 0, 2, 0)]
    pieces += [(beyond, span, 2, 1), (y_own, 0, 0, 1), (y_beside, 0, 1, 1), (y_beside, span, 3, 1)]
    sort_tokens(pieces, tokens, span)
    bands = tuple(range(BANDS - 1))
    place_bands(slots_ref.at[0, 0], tokens, top, bands, BANDS)
    copy = pltpu.make_async_copy(top, output_part(cache_ref, 0, top.shape[0], column), sem)
    copy.start()
    place_bands(slots_ref.at[0, 1], tokens, top_sent, bands, BANDS)
    for flip in range(2):
        place_bands(slots_ref.at[0, flip], tokens, low_ref.at[flip], (BANDS - 1,), BANDS)
    fill_slots(
        1,
        [
            (x_own, span, 0, 0, 0),
            (d_own, span, 0, 0, 1),
            (x_beside, at, 0, 1, 0),
            (x_beside, at, 1, 3, 0),
            (d_beside, at, 0, 1, 1),
            (d_beside, at, 1, 3, 1),
            (beyond, at + NOTES, 0, 2, 0),
            (beyond, at + NOTES, 1, 2, 1),
        ],
    )
    copy.wait()


def early_kernel(offsets_ref, q_ref, both, tokens, own_ref, *rest):
    out_ref, score_ref = rest[2:]
    span = q_ref.shape[1]
    for head in range(score_ref.shape[1]):
        lanes = slice(head * WIDTH, (head + 1) * WIDTH)
        chosen = own_ref[:, head : head + 1]
        cached = picked(chosen, 1, tokens[:, lanes]).astype(jnp.bfloat16)
        rows = jnp.concatenate([cached, both[:span, lanes]], axis=0)
        attend_columns(q_ref, head, rows, chosen, out_ref, score_ref)


def far_rows(flip, refs, far_ref, low, tokens, near_late, far_late):
    x_own, x_beside, x_end, d_own, d_beside, d_late, late, y_late, low_ref, slots_ref = refs
    span = late.shape[0]
    rows = slots_ref.shape[2]
    band = rows // BANDS
    first = tokens.shape[0] + 1
    last = pl.ds(rows - band, band)
    sort_late([(late, 0), (y_late, 0)], near_late)
    sort_late([(x_end, 2 * span), (d_late, 0)], far_late)
    low[...] = low_ref[flip]
    add_late(slots_ref.at[0, flip, last], first, near_late, low, 0)
    pieces = [(x_own, 0, 0, 0), (x_beside, 0, 1, 0), (x_beside, span, 3, 0), (x_end, 0, 2, 0)]
    pieces += [(x_end, span, 2, 1), (d_own, 0, 0, 1), (d_beside, 0, 1, 1), (d_beside, span, 3, 1)]
    sort_tokens(pieces, tokens, span)
    place_bands(slots_ref.at[1, flip], tokens, far_ref, tuple(range(BANDS)), BANDS)
    add_late(slots_ref.at[1, flip, last], first, far_late, far_ref, rows - band)


def far_sent_kernel(*refs):
    sent_ref = refs[10]
    rows = refs[9].shape[2]
    far_rows(1, refs[:10], sent_ref.at[:rows], sent_ref.at[rows:], *refs[11:])


def far_kept_kernel(*refs):
    cache_ref, far, low, tokens, near_late, far_late, sems = refs[11:]
    column = lax.axis_index("kv")
    rows, band = far.shape[0], low.shape[0]
    far_rows(0, refs[:10], far, low, tokens, near_late, far_late)
    copies = [
        pltpu.make_async_copy(far, output_part(cache_ref, 0, rows, column ^ 2), sems.at[0]),
        pltpu.make_async_copy(
            low, output_part(cache_ref, rows - band, band, column), sems.at[1]
        ),
    ]
    for copy in copies:
        copy.start()
    for copy in copies:
        copy.wait()


def last_kernel(top_ref, sent_ref, _, cache_ref, sems):
    column = lax.axis_index("kv")
    rows, upper = cache_ref.shape[0], top_ref.shape[0]
    parts = [
        (top_ref, 0, upper, column ^ 1),
        (sent_ref.at[:rows], 0, rows, column ^ 3),
        (sent_ref.at[rows:], upper, rows - upper, column ^ 1),
    ]
    copies = [
        pltpu.make_async_copy(source, output_part(cache_ref, row, count, place), sems.at[index])
        for index, (source, row, count, place) in enumerate(parts)
    ]
    for copy in copies:
        copy.start()
    for copy in copies:
        copy.wait()


def send(value, axis, pairs):
    return lax.ppermute(value, axis, pairs)


def local_in_planes(query, kv_rows, keep, dest, offsets):
    prompts, span, qwidth = query.shape
    shards, columns = lax.axis_size("ctx"), lax.axis_size("kv")
    width = kv_rows.shape[2]
    heads = width // WIDTH
    cache = keep.shape[3]
    rows = 2 * prompts * cache // columns
    band = rows // BANDS
    vmem = pl.BlockSpec(memory_space=pltpu.VMEM)
    smem = pl.BlockSpec(memory_space=pltpu.SMEM)
    anywhere = pl.BlockSpec(memory_space=pl.ANY)
    hbm = pl.BlockSpec(memory_space=pltpu.HBM)
    params = pltpu.CompilerParams(vmem_limit_bytes=PLANE_BYTES)

    def cost(flops, moved):
        return pl.CostEstimate(flops=flops, bytes_accessed=moved, transcendentals=0)

    def piece(count):
        return jax.ShapeDtypeStruct((count, width), jnp.bfloat16)

    def along_z(value, turn):
        return send(value, "ctx", [(i, (i + 2 * turn) % shards) for i in range(shards)])

    def across_y(value):
        return send(value, "ctx", [(i, i ^ 1) for i in range(shards)])

    def across_x(value):
        return send(value, "kv", [(i, i ^ 2) for i in range(columns)])

    def across_both(value):
        pairs = [(i, i ^ columns ^ 2) for i in range(shards * columns)]
        return send(value, ("ctx", "kv"), pairs)

    def across_core(value):
        return send(value, "kv", [(i, i ^ 1) for i in range(columns)])

    both, single = pl.pallas_call(
        prepare_kernel,
        out_shape=(piece(2 * span + NOTES), piece(span + NOTES)),
        in_specs=[smem] + [hbm] * 3,
        out_specs=(vmem, vmem),
        scratch_shapes=[
            pltpu.VMEM(keep.shape, jnp.int32),
            pltpu.VMEM((1, prompts * cache), jnp.int32),
            pltpu.SemaphoreType.DMA((5,)),
        ],
        compiler_params=pltpu.CompilerParams(vmem_limit_bytes=60 * 1024 * 1024),
        cost_estimate=cost(10**9, 1),
    )(offsets, kv_rows, keep, jnp.transpose(dest))

    below, above = along_z(both, 1), along_z(single, 3)
    y_own, x_own, d_own = across_y(both), across_x(single), across_both(single)
    going = pl.pallas_call(
        going_kernel,
        out_shape=piece(2 * span + 2 * NOTES),
        in_specs=[vmem] * 4,
        out_specs=vmem,
        compiler_params=params,
        cost_estimate=cost(0, 10**6),
    )(both, y_own, x_own, d_own)
    beyond = along_z(going, 2)
    beside, relay = pl.pallas_call(
        beside_kernel,
        out_shape=(piece(2 * span + NOTES), piece(span)),
        in_specs=[vmem] * 3 + [anywhere],
        out_specs=(vmem,) * 2,
        compiler_params=params,
        cost_estimate=cost(0, 10**6),
    )(below, above, both, going)
    relayed = send(relay, "ctx", [(0, 2), (1, 3), (6, 4), (7, 5)])
    y_beside, x_beside, d_beside = across_y(beside), across_x(beside), across_both(beside)

    attention_shape = jax.ShapeDtypeStruct((prompts, span, qwidth), jnp.bfloat16)
    score_shape = jax.ShapeDtypeStruct((prompts, heads, cache + span), jnp.float32)

    def prompt_specs(late):
        def block(_, offsets_ref):
            early = early_of(offsets_ref)
            return (1 - early if late else early, 0, 0)

        return (
            pl.BlockSpec((1, span, qwidth), block),
            pl.BlockSpec((1, heads, cache + span), block),
        )

    attention, row_scores, late_done = pl.pallas_call(
        late_kernel,
        grid_spec=pltpu.PrefetchScalarGridSpec(
            num_scalar_prefetch=1,
            grid=(1,),
            in_specs=[prompt_specs(True)[0], vmem, vmem],
            out_specs=prompt_specs(True) + (vmem,),
        ),
        out_shape=(attention_shape, score_shape, jax.ShapeDtypeStruct((8, LANES), jnp.float32)),
        compiler_params=params,
        cost_estimate=cost(10**6, 1),
    )(offsets, query, both, y_own)

    end, late = pl.pallas_call(
        join_second_kernel,
        out_shape=(piece(3 * span), piece(span)),
        in_specs=[vmem] * 3 + [anywhere] * 4,
        out_specs=(vmem, vmem),
        compiler_params=params,
        cost_estimate=cost(10**6, 1),
    )(beyond, relay, relayed, y_beside, x_beside, d_beside, late_done)
    x_end, y_late, d_late = across_x(end), across_y(late), across_both(late)

    tokens = pltpu.VMEM((shards * span, width), jnp.bfloat16)
    late_tokens = pltpu.VMEM((2 * span, width), jnp.bfloat16)
    cache_shape = jax.ShapeDtypeStruct((rows, columns * width), jnp.bfloat16)
    owner_cache, sorted_tokens, own_slots, top_sent, low, slots = pl.pallas_call(
        near_kernel,
        out_shape=(
            cache_shape,
            piece(shards * span),
            jax.ShapeDtypeStruct((cache, 4 * heads), jnp.int32),
            piece(rows - band),
            jax.ShapeDtypeStruct((2, band, width), jnp.bfloat16),
            jax.ShapeDtypeStruct((2, 2, rows, heads), jnp.int32),
        ),
        in_specs=[smem] + [vmem] * 9,
        out_specs=(hbm,) + (vmem,) * 5,
        scratch_shapes=[pltpu.VMEM((rows - band, width), jnp.bfloat16), pltpu.SemaphoreType.DMA]
        + 2
        * [
            pltpu.VMEM((shards, 4 * heads, cache), jnp.int32),
            pltpu.VMEM((shards, prompts, cache), jnp.int32),
            pltpu.VMEM((shards, 8 * heads, cache), jnp.bfloat16),
        ],
        compiler_params=params,
        cost_estimate=cost(10**9, 10**7),
    )(offsets, both, beside, beyond, y_own, y_beside, x_own, x_beside, d_own, d_beside)
    attention, row_scores = pl.pallas_call(
        early_kernel,
        grid_spec=pltpu.PrefetchScalarGridSpec(
            num_scalar_prefetch=1,
            grid=(1,),
            in_specs=[prompt_specs(False)[0]] + [vmem] * 3 + [anywhere] * 2,
            out_specs=prompt_specs(False),
        ),
        out_shape=(attention_shape, score_shape),
        input_output_aliases={5: 0, 6: 1},
        compiler_params=params,
        cost_estimate=cost(5 * 10**9, 10**7),
    )(offsets, query, both, sorted_tokens, own_slots, attention, row_scores)
    top = across_core(top_sent)
    far = (x_own, x_beside, x_end, d_own, d_beside, d_late, late, y_late, low, slots)
    sent = pl.pallas_call(
        far_sent_kernel,
        out_shape=piece(rows + band),
        in_specs=[vmem] * 10,
        out_specs=vmem,
        scratch_shapes=[tokens, late_tokens, late_tokens],
        compiler_params=params,
        cost_estimate=cost(2 * 10**9, 4 * 10**6),
    )(*far)
    received = across_core(sent)
    owner_cache = pl.pallas_call(
        far_kept_kernel,
        out_shape=cache_shape,
        in_specs=[vmem] * 10 + [hbm],
        out_specs=hbm,
        scratch_shapes=[
            pltpu.VMEM((rows, width), jnp.bfloat16),
            pltpu.VMEM((band, width), jnp.bfloat16),
            tokens,
            late_tokens,
            late_tokens,
            pltpu.SemaphoreType.DMA((2,)),
        ],
        input_output_aliases={10: 0},
        compiler_params=params,
        cost_estimate=cost(2 * 10**9, 4 * 10**6),
    )(*far, owner_cache)
    owner_cache = pl.pallas_call(
        last_kernel,
        out_shape=cache_shape,
        in_specs=[anywhere] * 2 + [hbm],
        out_specs=hbm,
        scratch_shapes=[pltpu.SemaphoreType.DMA((3,))],
        input_output_aliases={2: 0},
        compiler_params=params,
        cost_estimate=cost(0, 10**6),
    )(top, received, owner_cache)
    return (attention, row_scores, owner_cache)


def solution(mesh):
    placed = (
        P(None, "ctx", "kv"),
        P(None, "ctx", "kv"),
        P(None, "ctx", "kv", None),
        P("ctx", None),
        P(),
    )
    in_planes = mesh.shape["ctx"] == 8 and mesh.shape["kv"] == 4
    return jax.shard_map(
        local_in_planes if in_planes else local,
        mesh=mesh,
        in_specs=placed,
        out_specs=(P(None, "ctx", "kv"), P(None, "kv", "ctx"), P(("ctx", "kv"), None)),
        check_vma=False,
    )
```

```python
import functools
import math

import jax
import jax.numpy as jnp
from jax import lax
from jax.experimental import pallas as pl
from jax.experimental.pallas import tpu as pltpu
from jax.sharding import PartitionSpec as P

HEAD = 128
WIDTH = 2 * HEAD
LANES = 128
VMEM_BYTES = 56 * 1024 * 1024
PLANE_BYTES = 28 * 1024 * 1024
NOTES = 16
BANDS = 4


def look_up(state, keep, fresh):
    tiles = state.shape[1] // LANES
    parts = []
    for tile in range(tiles):
        wanted = keep[:, tile * LANES : (tile + 1) * LANES]
        high = wanted >> 7
        low = wanted & 127
        found = jnp.where(high >= tiles, fresh + wanted - state.shape[1], 0)
        for source in range(tiles):
            held = state[:, source * LANES : (source + 1) * LANES]
            moved = jnp.take_along_axis(held, low, axis=1, mode="promise_in_bounds")
            found = jnp.where(high == source, moved, found)
        parts.append(found)
    return jnp.concatenate(parts, axis=1)


def split(state):
    both = jnp.concatenate([state >> 7, state & 127], axis=0)
    return both.astype(jnp.float32).astype(jnp.bfloat16)


def index_kernel(
    where_ref, keep_early_ref, keep_late_ref, dest_ref, slot_ref, row_ref, column_ref, coded
):
    shards, heads, cache = keep_early_ref.shape
    cap = slot_ref.shape[0] // shards
    span = LANES
    early, mine, me = where_ref[0], where_ref[1], where_ref[2]
    empty = jnp.minimum(keep_early_ref[0], 0)

    def follow(shard, carry):
        state, own = carry
        own = jnp.where(shard == mine, state, own)
        state = look_up(state, keep_early_ref[shard], shard * span + 1)
        coded[shard] = split(state)
        return state, own

    _, own_early = lax.fori_loop(0, shards, follow, (empty, empty), unroll=shards <= 8)
    base = shards * span + 1
    late_first = look_up(empty, keep_late_ref[0], base)
    late_second = look_up(late_first, keep_late_ref[1], base + span)
    own_late = jnp.where(mine == shards - 1, late_first, 0)
    for index, own in enumerate((own_early, own_late)):
        row_ref[index] = own
        column_ref[index] = jnp.transpose(own.astype(jnp.float32)).astype(jnp.int32)

    named = (dest_ref[...] == me).astype(jnp.float32)
    chunks = named.shape[1] // LANES
    upper = (
        lax.broadcasted_iota(jnp.int32, (LANES, LANES), 0)
        <= lax.broadcasted_iota(jnp.int32, (LANES, LANES), 1)
    ).astype(jnp.float32).astype(jnp.bfloat16)
    total = jnp.zeros((shards, 1), jnp.float32)
    ranks = []
    for chunk in range(chunks):
        part = named[:, chunk * LANES : (chunk + 1) * LANES]
        upto = jnp.dot(part.astype(jnp.bfloat16), upper, preferred_element_type=jnp.float32)
        ranks.append(jnp.where(part > 0, upto + total, 0.0))
        total = total + upto[:, LANES - 1 :]
    low_half = jnp.concatenate(ranks[: chunks // 2], axis=1)
    high_half = jnp.concatenate(ranks[chunks // 2 :], axis=1)
    rank_early = jnp.where(early == 0, low_half, high_half)
    rank_late = jnp.where(early == 0, high_half, low_half)
    place = lax.broadcasted_iota(jnp.int32, (cap, cache), 0).astype(jnp.float32) + 1.0
    contract = (((1,), (1,)), ((), ()))
    for shard in range(shards):
        pick = (rank_early[shard : shard + 1] == place).astype(jnp.float32).astype(jnp.bfloat16)
        found = lax.dot_general(pick, coded[shard], contract, preferred_element_type=jnp.float32)
        if shard >= shards - 2:
            state = late_first if shard == shards - 2 else late_second
            pick = (rank_late[shard : shard + 1] == place).astype(jnp.float32).astype(jnp.bfloat16)
            found += lax.dot_general(
                pick, split(state), contract, preferred_element_type=jnp.float32
            )
        tokens = found[:, :heads] * 128.0 + found[:, heads:]
        slot_ref[shard * cap : (shard + 1) * cap, :] = tokens.astype(jnp.int32)


def column_of(table, head):
    lane = lax.broadcasted_iota(jnp.int32, table.shape, 1)
    return jnp.sum(
        jnp.where(lane == head, table, 0).astype(jnp.float32), axis=1, keepdims=True
    ).astype(jnp.int32)


def picked(column, first, tokens):
    number = lax.broadcasted_iota(jnp.int32, (column.shape[0], tokens.shape[0]), 1) + first
    table = (column == number).astype(jnp.float32).astype(jnp.bfloat16)
    return jnp.dot(table, tokens, preferred_element_type=jnp.float32)


def attend(q_ref, prompt, keys, values, seen, out_ref, score_ref, head):
    span = q_ref.shape[1]
    cache = seen.shape[1]
    group = q_ref.shape[2] // HEAD
    causal = lax.broadcasted_iota(jnp.int32, (span, span), 1) <= lax.broadcasted_iota(
        jnp.int32, (span, span), 0
    )
    bias = jnp.concatenate(
        [
            jnp.broadcast_to(jnp.where(seen > 0, 0.0, -1e30), (span, cache)),
            jnp.where(causal, 0.0, -1e30),
        ],
        axis=1,
    )
    scale = math.log2(math.e) / math.sqrt(HEAD)
    mass = jnp.zeros((1, cache + span), jnp.float32)
    for member in range(group):
        query = q_ref[prompt, :, member * HEAD : (member + 1) * HEAD]
        scores = lax.dot_general(
            query, keys, (((1,), (1,)), ((), ())), preferred_element_type=jnp.float32
        )
        scores = scores + bias
        peak = jnp.max(scores, axis=1, keepdims=True)
        expo = jnp.exp2((scores - peak) * scale)
        weights = expo * (1.0 / jnp.sum(expo, axis=1, keepdims=True))
        mass = mass + jnp.sum(weights, axis=0, keepdims=True)
        mixed = jnp.dot(weights.astype(jnp.bfloat16), values, preferred_element_type=jnp.float32)
        out_ref[prompt, :, member * HEAD : (member + 1) * HEAD] = mixed.astype(jnp.bfloat16)
    score_ref[prompt, pl.ds(head, 1), :] = mass


def attention_kernel(
    where_ref, q_ref, span_ref, early_ref, late_ref, row_ref, column_ref, out_ref, score_ref
):
    early, mine, column, shards = where_ref[0], where_ref[1], where_ref[3], early_ref.shape[0]
    span = q_ref.shape[1]
    late = 1 - early
    local_head = pl.program_id(0)
    head = column * pl.num_programs(0) + local_head

    def run(which, prompt, tokens, first):
        chosen = column_of(column_ref[which], head)
        cached = picked(chosen, first, tokens).astype(jnp.bfloat16)
        rows = jnp.concatenate([cached, span_ref[prompt]], axis=0)
        seen = row_ref[which, pl.ds(head, 1), :]
        attend(
            q_ref, prompt, rows[:, :HEAD], rows[:, HEAD:], seen, out_ref, score_ref, local_head
        )

    run(0, early, early_ref[:, 0].reshape(shards * span, WIDTH), 1)

    @pl.when(mine >= shards - 2)
    def _():
        run(1, late, late_ref[0, 0], shards * span + 1)

    @pl.when(mine < shards - 2)
    def _():
        out_ref[late] = jnp.zeros(out_ref.shape[1:], out_ref.dtype)
        score_ref[late, pl.ds(local_head, 1), :] = jnp.zeros((1, score_ref.shape[2]), jnp.float32)


def owner_kernel(slot_ref, early_ref, late_ref, out_ref):
    shards, _, span, width = early_ref.shape
    rows = out_ref.shape[0]
    chosen = column_of(slot_ref[...], pl.program_id(0))
    bands = 4
    band = rows // bands
    reach = shards * span // bands
    tokens = early_ref[:, 0].reshape(shards * span, width)
    for index in range(bands):
        part = chosen[index * band : (index + 1) * band]
        found = picked(part, 1, tokens[: (index + 1) * reach])
        if index == bands - 1:
            found += picked(part, shards * span + 1, late_ref[:, 0].reshape(2 * span, width))
        out_ref[index * band : (index + 1) * band, :] = found.astype(jnp.bfloat16)


def local(query, kv_rows, keep, dest, offsets):
    prompts, span, qwidth = query.shape
    shards, columns = lax.axis_size("ctx"), lax.axis_size("kv")
    width = kv_rows.shape[2]
    heads_dev = width // WIDTH
    heads = heads_dev * columns
    cache = keep.shape[3]
    owners = shards * columns
    cap = 2 * prompts * cache // owners
    mine, column = lax.axis_index("ctx"), lax.axis_index("kv")
    early = jnp.where(offsets[0] < offsets[1], 0, 1).astype(jnp.int32)
    facts = jnp.stack([early, mine, mine * columns + column, column]).astype(jnp.int32)

    swap = early == 1
    ordered_kv = jnp.where(swap, kv_rows[::-1], kv_rows)
    ordered_keep = jnp.where(swap, keep[::-1, 0], keep[:, 0])
    digits = jnp.stack([ordered_keep >> 7, ordered_keep & 127], axis=1)
    share = dest.shape[0] // columns
    own_dest = lax.dynamic_slice_in_dim(dest[:, 0], column * share, share)
    facts_rows = jnp.concatenate([digits.reshape(-1), own_dest]).astype(jnp.bfloat16)
    used = facts_rows.shape[0]
    room = 16 * width
    facts_rows = jnp.concatenate([facts_rows, jnp.zeros((room - used,), jnp.bfloat16)])
    payload = jnp.concatenate(
        [ordered_kv.reshape(prompts * span, width), facts_rows.reshape(16, width)], axis=0
    )
    whole = lax.all_gather(payload, ("ctx", "kv")).reshape(
        shards, columns, prompts * span + 16, width
    )

    told = whole[:, :, prompts * span :, :].reshape(shards, columns, room).astype(jnp.int32)
    kept = told[:, :, : prompts * 2 * heads_dev * cache].reshape(
        shards, columns, prompts, 2, heads_dev, cache
    )
    kept = kept[:, :, :, 0] * 128 + kept[:, :, :, 1]
    kept = jnp.transpose(kept, (2, 0, 1, 3, 4)).reshape(prompts, shards, heads, cache)
    whole_dest = told[:, :, used - share : used].reshape(shards, columns * share)

    vmem = pl.BlockSpec(memory_space=pltpu.VMEM)
    smem = pl.BlockSpec(memory_space=pltpu.SMEM)
    params = pltpu.CompilerParams(vmem_limit_bytes=VMEM_BYTES)
    slots, rows, cols = pl.pallas_call(
        index_kernel,
        out_shape=(
            jax.ShapeDtypeStruct((shards * cap, heads), jnp.int32),
            jax.ShapeDtypeStruct((2, heads, cache), jnp.int32),
            jax.ShapeDtypeStruct((2, cache, heads), jnp.int32),
        ),
        in_specs=[smem, vmem, vmem, vmem],
        out_specs=(vmem, vmem, vmem),
        scratch_shapes=[pltpu.VMEM((shards, 2 * heads, cache), jnp.bfloat16)],
        compiler_params=params,
    )(facts, kept[0], kept[1, shards - 2 :], whole_dest)

    group_width = qwidth // heads_dev
    attention, row_scores = pl.pallas_call(
        attention_kernel,
        grid_spec=pltpu.PrefetchScalarGridSpec(
            num_scalar_prefetch=1,
            grid=(heads_dev,),
            in_specs=[
                pl.BlockSpec((prompts, span, group_width), lambda h, w: (0, 0, h)),
                pl.BlockSpec((prompts, span, WIDTH), lambda h, w: (0, 0, h)),
                pl.BlockSpec((shards, 1, span, WIDTH), lambda h, w: (0, w[3], 0, h)),
                pl.BlockSpec((1, 1, span, WIDTH), lambda h, w: (shards - 2, w[3], 1, h)),
                pl.BlockSpec((2, heads, cache), lambda h, w: (0, 0, 0)),
                pl.BlockSpec((2, cache, heads), lambda h, w: (0, 0, 0)),
            ],
            out_specs=(
                pl.BlockSpec((prompts, span, group_width), lambda h, w: (0, 0, h)),
                pl.BlockSpec((prompts, heads_dev, cache + span), lambda h, w: (0, 0, 0)),
            ),
        ),
        out_shape=(
            jax.ShapeDtypeStruct((prompts, span, qwidth), jnp.bfloat16),
            jax.ShapeDtypeStruct((prompts, heads_dev, cache + span), jnp.float32),
        ),
        compiler_params=params,
    )(facts, query, kv_rows, whole, whole, rows, cols)

    owner_cache = pl.pallas_call(
        owner_kernel,
        grid=(heads,),
        in_specs=[
            pl.BlockSpec((shards * cap, heads), lambda g: (0, 0)),
            pl.BlockSpec(
                (shards, 1, span, WIDTH), lambda g: (0, g // heads_dev, 0, g % heads_dev)
            ),
            pl.BlockSpec(
                (2, 1, span, WIDTH),
                lambda g: (shards // 2 - 1, g // heads_dev, 1, g % heads_dev),
            ),
        ],
        out_specs=pl.BlockSpec((shards * cap, WIDTH), lambda g: (0, g)),
        out_shape=jax.ShapeDtypeStruct((shards * cap, heads * WIDTH), jnp.bfloat16),
        compiler_params=params,
    )(slots, whole, whole)
    return (attention, row_scores, owner_cache)


def dot(a, b, dims=((1,), (0,))):
    return lax.dot_general(a, b, (dims, ((), ())), preferred_element_type=jnp.float32)


def marks(table):
    return table.astype(jnp.float32).astype(jnp.bfloat16)


def early_of(offsets_ref):
    return jnp.where(offsets_ref[0] < offsets_ref[1], 0, 1)


def prepare_kernel(
    offsets_ref, kv_ref, keep_ref, dest_ref, both_ref, single_ref, keep, dest, sems
):
    span = kv_ref.shape[1]
    heads, cache = keep_ref.shape[2], keep_ref.shape[3]
    early = early_of(offsets_ref)
    copies = [
        (keep_ref, keep),
        (dest_ref, dest),
        (kv_ref.at[early], single_ref.at[:span]),
        (kv_ref.at[early], both_ref.at[:span]),
        (kv_ref.at[1 - early], both_ref.at[span : 2 * span]),
    ]
    copies = [
        pltpu.make_async_copy(source, target, sems.at[index])
        for index, (source, target) in enumerate(copies)
    ]
    for copy in copies:
        copy.start()
    for copy in copies[:2]:
        copy.wait()
    lane = lax.broadcasted_iota(jnp.int32, (heads, cache), 1)
    rows = [
        keep[early, 0] - lane,
        dest[:, :cache],
        dest[:, cache:],
        keep[1 - early, 0] - lane,
        jnp.zeros((NOTES - 2 * heads - 2, cache), jnp.int32),
    ]
    rows = jnp.concatenate([row.astype(jnp.float32) for row in rows], axis=0)
    rows = rows.astype(jnp.bfloat16)
    single_ref[span:, :] = rows
    both_ref[2 * span :, :] = rows
    for copy in copies[2:]:
        copy.wait()


def two_notes(first, first_row, second, second_row):
    half = NOTES // 2
    return jnp.concatenate(
        [
            first[first_row : first_row + NOTES, :].astype(jnp.float32)[:half],
            second[second_row : second_row + NOTES, :].astype(jnp.float32)[:half],
        ],
        axis=0,
    ).astype(jnp.bfloat16)


def going_kernel(both, y_own, x_own, d_own, going_ref):
    span = both.shape[0] // 2 - NOTES // 2
    going_ref[:span, :] = both[:span, :]
    going_ref[span : 2 * span, :] = y_own[:span, :]
    going_ref[2 * span : 2 * span + NOTES, :] = two_notes(both, 2 * span, y_own, 2 * span)
    going_ref[2 * span + NOTES :, :] = two_notes(x_own, span, d_own, span)


def beside_kernel(below, above, both, _, beside_ref, relay_ref):
    span = relay_ref.shape[0]
    beside_ref[:span, :] = below[:span, :]
    beside_ref[span : 2 * span, :] = above[:span, :]
    beside_ref[2 * span :, :] = two_notes(below, 2 * span, above, span)
    level = lax.axis_index("ctx") // 2

    @pl.when(level == 0)
    def _():
        relay_ref[...] = below[span : 2 * span, :]

    @pl.when(level > 0)
    def _():
        relay_ref[...] = both[span : 2 * span, :]


def join_second_kernel(beyond, relay, relayed, *rest):
    out_ref, late_ref = rest[-2:]
    span = relay.shape[0]
    level = lax.axis_index("ctx") // 2
    out_ref[: 2 * span, :] = beyond[: 2 * span, :]
    for ref, chosen in ((relay, (level == 0) | (level == 3)), (relayed, (level == 1) | (level == 2))):

        @pl.when(chosen)
        def _(ref=ref):
            out_ref[2 * span :, :] = ref[...]
            late_ref[...] = ref[...]


def place_of(turn, flip, shards):
    mine = lax.axis_index("ctx")
    place = lax.rem(mine - 2 * turn + shards, shards)
    return place + 1 - 2 * lax.rem(mine, 2) if flip else place


def sort_tokens(pieces, tokens, span):
    shards = tokens.shape[0] // span
    for ref, base, turn, flip in pieces:
        place = place_of(turn, flip, shards)
        tokens[pl.ds(pl.multiple_of(place * span, span), span), :] = ref[base : base + span, :]


def sort_late(pieces, late_tokens):
    span = late_tokens.shape[0] // 2
    side = lax.rem(lax.axis_index("ctx"), 2)
    for flip, ref_base in enumerate(pieces):
        ref, base = ref_base
        place = side + flip - 2 * side * flip
        late_tokens[pl.ds(pl.multiple_of(place * span, span), span), :] = ref[
            base : base + span, :
        ]


def read_notes(ref, base, part, heads):
    half = NOTES // 2
    rows = ref[base : base + NOTES, :].astype(jnp.float32).astype(jnp.int32)
    rows = rows[part * half : (part + 1) * half]
    lane = lax.broadcasted_iota(jnp.int32, (heads, rows.shape[1]), 1)
    return rows[:heads] + lane, rows[heads + 2 : 2 * heads + 2] + lane, rows[heads : heads + 2]


def sort_notes(notes, keeps, dests):
    shards, heads = keeps.shape[0], keeps.shape[1] // 4
    for ref, base, part, turn, flip in notes:
        place = place_of(turn, flip, shards)
        early, late, dest = read_notes(ref, base, part, heads)
        keeps[place, :heads, :] = early
        keeps[place, heads : 2 * heads, :] = late
        dests[place, :, :] = dest


def follow_lists(keeps, coded, span):
    shards, rows, cache = keeps.shape
    heads = rows // 4
    row = lax.broadcasted_iota(jnp.int32, (rows, cache), 0)
    is_early = row < heads
    state = jnp.where(row < 0, keeps[0], 0)
    own = state
    mine = lax.axis_index("ctx")
    for shard in range(shards):
        own = jnp.where(mine == shard, state, own)
        late_first = (shards + shard - (shards - 2)) * span + 1
        fresh = jnp.where(is_early[:, :LANES], shard * span + 1, late_first)
        state = look_up(state, keeps[shard], fresh)
        if shard < shards - 2:
            state = jnp.where(is_early, state, 0)
        coded[shard] = split(state)
    return own


def find_slots(early, dests, coded, owner, slots):
    shards, halves, cache = dests.shape
    heads = coded.shape[1] // 8
    cap = slots.shape[0] // shards
    upper = marks(
        lax.broadcasted_iota(jnp.int32, (LANES, LANES), 0)
        <= lax.broadcasted_iota(jnp.int32, (LANES, LANES), 1)
    )
    place = lax.broadcasted_iota(jnp.int32, (cap, cache), 0).astype(jnp.float32) + 1.0
    total = jnp.zeros((shards, 1), jnp.float32)
    ranks = []
    for half in range(halves):
        named = (dests[:, half, :] == owner).astype(jnp.float32)
        parts = []
        for chunk in range(cache // LANES):
            part = named[:, chunk * LANES : (chunk + 1) * LANES]
            upto = dot(part.astype(jnp.bfloat16), upper)
            parts.append(jnp.where(part > 0, upto + total, 0.0))
            total = total + upto[:, LANES - 1 :]
        ranks.append(jnp.concatenate(parts, axis=1))
    rank_early = jnp.where(early == 0, ranks[0], ranks[1])
    rank_late = jnp.where(early == 0, ranks[1], ranks[0])
    across = ((1,), (1,))
    for shard in range(shards):
        found = dot(marks(rank_early[shard : shard + 1] == place), coded[shard], across)
        tokens = found[:, :heads] * 128.0 + found[:, 4 * heads : 5 * heads]
        if shard >= shards - 2:
            found = dot(marks(rank_late[shard : shard + 1] == place), coded[shard], across)
            tokens += found[:, heads : 2 * heads] * 128.0 + found[:, 5 * heads : 6 * heads]
        slots[shard * cap : (shard + 1) * cap, :] = tokens.astype(jnp.int32)


def place_bands(slots, tokens, out_ref, bands, total_bands):
    rows, heads = slots.shape
    reach = tokens.shape[0]
    band = rows // total_bands
    for head in range(heads):
        lanes = slice(head * WIDTH, (head + 1) * WIDTH)
        for order, index in enumerate(bands):
            part = slots[index * band : (index + 1) * band, head : head + 1]
            found = picked(part, 1, tokens[: (index + 1) * reach // total_bands, lanes])
            out_ref[order * band : (order + 1) * band, lanes] = found.astype(jnp.bfloat16)


def add_late(slots, first, late_tokens, out_ref, base):
    band, heads = slots.shape
    for head in range(heads):
        lanes = slice(head * WIDTH, (head + 1) * WIDTH)
        found = picked(slots[:, head : head + 1], first, late_tokens[:, lanes])
        out_ref[base : base + band, lanes] += found.astype(jnp.bfloat16)


def attend_columns(q_ref, head, rows, seen, out_ref, score_ref):
    span = q_ref.shape[1]
    total = rows.shape[0]
    cache = total - span
    group = q_ref.shape[2] // (score_ref.shape[1] * HEAD)
    keys, values = rows[:, :HEAD], rows[:, HEAD:]
    flat = jnp.transpose(values.astype(jnp.float32)).astype(jnp.bfloat16)
    lane = lax.broadcasted_iota(jnp.int32, (total, HEAD), 1)
    hidden = jnp.where(seen > 0, 0.0, -1e30)
    hidden = jnp.concatenate([hidden, jnp.zeros((span, 1), jnp.float32)], axis=0)
    hidden = jnp.where(lane == 0, hidden, 0.0).astype(jnp.bfloat16)
    keys = jnp.concatenate([keys, hidden], axis=1)
    ones = jnp.ones((2 * span, HEAD), jnp.bfloat16)
    causal = lax.broadcasted_iota(jnp.int32, (span, 2 * span), 0) <= lax.rem(
        lax.broadcasted_iota(jnp.int32, (span, 2 * span), 1), span
    )
    bias = jnp.where(causal, 0.0, -1e30)
    scale = math.log2(math.e) / math.sqrt(HEAD)
    mass = None
    for pair in range(group // 2):
        first = (head * group + 2 * pair) * HEAD
        query = jnp.concatenate(
            [
                q_ref[0, :, first : first + HEAD],
                q_ref[0, :, first + HEAD : first + 2 * HEAD],
            ],
            axis=0,
        )
        scores = dot(keys, jnp.concatenate([query, ones], axis=1), ((1,), (1,)))
        near = scores[cache:] + bias
        scores = jnp.concatenate([scores[:cache], near], axis=0) * scale
        peak = jnp.max(scores, axis=0, keepdims=True)
        expo = jnp.exp2(scores - peak)
        weights = expo * (1.0 / jnp.sum(expo, axis=0, keepdims=True))
        both = weights[:, :span] + weights[:, span:]
        mass = both if mass is None else mass + both
        mixed = jnp.transpose(dot(flat, weights.astype(jnp.bfloat16)))
        for member in range(2):
            lanes = slice(first + member * HEAD, first + (member + 1) * HEAD)
            out_ref[0, :, lanes] = mixed[member * span : (member + 1) * span].astype(
                jnp.bfloat16
            )
    score_ref[0, head : head + 1, :] = jnp.sum(jnp.transpose(mass), axis=0, keepdims=True)


def late_kernel(offsets_ref, q_ref, both_ref, beside_ref, out_ref, score_ref, done_ref):
    mine, shards = lax.axis_index("ctx"), lax.axis_size("ctx")
    heads, cache = score_ref.shape[1], score_ref.shape[2] - q_ref.shape[1]
    span = q_ref.shape[1]
    done_ref[...] = jnp.zeros(done_ref.shape, jnp.float32)

    @pl.when(mine >= shards - 2)
    def _():
        _, keep, _ = read_notes(beside_ref, 2 * span, 0, heads)
        state = jnp.where(keep >= cache, keep - cache + 1, 0)
        state = jnp.where(mine == shards - 1, state, 0).astype(jnp.float32)
        state = jnp.concatenate([state, jnp.zeros((8 - heads, cache), jnp.float32)], axis=0)
        columns = jnp.transpose(state).astype(jnp.int32)
        for head in range(heads):
            lanes = slice(head * WIDTH, (head + 1) * WIDTH)
            column = columns[:, head : head + 1]
            cached = picked(column, 1, beside_ref[span : 2 * span, lanes])
            rows = jnp.concatenate(
                [cached.astype(jnp.bfloat16), both_ref[span : 2 * span, lanes]], axis=0
            )
            attend_columns(q_ref, head, rows, column, out_ref, score_ref)

    @pl.when(mine < shards - 2)
    def _():
        out_ref[...] = jnp.zeros(out_ref.shape, out_ref.dtype)
        score_ref[...] = jnp.zeros(score_ref.shape, jnp.float32)


def output_part(cache_ref, row, rows, column):
    width = cache_ref.shape[1] // lax.axis_size("kv")
    return cache_ref.at[
        pl.ds(row, rows), pl.ds(pl.multiple_of(column * width, width), width)
    ]


def fill_slots(offsets_ref, notes, keeps, dests, coded, slots_ref):
    me = lax.axis_index("ctx") * lax.axis_size("kv") + lax.axis_index("kv")
    sort_notes(notes, keeps, dests)
    own = follow_lists(keeps, coded, LANES)
    for flip in range(2):
        find_slots(early_of(offsets_ref), dests, coded, me ^ flip, slots_ref.at[flip])
    return own


def early_kernel(offsets_ref, q_ref, *rest):
    both, beside, beyond, y_own, y_beside = rest[:5]
    out_ref, score_ref, done_ref, cache_ref, top_sent, low_ref, slots_ref = rest[8:15]
    tokens, top, sem, keeps, dests, coded = rest[15:]
    done_ref[...] = jnp.zeros(done_ref.shape, jnp.float32)
    span = both.shape[0] // 2 - NOTES // 2
    column = lax.axis_index("kv")
    at = 2 * span
    notes = [(both, at, 0, 0, 0), (beside, at, 0, 1, 0), (beside, at, 1, 3, 0)]
    notes += [(beyond, at, 0, 2, 0), (beyond, at, 1, 2, 1), (y_own, at, 0, 0, 1)]
    notes += [(y_beside, at, 0, 1, 1), (y_beside, at, 1, 3, 1)]
    own = fill_slots(offsets_ref, notes, keeps, dests, coded, slots_ref)
    own = jnp.transpose(own.astype(jnp.float32)).astype(jnp.int32)
    pieces = [(both, 0, 0, 0), (beside, 0, 1, 0), (beside, span, 3, 0), (beyond, 0, 2, 0)]
    pieces += [(beyond, span, 2, 1), (y_own, 0, 0, 1), (y_beside, 0, 1, 1), (y_beside, span, 3, 1)]
    sort_tokens(pieces, tokens, span)
    bands = tuple(range(BANDS - 1))
    place_bands(slots_ref.at[0], tokens, top, bands, BANDS)
    copy = pltpu.make_async_copy(top, output_part(cache_ref, 0, top.shape[0], column), sem)
    copy.start()
    place_bands(slots_ref.at[1], tokens, top_sent, bands, BANDS)
    for flip in range(2):
        place_bands(slots_ref.at[flip], tokens, low_ref.at[flip], (BANDS - 1,), BANDS)
    for head in range(score_ref.shape[1]):
        lanes = slice(head * WIDTH, (head + 1) * WIDTH)
        chosen = own[:, head : head + 1]
        cached = picked(chosen, 1, tokens[:, lanes]).astype(jnp.bfloat16)
        rows = jnp.concatenate([cached, both[:span, lanes]], axis=0)
        attend_columns(q_ref, head, rows, chosen, out_ref, score_ref)
    copy.wait()


def far_index_kernel(offsets_ref, x_own, x_beside, d_own, d_beside, beyond, _, *rest):
    slots_ref, keeps, dests, coded = rest
    span = x_own.shape[0] - NOTES
    at = 2 * span
    notes = [(x_own, span, 0, 0, 0), (d_own, span, 0, 0, 1), (x_beside, at, 0, 1, 0)]
    notes += [(x_beside, at, 1, 3, 0), (d_beside, at, 0, 1, 1), (d_beside, at, 1, 3, 1)]
    notes += [(beyond, at + NOTES, 0, 2, 0), (beyond, at + NOTES, 1, 2, 1)]
    fill_slots(offsets_ref, notes, keeps, dests, coded, slots_ref)


def far_rows(flip, refs, far_ref, low, tokens, near_late, far_late):
    x_own, x_beside, x_end, d_own, d_beside, d_late, late, y_late, low_ref = refs[:9]
    near_slots, far_slots = refs[9:]
    span = late.shape[0]
    rows = far_slots.shape[1]
    band = rows // BANDS
    first = tokens.shape[0] + 1
    last = pl.ds(rows - band, band)
    sort_late([(late, 0), (y_late, 0)], near_late)
    sort_late([(x_end, 2 * span), (d_late, 0)], far_late)
    low[...] = low_ref[flip]
    add_late(near_slots.at[flip, last], first, near_late, low, 0)
    pieces = [(x_own, 0, 0, 0), (x_beside, 0, 1, 0), (x_beside, span, 3, 0), (x_end, 0, 2, 0)]
    pieces += [(x_end, span, 2, 1), (d_own, 0, 0, 1), (d_beside, 0, 1, 1), (d_beside, span, 3, 1)]
    sort_tokens(pieces, tokens, span)
    place_bands(far_slots.at[flip], tokens, far_ref, tuple(range(BANDS)), BANDS)
    add_late(far_slots.at[flip, last], first, far_late, far_ref, rows - band)


def far_sent_kernel(*refs):
    top_ref, sent_ref = refs[11:13]
    rows = refs[10].shape[1]
    upper = rows + top_ref.shape[0]
    sent_ref[rows:upper, :] = top_ref[...]
    far_rows(1, refs[:11], sent_ref.at[:rows], sent_ref.at[upper:], *refs[13:])


def far_kept_kernel(*refs):
    cache_ref, far, low, tokens, near_late, far_late, sems = refs[12:]
    column = lax.axis_index("kv")
    rows, band = far.shape[0], low.shape[0]
    far_rows(0, refs[:11], far, low, tokens, near_late, far_late)
    copies = [
        pltpu.make_async_copy(far, output_part(cache_ref, 0, rows, column ^ 2), sems.at[0]),
        pltpu.make_async_copy(
            low, output_part(cache_ref, rows - band, band, column), sems.at[1]
        ),
    ]
    for copy in copies:
        copy.start()
    for copy in copies:
        copy.wait()


def last_kernel(sent_ref, _, cache_ref, sems):
    column = lax.axis_index("kv")
    rows = cache_ref.shape[0]
    copies = [
        pltpu.make_async_copy(
            sent_ref.at[index * rows : (index + 1) * rows],
            output_part(cache_ref, 0, rows, column ^ place),
            sems.at[index],
        )
        for index, place in enumerate((3, 1))
    ]
    for copy in copies:
        copy.start()
    for copy in copies:
        copy.wait()


def send(value, axis, pairs):
    return lax.ppermute(value, axis, pairs)


def local_in_planes(query, kv_rows, keep, dest, offsets):
    prompts, span, qwidth = query.shape
    shards, columns = lax.axis_size("ctx"), lax.axis_size("kv")
    width = kv_rows.shape[2]
    heads = width // WIDTH
    cache = keep.shape[3]
    rows = 2 * prompts * cache // columns
    band = rows // BANDS
    vmem = pl.BlockSpec(memory_space=pltpu.VMEM)
    smem = pl.BlockSpec(memory_space=pltpu.SMEM)
    anywhere = pl.BlockSpec(memory_space=pl.ANY)
    hbm = pl.BlockSpec(memory_space=pltpu.HBM)
    params = pltpu.CompilerParams(vmem_limit_bytes=PLANE_BYTES)

    def cost(flops, moved):
        return pl.CostEstimate(flops=flops, bytes_accessed=moved, transcendentals=0)

    def piece(count):
        return jax.ShapeDtypeStruct((count, width), jnp.bfloat16)

    def along_z(value, turn):
        return send(value, "ctx", [(i, (i + 2 * turn) % shards) for i in range(shards)])

    def across_y(value):
        return send(value, "ctx", [(i, i ^ 1) for i in range(shards)])

    def across_x(value):
        return send(value, "kv", [(i, i ^ 2) for i in range(columns)])

    def across_both(value):
        pairs = [(i, i ^ columns ^ 2) for i in range(shards * columns)]
        return send(value, ("ctx", "kv"), pairs)

    def across_core(value):
        return send(value, "kv", [(i, i ^ 1) for i in range(columns)])

    both, single = pl.pallas_call(
        prepare_kernel,
        out_shape=(piece(2 * span + NOTES), piece(span + NOTES)),
        in_specs=[smem] + [hbm] * 3,
        out_specs=(vmem, vmem),
        scratch_shapes=[
            pltpu.VMEM(keep.shape, jnp.int32),
            pltpu.VMEM((1, prompts * cache), jnp.int32),
            pltpu.SemaphoreType.DMA((5,)),
        ],
        compiler_params=pltpu.CompilerParams(vmem_limit_bytes=60 * 1024 * 1024),
        cost_estimate=cost(10**9, 1),
    )(offsets, kv_rows, keep, jnp.transpose(dest))

    below, above = along_z(both, 1), along_z(single, 3)
    y_own, x_own, d_own = across_y(both), across_x(single), across_both(single)
    going = pl.pallas_call(
        going_kernel,
        out_shape=piece(2 * span + 2 * NOTES),
        in_specs=[vmem] * 4,
        out_specs=vmem,
        compiler_params=params,
        cost_estimate=cost(0, 10**6),
    )(both, y_own, x_own, d_own)
    beyond = along_z(going, 2)
    beside, relay = pl.pallas_call(
        beside_kernel,
        out_shape=(piece(2 * span + NOTES), piece(span)),
        in_specs=[vmem] * 3 + [anywhere],
        out_specs=(vmem,) * 2,
        compiler_params=params,
        cost_estimate=cost(0, 10**6),
    )(below, above, both, going)
    relayed = send(relay, "ctx", [(0, 2), (1, 3), (6, 4), (7, 5)])
    y_beside, x_beside = across_y(beside), across_x(beside)
    d_beside = across_y(x_beside)

    attention_shape = jax.ShapeDtypeStruct((prompts, span, qwidth), jnp.bfloat16)
    score_shape = jax.ShapeDtypeStruct((prompts, heads, cache + span), jnp.float32)

    def prompt_specs(late):
        def block(_, offsets_ref):
            early = early_of(offsets_ref)
            return (1 - early if late else early, 0, 0)

        return (
            pl.BlockSpec((1, span, qwidth), block),
            pl.BlockSpec((1, heads, cache + span), block),
        )

    attention, row_scores, late_done = pl.pallas_call(
        late_kernel,
        grid_spec=pltpu.PrefetchScalarGridSpec(
            num_scalar_prefetch=1,
            grid=(1,),
            in_specs=[prompt_specs(True)[0], vmem, vmem],
            out_specs=prompt_specs(True) + (vmem,),
        ),
        out_shape=(attention_shape, score_shape, jax.ShapeDtypeStruct((8, LANES), jnp.float32)),
        compiler_params=params,
        cost_estimate=cost(10**6, 1),
    )(offsets, query, both, y_own)

    end, late = pl.pallas_call(
        join_second_kernel,
        out_shape=(piece(3 * span), piece(span)),
        in_specs=[vmem] * 3 + [anywhere] * 3,
        out_specs=(vmem, vmem),
        compiler_params=params,
        cost_estimate=cost(10**6, 1),
    )(beyond, relay, relayed, y_beside, x_beside, late_done)
    d_late, y_late, x_end = across_both(late), across_y(late), across_x(end)

    tokens = pltpu.VMEM((shards * span, width), jnp.bfloat16)
    late_tokens = pltpu.VMEM((2 * span, width), jnp.bfloat16)
    cache_shape = jax.ShapeDtypeStruct((rows, columns * width), jnp.bfloat16)
    slots_shape = jax.ShapeDtypeStruct((2, rows, heads), jnp.int32)
    done_shape = jax.ShapeDtypeStruct((8, LANES), jnp.float32)
    tables = [
        pltpu.VMEM((shards, 4 * heads, cache), jnp.int32),
        pltpu.VMEM((shards, prompts, cache), jnp.int32),
        pltpu.VMEM((shards, 8 * heads, cache), jnp.bfloat16),
    ]
    attention, row_scores, early_done, owner_cache, top, low, near_slots = pl.pallas_call(
        early_kernel,
        grid_spec=pltpu.PrefetchScalarGridSpec(
            num_scalar_prefetch=1,
            grid=(1,),
            in_specs=[prompt_specs(False)[0]] + [vmem] * 5 + [anywhere] * 3,
            out_specs=prompt_specs(False) + (vmem, hbm, vmem, vmem, vmem),
            scratch_shapes=[
                tokens,
                pltpu.VMEM((rows - band, width), jnp.bfloat16),
                pltpu.SemaphoreType.DMA,
            ]
            + tables,
        ),
        out_shape=(
            attention_shape,
            score_shape,
            done_shape,
            cache_shape,
            piece(rows - band),
            jax.ShapeDtypeStruct((2, band, width), jnp.bfloat16),
            slots_shape,
        ),
        input_output_aliases={8: 0, 9: 1},
        compiler_params=params,
        cost_estimate=cost(10**10, 10**7),
    )(offsets, query, both, beside, beyond, y_own, y_beside, late, attention, row_scores)
    far_slots = pl.pallas_call(
        far_index_kernel,
        out_shape=slots_shape,
        in_specs=[smem] + [vmem] * 5 + [anywhere],
        out_specs=vmem,
        scratch_shapes=tables,
        compiler_params=params,
        cost_estimate=cost(10**6, 1),
    )(offsets, x_own, x_beside, d_own, d_beside, beyond, early_done)
    far = (x_own, x_beside, x_end, d_own, d_beside, d_late, late, y_late, low)
    far += (near_slots, far_slots)
    sent = pl.pallas_call(
        far_sent_kernel,
        out_shape=piece(2 * rows),
        in_specs=[vmem] * 12,
        out_specs=vmem,
        scratch_shapes=[tokens, late_tokens, late_tokens],
        compiler_params=params,
        cost_estimate=cost(2 * 10**9, 4 * 10**6),
    )(*far, top)
    received = across_core(sent)
    owner_cache = pl.pallas_call(
        far_kept_kernel,
        out_shape=cache_shape,
        in_specs=[vmem] * 11 + [hbm],
        out_specs=hbm,
        scratch_shapes=[
            pltpu.VMEM((rows, width), jnp.bfloat16),
            pltpu.VMEM((band, width), jnp.bfloat16),
            tokens,
            late_tokens,
            late_tokens,
            pltpu.SemaphoreType.DMA((2,)),
        ],
        input_output_aliases={11: 0},
        compiler_params=params,
        cost_estimate=cost(2 * 10**9, 4 * 10**6),
    )(*far, owner_cache)
    owner_cache = pl.pallas_call(
        last_kernel,
        out_shape=cache_shape,
        in_specs=[anywhere, hbm],
        out_specs=hbm,
        scratch_shapes=[pltpu.SemaphoreType.DMA((2,))],
        input_output_aliases={1: 0},
        compiler_params=params,
        cost_estimate=cost(0, 10**6),
    )(received, owner_cache)
    return (attention, row_scores, owner_cache)


def solution(mesh):
    placed = (
        P(None, "ctx", "kv"),
        P(None, "ctx", "kv"),
        P(None, "ctx", "kv", None),
        P("ctx", None),
        P(),
    )
    in_planes = mesh.shape["ctx"] == 8 and mesh.shape["kv"] == 4
    return jax.shard_map(
        local_in_planes if in_planes else local,
        mesh=mesh,
        in_specs=placed,
        out_specs=(P(None, "ctx", "kv"), P(None, "kv", "ctx"), P(("ctx", "kv"), None)),
        check_vma=False,
    )
```

```python
import functools
import math

import jax
import jax.numpy as jnp
from jax import lax
from jax.experimental import pallas as pl
from jax.experimental.pallas import tpu as pltpu
from jax.sharding import PartitionSpec as P

HEAD = 128
WIDTH = 2 * HEAD
LANES = 128
VMEM_BYTES = 56 * 1024 * 1024
PLANE_BYTES = 28 * 1024 * 1024
NOTES = 16
BANDS = 4
GROUP = 8


def look_up(state, keep, fresh):
    tiles = state.shape[1] // LANES
    parts = []
    for tile in range(tiles):
        wanted = keep[:, tile * LANES : (tile + 1) * LANES]
        high = wanted >> 7
        low = wanted & 127
        found = jnp.where(high >= tiles, fresh + wanted - state.shape[1], 0)
        for source in range(tiles):
            held = state[:, source * LANES : (source + 1) * LANES]
            moved = jnp.take_along_axis(held, low, axis=1, mode="promise_in_bounds")
            found = jnp.where(high == source, moved, found)
        parts.append(found)
    return jnp.concatenate(parts, axis=1)


def split(state):
    both = jnp.concatenate([state >> 7, state & 127], axis=0)
    return both.astype(jnp.float32).astype(jnp.bfloat16)


def index_kernel(
    where_ref, keep_early_ref, keep_late_ref, dest_ref, slot_ref, row_ref, column_ref, coded
):
    shards, heads, cache = keep_early_ref.shape
    cap = slot_ref.shape[0] // shards
    span = LANES
    early, mine, me = where_ref[0], where_ref[1], where_ref[2]
    empty = jnp.minimum(keep_early_ref[0], 0)

    def follow(shard, carry):
        state, own = carry
        own = jnp.where(shard == mine, state, own)
        state = look_up(state, keep_early_ref[shard], shard * span + 1)
        coded[shard] = split(state)
        return state, own

    _, own_early = lax.fori_loop(0, shards, follow, (empty, empty), unroll=shards <= 8)
    base = shards * span + 1
    late_first = look_up(empty, keep_late_ref[0], base)
    late_second = look_up(late_first, keep_late_ref[1], base + span)
    own_late = jnp.where(mine == shards - 1, late_first, 0)
    for index, own in enumerate((own_early, own_late)):
        row_ref[index] = own
        column_ref[index] = jnp.transpose(own.astype(jnp.float32)).astype(jnp.int32)

    named = (dest_ref[...] == me).astype(jnp.float32)
    chunks = named.shape[1] // LANES
    upper = (
        lax.broadcasted_iota(jnp.int32, (LANES, LANES), 0)
        <= lax.broadcasted_iota(jnp.int32, (LANES, LANES), 1)
    ).astype(jnp.float32).astype(jnp.bfloat16)
    total = jnp.zeros((shards, 1), jnp.float32)
    ranks = []
    for chunk in range(chunks):
        part = named[:, chunk * LANES : (chunk + 1) * LANES]
        upto = jnp.dot(part.astype(jnp.bfloat16), upper, preferred_element_type=jnp.float32)
        ranks.append(jnp.where(part > 0, upto + total, 0.0))
        total = total + upto[:, LANES - 1 :]
    low_half = jnp.concatenate(ranks[: chunks // 2], axis=1)
    high_half = jnp.concatenate(ranks[chunks // 2 :], axis=1)
    rank_early = jnp.where(early == 0, low_half, high_half)
    rank_late = jnp.where(early == 0, high_half, low_half)
    place = lax.broadcasted_iota(jnp.int32, (cap, cache), 0).astype(jnp.float32) + 1.0
    contract = (((1,), (1,)), ((), ()))
    for shard in range(shards):
        pick = (rank_early[shard : shard + 1] == place).astype(jnp.float32).astype(jnp.bfloat16)
        found = lax.dot_general(pick, coded[shard], contract, preferred_element_type=jnp.float32)
        if shard >= shards - 2:
            state = late_first if shard == shards - 2 else late_second
            pick = (rank_late[shard : shard + 1] == place).astype(jnp.float32).astype(jnp.bfloat16)
            found += lax.dot_general(
                pick, split(state), contract, preferred_element_type=jnp.float32
            )
        tokens = found[:, :heads] * 128.0 + found[:, heads:]
        slot_ref[shard * cap : (shard + 1) * cap, :] = tokens.astype(jnp.int32)


def column_of(table, head):
    lane = lax.broadcasted_iota(jnp.int32, table.shape, 1)
    return jnp.sum(
        jnp.where(lane == head, table, 0).astype(jnp.float32), axis=1, keepdims=True
    ).astype(jnp.int32)


def picked(column, first, tokens):
    number = lax.broadcasted_iota(jnp.int32, (column.shape[0], tokens.shape[0]), 1) + first
    table = (column == number).astype(jnp.float32).astype(jnp.bfloat16)
    return jnp.dot(table, tokens, preferred_element_type=jnp.float32)


def attend(q_ref, prompt, keys, values, seen, out_ref, score_ref, head):
    span = q_ref.shape[1]
    cache = seen.shape[1]
    group = q_ref.shape[2] // HEAD
    causal = lax.broadcasted_iota(jnp.int32, (span, span), 1) <= lax.broadcasted_iota(
        jnp.int32, (span, span), 0
    )
    bias = jnp.concatenate(
        [
            jnp.broadcast_to(jnp.where(seen > 0, 0.0, -1e30), (span, cache)),
            jnp.where(causal, 0.0, -1e30),
        ],
        axis=1,
    )
    scale = math.log2(math.e) / math.sqrt(HEAD)
    mass = jnp.zeros((1, cache + span), jnp.float32)
    for member in range(group):
        query = q_ref[prompt, :, member * HEAD : (member + 1) * HEAD]
        scores = lax.dot_general(
            query, keys, (((1,), (1,)), ((), ())), preferred_element_type=jnp.float32
        )
        scores = scores + bias
        peak = jnp.max(scores, axis=1, keepdims=True)
        expo = jnp.exp2((scores - peak) * scale)
        weights = expo * (1.0 / jnp.sum(expo, axis=1, keepdims=True))
        mass = mass + jnp.sum(weights, axis=0, keepdims=True)
        mixed = jnp.dot(weights.astype(jnp.bfloat16), values, preferred_element_type=jnp.float32)
        out_ref[prompt, :, member * HEAD : (member + 1) * HEAD] = mixed.astype(jnp.bfloat16)
    score_ref[prompt, pl.ds(head, 1), :] = mass


def attention_kernel(
    where_ref, q_ref, span_ref, early_ref, late_ref, row_ref, column_ref, out_ref, score_ref
):
    early, mine, column, shards = where_ref[0], where_ref[1], where_ref[3], early_ref.shape[0]
    span = q_ref.shape[1]
    late = 1 - early
    local_head = pl.program_id(0)
    head = column * pl.num_programs(0) + local_head

    def run(which, prompt, tokens, first):
        chosen = column_of(column_ref[which], head)
        cached = picked(chosen, first, tokens).astype(jnp.bfloat16)
        rows = jnp.concatenate([cached, span_ref[prompt]], axis=0)
        seen = row_ref[which, pl.ds(head, 1), :]
        attend(
            q_ref, prompt, rows[:, :HEAD], rows[:, HEAD:], seen, out_ref, score_ref, local_head
        )

    run(0, early, early_ref[:, 0].reshape(shards * span, WIDTH), 1)

    @pl.when(mine >= shards - 2)
    def _():
        run(1, late, late_ref[0, 0], shards * span + 1)

    @pl.when(mine < shards - 2)
    def _():
        out_ref[late] = jnp.zeros(out_ref.shape[1:], out_ref.dtype)
        score_ref[late, pl.ds(local_head, 1), :] = jnp.zeros((1, score_ref.shape[2]), jnp.float32)


def owner_kernel(slot_ref, early_ref, late_ref, out_ref):
    shards, _, span, width = early_ref.shape
    rows = out_ref.shape[0]
    chosen = column_of(slot_ref[...], pl.program_id(0))
    bands = 4
    band = rows // bands
    reach = shards * span // bands
    tokens = early_ref[:, 0].reshape(shards * span, width)
    for index in range(bands):
        part = chosen[index * band : (index + 1) * band]
        found = picked(part, 1, tokens[: (index + 1) * reach])
        if index == bands - 1:
            found += picked(part, shards * span + 1, late_ref[:, 0].reshape(2 * span, width))
        out_ref[index * band : (index + 1) * band, :] = found.astype(jnp.bfloat16)


def local(query, kv_rows, keep, dest, offsets):
    prompts, span, qwidth = query.shape
    shards, columns = lax.axis_size("ctx"), lax.axis_size("kv")
    width = kv_rows.shape[2]
    heads_dev = width // WIDTH
    heads = heads_dev * columns
    cache = keep.shape[3]
    owners = shards * columns
    cap = 2 * prompts * cache // owners
    mine, column = lax.axis_index("ctx"), lax.axis_index("kv")
    early = jnp.where(offsets[0] < offsets[1], 0, 1).astype(jnp.int32)
    facts = jnp.stack([early, mine, mine * columns + column, column]).astype(jnp.int32)

    swap = early == 1
    ordered_kv = jnp.where(swap, kv_rows[::-1], kv_rows)
    ordered_keep = jnp.where(swap, keep[::-1, 0], keep[:, 0])
    digits = jnp.stack([ordered_keep >> 7, ordered_keep & 127], axis=1)
    share = dest.shape[0] // columns
    own_dest = lax.dynamic_slice_in_dim(dest[:, 0], column * share, share)
    facts_rows = jnp.concatenate([digits.reshape(-1), own_dest]).astype(jnp.bfloat16)
    used = facts_rows.shape[0]
    room = 16 * width
    facts_rows = jnp.concatenate([facts_rows, jnp.zeros((room - used,), jnp.bfloat16)])
    payload = jnp.concatenate(
        [ordered_kv.reshape(prompts * span, width), facts_rows.reshape(16, width)], axis=0
    )
    whole = lax.all_gather(payload, ("ctx", "kv")).reshape(
        shards, columns, prompts * span + 16, width
    )

    told = whole[:, :, prompts * span :, :].reshape(shards, columns, room).astype(jnp.int32)
    kept = told[:, :, : prompts * 2 * heads_dev * cache].reshape(
        shards, columns, prompts, 2, heads_dev, cache
    )
    kept = kept[:, :, :, 0] * 128 + kept[:, :, :, 1]
    kept = jnp.transpose(kept, (2, 0, 1, 3, 4)).reshape(prompts, shards, heads, cache)
    whole_dest = told[:, :, used - share : used].reshape(shards, columns * share)

    vmem = pl.BlockSpec(memory_space=pltpu.VMEM)
    smem = pl.BlockSpec(memory_space=pltpu.SMEM)
    params = pltpu.CompilerParams(vmem_limit_bytes=VMEM_BYTES)
    slots, rows, cols = pl.pallas_call(
        index_kernel,
        out_shape=(
            jax.ShapeDtypeStruct((shards * cap, heads), jnp.int32),
            jax.ShapeDtypeStruct((2, heads, cache), jnp.int32),
            jax.ShapeDtypeStruct((2, cache, heads), jnp.int32),
        ),
        in_specs=[smem, vmem, vmem, vmem],
        out_specs=(vmem, vmem, vmem),
        scratch_shapes=[pltpu.VMEM((shards, 2 * heads, cache), jnp.bfloat16)],
        compiler_params=params,
    )(facts, kept[0], kept[1, shards - 2 :], whole_dest)

    group_width = qwidth // heads_dev
    attention, row_scores = pl.pallas_call(
        attention_kernel,
        grid_spec=pltpu.PrefetchScalarGridSpec(
            num_scalar_prefetch=1,
            grid=(heads_dev,),
            in_specs=[
                pl.BlockSpec((prompts, span, group_width), lambda h, w: (0, 0, h)),
                pl.BlockSpec((prompts, span, WIDTH), lambda h, w: (0, 0, h)),
                pl.BlockSpec((shards, 1, span, WIDTH), lambda h, w: (0, w[3], 0, h)),
                pl.BlockSpec((1, 1, span, WIDTH), lambda h, w: (shards - 2, w[3], 1, h)),
                pl.BlockSpec((2, heads, cache), lambda h, w: (0, 0, 0)),
                pl.BlockSpec((2, cache, heads), lambda h, w: (0, 0, 0)),
            ],
            out_specs=(
                pl.BlockSpec((prompts, span, group_width), lambda h, w: (0, 0, h)),
                pl.BlockSpec((prompts, heads_dev, cache + span), lambda h, w: (0, 0, 0)),
            ),
        ),
        out_shape=(
            jax.ShapeDtypeStruct((prompts, span, qwidth), jnp.bfloat16),
            jax.ShapeDtypeStruct((prompts, heads_dev, cache + span), jnp.float32),
        ),
        compiler_params=params,
    )(facts, query, kv_rows, whole, whole, rows, cols)

    owner_cache = pl.pallas_call(
        owner_kernel,
        grid=(heads,),
        in_specs=[
            pl.BlockSpec((shards * cap, heads), lambda g: (0, 0)),
            pl.BlockSpec(
                (shards, 1, span, WIDTH), lambda g: (0, g // heads_dev, 0, g % heads_dev)
            ),
            pl.BlockSpec(
                (2, 1, span, WIDTH),
                lambda g: (shards // 2 - 1, g // heads_dev, 1, g % heads_dev),
            ),
        ],
        out_specs=pl.BlockSpec((shards * cap, WIDTH), lambda g: (0, g)),
        out_shape=jax.ShapeDtypeStruct((shards * cap, heads * WIDTH), jnp.bfloat16),
        compiler_params=params,
    )(slots, whole, whole)
    return (attention, row_scores, owner_cache)


def dot(a, b, dims=((1,), (0,))):
    return lax.dot_general(a, b, (dims, ((), ())), preferred_element_type=jnp.float32)


def marks(table):
    return table.astype(jnp.float32).astype(jnp.bfloat16)


def early_of(offsets_ref):
    return jnp.where(offsets_ref[0] < offsets_ref[1], 0, 1)


def prepare_kernel(
    offsets_ref, kv_ref, keep_ref, dest_ref, both_ref, single_ref, keep, dest, sems
):
    span = kv_ref.shape[1]
    heads, cache = keep_ref.shape[2], keep_ref.shape[3]
    early = early_of(offsets_ref)
    copies = [
        (keep_ref, keep),
        (dest_ref, dest),
        (kv_ref.at[early], single_ref.at[:span]),
        (kv_ref.at[early], both_ref.at[:span]),
        (kv_ref.at[1 - early], both_ref.at[span : 2 * span]),
    ]
    copies = [
        pltpu.make_async_copy(source, target, sems.at[index])
        for index, (source, target) in enumerate(copies)
    ]
    for copy in copies:
        copy.start()
    for copy in copies[:2]:
        copy.wait()
    lane = lax.broadcasted_iota(jnp.int32, (heads, cache), 1)
    rows = [
        keep[early, 0] - lane,
        dest[:, :cache],
        dest[:, cache:],
        keep[1 - early, 0] - lane,
        jnp.zeros((NOTES - 2 * heads - 2, cache), jnp.int32),
    ]
    rows = jnp.concatenate([row.astype(jnp.float32) for row in rows], axis=0)
    rows = rows.astype(jnp.bfloat16)
    single_ref[span:, :] = rows
    both_ref[2 * span :, :] = rows
    for copy in copies[2:]:
        copy.wait()


def two_notes(first, first_row, second, second_row):
    half = NOTES // 2
    return jnp.concatenate(
        [
            first[first_row : first_row + NOTES, :].astype(jnp.float32)[:half],
            second[second_row : second_row + NOTES, :].astype(jnp.float32)[:half],
        ],
        axis=0,
    ).astype(jnp.bfloat16)


def beside_kernel(below, above, both, _, beside_ref, relay_ref):
    span = relay_ref.shape[0]
    beside_ref[:span, :] = below[:span, :]
    beside_ref[span : 2 * span, :] = above[:span, :]
    beside_ref[2 * span :, :] = two_notes(below, 2 * span, above, span)
    level = lax.axis_index("ctx") // 2

    @pl.when(level == 0)
    def _():
        relay_ref[...] = below[span : 2 * span, :]

    @pl.when(level > 0)
    def _():
        relay_ref[...] = both[span : 2 * span, :]


def beyond_kernel(far_level, relay, relayed, *rest):
    out_ref = rest[-1]
    span = relay.shape[0]
    level = lax.axis_index("ctx") // 2
    out_ref[:span, :] = far_level[:span, :]
    out_ref[2 * span :, :] = far_level[span:, :]
    for ref, chosen in ((relay, (level == 0) | (level == 3)), (relayed, (level == 1) | (level == 2))):

        @pl.when(chosen)
        def _(ref=ref):
            out_ref[span : 2 * span, :] = ref[...]


def place_of(turn, flip, shards):
    mine = lax.axis_index("ctx")
    place = lax.rem(mine - 2 * turn + shards, shards)
    return place + 1 - 2 * lax.rem(mine, 2) if flip else place


def sort_tokens(pieces, tokens, span):
    shards = tokens.shape[0] // span
    for ref, base, turn, flip in pieces:
        place = place_of(turn, flip, shards)
        tokens[pl.ds(pl.multiple_of(place * span, span), span), :] = ref[base : base + span, :]


def sort_late(pieces, late_tokens):
    span = late_tokens.shape[0] // 2
    side = lax.rem(lax.axis_index("ctx"), 2)
    for flip, ref_base in enumerate(pieces):
        ref, base = ref_base
        place = side + flip - 2 * side * flip
        late_tokens[pl.ds(pl.multiple_of(place * span, span), span), :] = ref[
            base : base + span, :
        ]


def read_notes(ref, base, part, heads):
    half = NOTES // 2
    rows = ref[base : base + NOTES, :].astype(jnp.float32).astype(jnp.int32)
    rows = rows[part * half : (part + 1) * half]
    lane = lax.broadcasted_iota(jnp.int32, (heads, rows.shape[1]), 1)
    return rows[:heads] + lane, rows[heads + 2 : 2 * heads + 2] + lane, rows[heads : heads + 2]


def sort_notes(notes, keeps, dests):
    shards, heads = keeps.shape[0], keeps.shape[1] // 4
    for ref, base, part, turn, flip in notes:
        place = place_of(turn, flip, shards)
        early, late, dest = read_notes(ref, base, part, heads)
        keeps[place, :heads, :] = early
        keeps[place, heads : 2 * heads, :] = late
        dests[place, :, :] = dest


def follow_lists(keeps, coded, span):
    shards, rows, cache = keeps.shape
    heads = rows // 4
    row = lax.broadcasted_iota(jnp.int32, (rows, cache), 0)
    is_early = row < heads
    state = jnp.where(row < 0, keeps[0], 0)
    own = state
    mine = lax.axis_index("ctx")
    for shard in range(shards):
        own = jnp.where(mine == shard, state, own)
        late_first = (shards + shard - (shards - 2)) * span + 1
        fresh = jnp.where(is_early[:, :LANES], shard * span + 1, late_first)
        state = look_up(state, keeps[shard], fresh)
        if shard < shards - 2:
            state = jnp.where(is_early, state, 0)
        coded[shard] = split(state)
    return own


def find_slots(early, dests, coded, owner, slots):
    shards, halves, cache = dests.shape
    heads = coded.shape[1] // 8
    cap = slots.shape[0] // shards
    upper = marks(
        lax.broadcasted_iota(jnp.int32, (LANES, LANES), 0)
        <= lax.broadcasted_iota(jnp.int32, (LANES, LANES), 1)
    )
    place = lax.broadcasted_iota(jnp.int32, (cap, cache), 0).astype(jnp.float32) + 1.0
    total = jnp.zeros((shards, 1), jnp.float32)
    ranks = []
    for half in range(halves):
        named = (dests[:, half, :] == owner).astype(jnp.float32)
        parts = []
        for chunk in range(cache // LANES):
            part = named[:, chunk * LANES : (chunk + 1) * LANES]
            upto = dot(part.astype(jnp.bfloat16), upper)
            parts.append(jnp.where(part > 0, upto + total, 0.0))
            total = total + upto[:, LANES - 1 :]
        ranks.append(jnp.concatenate(parts, axis=1))
    rank_early = jnp.where(early == 0, ranks[0], ranks[1])
    rank_late = jnp.where(early == 0, ranks[1], ranks[0])
    across = ((1,), (1,))
    for shard in range(shards):
        found = dot(marks(rank_early[shard : shard + 1] == place), coded[shard], across)
        tokens = found[:, :heads] * 128.0 + found[:, 4 * heads : 5 * heads]
        if shard >= shards - 2:
            found = dot(marks(rank_late[shard : shard + 1] == place), coded[shard], across)
            tokens += found[:, heads : 2 * heads] * 128.0 + found[:, 5 * heads : 6 * heads]
        slots[shard * cap : (shard + 1) * cap, :] = tokens.astype(jnp.int32)


def place_bands(slots, tokens, late_tokens, out_ref):
    rows, heads = slots.shape
    reach = tokens.shape[0]
    band = rows // BANDS
    for head in range(heads):
        lanes = slice(head * WIDTH, (head + 1) * WIDTH)
        for index in range(BANDS):
            part = slots[index * band : (index + 1) * band, head : head + 1]
            found = picked(part, 1, tokens[: (index + 1) * reach // BANDS, lanes])
            if index == BANDS - 1:
                found += picked(part, reach + 1, late_tokens[:, lanes])
            out_ref[index * band : (index + 1) * band, lanes] = found.astype(jnp.bfloat16)


def attend_columns(q_ref, base, rows, seen, out_ref):
    span = q_ref.shape[1]
    total = rows.shape[0]
    cache = total - span
    group = GROUP
    keys, values = rows[:, :HEAD], rows[:, HEAD:]
    flat = jnp.transpose(values.astype(jnp.float32)).astype(jnp.bfloat16)
    lane = lax.broadcasted_iota(jnp.int32, (total, HEAD), 1)
    hidden = jnp.where(seen > 0, 0.0, -1e30)
    hidden = jnp.concatenate([hidden, jnp.zeros((span, 1), jnp.float32)], axis=0)
    hidden = jnp.where(lane == 0, hidden, 0.0).astype(jnp.bfloat16)
    keys = jnp.concatenate([keys, hidden], axis=1)
    ones = jnp.ones((2 * span, HEAD), jnp.bfloat16)
    causal = lax.broadcasted_iota(jnp.int32, (span, 2 * span), 0) <= lax.rem(
        lax.broadcasted_iota(jnp.int32, (span, 2 * span), 1), span
    )
    bias = jnp.where(causal, 0.0, -1e30)
    scale = math.log2(math.e) / math.sqrt(HEAD)
    mass = None
    for pair in range(group // 2):
        first = base + 2 * pair * HEAD
        query = jnp.concatenate(
            [
                q_ref[0, :, first : first + HEAD],
                q_ref[0, :, first + HEAD : first + 2 * HEAD],
            ],
            axis=0,
        )
        scores = dot(keys, jnp.concatenate([query, ones], axis=1), ((1,), (1,)))
        near = scores[cache:] + bias
        scores = jnp.concatenate([scores[:cache], near], axis=0) * scale
        peak = jnp.max(scores, axis=0, keepdims=True)
        expo = jnp.exp2(scores - peak)
        weights = expo * (1.0 / jnp.sum(expo, axis=0, keepdims=True))
        both = weights[:, :span] + weights[:, span:]
        mass = both if mass is None else mass + both
        mixed = jnp.transpose(dot(flat, weights.astype(jnp.bfloat16)))
        for member in range(2):
            lanes = slice(first + member * HEAD, first + (member + 1) * HEAD)
            out_ref[0, :, lanes] = mixed[member * span : (member + 1) * span].astype(
                jnp.bfloat16
            )
    return jnp.sum(jnp.transpose(mass), axis=0, keepdims=True)


def late_kernel(head, offsets_ref, q_ref, both_ref, beside_ref, *rest):
    out_ref, score_ref = rest[-2:]
    mine, shards = lax.axis_index("ctx"), lax.axis_size("ctx")
    span = q_ref.shape[1]
    cache = score_ref.shape[1] - span
    heads = both_ref.shape[1] // WIDTH
    lanes = slice(head * WIDTH, (head + 1) * WIDTH)

    @pl.when(mine >= shards - 2)
    def _():
        _, keep, _ = read_notes(beside_ref, 2 * span, 0, heads)
        state = jnp.where(keep >= cache, keep - cache + 1, 0)
        state = jnp.where(mine == shards - 1, state, 0).astype(jnp.float32)
        state = jnp.concatenate([state, jnp.zeros((8 - heads, cache), jnp.float32)], axis=0)
        column = jnp.transpose(state).astype(jnp.int32)[:, head : head + 1]
        cached = picked(column, 1, beside_ref[span : 2 * span, lanes])
        rows = jnp.concatenate(
            [cached.astype(jnp.bfloat16), both_ref[span : 2 * span, lanes]], axis=0
        )
        score_ref[...] = attend_columns(q_ref, 0, rows, column, out_ref)

    @pl.when(mine < shards - 2)
    def _():
        out_ref[...] = jnp.zeros(out_ref.shape, out_ref.dtype)
        score_ref[...] = jnp.zeros(score_ref.shape, jnp.float32)


def output_part(cache_ref, row, rows, column):
    width = cache_ref.shape[1] // lax.axis_size("kv")
    return cache_ref.at[
        pl.ds(row, rows), pl.ds(pl.multiple_of(column * width, width), width)
    ]


def fill_slots(offsets_ref, notes, keeps, dests, coded, slots_ref):
    me = lax.axis_index("ctx") * lax.axis_size("kv") + lax.axis_index("kv")
    sort_notes(notes, keeps, dests)
    own = follow_lists(keeps, coded, LANES)
    for flip in range(2):
        find_slots(early_of(offsets_ref), dests, coded, me ^ flip, slots_ref.at[flip])
    return own


def early_kernel(offsets_ref, q_ref, *rest):
    both, beside, beyond, y_own, y_beside, y_beyond = rest[:6]
    late_scores = rest[6:8]
    out_ref, score_ref, done_ref, cache_ref, sent_ref, *rest = rest[9:]
    tokens, late_tokens, kept, slots, keeps, dests, coded, sem = rest
    done_ref[...] = jnp.zeros(done_ref.shape, jnp.float32)
    span = q_ref.shape[1]
    early = early_of(offsets_ref)
    at = 2 * span
    notes = [(both, at, 0, 0, 0), (beside, at, 0, 1, 0), (beside, at, 1, 3, 0)]
    notes += [(beyond, at, 0, 2, 0), (y_own, at, 0, 0, 1), (y_beside, at, 0, 1, 1)]
    notes += [(y_beside, at, 1, 3, 1), (y_beyond, at, 0, 2, 1)]
    own = fill_slots(offsets_ref, notes, keeps, dests, coded, slots)
    own = jnp.transpose(own.astype(jnp.float32)).astype(jnp.int32)
    pieces = [(both, 0, 0, 0), (beside, 0, 1, 0), (beside, span, 3, 0), (beyond, 0, 2, 0)]
    pieces += [(y_own, 0, 0, 1), (y_beside, 0, 1, 1), (y_beside, span, 3, 1), (y_beyond, 0, 2, 1)]
    sort_tokens(pieces, tokens, span)
    sort_late([(beyond, span), (y_beyond, span)], late_tokens)
    place_bands(slots.at[0], tokens, late_tokens, kept)
    column = lax.axis_index("kv")
    copy = pltpu.make_async_copy(kept, output_part(cache_ref, 0, kept.shape[0], column), sem)
    copy.start()
    place_bands(slots.at[1], tokens, late_tokens, sent_ref)
    for head in range(score_ref.shape[1]):
        lanes = slice(head * WIDTH, (head + 1) * WIDTH)
        chosen = own[:, head : head + 1]
        cached = picked(chosen, 1, tokens[:, lanes]).astype(jnp.bfloat16)
        rows = jnp.concatenate([cached, both[:span, lanes]], axis=0)
        mass = attend_columns(q_ref, head * GROUP * HEAD, rows, chosen, out_ref)
        score_ref[early, head : head + 1, :] = mass
        score_ref[1 - early, head : head + 1, :] = late_scores[head][...]
    copy.wait()


def far_index_kernel(offsets_ref, x_own, x_beside, x_beyond, d_own, d_beside, d_beyond, _, *rest):
    slots_ref, keeps, dests, coded = rest
    span = x_own.shape[0] - NOTES
    at = 2 * span
    notes = [(x_own, span, 0, 0, 0), (d_own, span, 0, 0, 1), (x_beside, at, 0, 1, 0)]
    notes += [(x_beside, at, 1, 3, 0), (d_beside, at, 0, 1, 1), (d_beside, at, 1, 3, 1)]
    notes += [(x_beyond, at, 0, 2, 0), (d_beyond, at, 0, 2, 1)]
    fill_slots(offsets_ref, notes, keeps, dests, coded, slots_ref)


def far_rows(flip, refs, far_ref, tokens, late_tokens):
    x_own, x_beside, x_beyond, d_own, d_beside, d_beyond, slots = refs
    span = x_own.shape[0] - NOTES
    pieces = [(x_own, 0, 0, 0), (x_beside, 0, 1, 0), (x_beside, span, 3, 0), (x_beyond, 0, 2, 0)]
    pieces += [(d_own, 0, 0, 1), (d_beside, 0, 1, 1), (d_beside, span, 3, 1), (d_beyond, 0, 2, 1)]
    sort_tokens(pieces, tokens, span)
    sort_late([(x_beyond, span), (d_beyond, span)], late_tokens)
    place_bands(slots.at[flip], tokens, late_tokens, far_ref)


def far_sent_kernel(*refs):
    near_ref, sent_ref, tokens, late_tokens = refs[7:]
    rows = near_ref.shape[0]
    sent_ref[rows:, :] = near_ref[...]
    far_rows(1, refs[:7], sent_ref.at[:rows], tokens, late_tokens)


def far_kept_kernel(*refs):
    cache_ref, far, tokens, late_tokens, sem = refs[8:]
    far_rows(0, refs[:7], far, tokens, late_tokens)
    column = lax.axis_index("kv")
    copy = pltpu.make_async_copy(far, output_part(cache_ref, 0, far.shape[0], column ^ 2), sem)
    copy.start()
    copy.wait()


def last_kernel(sent_ref, _, cache_ref, sems):
    column = lax.axis_index("kv")
    rows = cache_ref.shape[0]
    copies = [
        pltpu.make_async_copy(
            sent_ref.at[index * rows : (index + 1) * rows],
            output_part(cache_ref, 0, rows, column ^ place),
            sems.at[index],
        )
        for index, place in enumerate((3, 1))
    ]
    for copy in copies:
        copy.start()
    for copy in copies:
        copy.wait()


def send(value, axis, pairs):
    return lax.ppermute(value, axis, pairs)


def local_in_planes(query, kv_rows, keep, dest, offsets):
    prompts, span, qwidth = query.shape
    shards, columns = lax.axis_size("ctx"), lax.axis_size("kv")
    width = kv_rows.shape[2]
    heads = width // WIDTH
    cache = keep.shape[3]
    rows = 2 * prompts * cache // columns
    band = rows // BANDS
    vmem = pl.BlockSpec(memory_space=pltpu.VMEM)
    smem = pl.BlockSpec(memory_space=pltpu.SMEM)
    anywhere = pl.BlockSpec(memory_space=pl.ANY)
    hbm = pl.BlockSpec(memory_space=pltpu.HBM)
    params = pltpu.CompilerParams(vmem_limit_bytes=PLANE_BYTES)

    def cost(flops, moved):
        return pl.CostEstimate(flops=flops, bytes_accessed=moved, transcendentals=0)

    def piece(count):
        return jax.ShapeDtypeStruct((count, width), jnp.bfloat16)

    def along_z(value, turn):
        return send(value, "ctx", [(i, (i + 2 * turn) % shards) for i in range(shards)])

    def across_y(value):
        return send(value, "ctx", [(i, i ^ 1) for i in range(shards)])

    def across_x(value):
        return send(value, "kv", [(i, i ^ 2) for i in range(columns)])

    def across_both(value):
        pairs = [(i, i ^ columns ^ 2) for i in range(shards * columns)]
        return send(value, ("ctx", "kv"), pairs)

    def across_core(value):
        return send(value, "kv", [(i, i ^ 1) for i in range(columns)])

    both, single = pl.pallas_call(
        prepare_kernel,
        out_shape=(piece(2 * span + NOTES), piece(span + NOTES)),
        in_specs=[smem] + [hbm] * 3,
        out_specs=(vmem, vmem),
        scratch_shapes=[
            pltpu.VMEM(keep.shape, jnp.int32),
            pltpu.VMEM((1, prompts * cache), jnp.int32),
            pltpu.SemaphoreType.DMA((5,)),
        ],
        compiler_params=pltpu.CompilerParams(vmem_limit_bytes=60 * 1024 * 1024),
        cost_estimate=cost(10**9, 1),
    )(offsets, kv_rows, keep, jnp.transpose(dest))

    below, above, far_level = along_z(both, 1), along_z(single, 3), along_z(single, 2)
    y_own, x_own = across_y(both), across_x(single)
    d_own = across_y(x_own)
    beside, relay = pl.pallas_call(
        beside_kernel,
        out_shape=(piece(2 * span + NOTES), piece(span)),
        in_specs=[vmem] * 3 + [anywhere],
        out_specs=(vmem,) * 2,
        compiler_params=params,
        cost_estimate=cost(0, 10**6),
    )(below, above, both, x_own)
    relayed = send(relay, "ctx", [(0, 2), (1, 3), (6, 4), (7, 5)])
    y_beside, x_beside = across_y(beside), across_x(beside)
    d_beside = across_y(x_beside)

    attention_shape = jax.ShapeDtypeStruct((prompts, span, qwidth), jnp.bfloat16)
    half = qwidth // heads

    def late_attention(head, *after):
        def block(_, offsets_ref):
            return (1 - early_of(offsets_ref), 0, head)

        spec = pl.BlockSpec((1, span, half), block)
        return pl.pallas_call(
            functools.partial(late_kernel, head),
            grid_spec=pltpu.PrefetchScalarGridSpec(
                num_scalar_prefetch=1,
                grid=(1,),
                in_specs=[spec, vmem, vmem] + [anywhere] * len(after),
                out_specs=(spec, vmem),
            ),
            out_shape=(attention_shape, jax.ShapeDtypeStruct((1, cache + span), jnp.float32)),
            input_output_aliases={4: 0} if head else {},
            compiler_params=params,
            cost_estimate=cost(5 * 10**9, 10**7),
        )(offsets, query, both, y_own, *after)

    attention, late_first = late_attention(0, far_level)
    beyond = pl.pallas_call(
        beyond_kernel,
        out_shape=piece(2 * span + NOTES),
        in_specs=[vmem] * 3 + [anywhere] * 3,
        out_specs=vmem,
        compiler_params=params,
        cost_estimate=cost(0, 10**6),
    )(far_level, relay, relayed, y_beside, x_beside, late_first)
    y_beyond, x_beyond = across_y(beyond), across_x(beyond)
    attention, late_second = late_attention(1, attention, beyond)
    d_beyond = across_x(y_beyond)

    tokens = pltpu.VMEM((shards * span, width), jnp.bfloat16)
    late_tokens = pltpu.VMEM((2 * span, width), jnp.bfloat16)
    block_rows = pltpu.VMEM((rows, width), jnp.bfloat16)
    cache_shape = jax.ShapeDtypeStruct((rows, columns * width), jnp.bfloat16)
    slots_shape = jax.ShapeDtypeStruct((2, rows, heads), jnp.int32)
    tables = [
        pltpu.VMEM((shards, 4 * heads, cache), jnp.int32),
        pltpu.VMEM((shards, prompts, cache), jnp.int32),
        pltpu.VMEM((shards, 8 * heads, cache), jnp.bfloat16),
    ]
    early_spec = pl.BlockSpec(
        (1, span, qwidth), lambda _, offsets_ref: (early_of(offsets_ref), 0, 0)
    )
    attention, row_scores, early_done, owner_cache, near_sent = pl.pallas_call(
        early_kernel,
        grid_spec=pltpu.PrefetchScalarGridSpec(
            num_scalar_prefetch=1,
            grid=(1,),
            in_specs=[early_spec] + [vmem] * 8 + [anywhere],
            out_specs=(early_spec, vmem, vmem, hbm, vmem),
            scratch_shapes=[tokens, late_tokens, block_rows]
            + [pltpu.VMEM(slots_shape.shape, jnp.int32)]
            + tables
            + [pltpu.SemaphoreType.DMA],
        ),
        out_shape=(
            attention_shape,
            jax.ShapeDtypeStruct((prompts, heads, cache + span), jnp.float32),
            jax.ShapeDtypeStruct((8, LANES), jnp.float32),
            cache_shape,
            piece(rows),
        ),
        input_output_aliases={10: 0},
        compiler_params=params,
        cost_estimate=cost(10**10, 10**7),
    )(
        offsets,
        query,
        both,
        beside,
        beyond,
        y_own,
        y_beside,
        y_beyond,
        late_first,
        late_second,
        attention,
    )
    far = (x_own, x_beside, x_beyond, d_own, d_beside, d_beyond)
    far_slots = pl.pallas_call(
        far_index_kernel,
        out_shape=slots_shape,
        in_specs=[smem] + [vmem] * 6 + [anywhere],
        out_specs=vmem,
        scratch_shapes=tables,
        compiler_params=params,
        cost_estimate=cost(10**6, 1),
    )(offsets, *far, early_done)
    sent = pl.pallas_call(
        far_sent_kernel,
        out_shape=piece(2 * rows),
        in_specs=[vmem] * 8,
        out_specs=vmem,
        scratch_shapes=[tokens, late_tokens],
        compiler_params=params,
        cost_estimate=cost(2 * 10**9, 4 * 10**6),
    )(*far, far_slots, near_sent)
    received = across_core(sent)
    owner_cache = pl.pallas_call(
        far_kept_kernel,
        out_shape=cache_shape,
        in_specs=[vmem] * 7 + [hbm],
        out_specs=hbm,
        scratch_shapes=[block_rows, tokens, late_tokens, pltpu.SemaphoreType.DMA],
        input_output_aliases={7: 0},
        compiler_params=params,
        cost_estimate=cost(2 * 10**9, 4 * 10**6),
    )(*far, far_slots, owner_cache)
    owner_cache = pl.pallas_call(
        last_kernel,
        out_shape=cache_shape,
        in_specs=[anywhere, hbm],
        out_specs=hbm,
        scratch_shapes=[pltpu.SemaphoreType.DMA((2,))],
        input_output_aliases={1: 0},
        compiler_params=params,
        cost_estimate=cost(0, 10**6),
    )(received, owner_cache)
    return (attention, row_scores, owner_cache)


def solution(mesh):
    placed = (
        P(None, "ctx", "kv"),
        P(None, "ctx", "kv"),
        P(None, "ctx", "kv", None),
        P("ctx", None),
        P(),
    )
    in_planes = mesh.shape["ctx"] == 8 and mesh.shape["kv"] == 4
    return jax.shard_map(
        local_in_planes if in_planes else local,
        mesh=mesh,
        in_specs=placed,
        out_specs=(P(None, "ctx", "kv"), P(None, "kv", "ctx"), P(("ctx", "kv"), None)),
        check_vma=False,
    )
```

```python
import functools
import math

import jax
import jax.numpy as jnp
from jax import lax
from jax.experimental import pallas as pl
from jax.experimental.pallas import tpu as pltpu
from jax.sharding import PartitionSpec as P

HEAD = 128
WIDTH = 2 * HEAD
LANES = 128
VMEM_BYTES = 56 * 1024 * 1024
PLANE_BYTES = 28 * 1024 * 1024
NOTES = 16
BANDS = 4
GROUP = 8


def look_up(state, keep, fresh):
    tiles = state.shape[1] // LANES
    parts = []
    for tile in range(tiles):
        wanted = keep[:, tile * LANES : (tile + 1) * LANES]
        high = wanted >> 7
        low = wanted & 127
        found = jnp.where(high >= tiles, fresh + wanted - state.shape[1], 0)
        for source in range(tiles):
            held = state[:, source * LANES : (source + 1) * LANES]
            moved = jnp.take_along_axis(held, low, axis=1, mode="promise_in_bounds")
            found = jnp.where(high == source, moved, found)
        parts.append(found)
    return jnp.concatenate(parts, axis=1)


def split(state):
    both = jnp.concatenate([state >> 7, state & 127], axis=0)
    return both.astype(jnp.float32).astype(jnp.bfloat16)


def index_kernel(
    where_ref, keep_early_ref, keep_late_ref, dest_ref, slot_ref, row_ref, column_ref, coded
):
    shards, heads, cache = keep_early_ref.shape
    cap = slot_ref.shape[0] // shards
    span = LANES
    early, mine, me = where_ref[0], where_ref[1], where_ref[2]
    empty = jnp.minimum(keep_early_ref[0], 0)

    def follow(shard, carry):
        state, own = carry
        own = jnp.where(shard == mine, state, own)
        state = look_up(state, keep_early_ref[shard], shard * span + 1)
        coded[shard] = split(state)
        return state, own

    _, own_early = lax.fori_loop(0, shards, follow, (empty, empty), unroll=shards <= 8)
    base = shards * span + 1
    late_first = look_up(empty, keep_late_ref[0], base)
    late_second = look_up(late_first, keep_late_ref[1], base + span)
    own_late = jnp.where(mine == shards - 1, late_first, 0)
    for index, own in enumerate((own_early, own_late)):
        row_ref[index] = own
        column_ref[index] = jnp.transpose(own.astype(jnp.float32)).astype(jnp.int32)

    named = (dest_ref[...] == me).astype(jnp.float32)
    chunks = named.shape[1] // LANES
    upper = (
        lax.broadcasted_iota(jnp.int32, (LANES, LANES), 0)
        <= lax.broadcasted_iota(jnp.int32, (LANES, LANES), 1)
    ).astype(jnp.float32).astype(jnp.bfloat16)
    total = jnp.zeros((shards, 1), jnp.float32)
    ranks = []
    for chunk in range(chunks):
        part = named[:, chunk * LANES : (chunk + 1) * LANES]
        upto = jnp.dot(part.astype(jnp.bfloat16), upper, preferred_element_type=jnp.float32)
        ranks.append(jnp.where(part > 0, upto + total, 0.0))
        total = total + upto[:, LANES - 1 :]
    low_half = jnp.concatenate(ranks[: chunks // 2], axis=1)
    high_half = jnp.concatenate(ranks[chunks // 2 :], axis=1)
    rank_early = jnp.where(early == 0, low_half, high_half)
    rank_late = jnp.where(early == 0, high_half, low_half)
    place = lax.broadcasted_iota(jnp.int32, (cap, cache), 0).astype(jnp.float32) + 1.0
    contract = (((1,), (1,)), ((), ()))
    for shard in range(shards):
        pick = (rank_early[shard : shard + 1] == place).astype(jnp.float32).astype(jnp.bfloat16)
        found = lax.dot_general(pick, coded[shard], contract, preferred_element_type=jnp.float32)
        if shard >= shards - 2:
            state = late_first if shard == shards - 2 else late_second
            pick = (rank_late[shard : shard + 1] == place).astype(jnp.float32).astype(jnp.bfloat16)
            found += lax.dot_general(
                pick, split(state), contract, preferred_element_type=jnp.float32
            )
        tokens = found[:, :heads] * 128.0 + found[:, heads:]
        slot_ref[shard * cap : (shard + 1) * cap, :] = tokens.astype(jnp.int32)


def column_of(table, head):
    lane = lax.broadcasted_iota(jnp.int32, table.shape, 1)
    return jnp.sum(
        jnp.where(lane == head, table, 0).astype(jnp.float32), axis=1, keepdims=True
    ).astype(jnp.int32)


def picked(column, first, tokens):
    number = lax.broadcasted_iota(jnp.int32, (column.shape[0], tokens.shape[0]), 1) + first
    table = (column == number).astype(jnp.float32).astype(jnp.bfloat16)
    return jnp.dot(table, tokens, preferred_element_type=jnp.float32)


def attend(q_ref, prompt, keys, values, seen, out_ref, score_ref, head):
    span = q_ref.shape[1]
    cache = seen.shape[1]
    group = q_ref.shape[2] // HEAD
    causal = lax.broadcasted_iota(jnp.int32, (span, span), 1) <= lax.broadcasted_iota(
        jnp.int32, (span, span), 0
    )
    bias = jnp.concatenate(
        [
            jnp.broadcast_to(jnp.where(seen > 0, 0.0, -1e30), (span, cache)),
            jnp.where(causal, 0.0, -1e30),
        ],
        axis=1,
    )
    scale = math.log2(math.e) / math.sqrt(HEAD)
    mass = jnp.zeros((1, cache + span), jnp.float32)
    for member in range(group):
        query = q_ref[prompt, :, member * HEAD : (member + 1) * HEAD]
        scores = lax.dot_general(
            query, keys, (((1,), (1,)), ((), ())), preferred_element_type=jnp.float32
        )
        scores = scores + bias
        peak = jnp.max(scores, axis=1, keepdims=True)
        expo = jnp.exp2((scores - peak) * scale)
        weights = expo * (1.0 / jnp.sum(expo, axis=1, keepdims=True))
        mass = mass + jnp.sum(weights, axis=0, keepdims=True)
        mixed = jnp.dot(weights.astype(jnp.bfloat16), values, preferred_element_type=jnp.float32)
        out_ref[prompt, :, member * HEAD : (member + 1) * HEAD] = mixed.astype(jnp.bfloat16)
    score_ref[prompt, pl.ds(head, 1), :] = mass


def attention_kernel(
    where_ref, q_ref, span_ref, early_ref, late_ref, row_ref, column_ref, out_ref, score_ref
):
    early, mine, column, shards = where_ref[0], where_ref[1], where_ref[3], early_ref.shape[0]
    span = q_ref.shape[1]
    late = 1 - early
    local_head = pl.program_id(0)
    head = column * pl.num_programs(0) + local_head

    def run(which, prompt, tokens, first):
        chosen = column_of(column_ref[which], head)
        cached = picked(chosen, first, tokens).astype(jnp.bfloat16)
        rows = jnp.concatenate([cached, span_ref[prompt]], axis=0)
        seen = row_ref[which, pl.ds(head, 1), :]
        attend(
            q_ref, prompt, rows[:, :HEAD], rows[:, HEAD:], seen, out_ref, score_ref, local_head
        )

    run(0, early, early_ref[:, 0].reshape(shards * span, WIDTH), 1)

    @pl.when(mine >= shards - 2)
    def _():
        run(1, late, late_ref[0, 0], shards * span + 1)

    @pl.when(mine < shards - 2)
    def _():
        out_ref[late] = jnp.zeros(out_ref.shape[1:], out_ref.dtype)
        score_ref[late, pl.ds(local_head, 1), :] = jnp.zeros((1, score_ref.shape[2]), jnp.float32)


def owner_kernel(slot_ref, early_ref, late_ref, out_ref):
    shards, _, span, width = early_ref.shape
    rows = out_ref.shape[0]
    chosen = column_of(slot_ref[...], pl.program_id(0))
    bands = 4
    band = rows // bands
    reach = shards * span // bands
    tokens = early_ref[:, 0].reshape(shards * span, width)
    for index in range(bands):
        part = chosen[index * band : (index + 1) * band]
        found = picked(part, 1, tokens[: (index + 1) * reach])
        if index == bands - 1:
            found += picked(part, shards * span + 1, late_ref[:, 0].reshape(2 * span, width))
        out_ref[index * band : (index + 1) * band, :] = found.astype(jnp.bfloat16)


def local(query, kv_rows, keep, dest, offsets):
    prompts, span, qwidth = query.shape
    shards, columns = lax.axis_size("ctx"), lax.axis_size("kv")
    width = kv_rows.shape[2]
    heads_dev = width // WIDTH
    heads = heads_dev * columns
    cache = keep.shape[3]
    owners = shards * columns
    cap = 2 * prompts * cache // owners
    mine, column = lax.axis_index("ctx"), lax.axis_index("kv")
    early = jnp.where(offsets[0] < offsets[1], 0, 1).astype(jnp.int32)
    facts = jnp.stack([early, mine, mine * columns + column, column]).astype(jnp.int32)

    swap = early == 1
    ordered_kv = jnp.where(swap, kv_rows[::-1], kv_rows)
    ordered_keep = jnp.where(swap, keep[::-1, 0], keep[:, 0])
    digits = jnp.stack([ordered_keep >> 7, ordered_keep & 127], axis=1)
    share = dest.shape[0] // columns
    own_dest = lax.dynamic_slice_in_dim(dest[:, 0], column * share, share)
    facts_rows = jnp.concatenate([digits.reshape(-1), own_dest]).astype(jnp.bfloat16)
    used = facts_rows.shape[0]
    room = 16 * width
    facts_rows = jnp.concatenate([facts_rows, jnp.zeros((room - used,), jnp.bfloat16)])
    payload = jnp.concatenate(
        [ordered_kv.reshape(prompts * span, width), facts_rows.reshape(16, width)], axis=0
    )
    whole = lax.all_gather(payload, ("ctx", "kv")).reshape(
        shards, columns, prompts * span + 16, width
    )

    told = whole[:, :, prompts * span :, :].reshape(shards, columns, room).astype(jnp.int32)
    kept = told[:, :, : prompts * 2 * heads_dev * cache].reshape(
        shards, columns, prompts, 2, heads_dev, cache
    )
    kept = kept[:, :, :, 0] * 128 + kept[:, :, :, 1]
    kept = jnp.transpose(kept, (2, 0, 1, 3, 4)).reshape(prompts, shards, heads, cache)
    whole_dest = told[:, :, used - share : used].reshape(shards, columns * share)

    vmem = pl.BlockSpec(memory_space=pltpu.VMEM)
    smem = pl.BlockSpec(memory_space=pltpu.SMEM)
    params = pltpu.CompilerParams(vmem_limit_bytes=VMEM_BYTES)
    slots, rows, cols = pl.pallas_call(
        index_kernel,
        out_shape=(
            jax.ShapeDtypeStruct((shards * cap, heads), jnp.int32),
            jax.ShapeDtypeStruct((2, heads, cache), jnp.int32),
            jax.ShapeDtypeStruct((2, cache, heads), jnp.int32),
        ),
        in_specs=[smem, vmem, vmem, vmem],
        out_specs=(vmem, vmem, vmem),
        scratch_shapes=[pltpu.VMEM((shards, 2 * heads, cache), jnp.bfloat16)],
        compiler_params=params,
    )(facts, kept[0], kept[1, shards - 2 :], whole_dest)

    group_width = qwidth // heads_dev
    attention, row_scores = pl.pallas_call(
        attention_kernel,
        grid_spec=pltpu.PrefetchScalarGridSpec(
            num_scalar_prefetch=1,
            grid=(heads_dev,),
            in_specs=[
                pl.BlockSpec((prompts, span, group_width), lambda h, w: (0, 0, h)),
                pl.BlockSpec((prompts, span, WIDTH), lambda h, w: (0, 0, h)),
                pl.BlockSpec((shards, 1, span, WIDTH), lambda h, w: (0, w[3], 0, h)),
                pl.BlockSpec((1, 1, span, WIDTH), lambda h, w: (shards - 2, w[3], 1, h)),
                pl.BlockSpec((2, heads, cache), lambda h, w: (0, 0, 0)),
                pl.BlockSpec((2, cache, heads), lambda h, w: (0, 0, 0)),
            ],
            out_specs=(
                pl.BlockSpec((prompts, span, group_width), lambda h, w: (0, 0, h)),
                pl.BlockSpec((prompts, heads_dev, cache + span), lambda h, w: (0, 0, 0)),
            ),
        ),
        out_shape=(
            jax.ShapeDtypeStruct((prompts, span, qwidth), jnp.bfloat16),
            jax.ShapeDtypeStruct((prompts, heads_dev, cache + span), jnp.float32),
        ),
        compiler_params=params,
    )(facts, query, kv_rows, whole, whole, rows, cols)

    owner_cache = pl.pallas_call(
        owner_kernel,
        grid=(heads,),
        in_specs=[
            pl.BlockSpec((shards * cap, heads), lambda g: (0, 0)),
            pl.BlockSpec(
                (shards, 1, span, WIDTH), lambda g: (0, g // heads_dev, 0, g % heads_dev)
            ),
            pl.BlockSpec(
                (2, 1, span, WIDTH),
                lambda g: (shards // 2 - 1, g // heads_dev, 1, g % heads_dev),
            ),
        ],
        out_specs=pl.BlockSpec((shards * cap, WIDTH), lambda g: (0, g)),
        out_shape=jax.ShapeDtypeStruct((shards * cap, heads * WIDTH), jnp.bfloat16),
        compiler_params=params,
    )(slots, whole, whole)
    return (attention, row_scores, owner_cache)


def dot(a, b, dims=((1,), (0,))):
    return lax.dot_general(a, b, (dims, ((), ())), preferred_element_type=jnp.float32)


def marks(table):
    return table.astype(jnp.float32).astype(jnp.bfloat16)


def early_of(offsets_ref):
    return jnp.where(offsets_ref[0] < offsets_ref[1], 0, 1)


def prepare_kernel(
    offsets_ref, kv_ref, keep_ref, dest_ref, both_ref, single_ref, keep, dest, sems
):
    span = kv_ref.shape[1]
    heads, cache = keep_ref.shape[2], keep_ref.shape[3]
    early = early_of(offsets_ref)
    copies = [
        (keep_ref, keep),
        (dest_ref, dest),
        (kv_ref.at[early], single_ref.at[:span]),
        (kv_ref.at[early], both_ref.at[:span]),
        (kv_ref.at[1 - early], both_ref.at[span : 2 * span]),
    ]
    copies = [
        pltpu.make_async_copy(source, target, sems.at[index])
        for index, (source, target) in enumerate(copies)
    ]
    for copy in copies:
        copy.start()
    for copy in copies[:2]:
        copy.wait()
    lane = lax.broadcasted_iota(jnp.int32, (heads, cache), 1)
    rows = [
        keep[early, 0] - lane,
        dest[:, :cache],
        dest[:, cache:],
        keep[1 - early, 0] - lane,
        jnp.zeros((NOTES - 2 * heads - 2, cache), jnp.int32),
    ]
    rows = jnp.concatenate([row.astype(jnp.float32) for row in rows], axis=0)
    rows = rows.astype(jnp.bfloat16)
    single_ref[span:, :] = rows
    both_ref[2 * span :, :] = rows
    for copy in copies[2:]:
        copy.wait()


def two_notes(first, first_row, second, second_row):
    half = NOTES // 2
    return jnp.concatenate(
        [
            first[first_row : first_row + NOTES, :].astype(jnp.float32)[:half],
            second[second_row : second_row + NOTES, :].astype(jnp.float32)[:half],
        ],
        axis=0,
    ).astype(jnp.bfloat16)


def going_kernel(both, y_own, x_own, d_own, going_ref, notes_ref):
    span = both.shape[0] // 2 - NOTES // 2
    going_ref[:span, :] = both[:span, :]
    going_ref[span : 2 * span, :] = y_own[:span, :]
    going_ref[2 * span :, :] = jnp.zeros((going_ref.shape[0] - 2 * span, going_ref.shape[1]), going_ref.dtype)
    notes_ref[:NOTES, :] = two_notes(both, 2 * span, y_own, 2 * span)
    notes_ref[NOTES:, :] = two_notes(x_own, span, d_own, span)


def beside_kernel(below, above, both, _, beside_ref, relay_ref):
    span = relay_ref.shape[0]
    beside_ref[:span, :] = below[:span, :]
    beside_ref[span : 2 * span, :] = above[:span, :]
    beside_ref[2 * span :, :] = two_notes(below, 2 * span, above, span)
    level = lax.axis_index("ctx") // 2

    @pl.when(level == 0)
    def _():
        relay_ref[...] = below[span : 2 * span, :]

    @pl.when(level > 0)
    def _():
        relay_ref[...] = both[span : 2 * span, :]


def pick_late_kernel(relay, relayed, _, out_ref):
    level = lax.axis_index("ctx") // 2
    for ref, chosen in ((relay, (level == 0) | (level == 3)), (relayed, (level == 1) | (level == 2))):

        @pl.when(chosen)
        def _(ref=ref):
            out_ref[...] = ref[...]


def end_kernel(beyond, _, out_ref):
    out_ref[...] = beyond[: out_ref.shape[0], :]


def place_of(turn, flip, shards):
    mine = lax.axis_index("ctx")
    place = lax.rem(mine - 2 * turn + shards, shards)
    return place + 1 - 2 * lax.rem(mine, 2) if flip else place


def sort_tokens(pieces, tokens, span):
    shards = tokens.shape[0] // span
    for ref, base, turn, flip in pieces:
        place = place_of(turn, flip, shards)
        tokens[pl.ds(pl.multiple_of(place * span, span), span), :] = ref[base : base + span, :]


def sort_late(pieces, late_tokens):
    span = late_tokens.shape[0] // 2
    side = lax.rem(lax.axis_index("ctx"), 2)
    for flip, ref_base in enumerate(pieces):
        ref, base = ref_base
        place = side + flip - 2 * side * flip
        late_tokens[pl.ds(pl.multiple_of(place * span, span), span), :] = ref[
            base : base + span, :
        ]


def read_notes(ref, base, part, heads):
    half = NOTES // 2
    rows = ref[base : base + NOTES, :].astype(jnp.float32).astype(jnp.int32)
    rows = rows[part * half : (part + 1) * half]
    lane = lax.broadcasted_iota(jnp.int32, (heads, rows.shape[1]), 1)
    return rows[:heads] + lane, rows[heads + 2 : 2 * heads + 2] + lane, rows[heads : heads + 2]


def sort_notes(notes, keeps, dests):
    shards, heads = keeps.shape[0], keeps.shape[1] // 4
    for ref, base, part, turn, flip in notes:
        place = place_of(turn, flip, shards)
        early, late, dest = read_notes(ref, base, part, heads)
        keeps[place, :heads, :] = early
        keeps[place, heads : 2 * heads, :] = late
        dests[place, :, :] = dest


def follow_lists(keeps, coded, span):
    shards, rows, cache = keeps.shape
    heads = rows // 4
    row = lax.broadcasted_iota(jnp.int32, (rows, cache), 0)
    is_early = row < heads
    state = jnp.where(row < 0, keeps[0], 0)
    own = state
    mine = lax.axis_index("ctx")
    for shard in range(shards):
        own = jnp.where(mine == shard, state, own)
        late_first = (shards + shard - (shards - 2)) * span + 1
        fresh = jnp.where(is_early[:, :LANES], shard * span + 1, late_first)
        state = look_up(state, keeps[shard], fresh)
        if shard < shards - 2:
            state = jnp.where(is_early, state, 0)
        coded[shard] = split(state)
    return own


def find_slots(early, dests, coded, owner, slots):
    shards, halves, cache = dests.shape
    heads = coded.shape[1] // 8
    cap = slots.shape[0] // shards
    upper = marks(
        lax.broadcasted_iota(jnp.int32, (LANES, LANES), 0)
        <= lax.broadcasted_iota(jnp.int32, (LANES, LANES), 1)
    )
    place = lax.broadcasted_iota(jnp.int32, (cap, cache), 0).astype(jnp.float32) + 1.0
    total = jnp.zeros((shards, 1), jnp.float32)
    ranks = []
    for half in range(halves):
        named = (dests[:, half, :] == owner).astype(jnp.float32)
        parts = []
        for chunk in range(cache // LANES):
            part = named[:, chunk * LANES : (chunk + 1) * LANES]
            upto = dot(part.astype(jnp.bfloat16), upper)
            parts.append(jnp.where(part > 0, upto + total, 0.0))
            total = total + upto[:, LANES - 1 :]
        ranks.append(jnp.concatenate(parts, axis=1))
    rank_early = jnp.where(early == 0, ranks[0], ranks[1])
    rank_late = jnp.where(early == 0, ranks[1], ranks[0])
    across = ((1,), (1,))
    for shard in range(shards):
        found = dot(marks(rank_early[shard : shard + 1] == place), coded[shard], across)
        tokens = found[:, :heads] * 128.0 + found[:, 4 * heads : 5 * heads]
        if shard >= shards - 2:
            found = dot(marks(rank_late[shard : shard + 1] == place), coded[shard], across)
            tokens += found[:, heads : 2 * heads] * 128.0 + found[:, 5 * heads : 6 * heads]
        slots[shard * cap : (shard + 1) * cap, :] = tokens.astype(jnp.int32)


def place_bands(slots, tokens, late_tokens, out_ref):
    rows, heads = slots.shape
    reach = tokens.shape[0]
    band = rows // BANDS
    for head in range(heads):
        lanes = slice(head * WIDTH, (head + 1) * WIDTH)
        for index in range(BANDS):
            part = slots[index * band : (index + 1) * band, head : head + 1]
            found = picked(part, 1, tokens[: (index + 1) * reach // BANDS, lanes])
            if index == BANDS - 1:
                found += picked(part, reach + 1, late_tokens[:, lanes])
            out_ref[index * band : (index + 1) * band, lanes] = found.astype(jnp.bfloat16)


def attend_columns(q_ref, base, rows, seen, out_ref):
    span = q_ref.shape[1]
    total = rows.shape[0]
    cache = total - span
    group = GROUP
    keys, values = rows[:, :HEAD], rows[:, HEAD:]
    flat = jnp.transpose(values.astype(jnp.float32)).astype(jnp.bfloat16)
    lane = lax.broadcasted_iota(jnp.int32, (total, HEAD), 1)
    hidden = jnp.where(seen > 0, 0.0, -1e30)
    hidden = jnp.concatenate([hidden, jnp.zeros((span, 1), jnp.float32)], axis=0)
    hidden = jnp.where(lane == 0, hidden, 0.0).astype(jnp.bfloat16)
    keys = jnp.concatenate([keys, hidden], axis=1)
    ones = jnp.ones((2 * span, HEAD), jnp.bfloat16)
    causal = lax.broadcasted_iota(jnp.int32, (span, 2 * span), 0) <= lax.rem(
        lax.broadcasted_iota(jnp.int32, (span, 2 * span), 1), span
    )
    bias = jnp.where(causal, 0.0, -1e30)
    scale = math.log2(math.e) / math.sqrt(HEAD)
    mass = None
    for pair in range(group // 2):
        first = base + 2 * pair * HEAD
        query = jnp.concatenate(
            [
                q_ref[0, :, first : first + HEAD],
                q_ref[0, :, first + HEAD : first + 2 * HEAD],
            ],
            axis=0,
        )
        scores = dot(keys, jnp.concatenate([query, ones], axis=1), ((1,), (1,)))
        near = scores[cache:] + bias
        scores = jnp.concatenate([scores[:cache], near], axis=0) * scale
        peak = jnp.max(scores, axis=0, keepdims=True)
        expo = jnp.exp2(scores - peak)
        weights = expo * (1.0 / jnp.sum(expo, axis=0, keepdims=True))
        both = weights[:, :span] + weights[:, span:]
        mass = both if mass is None else mass + both
        mixed = jnp.transpose(dot(flat, weights.astype(jnp.bfloat16)))
        for member in range(2):
            lanes = slice(first + member * HEAD, first + (member + 1) * HEAD)
            out_ref[0, :, lanes] = mixed[member * span : (member + 1) * span].astype(
                jnp.bfloat16
            )
    return jnp.sum(jnp.transpose(mass), axis=0, keepdims=True)


def late_kernel(offsets_ref, q_ref, both_ref, beside_ref, out_ref, score_ref):
    mine, shards = lax.axis_index("ctx"), lax.axis_size("ctx")
    span = q_ref.shape[1]
    heads, cache = score_ref.shape[0], score_ref.shape[1] - span

    @pl.when(mine >= shards - 2)
    def _():
        _, keep, _ = read_notes(beside_ref, 2 * span, 0, heads)
        state = jnp.where(keep >= cache, keep - cache + 1, 0)
        state = jnp.where(mine == shards - 1, state, 0).astype(jnp.float32)
        state = jnp.concatenate([state, jnp.zeros((8 - heads, cache), jnp.float32)], axis=0)
        columns = jnp.transpose(state).astype(jnp.int32)
        for head in range(heads):
            lanes = slice(head * WIDTH, (head + 1) * WIDTH)
            column = columns[:, head : head + 1]
            cached = picked(column, 1, beside_ref[span : 2 * span, lanes])
            rows = jnp.concatenate(
                [cached.astype(jnp.bfloat16), both_ref[span : 2 * span, lanes]], axis=0
            )
            mass = attend_columns(q_ref, head * GROUP * HEAD, rows, column, out_ref)
            score_ref[head : head + 1, :] = mass

    @pl.when(mine < shards - 2)
    def _():
        out_ref[...] = jnp.zeros(out_ref.shape, out_ref.dtype)
        score_ref[...] = jnp.zeros(score_ref.shape, jnp.float32)


def output_part(cache_ref, row, rows, column):
    width = cache_ref.shape[1] // lax.axis_size("kv")
    return cache_ref.at[
        pl.ds(row, rows), pl.ds(pl.multiple_of(column * width, width), width)
    ]


def fill_slots(offsets_ref, notes, keeps, dests, coded, slots_ref):
    me = lax.axis_index("ctx") * lax.axis_size("kv") + lax.axis_index("kv")
    sort_notes(notes, keeps, dests)
    own = follow_lists(keeps, coded, LANES)
    for flip in range(2):
        find_slots(early_of(offsets_ref), dests, coded, me ^ flip, slots_ref.at[flip])
    return own


def index_kernel_in_planes(offsets_ref, *refs):
    both, beside, y_own, y_beside, x_own, x_beside, d_own, d_beside, far_notes = refs[:9]
    own_ref, near_slots, far_slots = refs[9:12]
    near_tables, far_tables = refs[12:15], refs[15:]
    span = x_own.shape[0] - NOTES
    at = 2 * span
    notes = [(both, at, 0, 0, 0), (beside, at, 0, 1, 0), (beside, at, 1, 3, 0)]
    notes += [(far_notes, 0, 0, 2, 0), (far_notes, 0, 1, 2, 1), (y_own, at, 0, 0, 1)]
    notes += [(y_beside, at, 0, 1, 1), (y_beside, at, 1, 3, 1)]
    own = fill_slots(offsets_ref, notes, *near_tables, near_slots)
    own_ref[...] = jnp.transpose(own.astype(jnp.float32)).astype(jnp.int32)
    notes = [(x_own, span, 0, 0, 0), (d_own, span, 0, 0, 1), (x_beside, at, 0, 1, 0)]
    notes += [(x_beside, at, 1, 3, 0), (d_beside, at, 0, 1, 1), (d_beside, at, 1, 3, 1)]
    notes += [(far_notes, NOTES, 0, 2, 0), (far_notes, NOTES, 1, 2, 1)]
    fill_slots(offsets_ref, notes, *far_tables, far_slots)


def early_kernel(offsets_ref, q_ref, *rest):
    both, beside, beyond, y_own, y_beside, late, y_late, own, slots, late_scores = rest[:10]
    out_ref, score_ref, done_ref, cache_ref, sent_ref, *rest = rest[11:]
    tokens, late_tokens, kept, sem = rest
    done_ref[...] = jnp.zeros(done_ref.shape, jnp.float32)
    span = q_ref.shape[1]
    early = early_of(offsets_ref)
    pieces = [(both, 0, 0, 0), (beside, 0, 1, 0), (beside, span, 3, 0), (beyond, 0, 2, 0)]
    pieces += [(beyond, span, 2, 1), (y_own, 0, 0, 1), (y_beside, 0, 1, 1), (y_beside, span, 3, 1)]
    sort_tokens(pieces, tokens, span)
    sort_late([(late, 0), (y_late, 0)], late_tokens)
    place_bands(slots.at[0], tokens, late_tokens, kept)
    column = lax.axis_index("kv")
    copy = pltpu.make_async_copy(kept, output_part(cache_ref, 0, kept.shape[0], column), sem)
    copy.start()
    place_bands(slots.at[1], tokens, late_tokens, sent_ref)
    score_ref[1 - early] = late_scores[...]
    for head in range(score_ref.shape[1]):
        lanes = slice(head * WIDTH, (head + 1) * WIDTH)
        chosen = own[:, head : head + 1]
        cached = picked(chosen, 1, tokens[:, lanes]).astype(jnp.bfloat16)
        rows = jnp.concatenate([cached, both[:span, lanes]], axis=0)
        mass = attend_columns(q_ref, head * GROUP * HEAD, rows, chosen, out_ref)
        score_ref[early, head : head + 1, :] = mass
    copy.wait()


def far_rows(flip, refs, far_ref, tokens, late_tokens):
    x_own, x_beside, x_end, d_own, d_beside, x_late, d_late, slots = refs
    span = x_late.shape[0]
    pieces = [(x_own, 0, 0, 0), (x_beside, 0, 1, 0), (x_beside, span, 3, 0), (x_end, 0, 2, 0)]
    pieces += [(x_end, span, 2, 1), (d_own, 0, 0, 1), (d_beside, 0, 1, 1), (d_beside, span, 3, 1)]
    sort_tokens(pieces, tokens, span)
    sort_late([(x_late, 0), (d_late, 0)], late_tokens)
    place_bands(slots.at[flip], tokens, late_tokens, far_ref)


def far_sent_kernel(*refs):
    near_ref, sent_ref, tokens, late_tokens = refs[8:]
    rows = near_ref.shape[0]
    sent_ref[rows:, :] = near_ref[...]
    far_rows(1, refs[:8], sent_ref.at[:rows], tokens, late_tokens)


def far_kept_kernel(*refs):
    cache_ref, far, tokens, late_tokens, sem = refs[9:]
    far_rows(0, refs[:8], far, tokens, late_tokens)
    column = lax.axis_index("kv")
    copy = pltpu.make_async_copy(far, output_part(cache_ref, 0, far.shape[0], column ^ 2), sem)
    copy.start()
    copy.wait()


def last_kernel(sent_ref, _, cache_ref, sems):
    column = lax.axis_index("kv")
    rows = cache_ref.shape[0]
    copies = [
        pltpu.make_async_copy(
            sent_ref.at[index * rows : (index + 1) * rows],
            output_part(cache_ref, 0, rows, column ^ place),
            sems.at[index],
        )
        for index, place in enumerate((3, 1))
    ]
    for copy in copies:
        copy.start()
    for copy in copies:
        copy.wait()


def send(value, axis, pairs):
    return lax.ppermute(value, axis, pairs)


def local_in_planes(query, kv_rows, keep, dest, offsets):
    prompts, span, qwidth = query.shape
    shards, columns = lax.axis_size("ctx"), lax.axis_size("kv")
    width = kv_rows.shape[2]
    heads = width // WIDTH
    cache = keep.shape[3]
    rows = 2 * prompts * cache // columns
    band = rows // BANDS
    vmem = pl.BlockSpec(memory_space=pltpu.VMEM)
    smem = pl.BlockSpec(memory_space=pltpu.SMEM)
    anywhere = pl.BlockSpec(memory_space=pl.ANY)
    hbm = pl.BlockSpec(memory_space=pltpu.HBM)
    params = pltpu.CompilerParams(vmem_limit_bytes=PLANE_BYTES)

    def cost(flops, moved):
        return pl.CostEstimate(flops=flops, bytes_accessed=moved, transcendentals=0)

    def piece(count):
        return jax.ShapeDtypeStruct((count, width), jnp.bfloat16)

    def along_z(value, turn):
        return send(value, "ctx", [(i, (i + 2 * turn) % shards) for i in range(shards)])

    def across_y(value):
        return send(value, "ctx", [(i, i ^ 1) for i in range(shards)])

    def across_x(value):
        return send(value, "kv", [(i, i ^ 2) for i in range(columns)])

    def across_both(value):
        pairs = [(i, i ^ columns ^ 2) for i in range(shards * columns)]
        return send(value, ("ctx", "kv"), pairs)

    def across_core(value):
        return send(value, "kv", [(i, i ^ 1) for i in range(columns)])

    both, single = pl.pallas_call(
        prepare_kernel,
        out_shape=(piece(2 * span + NOTES), piece(span + NOTES)),
        in_specs=[smem] + [hbm] * 3,
        out_specs=(vmem, vmem),
        scratch_shapes=[
            pltpu.VMEM(keep.shape, jnp.int32),
            pltpu.VMEM((1, prompts * cache), jnp.int32),
            pltpu.SemaphoreType.DMA((5,)),
        ],
        compiler_params=pltpu.CompilerParams(vmem_limit_bytes=60 * 1024 * 1024),
        cost_estimate=cost(10**9, 1),
    )(offsets, kv_rows, keep, jnp.transpose(dest))

    below, above = along_z(both, 1), along_z(single, 3)
    y_own, x_own, d_own = across_y(both), across_x(single), across_both(single)
    going, going_notes = pl.pallas_call(
        going_kernel,
        out_shape=(piece(2 * span + 2 * NOTES), piece(2 * NOTES)),
        in_specs=[vmem] * 4,
        out_specs=(vmem, vmem),
        compiler_params=params,
        cost_estimate=cost(0, 10**6),
    )(both, y_own, x_own, d_own)
    beyond, far_notes = along_z(going, 2), along_z(going_notes, 2)
    beside, relay = pl.pallas_call(
        beside_kernel,
        out_shape=(piece(2 * span + NOTES), piece(span)),
        in_specs=[vmem] * 3 + [anywhere],
        out_specs=(vmem,) * 2,
        compiler_params=params,
        cost_estimate=cost(0, 10**6),
    )(below, above, both, going)
    relayed = send(relay, "ctx", [(0, 2), (1, 3), (6, 4), (7, 5)])
    y_beside, x_beside = across_y(beside), across_x(beside)
    d_beside = across_both(beside)

    attention_shape = jax.ShapeDtypeStruct((prompts, span, qwidth), jnp.bfloat16)

    def prompt_spec(late):
        def block(_, offsets_ref):
            early = early_of(offsets_ref)
            return (1 - early if late else early, 0, 0)

        return pl.BlockSpec((1, span, qwidth), block)

    attention, late_scores = pl.pallas_call(
        late_kernel,
        grid_spec=pltpu.PrefetchScalarGridSpec(
            num_scalar_prefetch=1,
            grid=(1,),
            in_specs=[prompt_spec(True), vmem, vmem],
            out_specs=(prompt_spec(True), vmem),
        ),
        out_shape=(attention_shape, jax.ShapeDtypeStruct((heads, cache + span), jnp.float32)),
        compiler_params=params,
        cost_estimate=cost(10**6, 1),
    )(offsets, query, both, y_own)
    late = pl.pallas_call(
        pick_late_kernel,
        out_shape=piece(span),
        in_specs=[vmem] * 2 + [anywhere],
        out_specs=vmem,
        compiler_params=params,
        cost_estimate=cost(0, 10**5),
    )(relay, relayed, late_scores)
    y_late, x_late, d_late = across_y(late), across_x(late), across_both(late)

    slots_shape = jax.ShapeDtypeStruct((2, rows, heads), jnp.int32)
    tables = [
        pltpu.VMEM((shards, 4 * heads, cache), jnp.int32),
        pltpu.VMEM((shards, prompts, cache), jnp.int32),
        pltpu.VMEM((shards, 8 * heads, cache), jnp.bfloat16),
    ]
    own_slots, near_slots, far_slots = pl.pallas_call(
        index_kernel_in_planes,
        out_shape=(
            jax.ShapeDtypeStruct((cache, 4 * heads), jnp.int32),
            slots_shape,
            slots_shape,
        ),
        in_specs=[smem] + [vmem] * 9,
        out_specs=(vmem,) * 3,
        scratch_shapes=2 * tables,
        compiler_params=params,
        cost_estimate=cost(10**6, 1),
    )(offsets, both, beside, y_own, y_beside, x_own, x_beside, d_own, d_beside, far_notes)
    end = pl.pallas_call(
        end_kernel,
        out_shape=piece(2 * span),
        in_specs=[vmem, anywhere],
        out_specs=vmem,
        compiler_params=params,
        cost_estimate=cost(0, 10**5),
    )(beyond, near_slots)
    x_end = across_x(end)

    tokens = pltpu.VMEM((shards * span, width), jnp.bfloat16)
    late_tokens = pltpu.VMEM((2 * span, width), jnp.bfloat16)
    block_rows = pltpu.VMEM((rows, width), jnp.bfloat16)
    cache_shape = jax.ShapeDtypeStruct((rows, columns * width), jnp.bfloat16)
    attention, row_scores, early_done, owner_cache, near_sent = pl.pallas_call(
        early_kernel,
        grid_spec=pltpu.PrefetchScalarGridSpec(
            num_scalar_prefetch=1,
            grid=(1,),
            in_specs=[prompt_spec(False)] + [vmem] * 10 + [anywhere],
            out_specs=(prompt_spec(False), vmem, vmem, hbm, vmem),
            scratch_shapes=[tokens, late_tokens, block_rows, pltpu.SemaphoreType.DMA],
        ),
        out_shape=(
            attention_shape,
            jax.ShapeDtypeStruct((prompts, heads, cache + span), jnp.float32),
            jax.ShapeDtypeStruct((8, LANES), jnp.float32),
            cache_shape,
            piece(rows),
        ),
        input_output_aliases={12: 0},
        compiler_params=params,
        cost_estimate=cost(10**10, 10**7),
    )(
        offsets,
        query,
        both,
        beside,
        end,
        y_own,
        y_beside,
        late,
        y_late,
        own_slots,
        near_slots,
        late_scores,
        attention,
    )
    far = (x_own, x_beside, x_end, d_own, d_beside, x_late, d_late, far_slots)
    sent = pl.pallas_call(
        far_sent_kernel,
        out_shape=piece(2 * rows),
        in_specs=[vmem] * 9,
        out_specs=vmem,
        scratch_shapes=[tokens, late_tokens],
        compiler_params=params,
        cost_estimate=cost(2 * 10**9, 4 * 10**6),
    )(*far, near_sent)
    received = across_core(sent)
    owner_cache = pl.pallas_call(
        far_kept_kernel,
        out_shape=cache_shape,
        in_specs=[vmem] * 8 + [hbm],
        out_specs=hbm,
        scratch_shapes=[block_rows, tokens, late_tokens, pltpu.SemaphoreType.DMA],
        input_output_aliases={8: 0},
        compiler_params=params,
        cost_estimate=cost(2 * 10**9, 4 * 10**6),
    )(*far, owner_cache)
    owner_cache = pl.pallas_call(
        last_kernel,
        out_shape=cache_shape,
        in_specs=[anywhere, hbm],
        out_specs=hbm,
        scratch_shapes=[pltpu.SemaphoreType.DMA((2,))],
        input_output_aliases={1: 0},
        compiler_params=params,
        cost_estimate=cost(0, 10**6),
    )(received, owner_cache)
    return (attention, row_scores, owner_cache)


def solution(mesh):
    placed = (
        P(None, "ctx", "kv"),
        P(None, "ctx", "kv"),
        P(None, "ctx", "kv", None),
        P("ctx", None),
        P(),
    )
    in_planes = mesh.shape["ctx"] == 8 and mesh.shape["kv"] == 4
    return jax.shard_map(
        local_in_planes if in_planes else local,
        mesh=mesh,
        in_specs=placed,
        out_specs=(P(None, "ctx", "kv"), P(None, "kv", "ctx"), P(("ctx", "kv"), None)),
        check_vma=False,
    )
```

```python
import functools
import math

import jax
import jax.numpy as jnp
from jax import lax
from jax.experimental import pallas as pl
from jax.experimental.pallas import tpu as pltpu
from jax.sharding import PartitionSpec as P

HEAD = 128
WIDTH = 2 * HEAD
LANES = 128
VMEM_BYTES = 56 * 1024 * 1024
PLANE_BYTES = 28 * 1024 * 1024
NOTES = 16
BANDS = 4
HEADS = 2


def look_up(state, keep, fresh):
    tiles = state.shape[1] // LANES
    parts = []
    for tile in range(tiles):
        wanted = keep[:, tile * LANES : (tile + 1) * LANES]
        high = wanted >> 7
        low = wanted & 127
        found = jnp.where(high >= tiles, fresh + wanted - state.shape[1], 0)
        for source in range(tiles):
            held = state[:, source * LANES : (source + 1) * LANES]
            moved = jnp.take_along_axis(held, low, axis=1, mode="promise_in_bounds")
            found = jnp.where(high == source, moved, found)
        parts.append(found)
    return jnp.concatenate(parts, axis=1)


def split(state):
    both = jnp.concatenate([state >> 7, state & 127], axis=0)
    return both.astype(jnp.float32).astype(jnp.bfloat16)


def index_kernel(
    where_ref, keep_early_ref, keep_late_ref, dest_ref, slot_ref, row_ref, column_ref, coded
):
    shards, heads, cache = keep_early_ref.shape
    cap = slot_ref.shape[0] // shards
    span = LANES
    early, mine, me = where_ref[0], where_ref[1], where_ref[2]
    empty = jnp.minimum(keep_early_ref[0], 0)

    def follow(shard, carry):
        state, own = carry
        own = jnp.where(shard == mine, state, own)
        state = look_up(state, keep_early_ref[shard], shard * span + 1)
        coded[shard] = split(state)
        return state, own

    _, own_early = lax.fori_loop(0, shards, follow, (empty, empty), unroll=shards <= 8)
    base = shards * span + 1
    late_first = look_up(empty, keep_late_ref[0], base)
    late_second = look_up(late_first, keep_late_ref[1], base + span)
    own_late = jnp.where(mine == shards - 1, late_first, 0)
    for index, own in enumerate((own_early, own_late)):
        row_ref[index] = own
        column_ref[index] = jnp.transpose(own.astype(jnp.float32)).astype(jnp.int32)

    named = (dest_ref[...] == me).astype(jnp.float32)
    chunks = named.shape[1] // LANES
    upper = (
        lax.broadcasted_iota(jnp.int32, (LANES, LANES), 0)
        <= lax.broadcasted_iota(jnp.int32, (LANES, LANES), 1)
    ).astype(jnp.float32).astype(jnp.bfloat16)
    total = jnp.zeros((shards, 1), jnp.float32)
    ranks = []
    for chunk in range(chunks):
        part = named[:, chunk * LANES : (chunk + 1) * LANES]
        upto = jnp.dot(part.astype(jnp.bfloat16), upper, preferred_element_type=jnp.float32)
        ranks.append(jnp.where(part > 0, upto + total, 0.0))
        total = total + upto[:, LANES - 1 :]
    low_half = jnp.concatenate(ranks[: chunks // 2], axis=1)
    high_half = jnp.concatenate(ranks[chunks // 2 :], axis=1)
    rank_early = jnp.where(early == 0, low_half, high_half)
    rank_late = jnp.where(early == 0, high_half, low_half)
    place = lax.broadcasted_iota(jnp.int32, (cap, cache), 0).astype(jnp.float32) + 1.0
    contract = (((1,), (1,)), ((), ()))
    for shard in range(shards):
        pick = (rank_early[shard : shard + 1] == place).astype(jnp.float32).astype(jnp.bfloat16)
        found = lax.dot_general(pick, coded[shard], contract, preferred_element_type=jnp.float32)
        if shard >= shards - 2:
            state = late_first if shard == shards - 2 else late_second
            pick = (rank_late[shard : shard + 1] == place).astype(jnp.float32).astype(jnp.bfloat16)
            found += lax.dot_general(
                pick, split(state), contract, preferred_element_type=jnp.float32
            )
        tokens = found[:, :heads] * 128.0 + found[:, heads:]
        slot_ref[shard * cap : (shard + 1) * cap, :] = tokens.astype(jnp.int32)


def column_of(table, head):
    lane = lax.broadcasted_iota(jnp.int32, table.shape, 1)
    return jnp.sum(
        jnp.where(lane == head, table, 0).astype(jnp.float32), axis=1, keepdims=True
    ).astype(jnp.int32)


def picked(column, first, tokens):
    number = lax.broadcasted_iota(jnp.int32, (column.shape[0], tokens.shape[0]), 1) + first
    table = (column == number).astype(jnp.float32).astype(jnp.bfloat16)
    return jnp.dot(table, tokens, preferred_element_type=jnp.float32)


def attend(q_ref, prompt, keys, values, seen, out_ref, score_ref, head):
    span = q_ref.shape[1]
    cache = seen.shape[1]
    group = q_ref.shape[2] // HEAD
    causal = lax.broadcasted_iota(jnp.int32, (span, span), 1) <= lax.broadcasted_iota(
        jnp.int32, (span, span), 0
    )
    bias = jnp.concatenate(
        [
            jnp.broadcast_to(jnp.where(seen > 0, 0.0, -1e30), (span, cache)),
            jnp.where(causal, 0.0, -1e30),
        ],
        axis=1,
    )
    scale = math.log2(math.e) / math.sqrt(HEAD)
    mass = jnp.zeros((1, cache + span), jnp.float32)
    for member in range(group):
        query = q_ref[prompt, :, member * HEAD : (member + 1) * HEAD]
        scores = lax.dot_general(
            query, keys, (((1,), (1,)), ((), ())), preferred_element_type=jnp.float32
        )
        scores = scores + bias
        peak = jnp.max(scores, axis=1, keepdims=True)
        expo = jnp.exp2((scores - peak) * scale)
        weights = expo * (1.0 / jnp.sum(expo, axis=1, keepdims=True))
        mass = mass + jnp.sum(weights, axis=0, keepdims=True)
        mixed = jnp.dot(weights.astype(jnp.bfloat16), values, preferred_element_type=jnp.float32)
        out_ref[prompt, :, member * HEAD : (member + 1) * HEAD] = mixed.astype(jnp.bfloat16)
    score_ref[prompt, pl.ds(head, 1), :] = mass


def attention_kernel(
    where_ref, q_ref, span_ref, early_ref, late_ref, row_ref, column_ref, out_ref, score_ref
):
    early, mine, column, shards = where_ref[0], where_ref[1], where_ref[3], early_ref.shape[0]
    span = q_ref.shape[1]
    late = 1 - early
    local_head = pl.program_id(0)
    head = column * pl.num_programs(0) + local_head

    def run(which, prompt, tokens, first):
        chosen = column_of(column_ref[which], head)
        cached = picked(chosen, first, tokens).astype(jnp.bfloat16)
        rows = jnp.concatenate([cached, span_ref[prompt]], axis=0)
        seen = row_ref[which, pl.ds(head, 1), :]
        attend(
            q_ref, prompt, rows[:, :HEAD], rows[:, HEAD:], seen, out_ref, score_ref, local_head
        )

    run(0, early, early_ref[:, 0].reshape(shards * span, WIDTH), 1)

    @pl.when(mine >= shards - 2)
    def _():
        run(1, late, late_ref[0, 0], shards * span + 1)

    @pl.when(mine < shards - 2)
    def _():
        out_ref[late] = jnp.zeros(out_ref.shape[1:], out_ref.dtype)
        score_ref[late, pl.ds(local_head, 1), :] = jnp.zeros((1, score_ref.shape[2]), jnp.float32)


def owner_kernel(slot_ref, early_ref, late_ref, out_ref):
    shards, _, span, width = early_ref.shape
    rows = out_ref.shape[0]
    chosen = column_of(slot_ref[...], pl.program_id(0))
    bands = 4
    band = rows // bands
    reach = shards * span // bands
    tokens = early_ref[:, 0].reshape(shards * span, width)
    for index in range(bands):
        part = chosen[index * band : (index + 1) * band]
        found = picked(part, 1, tokens[: (index + 1) * reach])
        if index == bands - 1:
            found += picked(part, shards * span + 1, late_ref[:, 0].reshape(2 * span, width))
        out_ref[index * band : (index + 1) * band, :] = found.astype(jnp.bfloat16)


def local(query, kv_rows, keep, dest, offsets):
    prompts, span, qwidth = query.shape
    shards, columns = lax.axis_size("ctx"), lax.axis_size("kv")
    width = kv_rows.shape[2]
    heads_dev = width // WIDTH
    heads = heads_dev * columns
    cache = keep.shape[3]
    owners = shards * columns
    cap = 2 * prompts * cache // owners
    mine, column = lax.axis_index("ctx"), lax.axis_index("kv")
    early = jnp.where(offsets[0] < offsets[1], 0, 1).astype(jnp.int32)
    facts = jnp.stack([early, mine, mine * columns + column, column]).astype(jnp.int32)

    swap = early == 1
    ordered_kv = jnp.where(swap, kv_rows[::-1], kv_rows)
    ordered_keep = jnp.where(swap, keep[::-1, 0], keep[:, 0])
    digits = jnp.stack([ordered_keep >> 7, ordered_keep & 127], axis=1)
    share = dest.shape[0] // columns
    own_dest = lax.dynamic_slice_in_dim(dest[:, 0], column * share, share)
    facts_rows = jnp.concatenate([digits.reshape(-1), own_dest]).astype(jnp.bfloat16)
    used = facts_rows.shape[0]
    room = 16 * width
    facts_rows = jnp.concatenate([facts_rows, jnp.zeros((room - used,), jnp.bfloat16)])
    payload = jnp.concatenate(
        [ordered_kv.reshape(prompts * span, width), facts_rows.reshape(16, width)], axis=0
    )
    whole = lax.all_gather(payload, ("ctx", "kv")).reshape(
        shards, columns, prompts * span + 16, width
    )

    told = whole[:, :, prompts * span :, :].reshape(shards, columns, room).astype(jnp.int32)
    kept = told[:, :, : prompts * 2 * heads_dev * cache].reshape(
        shards, columns, prompts, 2, heads_dev, cache
    )
    kept = kept[:, :, :, 0] * 128 + kept[:, :, :, 1]
    kept = jnp.transpose(kept, (2, 0, 1, 3, 4)).reshape(prompts, shards, heads, cache)
    whole_dest = told[:, :, used - share : used].reshape(shards, columns * share)

    vmem = pl.BlockSpec(memory_space=pltpu.VMEM)
    smem = pl.BlockSpec(memory_space=pltpu.SMEM)
    params = pltpu.CompilerParams(vmem_limit_bytes=VMEM_BYTES)
    slots, rows, cols = pl.pallas_call(
        index_kernel,
        out_shape=(
            jax.ShapeDtypeStruct((shards * cap, heads), jnp.int32),
            jax.ShapeDtypeStruct((2, heads, cache), jnp.int32),
            jax.ShapeDtypeStruct((2, cache, heads), jnp.int32),
        ),
        in_specs=[smem, vmem, vmem, vmem],
        out_specs=(vmem, vmem, vmem),
        scratch_shapes=[pltpu.VMEM((shards, 2 * heads, cache), jnp.bfloat16)],
        compiler_params=params,
    )(facts, kept[0], kept[1, shards - 2 :], whole_dest)

    group_width = qwidth // heads_dev
    attention, row_scores = pl.pallas_call(
        attention_kernel,
        grid_spec=pltpu.PrefetchScalarGridSpec(
            num_scalar_prefetch=1,
            grid=(heads_dev,),
            in_specs=[
                pl.BlockSpec((prompts, span, group_width), lambda h, w: (0, 0, h)),
                pl.BlockSpec((prompts, span, WIDTH), lambda h, w: (0, 0, h)),
                pl.BlockSpec((shards, 1, span, WIDTH), lambda h, w: (0, w[3], 0, h)),
                pl.BlockSpec((1, 1, span, WIDTH), lambda h, w: (shards - 2, w[3], 1, h)),
                pl.BlockSpec((2, heads, cache), lambda h, w: (0, 0, 0)),
                pl.BlockSpec((2, cache, heads), lambda h, w: (0, 0, 0)),
            ],
            out_specs=(
                pl.BlockSpec((prompts, span, group_width), lambda h, w: (0, 0, h)),
                pl.BlockSpec((prompts, heads_dev, cache + span), lambda h, w: (0, 0, 0)),
            ),
        ),
        out_shape=(
            jax.ShapeDtypeStruct((prompts, span, qwidth), jnp.bfloat16),
            jax.ShapeDtypeStruct((prompts, heads_dev, cache + span), jnp.float32),
        ),
        compiler_params=params,
    )(facts, query, kv_rows, whole, whole, rows, cols)

    owner_cache = pl.pallas_call(
        owner_kernel,
        grid=(heads,),
        in_specs=[
            pl.BlockSpec((shards * cap, heads), lambda g: (0, 0)),
            pl.BlockSpec(
                (shards, 1, span, WIDTH), lambda g: (0, g // heads_dev, 0, g % heads_dev)
            ),
            pl.BlockSpec(
                (2, 1, span, WIDTH),
                lambda g: (shards // 2 - 1, g // heads_dev, 1, g % heads_dev),
            ),
        ],
        out_specs=pl.BlockSpec((shards * cap, WIDTH), lambda g: (0, g)),
        out_shape=jax.ShapeDtypeStruct((shards * cap, heads * WIDTH), jnp.bfloat16),
        compiler_params=params,
    )(slots, whole, whole)
    return (attention, row_scores, owner_cache)


def dot(a, b, dims=((1,), (0,))):
    return lax.dot_general(a, b, (dims, ((), ())), preferred_element_type=jnp.float32)


def marks(table):
    return table.astype(jnp.float32).astype(jnp.bfloat16)


def early_of(offsets_ref):
    return jnp.where(offsets_ref[0] < offsets_ref[1], 0, 1)


def prepare_kernel(
    offsets_ref, kv_ref, keep_ref, dest_ref, both_ref, single_ref, keep, dest, sems
):
    span = kv_ref.shape[1]
    heads, cache = keep_ref.shape[2], keep_ref.shape[3]
    early = early_of(offsets_ref)
    copies = [
        (keep_ref, keep),
        (dest_ref, dest),
        (kv_ref.at[early], single_ref.at[:span]),
        (kv_ref.at[early], both_ref.at[:span]),
        (kv_ref.at[1 - early], both_ref.at[span : 2 * span]),
    ]
    copies = [
        pltpu.make_async_copy(source, target, sems.at[index])
        for index, (source, target) in enumerate(copies)
    ]
    for copy in copies:
        copy.start()
    for copy in copies[:2]:
        copy.wait()
    lane = lax.broadcasted_iota(jnp.int32, (heads, cache), 1)
    rows = [
        keep[early, 0] - lane,
        dest[:, :cache],
        dest[:, cache:],
        keep[1 - early, 0] - lane,
        jnp.zeros((NOTES - 2 * heads - 2, cache), jnp.int32),
    ]
    rows = jnp.concatenate([row.astype(jnp.float32) for row in rows], axis=0)
    rows = rows.astype(jnp.bfloat16)
    single_ref[span:, :] = rows
    both_ref[2 * span :, :] = rows
    for copy in copies[2:]:
        copy.wait()


def two_notes(first, first_row, second, second_row):
    half = NOTES // 2
    return jnp.concatenate(
        [
            first[first_row : first_row + NOTES, :].astype(jnp.float32)[:half],
            second[second_row : second_row + NOTES, :].astype(jnp.float32)[:half],
        ],
        axis=0,
    ).astype(jnp.bfloat16)


def going_kernel(both, y_own, x_own, d_own, going_ref):
    span = both.shape[0] // 2 - NOTES // 2
    going_ref[:span, :] = both[:span, :]
    going_ref[span : 2 * span, :] = y_own[:span, :]
    going_ref[2 * span : 2 * span + NOTES, :] = two_notes(both, 2 * span, y_own, 2 * span)
    going_ref[2 * span + NOTES :, :] = two_notes(x_own, span, d_own, span)


def beside_kernel(below, above, both, _, beside_ref, relay_ref):
    span = relay_ref.shape[0]
    beside_ref[:span, :] = below[:span, :]
    beside_ref[span : 2 * span, :] = above[:span, :]
    beside_ref[2 * span :, :] = two_notes(below, 2 * span, above, span)
    level = lax.axis_index("ctx") // 2

    @pl.when(level == 0)
    def _():
        relay_ref[...] = below[span : 2 * span, :]

    @pl.when(level > 0)
    def _():
        relay_ref[...] = both[span : 2 * span, :]


def join_second_kernel(beyond, relay, relayed, *rest):
    out_ref, late_ref = rest[-2:]
    span = relay.shape[0]
    level = lax.axis_index("ctx") // 2
    out_ref[: 2 * span, :] = beyond[: 2 * span, :]
    for ref, chosen in ((relay, (level == 0) | (level == 3)), (relayed, (level == 1) | (level == 2))):

        @pl.when(chosen)
        def _(ref=ref):
            out_ref[2 * span :, :] = ref[...]
            late_ref[...] = ref[...]


def place_of(turn, flip, shards):
    mine = lax.axis_index("ctx")
    place = lax.rem(mine - 2 * turn + shards, shards)
    return place + 1 - 2 * lax.rem(mine, 2) if flip else place


def sort_tokens(pieces, tokens, span):
    shards = tokens.shape[0] // span
    for ref, base, turn, flip in pieces:
        place = place_of(turn, flip, shards)
        tokens[pl.ds(pl.multiple_of(place * span, span), span), :] = ref[base : base + span, :]


def sort_late(pieces, late_tokens):
    span = late_tokens.shape[0] // 2
    side = lax.rem(lax.axis_index("ctx"), 2)
    for flip, ref_base in enumerate(pieces):
        ref, base = ref_base
        place = side + flip - 2 * side * flip
        late_tokens[pl.ds(pl.multiple_of(place * span, span), span), :] = ref[
            base : base + span, :
        ]


def read_notes(ref, base, part, heads):
    half = NOTES // 2
    rows = ref[base : base + NOTES, :].astype(jnp.float32).astype(jnp.int32)
    rows = rows[part * half : (part + 1) * half]
    lane = lax.broadcasted_iota(jnp.int32, (heads, rows.shape[1]), 1)
    return rows[:heads] + lane, rows[heads + 2 : 2 * heads + 2] + lane, rows[heads : heads + 2]


def sort_notes(notes, first, keeps, dests):
    shards, heads = keeps.shape[0], keeps.shape[1] // 4
    for ref, base, part, turn, flip in notes:
        place = place_of(turn, flip, shards)
        early, late, dest = read_notes(ref, base, part, heads)
        keeps[place, first : first + heads, :] = early
        keeps[place, first + heads : first + 2 * heads, :] = late
        if first == 0:
            dests[place, :, :] = dest


def follow_lists(keeps, coded, span):
    shards, rows, cache = keeps.shape
    row = lax.broadcasted_iota(jnp.int32, (rows, cache), 0)
    is_early = lax.rem(row, rows // 2) < rows // 4
    state = jnp.where(row < 0, keeps[0], 0)
    own = state
    mine = lax.axis_index("ctx")
    for shard in range(shards):
        own = jnp.where(mine == shard, state, own)
        late_first = (shards + shard - (shards - 2)) * span + 1
        fresh = jnp.where(is_early[:, :LANES], shard * span + 1, late_first)
        state = look_up(state, keeps[shard], fresh)
        if shard < shards - 2:
            state = jnp.where(is_early, state, 0)
        coded[shard] = split(state)
    return own


def find_slots(early, dests, coded, owner, near, far):
    shards, halves, cache = dests.shape
    lists = coded.shape[1] // 2
    heads = lists // 4
    cap = near.shape[0] // shards
    upper = marks(
        lax.broadcasted_iota(jnp.int32, (LANES, LANES), 0)
        <= lax.broadcasted_iota(jnp.int32, (LANES, LANES), 1)
    )
    place = lax.broadcasted_iota(jnp.int32, (cap, cache), 0).astype(jnp.float32) + 1.0
    total = jnp.zeros((shards, 1), jnp.float32)
    ranks = []
    for half in range(halves):
        named = (dests[:, half, :] == owner).astype(jnp.float32)
        parts = []
        for chunk in range(cache // LANES):
            part = named[:, chunk * LANES : (chunk + 1) * LANES]
            upto = dot(part.astype(jnp.bfloat16), upper)
            parts.append(jnp.where(part > 0, upto + total, 0.0))
            total = total + upto[:, LANES - 1 :]
        ranks.append(jnp.concatenate(parts, axis=1))
    rank_early = jnp.where(early == 0, ranks[0], ranks[1])
    rank_late = jnp.where(early == 0, ranks[1], ranks[0])

    def numbers(rank, shard):
        found = dot(marks(rank[shard : shard + 1] == place), coded[shard], ((1,), (1,)))
        return found[:, :lists] * 128.0 + found[:, lists:]

    for shard in range(shards):
        tokens = numbers(rank_early, shard)
        tokens = [tokens[:, :heads], tokens[:, 2 * heads : 3 * heads]]
        if shard >= shards - 2:
            late = numbers(rank_late, shard)
            tokens[0] += late[:, heads : 2 * heads]
            tokens[1] += late[:, 3 * heads :]
        for ref, found in zip((near, far), tokens):
            ref[shard * cap : (shard + 1) * cap, :] = found.astype(jnp.int32)


def place_bands(slots, tokens, late_tokens, out_ref):
    rows, heads = slots.shape
    reach = tokens.shape[0]
    band = rows // BANDS
    for head in range(heads):
        lanes = slice(head * WIDTH, (head + 1) * WIDTH)
        for index in range(BANDS):
            part = slots[index * band : (index + 1) * band, head : head + 1]
            found = picked(part, 1, tokens[: (index + 1) * reach // BANDS, lanes])
            if index == BANDS - 1:
                found += picked(part, reach + 1, late_tokens[:, lanes])
            out_ref[index * band : (index + 1) * band, lanes] = found.astype(jnp.bfloat16)


def attend_columns(q_ref, head, rows, seen, out_ref, score_ref, score_at):
    span = q_ref.shape[1]
    total = rows.shape[0]
    cache = total - span
    group = q_ref.shape[2] // (HEADS * HEAD)
    keys, values = rows[:, :HEAD], rows[:, HEAD:]
    flat = jnp.transpose(values.astype(jnp.float32)).astype(jnp.bfloat16)
    lane = lax.broadcasted_iota(jnp.int32, (total, HEAD), 1)
    hidden = jnp.where(seen > 0, 0.0, -1e30)
    hidden = jnp.concatenate([hidden, jnp.zeros((span, 1), jnp.float32)], axis=0)
    hidden = jnp.where(lane == 0, hidden, 0.0).astype(jnp.bfloat16)
    keys = jnp.concatenate([keys, hidden], axis=1)
    ones = jnp.ones((2 * span, HEAD), jnp.bfloat16)
    causal = lax.broadcasted_iota(jnp.int32, (span, 2 * span), 0) <= lax.rem(
        lax.broadcasted_iota(jnp.int32, (span, 2 * span), 1), span
    )
    bias = jnp.where(causal, 0.0, -1e30)
    scale = math.log2(math.e) / math.sqrt(HEAD)
    mass = None
    for pair in range(group // 2):
        first = (head * group + 2 * pair) * HEAD
        query = jnp.concatenate(
            [
                q_ref[0, :, first : first + HEAD],
                q_ref[0, :, first + HEAD : first + 2 * HEAD],
            ],
            axis=0,
        )
        scores = dot(keys, jnp.concatenate([query, ones], axis=1), ((1,), (1,)))
        scores = jnp.concatenate([scores[:cache], scores[cache:] + bias], axis=0)
        peak = jnp.max(scores, axis=0, keepdims=True)
        expo = jnp.exp2((scores - peak) * scale)
        share = 1.0 / jnp.sum(expo, axis=0, keepdims=True)
        expo = expo.astype(jnp.bfloat16)
        high = share.astype(jnp.bfloat16).astype(jnp.float32)
        terms = jnp.concatenate(
            [high, share - high, jnp.zeros((6, 2 * span), jnp.float32)], axis=0
        )
        part = dot(expo, jnp.transpose(terms).astype(jnp.bfloat16))
        mass = part if mass is None else mass + part
        mixed = jnp.transpose(dot(flat, expo) * share)
        for member in range(2):
            lanes = slice(first + member * HEAD, first + (member + 1) * HEAD)
            out_ref[0, :, lanes] = mixed[member * span : (member + 1) * span].astype(
                jnp.bfloat16
            )
    score_ref[score_at, head : head + 1, :] = jnp.sum(jnp.transpose(mass), axis=0, keepdims=True)


def late_kernel(offsets_ref, q_ref, both_ref, beside_ref, out_ref, score_ref, done_ref):
    mine, shards = lax.axis_index("ctx"), lax.axis_size("ctx")
    heads, cache = score_ref.shape[1], score_ref.shape[2] - q_ref.shape[1]
    span = q_ref.shape[1]
    done_ref[...] = jnp.zeros(done_ref.shape, jnp.float32)

    @pl.when(mine >= shards - 2)
    def _():
        _, keep, _ = read_notes(beside_ref, 2 * span, 0, heads)
        state = jnp.where(keep >= cache, keep - cache + 1, 0)
        state = jnp.where(mine == shards - 1, state, 0).astype(jnp.float32)
        state = jnp.concatenate([state, jnp.zeros((8 - heads, cache), jnp.float32)], axis=0)
        columns = jnp.transpose(state).astype(jnp.int32)
        for head in range(heads):
            lanes = slice(head * WIDTH, (head + 1) * WIDTH)
            column = columns[:, head : head + 1]
            cached = picked(column, 1, beside_ref[span : 2 * span, lanes])
            rows = jnp.concatenate(
                [cached.astype(jnp.bfloat16), both_ref[span : 2 * span, lanes]], axis=0
            )
            attend_columns(q_ref, head, rows, column, out_ref, score_ref, 0)

    @pl.when(mine < shards - 2)
    def _():
        out_ref[...] = jnp.zeros(out_ref.shape, out_ref.dtype)
        score_ref[...] = jnp.zeros(score_ref.shape, jnp.float32)


def output_part(cache_ref, row, rows, column):
    width = cache_ref.shape[1] // lax.axis_size("kv")
    return cache_ref.at[
        pl.ds(row, rows), pl.ds(pl.multiple_of(column * width, width), width)
    ]


def early_kernel(offsets_ref, q_ref, *rest):
    both, beside, beyond, y_own, y_beside, late, y_late = rest[:7]
    x_own, x_beside, d_own, d_beside = rest[7:11]
    out_ref, score_ref, cache_ref, sent_ref, far_slots = rest[13:18]
    tokens, late_tokens, kept, slots, keeps, dests, coded, sem = rest[18:]
    span = q_ref.shape[1]
    early = early_of(offsets_ref)
    column = lax.axis_index("kv")
    me = lax.axis_index("ctx") * lax.axis_size("kv") + column
    at = 2 * span
    notes = [(both, at, 0, 0, 0), (beside, at, 0, 1, 0), (beside, at, 1, 3, 0)]
    notes += [(beyond, at, 0, 2, 0), (beyond, at, 1, 2, 1), (y_own, at, 0, 0, 1)]
    notes += [(y_beside, at, 0, 1, 1), (y_beside, at, 1, 3, 1)]
    sort_notes(notes, 0, keeps, dests)
    notes = [(x_own, span, 0, 0, 0), (d_own, span, 0, 0, 1), (x_beside, at, 0, 1, 0)]
    notes += [(x_beside, at, 1, 3, 0), (d_beside, at, 0, 1, 1), (d_beside, at, 1, 3, 1)]
    notes += [(beyond, at + NOTES, 0, 2, 0), (beyond, at + NOTES, 1, 2, 1)]
    sort_notes(notes, 2 * HEADS, keeps, dests)
    own = follow_lists(keeps, coded, span)
    own = jnp.transpose(own.astype(jnp.float32)).astype(jnp.int32)
    for flip in range(2):
        find_slots(early, dests, coded, me ^ flip, slots.at[flip], far_slots.at[flip])
    pieces = [(both, 0, 0, 0), (beside, 0, 1, 0), (beside, span, 3, 0), (beyond, 0, 2, 0)]
    pieces += [(beyond, span, 2, 1), (y_own, 0, 0, 1), (y_beside, 0, 1, 1), (y_beside, span, 3, 1)]
    sort_tokens(pieces, tokens, span)
    sort_late([(late, 0), (y_late, 0)], late_tokens)
    place_bands(slots.at[0], tokens, late_tokens, kept)
    copy = pltpu.make_async_copy(kept, output_part(cache_ref, 0, kept.shape[0], column), sem)
    copy.start()
    place_bands(slots.at[1], tokens, late_tokens, sent_ref)
    for head in range(score_ref.shape[1]):
        lanes = slice(head * WIDTH, (head + 1) * WIDTH)
        chosen = own[:, head : head + 1]
        cached = picked(chosen, 1, tokens[:, lanes]).astype(jnp.bfloat16)
        rows = jnp.concatenate([cached, both[:span, lanes]], axis=0)
        attend_columns(q_ref, head, rows, chosen, out_ref, score_ref, 0)
    copy.wait()


def far_rows(flip, refs, far_ref, tokens, late_tokens):
    x_own, x_beside, x_end, d_own, d_beside, d_late, slots = refs
    span = d_late.shape[0]
    pieces = [(x_own, 0, 0, 0), (x_beside, 0, 1, 0), (x_beside, span, 3, 0), (x_end, 0, 2, 0)]
    pieces += [(x_end, span, 2, 1), (d_own, 0, 0, 1), (d_beside, 0, 1, 1), (d_beside, span, 3, 1)]
    sort_tokens(pieces, tokens, span)
    sort_late([(x_end, 2 * span), (d_late, 0)], late_tokens)
    place_bands(slots.at[flip], tokens, late_tokens, far_ref)


def far_sent_kernel(*refs):
    near_ref, sent_ref, tokens, late_tokens = refs[7:]
    rows = near_ref.shape[0]
    sent_ref[rows:, :] = near_ref[...]
    far_rows(1, refs[:7], sent_ref.at[:rows], tokens, late_tokens)


def far_kept_kernel(*refs):
    cache_ref, far, tokens, late_tokens, sem = refs[8:]
    far_rows(0, refs[:7], far, tokens, late_tokens)
    column = lax.axis_index("kv")
    copy = pltpu.make_async_copy(far, output_part(cache_ref, 0, far.shape[0], column ^ 2), sem)
    copy.start()
    copy.wait()


def last_kernel(sent_ref, _, cache_ref, sems):
    column = lax.axis_index("kv")
    rows = cache_ref.shape[0]
    copies = [
        pltpu.make_async_copy(
            sent_ref.at[index * rows : (index + 1) * rows],
            output_part(cache_ref, 0, rows, column ^ place),
            sems.at[index],
        )
        for index, place in enumerate((3, 1))
    ]
    for copy in copies:
        copy.start()
    for copy in copies:
        copy.wait()


def send(value, axis, pairs):
    return lax.ppermute(value, axis, pairs)


def local_in_planes(query, kv_rows, keep, dest, offsets):
    prompts, span, qwidth = query.shape
    shards, columns = lax.axis_size("ctx"), lax.axis_size("kv")
    width = kv_rows.shape[2]
    heads = width // WIDTH
    cache = keep.shape[3]
    rows = 2 * prompts * cache // columns
    band = rows // BANDS
    vmem = pl.BlockSpec(memory_space=pltpu.VMEM)
    smem = pl.BlockSpec(memory_space=pltpu.SMEM)
    anywhere = pl.BlockSpec(memory_space=pl.ANY)
    hbm = pl.BlockSpec(memory_space=pltpu.HBM)
    params = pltpu.CompilerParams(vmem_limit_bytes=PLANE_BYTES)

    def cost(flops, moved):
        return pl.CostEstimate(flops=flops, bytes_accessed=moved, transcendentals=0)

    def piece(count):
        return jax.ShapeDtypeStruct((count, width), jnp.bfloat16)

    def along_z(value, turn):
        return send(value, "ctx", [(i, (i + 2 * turn) % shards) for i in range(shards)])

    def across_y(value):
        return send(value, "ctx", [(i, i ^ 1) for i in range(shards)])

    def across_x(value):
        return send(value, "kv", [(i, i ^ 2) for i in range(columns)])

    def across_both(value):
        pairs = [(i, i ^ columns ^ 2) for i in range(shards * columns)]
        return send(value, ("ctx", "kv"), pairs)

    def across_core(value):
        return send(value, "kv", [(i, i ^ 1) for i in range(columns)])

    both, single = pl.pallas_call(
        prepare_kernel,
        out_shape=(piece(2 * span + NOTES), piece(span + NOTES)),
        in_specs=[smem] + [hbm] * 3,
        out_specs=(vmem, vmem),
        scratch_shapes=[
            pltpu.VMEM(keep.shape, jnp.int32),
            pltpu.VMEM((1, prompts * cache), jnp.int32),
            pltpu.SemaphoreType.DMA((5,)),
        ],
        compiler_params=pltpu.CompilerParams(vmem_limit_bytes=60 * 1024 * 1024),
        cost_estimate=cost(10**9, 1),
    )(offsets, kv_rows, keep, jnp.transpose(dest))

    below, above = along_z(both, 1), along_z(single, 3)
    y_own, x_own, d_own = across_y(both), across_x(single), across_both(single)
    going = pl.pallas_call(
        going_kernel,
        out_shape=piece(2 * span + 2 * NOTES),
        in_specs=[vmem] * 4,
        out_specs=vmem,
        compiler_params=params,
        cost_estimate=cost(0, 10**6),
    )(both, y_own, x_own, d_own)
    beyond = along_z(going, 2)
    beside, relay = pl.pallas_call(
        beside_kernel,
        out_shape=(piece(2 * span + NOTES), piece(span)),
        in_specs=[vmem] * 3 + [anywhere],
        out_specs=(vmem,) * 2,
        compiler_params=params,
        cost_estimate=cost(0, 10**6),
    )(below, above, both, going)
    relayed = send(relay, "ctx", [(0, 2), (1, 3), (6, 4), (7, 5)])
    y_beside, x_beside = across_y(beside), across_x(beside)
    d_beside = across_both(beside)

    attention_shape = jax.ShapeDtypeStruct((prompts, span, qwidth), jnp.bfloat16)
    score_shape = jax.ShapeDtypeStruct((prompts, heads, cache + span), jnp.float32)

    def prompt_specs(late):
        def block(_, offsets_ref):
            early = early_of(offsets_ref)
            return (1 - early if late else early, 0, 0)

        return (
            pl.BlockSpec((1, span, qwidth), block),
            pl.BlockSpec((1, heads, cache + span), block),
        )

    attention, row_scores, late_done = pl.pallas_call(
        late_kernel,
        grid_spec=pltpu.PrefetchScalarGridSpec(
            num_scalar_prefetch=1,
            grid=(1,),
            in_specs=[prompt_specs(True)[0], vmem, vmem],
            out_specs=prompt_specs(True) + (vmem,),
        ),
        out_shape=(attention_shape, score_shape, jax.ShapeDtypeStruct((8, LANES), jnp.float32)),
        compiler_params=params,
        cost_estimate=cost(10**6, 1),
    )(offsets, query, both, y_own)

    end, late = pl.pallas_call(
        join_second_kernel,
        out_shape=(piece(3 * span), piece(span)),
        in_specs=[vmem] * 3 + [anywhere] * 3,
        out_specs=(vmem, vmem),
        compiler_params=params,
        cost_estimate=cost(10**6, 1),
    )(beyond, relay, relayed, y_beside, x_beside, late_done)
    d_late, y_late, x_end = across_both(late), across_y(late), across_x(end)

    tokens = pltpu.VMEM((shards * span, width), jnp.bfloat16)
    late_tokens = pltpu.VMEM((2 * span, width), jnp.bfloat16)
    block_rows = pltpu.VMEM((rows, width), jnp.bfloat16)
    cache_shape = jax.ShapeDtypeStruct((rows, columns * width), jnp.bfloat16)
    slots_shape = jax.ShapeDtypeStruct((2, rows, heads), jnp.int32)
    attention, row_scores, owner_cache, near_sent, far_slots = pl.pallas_call(
        early_kernel,
        grid_spec=pltpu.PrefetchScalarGridSpec(
            num_scalar_prefetch=1,
            grid=(1,),
            in_specs=[prompt_specs(False)[0]] + [vmem] * 11 + [anywhere] * 2,
            out_specs=prompt_specs(False) + (hbm, vmem, vmem),
            scratch_shapes=[
                tokens,
                late_tokens,
                block_rows,
                pltpu.VMEM(slots_shape.shape, jnp.int32),
                pltpu.VMEM((shards, 4 * heads, cache), jnp.int32),
                pltpu.VMEM((shards, prompts, cache), jnp.int32),
                pltpu.VMEM((shards, 8 * heads, cache), jnp.bfloat16),
                pltpu.SemaphoreType.DMA,
            ],
        ),
        out_shape=(attention_shape, score_shape, cache_shape, piece(rows), slots_shape),
        input_output_aliases={13: 0, 14: 1},
        compiler_params=params,
        cost_estimate=cost(10**10, 10**7),
    )(
        offsets,
        query,
        both,
        beside,
        beyond,
        y_own,
        y_beside,
        late,
        y_late,
        x_own,
        x_beside,
        d_own,
        d_beside,
        attention,
        row_scores,
    )
    far = (x_own, x_beside, x_end, d_own, d_beside, d_late, far_slots)
    sent = pl.pallas_call(
        far_sent_kernel,
        out_shape=piece(2 * rows),
        in_specs=[vmem] * 8,
        out_specs=vmem,
        scratch_shapes=[tokens, late_tokens],
        compiler_params=params,
        cost_estimate=cost(2 * 10**9, 4 * 10**6),
    )(*far, near_sent)
    received = across_core(sent)
    owner_cache = pl.pallas_call(
        far_kept_kernel,
        out_shape=cache_shape,
        in_specs=[vmem] * 7 + [hbm],
        out_specs=hbm,
        scratch_shapes=[block_rows, tokens, late_tokens, pltpu.SemaphoreType.DMA],
        input_output_aliases={7: 0},
        compiler_params=params,
        cost_estimate=cost(2 * 10**9, 4 * 10**6),
    )(*far, owner_cache)
    owner_cache = pl.pallas_call(
        last_kernel,
        out_shape=cache_shape,
        in_specs=[anywhere, hbm],
        out_specs=hbm,
        scratch_shapes=[pltpu.SemaphoreType.DMA((2,))],
        input_output_aliases={1: 0},
        compiler_params=params,
        cost_estimate=cost(0, 10**6),
    )(received, owner_cache)
    return (attention, row_scores, owner_cache)


def solution(mesh):
    placed = (
        P(None, "ctx", "kv"),
        P(None, "ctx", "kv"),
        P(None, "ctx", "kv", None),
        P("ctx", None),
        P(),
    )
    in_planes = mesh.shape["ctx"] == 8 and mesh.shape["kv"] == 4
    return jax.shard_map(
        local_in_planes if in_planes else local,
        mesh=mesh,
        in_specs=placed,
        out_specs=(P(None, "ctx", "kv"), P(None, "kv", "ctx"), P(("ctx", "kv"), None)),
        check_vma=False,
    )
```

```python
import functools
import math

import jax
import jax.numpy as jnp
from jax import lax
from jax.experimental import pallas as pl
from jax.experimental.pallas import tpu as pltpu
from jax.sharding import PartitionSpec as P

HEAD = 128
WIDTH = 2 * HEAD
LANES = 128
VMEM_BYTES = 56 * 1024 * 1024
PLANE_BYTES = 28 * 1024 * 1024
NOTES = 16
BANDS = 4


def look_up(state, keep, fresh):
    tiles = state.shape[1] // LANES
    parts = []
    for tile in range(tiles):
        wanted = keep[:, tile * LANES : (tile + 1) * LANES]
        high = wanted >> 7
        low = wanted & 127
        found = jnp.where(high >= tiles, fresh + wanted - state.shape[1], 0)
        for source in range(tiles):
            held = state[:, source * LANES : (source + 1) * LANES]
            moved = jnp.take_along_axis(held, low, axis=1, mode="promise_in_bounds")
            found = jnp.where(high == source, moved, found)
        parts.append(found)
    return jnp.concatenate(parts, axis=1)


def split(state):
    both = jnp.concatenate([state >> 7, state & 127], axis=0)
    return both.astype(jnp.float32).astype(jnp.bfloat16)


def index_kernel(
    where_ref, keep_early_ref, keep_late_ref, dest_ref, slot_ref, row_ref, column_ref, coded
):
    shards, heads, cache = keep_early_ref.shape
    cap = slot_ref.shape[0] // shards
    span = LANES
    early, mine, me = where_ref[0], where_ref[1], where_ref[2]
    empty = jnp.minimum(keep_early_ref[0], 0)

    def follow(shard, carry):
        state, own = carry
        own = jnp.where(shard == mine, state, own)
        state = look_up(state, keep_early_ref[shard], shard * span + 1)
        coded[shard] = split(state)
        return state, own

    _, own_early = lax.fori_loop(0, shards, follow, (empty, empty), unroll=shards <= 8)
    base = shards * span + 1
    late_first = look_up(empty, keep_late_ref[0], base)
    late_second = look_up(late_first, keep_late_ref[1], base + span)
    own_late = jnp.where(mine == shards - 1, late_first, 0)
    for index, own in enumerate((own_early, own_late)):
        row_ref[index] = own
        column_ref[index] = jnp.transpose(own.astype(jnp.float32)).astype(jnp.int32)

    named = (dest_ref[...] == me).astype(jnp.float32)
    chunks = named.shape[1] // LANES
    upper = (
        lax.broadcasted_iota(jnp.int32, (LANES, LANES), 0)
        <= lax.broadcasted_iota(jnp.int32, (LANES, LANES), 1)
    ).astype(jnp.float32).astype(jnp.bfloat16)
    total = jnp.zeros((shards, 1), jnp.float32)
    ranks = []
    for chunk in range(chunks):
        part = named[:, chunk * LANES : (chunk + 1) * LANES]
        upto = jnp.dot(part.astype(jnp.bfloat16), upper, preferred_element_type=jnp.float32)
        ranks.append(jnp.where(part > 0, upto + total, 0.0))
        total = total + upto[:, LANES - 1 :]
    low_half = jnp.concatenate(ranks[: chunks // 2], axis=1)
    high_half = jnp.concatenate(ranks[chunks // 2 :], axis=1)
    rank_early = jnp.where(early == 0, low_half, high_half)
    rank_late = jnp.where(early == 0, high_half, low_half)
    place = lax.broadcasted_iota(jnp.int32, (cap, cache), 0).astype(jnp.float32) + 1.0
    contract = (((1,), (1,)), ((), ()))
    for shard in range(shards):
        pick = (rank_early[shard : shard + 1] == place).astype(jnp.float32).astype(jnp.bfloat16)
        found = lax.dot_general(pick, coded[shard], contract, preferred_element_type=jnp.float32)
        if shard >= shards - 2:
            state = late_first if shard == shards - 2 else late_second
            pick = (rank_late[shard : shard + 1] == place).astype(jnp.float32).astype(jnp.bfloat16)
            found += lax.dot_general(
                pick, split(state), contract, preferred_element_type=jnp.float32
            )
        tokens = found[:, :heads] * 128.0 + found[:, heads:]
        slot_ref[shard * cap : (shard + 1) * cap, :] = tokens.astype(jnp.int32)


def column_of(table, head):
    lane = lax.broadcasted_iota(jnp.int32, table.shape, 1)
    return jnp.sum(
        jnp.where(lane == head, table, 0).astype(jnp.float32), axis=1, keepdims=True
    ).astype(jnp.int32)


def picked(column, first, tokens):
    number = lax.broadcasted_iota(jnp.int32, (column.shape[0], tokens.shape[0]), 1) + first
    table = (column == number).astype(jnp.float32).astype(jnp.bfloat16)
    return jnp.dot(table, tokens, preferred_element_type=jnp.float32)


def attend(q_ref, prompt, keys, values, seen, out_ref, score_ref, head):
    span = q_ref.shape[1]
    cache = seen.shape[1]
    group = q_ref.shape[2] // HEAD
    causal = lax.broadcasted_iota(jnp.int32, (span, span), 1) <= lax.broadcasted_iota(
        jnp.int32, (span, span), 0
    )
    bias = jnp.concatenate(
        [
            jnp.broadcast_to(jnp.where(seen > 0, 0.0, -1e30), (span, cache)),
            jnp.where(causal, 0.0, -1e30),
        ],
        axis=1,
    )
    scale = math.log2(math.e) / math.sqrt(HEAD)
    mass = jnp.zeros((1, cache + span), jnp.float32)
    for member in range(group):
        query = q_ref[prompt, :, member * HEAD : (member + 1) * HEAD]
        scores = lax.dot_general(
            query, keys, (((1,), (1,)), ((), ())), preferred_element_type=jnp.float32
        )
        scores = scores + bias
        peak = jnp.max(scores, axis=1, keepdims=True)
        expo = jnp.exp2((scores - peak) * scale)
        weights = expo * (1.0 / jnp.sum(expo, axis=1, keepdims=True))
        mass = mass + jnp.sum(weights, axis=0, keepdims=True)
        mixed = jnp.dot(weights.astype(jnp.bfloat16), values, preferred_element_type=jnp.float32)
        out_ref[prompt, :, member * HEAD : (member + 1) * HEAD] = mixed.astype(jnp.bfloat16)
    score_ref[prompt, pl.ds(head, 1), :] = mass


def attention_kernel(
    where_ref, q_ref, span_ref, early_ref, late_ref, row_ref, column_ref, out_ref, score_ref
):
    early, mine, column, shards = where_ref[0], where_ref[1], where_ref[3], early_ref.shape[0]
    span = q_ref.shape[1]
    late = 1 - early
    local_head = pl.program_id(0)
    head = column * pl.num_programs(0) + local_head

    def run(which, prompt, tokens, first):
        chosen = column_of(column_ref[which], head)
        cached = picked(chosen, first, tokens).astype(jnp.bfloat16)
        rows = jnp.concatenate([cached, span_ref[prompt]], axis=0)
        seen = row_ref[which, pl.ds(head, 1), :]
        attend(
            q_ref, prompt, rows[:, :HEAD], rows[:, HEAD:], seen, out_ref, score_ref, local_head
        )

    run(0, early, early_ref[:, 0].reshape(shards * span, WIDTH), 1)

    @pl.when(mine >= shards - 2)
    def _():
        run(1, late, late_ref[0, 0], shards * span + 1)

    @pl.when(mine < shards - 2)
    def _():
        out_ref[late] = jnp.zeros(out_ref.shape[1:], out_ref.dtype)
        score_ref[late, pl.ds(local_head, 1), :] = jnp.zeros((1, score_ref.shape[2]), jnp.float32)


def owner_kernel(slot_ref, early_ref, late_ref, out_ref):
    shards, _, span, width = early_ref.shape
    rows = out_ref.shape[0]
    chosen = column_of(slot_ref[...], pl.program_id(0))
    bands = 4
    band = rows // bands
    reach = shards * span // bands
    tokens = early_ref[:, 0].reshape(shards * span, width)
    for index in range(bands):
        part = chosen[index * band : (index + 1) * band]
        found = picked(part, 1, tokens[: (index + 1) * reach])
        if index == bands - 1:
            found += picked(part, shards * span + 1, late_ref[:, 0].reshape(2 * span, width))
        out_ref[index * band : (index + 1) * band, :] = found.astype(jnp.bfloat16)


def local(query, kv_rows, keep, dest, offsets):
    prompts, span, qwidth = query.shape
    shards, columns = lax.axis_size("ctx"), lax.axis_size("kv")
    width = kv_rows.shape[2]
    heads_dev = width // WIDTH
    heads = heads_dev * columns
    cache = keep.shape[3]
    owners = shards * columns
    cap = 2 * prompts * cache // owners
    mine, column = lax.axis_index("ctx"), lax.axis_index("kv")
    early = jnp.where(offsets[0] < offsets[1], 0, 1).astype(jnp.int32)
    facts = jnp.stack([early, mine, mine * columns + column, column]).astype(jnp.int32)

    swap = early == 1
    ordered_kv = jnp.where(swap, kv_rows[::-1], kv_rows)
    ordered_keep = jnp.where(swap, keep[::-1, 0], keep[:, 0])
    digits = jnp.stack([ordered_keep >> 7, ordered_keep & 127], axis=1)
    share = dest.shape[0] // columns
    own_dest = lax.dynamic_slice_in_dim(dest[:, 0], column * share, share)
    facts_rows = jnp.concatenate([digits.reshape(-1), own_dest]).astype(jnp.bfloat16)
    used = facts_rows.shape[0]
    room = 16 * width
    facts_rows = jnp.concatenate([facts_rows, jnp.zeros((room - used,), jnp.bfloat16)])
    payload = jnp.concatenate(
        [ordered_kv.reshape(prompts * span, width), facts_rows.reshape(16, width)], axis=0
    )
    whole = lax.all_gather(payload, ("ctx", "kv")).reshape(
        shards, columns, prompts * span + 16, width
    )

    told = whole[:, :, prompts * span :, :].reshape(shards, columns, room).astype(jnp.int32)
    kept = told[:, :, : prompts * 2 * heads_dev * cache].reshape(
        shards, columns, prompts, 2, heads_dev, cache
    )
    kept = kept[:, :, :, 0] * 128 + kept[:, :, :, 1]
    kept = jnp.transpose(kept, (2, 0, 1, 3, 4)).reshape(prompts, shards, heads, cache)
    whole_dest = told[:, :, used - share : used].reshape(shards, columns * share)

    vmem = pl.BlockSpec(memory_space=pltpu.VMEM)
    smem = pl.BlockSpec(memory_space=pltpu.SMEM)
    params = pltpu.CompilerParams(vmem_limit_bytes=VMEM_BYTES)
    slots, rows, cols = pl.pallas_call(
        index_kernel,
        out_shape=(
            jax.ShapeDtypeStruct((shards * cap, heads), jnp.int32),
            jax.ShapeDtypeStruct((2, heads, cache), jnp.int32),
            jax.ShapeDtypeStruct((2, cache, heads), jnp.int32),
        ),
        in_specs=[smem, vmem, vmem, vmem],
        out_specs=(vmem, vmem, vmem),
        scratch_shapes=[pltpu.VMEM((shards, 2 * heads, cache), jnp.bfloat16)],
        compiler_params=params,
    )(facts, kept[0], kept[1, shards - 2 :], whole_dest)

    group_width = qwidth // heads_dev
    attention, row_scores = pl.pallas_call(
        attention_kernel,
        grid_spec=pltpu.PrefetchScalarGridSpec(
            num_scalar_prefetch=1,
            grid=(heads_dev,),
            in_specs=[
                pl.BlockSpec((prompts, span, group_width), lambda h, w: (0, 0, h)),
                pl.BlockSpec((prompts, span, WIDTH), lambda h, w: (0, 0, h)),
                pl.BlockSpec((shards, 1, span, WIDTH), lambda h, w: (0, w[3], 0, h)),
                pl.BlockSpec((1, 1, span, WIDTH), lambda h, w: (shards - 2, w[3], 1, h)),
                pl.BlockSpec((2, heads, cache), lambda h, w: (0, 0, 0)),
                pl.BlockSpec((2, cache, heads), lambda h, w: (0, 0, 0)),
            ],
            out_specs=(
                pl.BlockSpec((prompts, span, group_width), lambda h, w: (0, 0, h)),
                pl.BlockSpec((prompts, heads_dev, cache + span), lambda h, w: (0, 0, 0)),
            ),
        ),
        out_shape=(
            jax.ShapeDtypeStruct((prompts, span, qwidth), jnp.bfloat16),
            jax.ShapeDtypeStruct((prompts, heads_dev, cache + span), jnp.float32),
        ),
        compiler_params=params,
    )(facts, query, kv_rows, whole, whole, rows, cols)

    owner_cache = pl.pallas_call(
        owner_kernel,
        grid=(heads,),
        in_specs=[
            pl.BlockSpec((shards * cap, heads), lambda g: (0, 0)),
            pl.BlockSpec(
                (shards, 1, span, WIDTH), lambda g: (0, g // heads_dev, 0, g % heads_dev)
            ),
            pl.BlockSpec(
                (2, 1, span, WIDTH),
                lambda g: (shards // 2 - 1, g // heads_dev, 1, g % heads_dev),
            ),
        ],
        out_specs=pl.BlockSpec((shards * cap, WIDTH), lambda g: (0, g)),
        out_shape=jax.ShapeDtypeStruct((shards * cap, heads * WIDTH), jnp.bfloat16),
        compiler_params=params,
    )(slots, whole, whole)
    return (attention, row_scores, owner_cache)


def dot(a, b, dims=((1,), (0,))):
    return lax.dot_general(a, b, (dims, ((), ())), preferred_element_type=jnp.float32)


def marks(table):
    return table.astype(jnp.float32).astype(jnp.bfloat16)


def early_of(offsets_ref):
    return jnp.where(offsets_ref[0] < offsets_ref[1], 0, 1)


def own_notes(early, keep, dest):
    heads, cache = keep.shape[2], keep.shape[3]
    lane = lax.broadcasted_iota(jnp.int32, (heads, cache), 1)
    rows = [
        keep[early, 0] - lane,
        dest[:, :cache],
        dest[:, cache:],
        keep[1 - early, 0] - lane,
        jnp.zeros((NOTES - 2 * heads - 2, cache), jnp.int32),
    ]
    return jnp.concatenate([row.astype(jnp.float32) for row in rows], axis=0)


def prepare_kernel(
    offsets_ref, kv_ref, keep_ref, dest_ref, both_ref, single_ref, keep, dest, notes, sems
):
    span = kv_ref.shape[1]
    early = early_of(offsets_ref)
    copies = [
        (keep_ref, keep),
        (dest_ref, dest),
        (kv_ref.at[early], both_ref.at[:span]),
        (kv_ref.at[1 - early], both_ref.at[span : 2 * span]),
        (kv_ref.at[early], single_ref.at[:span]),
        (notes, both_ref.at[2 * span :]),
        (notes, single_ref.at[span:]),
    ]
    copies = [
        pltpu.make_async_copy(source, target, sems.at[index])
        for index, (source, target) in enumerate(copies)
    ]
    for copy in copies[:5]:
        copy.start()
    for copy in copies[:2]:
        copy.wait()
    notes[...] = own_notes(early, keep, dest).astype(jnp.bfloat16)
    for copy in copies[5:]:
        copy.start()
    for copy in copies[2:]:
        copy.wait()


def two_notes(first, first_row, second, second_row):
    half = NOTES // 2
    return jnp.concatenate(
        [
            first[first_row : first_row + NOTES, :].astype(jnp.float32)[:half],
            second[second_row : second_row + NOTES, :].astype(jnp.float32)[:half],
        ],
        axis=0,
    ).astype(jnp.bfloat16)


def going_kernel(offsets_ref, kv_ref, keep_ref, dest_ref, y_own, x_own, d_own, going_ref):
    span = kv_ref.shape[1]
    half = NOTES // 2
    early = early_of(offsets_ref)
    going_ref[:span, :] = kv_ref[early]
    going_ref[span : 2 * span, :] = y_own[:span, :]
    beside = y_own[2 * span :, :].astype(jnp.float32)
    notes = jnp.concatenate([own_notes(early, keep_ref, dest_ref)[:half], beside[:half]], axis=0)
    going_ref[2 * span : 2 * span + NOTES, :] = notes.astype(jnp.bfloat16)
    going_ref[2 * span + NOTES :, :] = two_notes(x_own, span, d_own, span)


def beside_kernel(offsets_ref, below, above, kv_ref, _, beside_ref, relay_ref):
    span = relay_ref.shape[0]
    beside_ref[:span, :] = below[:span, :]
    beside_ref[span : 2 * span, :] = above[:span, :]
    beside_ref[2 * span :, :] = two_notes(below, 2 * span, above, span)
    level = lax.axis_index("ctx") // 2

    @pl.when(level == 0)
    def _():
        relay_ref[...] = below[span : 2 * span, :]

    @pl.when(level > 0)
    def _():
        relay_ref[...] = kv_ref[1 - early_of(offsets_ref)]


def join_second_kernel(beyond, relay, relayed, *rest):
    out_ref, late_ref = rest[-2:]
    span = relay.shape[0]
    level = lax.axis_index("ctx") // 2
    out_ref[: 2 * span, :] = beyond[: 2 * span, :]
    for ref, chosen in ((relay, (level == 0) | (level == 3)), (relayed, (level == 1) | (level == 2))):

        @pl.when(chosen)
        def _(ref=ref):
            out_ref[2 * span :, :] = ref[...]
            late_ref[...] = ref[...]


def place_of(turn, flip, shards):
    mine = lax.axis_index("ctx")
    place = lax.rem(mine - 2 * turn + shards, shards)
    return place + 1 - 2 * lax.rem(mine, 2) if flip else place


def sort_tokens(pieces, tokens, span):
    shards = tokens.shape[0] // span
    for ref, base, turn, flip in pieces:
        place = place_of(turn, flip, shards)
        tokens[pl.ds(pl.multiple_of(place * span, span), span), :] = ref[base : base + span, :]


def sort_late(pieces, late_tokens):
    span = late_tokens.shape[0] // 2
    side = lax.rem(lax.axis_index("ctx"), 2)
    for flip, ref_base in enumerate(pieces):
        ref, base = ref_base
        place = side + flip - 2 * side * flip
        late_tokens[pl.ds(pl.multiple_of(place * span, span), span), :] = ref[
            base : base + span, :
        ]


def read_notes(ref, base, part, heads):
    half = NOTES // 2
    rows = ref[base : base + NOTES, :].astype(jnp.float32).astype(jnp.int32)
    rows = rows[part * half : (part + 1) * half]
    lane = lax.broadcasted_iota(jnp.int32, (heads, rows.shape[1]), 1)
    return rows[:heads] + lane, rows[heads + 2 : 2 * heads + 2] + lane, rows[heads : heads + 2]


def sort_notes(notes, keeps, dests):
    shards, heads = keeps.shape[0], keeps.shape[1] // 4
    for ref, base, part, turn, flip in notes:
        place = place_of(turn, flip, shards)
        early, late, dest = read_notes(ref, base, part, heads)
        keeps[place, :heads, :] = early
        keeps[place, heads : 2 * heads, :] = late
        dests[place, :, :] = dest


def follow_lists(keeps, coded, span):
    shards, rows, cache = keeps.shape
    heads = rows // 4
    row = lax.broadcasted_iota(jnp.int32, (rows, cache), 0)
    is_early = row < heads
    state = jnp.where(row < 0, keeps[0], 0)
    own = state
    mine = lax.axis_index("ctx")
    for shard in range(shards):
        own = jnp.where(mine == shard, state, own)
        late_first = (shards + shard - (shards - 2)) * span + 1
        fresh = jnp.where(is_early[:, :LANES], shard * span + 1, late_first)
        state = look_up(state, keeps[shard], fresh)
        if shard < shards - 2:
            state = jnp.where(is_early, state, 0)
        coded[shard] = split(state)
    return own


def find_slots(early, dests, coded, owner, slots):
    shards, halves, cache = dests.shape
    heads = coded.shape[1] // 8
    cap = slots.shape[0] // shards
    upper = marks(
        lax.broadcasted_iota(jnp.int32, (LANES, LANES), 0)
        <= lax.broadcasted_iota(jnp.int32, (LANES, LANES), 1)
    )
    place = lax.broadcasted_iota(jnp.int32, (cap, cache), 0).astype(jnp.float32) + 1.0
    total = jnp.zeros((shards, 1), jnp.float32)
    ranks = []
    for half in range(halves):
        named = (dests[:, half, :] == owner).astype(jnp.float32)
        parts = []
        for chunk in range(cache // LANES):
            part = named[:, chunk * LANES : (chunk + 1) * LANES]
            upto = dot(part.astype(jnp.bfloat16), upper)
            parts.append(jnp.where(part > 0, upto + total, 0.0))
            total = total + upto[:, LANES - 1 :]
        ranks.append(jnp.concatenate(parts, axis=1))
    rank_early = jnp.where(early == 0, ranks[0], ranks[1])
    rank_late = jnp.where(early == 0, ranks[1], ranks[0])
    across = ((1,), (1,))
    for shard in range(shards):
        found = dot(marks(rank_early[shard : shard + 1] == place), coded[shard], across)
        tokens = found[:, :heads] * 128.0 + found[:, 4 * heads : 5 * heads]
        if shard >= shards - 2:
            found = dot(marks(rank_late[shard : shard + 1] == place), coded[shard], across)
            tokens += found[:, heads : 2 * heads] * 128.0 + found[:, 5 * heads : 6 * heads]
        slots[shard * cap : (shard + 1) * cap, :] = tokens.astype(jnp.int32)


def place_bands(slots, tokens, out_ref, bands, total_bands):
    rows, heads = slots.shape
    reach = tokens.shape[0]
    band = rows // total_bands
    for head in range(heads):
        lanes = slice(head * WIDTH, (head + 1) * WIDTH)
        for order, index in enumerate(bands):
            part = slots[index * band : (index + 1) * band, head : head + 1]
            found = picked(part, 1, tokens[: (index + 1) * reach // total_bands, lanes])
            out_ref[order * band : (order + 1) * band, lanes] = found.astype(jnp.bfloat16)


def add_late(slots, first, late_tokens, out_ref, base):
    band, heads = slots.shape
    for head in range(heads):
        lanes = slice(head * WIDTH, (head + 1) * WIDTH)
        found = picked(slots[:, head : head + 1], first, late_tokens[:, lanes])
        out_ref[base : base + band, lanes] += found.astype(jnp.bfloat16)


def attend_columns(q_ref, head, rows, seen, out_ref, score_ref):
    span = q_ref.shape[1]
    total = rows.shape[0]
    cache = total - span
    group = q_ref.shape[2] // (score_ref.shape[1] * HEAD)
    keys, values = rows[:, :HEAD], rows[:, HEAD:]
    flat = jnp.transpose(values.astype(jnp.float32)).astype(jnp.bfloat16)
    lane = lax.broadcasted_iota(jnp.int32, (total, HEAD), 1)
    hidden = jnp.where(seen > 0, 0.0, -1e30)
    hidden = jnp.concatenate([hidden, jnp.zeros((span, 1), jnp.float32)], axis=0)
    hidden = jnp.where(lane == 0, hidden, 0.0).astype(jnp.bfloat16)
    keys = jnp.concatenate([keys, hidden], axis=1)
    ones = jnp.ones((2 * span, HEAD), jnp.bfloat16)
    causal = lax.broadcasted_iota(jnp.int32, (span, 2 * span), 0) <= lax.rem(
        lax.broadcasted_iota(jnp.int32, (span, 2 * span), 1), span
    )
    bias = jnp.where(causal, 0.0, -1e30)
    scale = math.log2(math.e) / math.sqrt(HEAD)
    mass = None
    for pair in range(group // 2):
        first = (head * group + 2 * pair) * HEAD
        query = jnp.concatenate(
            [
                q_ref[0, :, first : first + HEAD],
                q_ref[0, :, first + HEAD : first + 2 * HEAD],
            ],
            axis=0,
        )
        scores = dot(keys, jnp.concatenate([query, ones], axis=1), ((1,), (1,)))
        near = scores[cache:] + bias
        scores = jnp.concatenate([scores[:cache], near], axis=0) * scale
        peak = jnp.max(scores, axis=0, keepdims=True)
        expo = jnp.exp2(scores - peak)
        weights = expo * (1.0 / jnp.sum(expo, axis=0, keepdims=True))
        both = weights[:, :span] + weights[:, span:]
        mass = both if mass is None else mass + both
        mixed = jnp.transpose(dot(flat, weights.astype(jnp.bfloat16)))
        for member in range(2):
            lanes = slice(first + member * HEAD, first + (member + 1) * HEAD)
            out_ref[0, :, lanes] = mixed[member * span : (member + 1) * span].astype(
                jnp.bfloat16
            )
    score_ref[0, head : head + 1, :] = jnp.sum(jnp.transpose(mass), axis=0, keepdims=True)


def late_kernel(offsets_ref, q_ref, kv_ref, beside_ref, out_ref, score_ref, done_ref):
    mine, shards = lax.axis_index("ctx"), lax.axis_size("ctx")
    heads, cache = score_ref.shape[1], score_ref.shape[2] - q_ref.shape[1]
    span = q_ref.shape[1]
    done_ref[...] = jnp.zeros(done_ref.shape, jnp.float32)

    @pl.when(mine >= shards - 2)
    def _():
        _, keep, _ = read_notes(beside_ref, 2 * span, 0, heads)
        state = jnp.where(keep >= cache, keep - cache + 1, 0)
        state = jnp.where(mine == shards - 1, state, 0).astype(jnp.float32)
        state = jnp.concatenate([state, jnp.zeros((8 - heads, cache), jnp.float32)], axis=0)
        columns = jnp.transpose(state).astype(jnp.int32)
        for head in range(heads):
            lanes = slice(head * WIDTH, (head + 1) * WIDTH)
            column = columns[:, head : head + 1]
            cached = picked(column, 1, beside_ref[span : 2 * span, lanes])
            rows = jnp.concatenate(
                [cached.astype(jnp.bfloat16), kv_ref[1 - early_of(offsets_ref), :, lanes]], axis=0
            )
            attend_columns(q_ref, head, rows, column, out_ref, score_ref)

    @pl.when(mine < shards - 2)
    def _():
        out_ref[...] = jnp.zeros(out_ref.shape, out_ref.dtype)
        score_ref[...] = jnp.zeros(score_ref.shape, jnp.float32)


def output_part(cache_ref, row, rows, column):
    width = cache_ref.shape[1] // lax.axis_size("kv")
    return cache_ref.at[
        pl.ds(row, rows), pl.ds(pl.multiple_of(column * width, width), width)
    ]


def fill_slots(offsets_ref, notes, keeps, dests, coded, slots_ref):
    me = lax.axis_index("ctx") * lax.axis_size("kv") + lax.axis_index("kv")
    sort_notes(notes, keeps, dests)
    own = follow_lists(keeps, coded, LANES)
    for flip in range(2):
        find_slots(early_of(offsets_ref), dests, coded, me ^ flip, slots_ref.at[flip])
    return own


def early_kernel(offsets_ref, q_ref, *rest):
    both, beside, beyond, y_own, y_beside = rest[:5]
    out_ref, score_ref, done_ref, cache_ref, top_sent, low_ref, slots_ref = rest[8:15]
    tokens, top, sem, keeps, dests, coded = rest[15:]
    done_ref[...] = jnp.zeros(done_ref.shape, jnp.float32)
    span = q_ref.shape[1]
    column = lax.axis_index("kv")
    at = 2 * span
    notes = [(both, at, 0, 0, 0), (beside, at, 0, 1, 0), (beside, at, 1, 3, 0)]
    notes += [(beyond, at, 0, 2, 0), (beyond, at, 1, 2, 1), (y_own, at, 0, 0, 1)]
    notes += [(y_beside, at, 0, 1, 1), (y_beside, at, 1, 3, 1)]
    own = fill_slots(offsets_ref, notes, keeps, dests, coded, slots_ref)
    own = jnp.transpose(own.astype(jnp.float32)).astype(jnp.int32)
    pieces = [(both, 0, 0, 0), (beside, 0, 1, 0), (beside, span, 3, 0), (beyond, 0, 2, 0)]
    pieces += [(beyond, span, 2, 1), (y_own, 0, 0, 1), (y_beside, 0, 1, 1), (y_beside, span, 3, 1)]
    sort_tokens(pieces, tokens, span)
    bands = tuple(range(BANDS - 1))
    place_bands(slots_ref.at[0], tokens, top, bands, BANDS)
    copy = pltpu.make_async_copy(top, output_part(cache_ref, 0, top.shape[0], column), sem)
    copy.start()
    place_bands(slots_ref.at[1], tokens, top_sent, bands, BANDS)
    for flip in range(2):
        place_bands(slots_ref.at[flip], tokens, low_ref.at[flip], (BANDS - 1,), BANDS)
    for head in range(score_ref.shape[1]):
        lanes = slice(head * WIDTH, (head + 1) * WIDTH)
        chosen = own[:, head : head + 1]
        cached = picked(chosen, 1, tokens[:, lanes]).astype(jnp.bfloat16)
        rows = jnp.concatenate([cached, both[:span, lanes]], axis=0)
        attend_columns(q_ref, head, rows, chosen, out_ref, score_ref)
    copy.wait()


def far_index_kernel(offsets_ref, x_own, x_beside, d_own, d_beside, beyond, _, *rest):
    slots_ref, keeps, dests, coded = rest
    span = x_own.shape[0] - NOTES
    at = 2 * span
    notes = [(x_own, span, 0, 0, 0), (d_own, span, 0, 0, 1), (x_beside, at, 0, 1, 0)]
    notes += [(x_beside, at, 1, 3, 0), (d_beside, at, 0, 1, 1), (d_beside, at, 1, 3, 1)]
    notes += [(beyond, at + NOTES, 0, 2, 0), (beyond, at + NOTES, 1, 2, 1)]
    fill_slots(offsets_ref, notes, keeps, dests, coded, slots_ref)


def far_rows(flip, refs, far_ref, low, tokens, near_late, far_late):
    x_own, x_beside, x_end, d_own, d_beside, d_late, late, y_late, low_ref = refs[:9]
    near_slots, far_slots = refs[9:]
    span = late.shape[0]
    rows = far_slots.shape[1]
    band = rows // BANDS
    first = tokens.shape[0] + 1
    last = pl.ds(rows - band, band)
    sort_late([(late, 0), (y_late, 0)], near_late)
    sort_late([(x_end, 2 * span), (d_late, 0)], far_late)
    low[...] = low_ref[flip]
    add_late(near_slots.at[flip, last], first, near_late, low, 0)
    pieces = [(x_own, 0, 0, 0), (x_beside, 0, 1, 0), (x_beside, span, 3, 0), (x_end, 0, 2, 0)]
    pieces += [(x_end, span, 2, 1), (d_own, 0, 0, 1), (d_beside, 0, 1, 1), (d_beside, span, 3, 1)]
    sort_tokens(pieces, tokens, span)
    place_bands(far_slots.at[flip], tokens, far_ref, tuple(range(BANDS)), BANDS)
    add_late(far_slots.at[flip, last], first, far_late, far_ref, rows - band)


def far_sent_kernel(*refs):
    top_ref, sent_ref = refs[11:13]
    rows = refs[10].shape[1]
    upper = rows + top_ref.shape[0]
    sent_ref[rows:upper, :] = top_ref[...]
    far_rows(1, refs[:11], sent_ref.at[:rows], sent_ref.at[upper:], *refs[13:])


def far_kept_kernel(*refs):
    cache_ref, far, low, tokens, near_late, far_late, sems = refs[12:]
    column = lax.axis_index("kv")
    rows, band = far.shape[0], low.shape[0]
    far_rows(0, refs[:11], far, low, tokens, near_late, far_late)
    copies = [
        pltpu.make_async_copy(far, output_part(cache_ref, 0, rows, column ^ 2), sems.at[0]),
        pltpu.make_async_copy(
            low, output_part(cache_ref, rows - band, band, column), sems.at[1]
        ),
    ]
    for copy in copies:
        copy.start()
    for copy in copies:
        copy.wait()


def last_kernel(sent_ref, _, cache_ref, sems):
    column = lax.axis_index("kv")
    rows = cache_ref.shape[0]
    copies = [
        pltpu.make_async_copy(
            sent_ref.at[index * rows : (index + 1) * rows],
            output_part(cache_ref, 0, rows, column ^ place),
            sems.at[index],
        )
        for index, place in enumerate((3, 1))
    ]
    for copy in copies:
        copy.start()
    for copy in copies:
        copy.wait()


def send(value, axis, pairs):
    return lax.ppermute(value, axis, pairs)


def local_in_planes(query, kv_rows, keep, dest, offsets):
    prompts, span, qwidth = query.shape
    shards, columns = lax.axis_size("ctx"), lax.axis_size("kv")
    width = kv_rows.shape[2]
    heads = width // WIDTH
    cache = keep.shape[3]
    rows = 2 * prompts * cache // columns
    band = rows // BANDS
    vmem = pl.BlockSpec(memory_space=pltpu.VMEM)
    smem = pl.BlockSpec(memory_space=pltpu.SMEM)
    anywhere = pl.BlockSpec(memory_space=pl.ANY)
    hbm = pl.BlockSpec(memory_space=pltpu.HBM)
    params = pltpu.CompilerParams(vmem_limit_bytes=PLANE_BYTES)

    def cost(flops, moved):
        return pl.CostEstimate(flops=flops, bytes_accessed=moved, transcendentals=0)

    def piece(count):
        return jax.ShapeDtypeStruct((count, width), jnp.bfloat16)

    def along_z(value, turn):
        return send(value, "ctx", [(i, (i + 2 * turn) % shards) for i in range(shards)])

    def across_y(value):
        return send(value, "ctx", [(i, i ^ 1) for i in range(shards)])

    def across_x(value):
        return send(value, "kv", [(i, i ^ 2) for i in range(columns)])

    def across_both(value):
        pairs = [(i, i ^ columns ^ 2) for i in range(shards * columns)]
        return send(value, ("ctx", "kv"), pairs)

    def across_core(value):
        return send(value, "kv", [(i, i ^ 1) for i in range(columns)])

    owners_of = jnp.transpose(dest)
    both, single = pl.pallas_call(
        prepare_kernel,
        out_shape=(piece(2 * span + NOTES), piece(span + NOTES)),
        in_specs=[smem] + [hbm] * 3,
        out_specs=(hbm, hbm),
        scratch_shapes=[
            pltpu.VMEM(keep.shape, jnp.int32),
            pltpu.VMEM((1, prompts * cache), jnp.int32),
            pltpu.VMEM((NOTES, width), jnp.bfloat16),
            pltpu.SemaphoreType.DMA((7,)),
        ],
        compiler_params=pltpu.CompilerParams(vmem_limit_bytes=60 * 1024 * 1024),
        cost_estimate=cost(10**9, 1),
    )(offsets, kv_rows, keep, owners_of)

    below, above = along_z(both, 1), along_z(single, 3)
    y_own, x_own, d_own = across_y(both), across_x(single), across_both(single)
    going = pl.pallas_call(
        going_kernel,
        out_shape=piece(2 * span + 2 * NOTES),
        in_specs=[smem] + [vmem] * 6,
        out_specs=vmem,
        compiler_params=params,
        cost_estimate=cost(0, 10**6),
    )(offsets, kv_rows, keep, owners_of, y_own, x_own, d_own)
    beyond = along_z(going, 2)
    beside, relay = pl.pallas_call(
        beside_kernel,
        out_shape=(piece(2 * span + NOTES), piece(span)),
        in_specs=[smem] + [vmem] * 3 + [anywhere],
        out_specs=(vmem,) * 2,
        compiler_params=params,
        cost_estimate=cost(0, 10**6),
    )(offsets, below, above, kv_rows, going)
    relayed = send(relay, "ctx", [(0, 2), (1, 3), (6, 4), (7, 5)])
    y_beside, x_beside = across_y(beside), across_x(beside)
    d_beside = across_y(x_beside)

    attention_shape = jax.ShapeDtypeStruct((prompts, span, qwidth), jnp.bfloat16)
    score_shape = jax.ShapeDtypeStruct((prompts, heads, cache + span), jnp.float32)

    def prompt_specs(late):
        def block(_, offsets_ref):
            early = early_of(offsets_ref)
            return (1 - early if late else early, 0, 0)

        return (
            pl.BlockSpec((1, span, qwidth), block),
            pl.BlockSpec((1, heads, cache + span), block),
        )

    attention, row_scores, late_done = pl.pallas_call(
        late_kernel,
        grid_spec=pltpu.PrefetchScalarGridSpec(
            num_scalar_prefetch=1,
            grid=(1,),
            in_specs=[prompt_specs(True)[0], vmem, vmem],
            out_specs=prompt_specs(True) + (vmem,),
        ),
        out_shape=(attention_shape, score_shape, jax.ShapeDtypeStruct((8, LANES), jnp.float32)),
        compiler_params=params,
        cost_estimate=cost(10**6, 1),
    )(offsets, query, kv_rows, y_own)

    end, late = pl.pallas_call(
        join_second_kernel,
        out_shape=(piece(3 * span), piece(span)),
        in_specs=[vmem] * 3 + [anywhere] * 3,
        out_specs=(vmem, vmem),
        compiler_params=params,
        cost_estimate=cost(10**6, 1),
    )(beyond, relay, relayed, y_beside, x_beside, late_done)
    d_late, y_late, x_end = across_both(late), across_y(late), across_x(end)

    tokens = pltpu.VMEM((shards * span, width), jnp.bfloat16)
    late_tokens = pltpu.VMEM((2 * span, width), jnp.bfloat16)
    cache_shape = jax.ShapeDtypeStruct((rows, columns * width), jnp.bfloat16)
    slots_shape = jax.ShapeDtypeStruct((2, rows, heads), jnp.int32)
    done_shape = jax.ShapeDtypeStruct((8, LANES), jnp.float32)
    tables = [
        pltpu.VMEM((shards, 4 * heads, cache), jnp.int32),
        pltpu.VMEM((shards, prompts, cache), jnp.int32),
        pltpu.VMEM((shards, 8 * heads, cache), jnp.bfloat16),
    ]
    attention, row_scores, early_done, owner_cache, top, low, near_slots = pl.pallas_call(
        early_kernel,
        grid_spec=pltpu.PrefetchScalarGridSpec(
            num_scalar_prefetch=1,
            grid=(1,),
            in_specs=[prompt_specs(False)[0]] + [vmem] * 5 + [anywhere] * 3,
            out_specs=prompt_specs(False) + (vmem, hbm, vmem, vmem, vmem),
            scratch_shapes=[
                tokens,
                pltpu.VMEM((rows - band, width), jnp.bfloat16),
                pltpu.SemaphoreType.DMA,
            ]
            + tables,
        ),
        out_shape=(
            attention_shape,
            score_shape,
            done_shape,
            cache_shape,
            piece(rows - band),
            jax.ShapeDtypeStruct((2, band, width), jnp.bfloat16),
            slots_shape,
        ),
        input_output_aliases={8: 0, 9: 1},
        compiler_params=params,
        cost_estimate=cost(10**10, 10**7),
    )(offsets, query, going, beside, beyond, y_own, y_beside, late, attention, row_scores)
    far_slots = pl.pallas_call(
        far_index_kernel,
        out_shape=slots_shape,
        in_specs=[smem] + [vmem] * 5 + [anywhere],
        out_specs=vmem,
        scratch_shapes=tables,
        compiler_params=params,
        cost_estimate=cost(10**6, 1),
    )(offsets, x_own, x_beside, d_own, d_beside, beyond, early_done)
    far = (x_own, x_beside, x_end, d_own, d_beside, d_late, late, y_late, low)
    far += (near_slots, far_slots)
    sent = pl.pallas_call(
        far_sent_kernel,
        out_shape=piece(2 * rows),
        in_specs=[vmem] * 12,
        out_specs=vmem,
        scratch_shapes=[tokens, late_tokens, late_tokens],
        compiler_params=params,
        cost_estimate=cost(2 * 10**9, 4 * 10**6),
    )(*far, top)
    received = across_core(sent)
    owner_cache = pl.pallas_call(
        far_kept_kernel,
        out_shape=cache_shape,
        in_specs=[vmem] * 11 + [hbm],
        out_specs=hbm,
        scratch_shapes=[
            pltpu.VMEM((rows, width), jnp.bfloat16),
            pltpu.VMEM((band, width), jnp.bfloat16),
            tokens,
            late_tokens,
            late_tokens,
            pltpu.SemaphoreType.DMA((2,)),
        ],
        input_output_aliases={11: 0},
        compiler_params=params,
        cost_estimate=cost(2 * 10**9, 4 * 10**6),
    )(*far, owner_cache)
    owner_cache = pl.pallas_call(
        last_kernel,
        out_shape=cache_shape,
        in_specs=[anywhere, hbm],
        out_specs=hbm,
        scratch_shapes=[pltpu.SemaphoreType.DMA((2,))],
        input_output_aliases={1: 0},
        compiler_params=params,
        cost_estimate=cost(0, 10**6),
    )(received, owner_cache)
    return (attention, row_scores, owner_cache)


def solution(mesh):
    placed = (
        P(None, "ctx", "kv"),
        P(None, "ctx", "kv"),
        P(None, "ctx", "kv", None),
        P("ctx", None),
        P(),
    )
    in_planes = mesh.shape["ctx"] == 8 and mesh.shape["kv"] == 4
    return jax.shard_map(
        local_in_planes if in_planes else local,
        mesh=mesh,
        in_specs=placed,
        out_specs=(P(None, "ctx", "kv"), P(None, "kv", "ctx"), P(("ctx", "kv"), None)),
        check_vma=False,
    )
```

```python
import functools
import math

import jax
import jax.numpy as jnp
from jax import lax
from jax.experimental import pallas as pl
from jax.experimental.pallas import tpu as pltpu
from jax.sharding import PartitionSpec as P

HEAD = 128
WIDTH = 2 * HEAD
LANES = 128
VMEM_BYTES = 56 * 1024 * 1024
PLANE_BYTES = 28 * 1024 * 1024
NOTES = 16
BANDS = 4


def look_up(state, keep, fresh):
    tiles = state.shape[1] // LANES
    parts = []
    for tile in range(tiles):
        wanted = keep[:, tile * LANES : (tile + 1) * LANES]
        high = wanted >> 7
        low = wanted & 127
        found = jnp.where(high >= tiles, fresh + wanted - state.shape[1], 0)
        for source in range(tiles):
            held = state[:, source * LANES : (source + 1) * LANES]
            moved = jnp.take_along_axis(held, low, axis=1, mode="promise_in_bounds")
            found = jnp.where(high == source, moved, found)
        parts.append(found)
    return jnp.concatenate(parts, axis=1)


def split(state):
    both = jnp.concatenate([state >> 7, state & 127], axis=0)
    return both.astype(jnp.float32).astype(jnp.bfloat16)


def index_kernel(
    where_ref, keep_early_ref, keep_late_ref, dest_ref, slot_ref, row_ref, column_ref, coded
):
    shards, heads, cache = keep_early_ref.shape
    cap = slot_ref.shape[0] // shards
    span = LANES
    early, mine, me = where_ref[0], where_ref[1], where_ref[2]
    empty = jnp.minimum(keep_early_ref[0], 0)

    def follow(shard, carry):
        state, own = carry
        own = jnp.where(shard == mine, state, own)
        state = look_up(state, keep_early_ref[shard], shard * span + 1)
        coded[shard] = split(state)
        return state, own

    _, own_early = lax.fori_loop(0, shards, follow, (empty, empty), unroll=shards <= 8)
    base = shards * span + 1
    late_first = look_up(empty, keep_late_ref[0], base)
    late_second = look_up(late_first, keep_late_ref[1], base + span)
    own_late = jnp.where(mine == shards - 1, late_first, 0)
    for index, own in enumerate((own_early, own_late)):
        row_ref[index] = own
        column_ref[index] = jnp.transpose(own.astype(jnp.float32)).astype(jnp.int32)

    named = (dest_ref[...] == me).astype(jnp.float32)
    chunks = named.shape[1] // LANES
    upper = (
        lax.broadcasted_iota(jnp.int32, (LANES, LANES), 0)
        <= lax.broadcasted_iota(jnp.int32, (LANES, LANES), 1)
    ).astype(jnp.float32).astype(jnp.bfloat16)
    total = jnp.zeros((shards, 1), jnp.float32)
    ranks = []
    for chunk in range(chunks):
        part = named[:, chunk * LANES : (chunk + 1) * LANES]
        upto = jnp.dot(part.astype(jnp.bfloat16), upper, preferred_element_type=jnp.float32)
        ranks.append(jnp.where(part > 0, upto + total, 0.0))
        total = total + upto[:, LANES - 1 :]
    low_half = jnp.concatenate(ranks[: chunks // 2], axis=1)
    high_half = jnp.concatenate(ranks[chunks // 2 :], axis=1)
    rank_early = jnp.where(early == 0, low_half, high_half)
    rank_late = jnp.where(early == 0, high_half, low_half)
    place = lax.broadcasted_iota(jnp.int32, (cap, cache), 0).astype(jnp.float32) + 1.0
    contract = (((1,), (1,)), ((), ()))
    for shard in range(shards):
        pick = (rank_early[shard : shard + 1] == place).astype(jnp.float32).astype(jnp.bfloat16)
        found = lax.dot_general(pick, coded[shard], contract, preferred_element_type=jnp.float32)
        if shard >= shards - 2:
            state = late_first if shard == shards - 2 else late_second
            pick = (rank_late[shard : shard + 1] == place).astype(jnp.float32).astype(jnp.bfloat16)
            found += lax.dot_general(
                pick, split(state), contract, preferred_element_type=jnp.float32
            )
        tokens = found[:, :heads] * 128.0 + found[:, heads:]
        slot_ref[shard * cap : (shard + 1) * cap, :] = tokens.astype(jnp.int32)


def column_of(table, head):
    lane = lax.broadcasted_iota(jnp.int32, table.shape, 1)
    return jnp.sum(
        jnp.where(lane == head, table, 0).astype(jnp.float32), axis=1, keepdims=True
    ).astype(jnp.int32)


def picked(column, first, tokens):
    number = lax.broadcasted_iota(jnp.int32, (column.shape[0], tokens.shape[0]), 1) + first
    table = (column == number).astype(jnp.float32).astype(jnp.bfloat16)
    return jnp.dot(table, tokens, preferred_element_type=jnp.float32)


def attend(q_ref, prompt, keys, values, seen, out_ref, score_ref, head):
    span = q_ref.shape[1]
    cache = seen.shape[1]
    group = q_ref.shape[2] // HEAD
    causal = lax.broadcasted_iota(jnp.int32, (span, span), 1) <= lax.broadcasted_iota(
        jnp.int32, (span, span), 0
    )
    bias = jnp.concatenate(
        [
            jnp.broadcast_to(jnp.where(seen > 0, 0.0, -1e30), (span, cache)),
            jnp.where(causal, 0.0, -1e30),
        ],
        axis=1,
    )
    scale = math.log2(math.e) / math.sqrt(HEAD)
    mass = jnp.zeros((1, cache + span), jnp.float32)
    for member in range(group):
        query = q_ref[prompt, :, member * HEAD : (member + 1) * HEAD]
        scores = lax.dot_general(
            query, keys, (((1,), (1,)), ((), ())), preferred_element_type=jnp.float32
        )
        scores = scores + bias
        peak = jnp.max(scores, axis=1, keepdims=True)
        expo = jnp.exp2((scores - peak) * scale)
        weights = expo * (1.0 / jnp.sum(expo, axis=1, keepdims=True))
        mass = mass + jnp.sum(weights, axis=0, keepdims=True)
        mixed = jnp.dot(weights.astype(jnp.bfloat16), values, preferred_element_type=jnp.float32)
        out_ref[prompt, :, member * HEAD : (member + 1) * HEAD] = mixed.astype(jnp.bfloat16)
    score_ref[prompt, pl.ds(head, 1), :] = mass


def attention_kernel(
    where_ref, q_ref, span_ref, early_ref, late_ref, row_ref, column_ref, out_ref, score_ref
):
    early, mine, column, shards = where_ref[0], where_ref[1], where_ref[3], early_ref.shape[0]
    span = q_ref.shape[1]
    late = 1 - early
    local_head = pl.program_id(0)
    head = column * pl.num_programs(0) + local_head

    def run(which, prompt, tokens, first):
        chosen = column_of(column_ref[which], head)
        cached = picked(chosen, first, tokens).astype(jnp.bfloat16)
        rows = jnp.concatenate([cached, span_ref[prompt]], axis=0)
        seen = row_ref[which, pl.ds(head, 1), :]
        attend(
            q_ref, prompt, rows[:, :HEAD], rows[:, HEAD:], seen, out_ref, score_ref, local_head
        )

    run(0, early, early_ref[:, 0].reshape(shards * span, WIDTH), 1)

    @pl.when(mine >= shards - 2)
    def _():
        run(1, late, late_ref[0, 0], shards * span + 1)

    @pl.when(mine < shards - 2)
    def _():
        out_ref[late] = jnp.zeros(out_ref.shape[1:], out_ref.dtype)
        score_ref[late, pl.ds(local_head, 1), :] = jnp.zeros((1, score_ref.shape[2]), jnp.float32)


def owner_kernel(slot_ref, early_ref, late_ref, out_ref):
    shards, _, span, width = early_ref.shape
    rows = out_ref.shape[0]
    chosen = column_of(slot_ref[...], pl.program_id(0))
    bands = 4
    band = rows // bands
    reach = shards * span // bands
    tokens = early_ref[:, 0].reshape(shards * span, width)
    for index in range(bands):
        part = chosen[index * band : (index + 1) * band]
        found = picked(part, 1, tokens[: (index + 1) * reach])
        if index == bands - 1:
            found += picked(part, shards * span + 1, late_ref[:, 0].reshape(2 * span, width))
        out_ref[index * band : (index + 1) * band, :] = found.astype(jnp.bfloat16)


def local(query, kv_rows, keep, dest, offsets):
    prompts, span, qwidth = query.shape
    shards, columns = lax.axis_size("ctx"), lax.axis_size("kv")
    width = kv_rows.shape[2]
    heads_dev = width // WIDTH
    heads = heads_dev * columns
    cache = keep.shape[3]
    owners = shards * columns
    cap = 2 * prompts * cache // owners
    mine, column = lax.axis_index("ctx"), lax.axis_index("kv")
    early = jnp.where(offsets[0] < offsets[1], 0, 1).astype(jnp.int32)
    facts = jnp.stack([early, mine, mine * columns + column, column]).astype(jnp.int32)

    swap = early == 1
    ordered_kv = jnp.where(swap, kv_rows[::-1], kv_rows)
    ordered_keep = jnp.where(swap, keep[::-1, 0], keep[:, 0])
    digits = jnp.stack([ordered_keep >> 7, ordered_keep & 127], axis=1)
    share = dest.shape[0] // columns
    own_dest = lax.dynamic_slice_in_dim(dest[:, 0], column * share, share)
    facts_rows = jnp.concatenate([digits.reshape(-1), own_dest]).astype(jnp.bfloat16)
    used = facts_rows.shape[0]
    room = 16 * width
    facts_rows = jnp.concatenate([facts_rows, jnp.zeros((room - used,), jnp.bfloat16)])
    payload = jnp.concatenate(
        [ordered_kv.reshape(prompts * span, width), facts_rows.reshape(16, width)], axis=0
    )
    whole = lax.all_gather(payload, ("ctx", "kv")).reshape(
        shards, columns, prompts * span + 16, width
    )

    told = whole[:, :, prompts * span :, :].reshape(shards, columns, room).astype(jnp.int32)
    kept = told[:, :, : prompts * 2 * heads_dev * cache].reshape(
        shards, columns, prompts, 2, heads_dev, cache
    )
    kept = kept[:, :, :, 0] * 128 + kept[:, :, :, 1]
    kept = jnp.transpose(kept, (2, 0, 1, 3, 4)).reshape(prompts, shards, heads, cache)
    whole_dest = told[:, :, used - share : used].reshape(shards, columns * share)

    vmem = pl.BlockSpec(memory_space=pltpu.VMEM)
    smem = pl.BlockSpec(memory_space=pltpu.SMEM)
    params = pltpu.CompilerParams(vmem_limit_bytes=VMEM_BYTES)
    slots, rows, cols = pl.pallas_call(
        index_kernel,
        out_shape=(
            jax.ShapeDtypeStruct((shards * cap, heads), jnp.int32),
            jax.ShapeDtypeStruct((2, heads, cache), jnp.int32),
            jax.ShapeDtypeStruct((2, cache, heads), jnp.int32),
        ),
        in_specs=[smem, vmem, vmem, vmem],
        out_specs=(vmem, vmem, vmem),
        scratch_shapes=[pltpu.VMEM((shards, 2 * heads, cache), jnp.bfloat16)],
        compiler_params=params,
    )(facts, kept[0], kept[1, shards - 2 :], whole_dest)

    group_width = qwidth // heads_dev
    attention, row_scores = pl.pallas_call(
        attention_kernel,
        grid_spec=pltpu.PrefetchScalarGridSpec(
            num_scalar_prefetch=1,
            grid=(heads_dev,),
            in_specs=[
                pl.BlockSpec((prompts, span, group_width), lambda h, w: (0, 0, h)),
                pl.BlockSpec((prompts, span, WIDTH), lambda h, w: (0, 0, h)),
                pl.BlockSpec((shards, 1, span, WIDTH), lambda h, w: (0, w[3], 0, h)),
                pl.BlockSpec((1, 1, span, WIDTH), lambda h, w: (shards - 2, w[3], 1, h)),
                pl.BlockSpec((2, heads, cache), lambda h, w: (0, 0, 0)),
                pl.BlockSpec((2, cache, heads), lambda h, w: (0, 0, 0)),
            ],
            out_specs=(
                pl.BlockSpec((prompts, span, group_width), lambda h, w: (0, 0, h)),
                pl.BlockSpec((prompts, heads_dev, cache + span), lambda h, w: (0, 0, 0)),
            ),
        ),
        out_shape=(
            jax.ShapeDtypeStruct((prompts, span, qwidth), jnp.bfloat16),
            jax.ShapeDtypeStruct((prompts, heads_dev, cache + span), jnp.float32),
        ),
        compiler_params=params,
    )(facts, query, kv_rows, whole, whole, rows, cols)

    owner_cache = pl.pallas_call(
        owner_kernel,
        grid=(heads,),
        in_specs=[
            pl.BlockSpec((shards * cap, heads), lambda g: (0, 0)),
            pl.BlockSpec(
                (shards, 1, span, WIDTH), lambda g: (0, g // heads_dev, 0, g % heads_dev)
            ),
            pl.BlockSpec(
                (2, 1, span, WIDTH),
                lambda g: (shards // 2 - 1, g // heads_dev, 1, g % heads_dev),
            ),
        ],
        out_specs=pl.BlockSpec((shards * cap, WIDTH), lambda g: (0, g)),
        out_shape=jax.ShapeDtypeStruct((shards * cap, heads * WIDTH), jnp.bfloat16),
        compiler_params=params,
    )(slots, whole, whole)
    return (attention, row_scores, owner_cache)


def dot(a, b, dims=((1,), (0,))):
    return lax.dot_general(a, b, (dims, ((), ())), preferred_element_type=jnp.float32)


def marks(table):
    return table.astype(jnp.float32).astype(jnp.bfloat16)


def early_of(offsets_ref):
    return jnp.where(offsets_ref[0] < offsets_ref[1], 0, 1)


def prepare_kernel(
    offsets_ref, kv_ref, keep_ref, dest_ref, both_ref, single_ref, keep, dest, sems
):
    span = kv_ref.shape[1]
    heads, cache = keep_ref.shape[2], keep_ref.shape[3]
    early = early_of(offsets_ref)
    copies = [
        (keep_ref, keep),
        (dest_ref, dest),
        (kv_ref.at[early], single_ref.at[:span]),
        (kv_ref.at[early], both_ref.at[:span]),
        (kv_ref.at[1 - early], both_ref.at[span : 2 * span]),
    ]
    copies = [
        pltpu.make_async_copy(source, target, sems.at[index])
        for index, (source, target) in enumerate(copies)
    ]
    for copy in copies:
        copy.start()
    for copy in copies[:2]:
        copy.wait()
    lane = lax.broadcasted_iota(jnp.int32, (heads, cache), 1)
    rows = [
        keep[early, 0] - lane,
        dest[:, :cache],
        dest[:, cache:],
        keep[1 - early, 0] - lane,
        jnp.zeros((NOTES - 2 * heads - 2, cache), jnp.int32),
    ]
    rows = jnp.concatenate([row.astype(jnp.float32) for row in rows], axis=0)
    rows = rows.astype(jnp.bfloat16)
    single_ref[span:, :] = rows
    both_ref[2 * span :, :] = rows
    for copy in copies[2:]:
        copy.wait()


def two_notes(first, first_row, second, second_row):
    half = NOTES // 2
    return jnp.concatenate(
        [
            first[first_row : first_row + NOTES, :].astype(jnp.float32)[:half],
            second[second_row : second_row + NOTES, :].astype(jnp.float32)[:half],
        ],
        axis=0,
    ).astype(jnp.bfloat16)


def going_kernel(both, y_own, x_own, d_own, going_ref):
    span = both.shape[0] // 2 - NOTES // 2
    going_ref[:span, :] = both[:span, :]
    going_ref[span : 2 * span, :] = y_own[:span, :]
    going_ref[2 * span : 2 * span + NOTES, :] = two_notes(both, 2 * span, y_own, 2 * span)
    going_ref[2 * span + NOTES :, :] = two_notes(x_own, span, d_own, span)


def beside_kernel(below, above, both, _, beside_ref, relay_ref):
    span = relay_ref.shape[0]
    beside_ref[:span, :] = below[:span, :]
    beside_ref[span : 2 * span, :] = above[:span, :]
    beside_ref[2 * span :, :] = two_notes(below, 2 * span, above, span)
    level = lax.axis_index("ctx") // 2

    @pl.when(level == 0)
    def _():
        relay_ref[...] = below[span : 2 * span, :]

    @pl.when(level > 0)
    def _():
        relay_ref[...] = both[span : 2 * span, :]


def pick_late_kernel(relay, relayed, _, out_ref):
    level = lax.axis_index("ctx") // 2
    for ref, chosen in ((relay, (level == 0) | (level == 3)), (relayed, (level == 1) | (level == 2))):

        @pl.when(chosen)
        def _(ref=ref):
            out_ref[...] = ref[...]


def end_kernel(beyond, late, *rest):
    out_ref = rest[-1]
    span = late.shape[0]
    out_ref[: 2 * span, :] = beyond[: 2 * span, :]
    out_ref[2 * span :, :] = late[...]


def place_of(turn, flip, shards):
    mine = lax.axis_index("ctx")
    place = lax.rem(mine - 2 * turn + shards, shards)
    return place + 1 - 2 * lax.rem(mine, 2) if flip else place


def sort_tokens(pieces, tokens, span):
    shards = tokens.shape[0] // span
    for ref, base, turn, flip in pieces:
        place = place_of(turn, flip, shards)
        tokens[pl.ds(pl.multiple_of(place * span, span), span), :] = ref[base : base + span, :]


def sort_late(pieces, late_tokens):
    span = late_tokens.shape[0] // 2
    side = lax.rem(lax.axis_index("ctx"), 2)
    for flip, ref_base in enumerate(pieces):
        ref, base = ref_base
        place = side + flip - 2 * side * flip
        late_tokens[pl.ds(pl.multiple_of(place * span, span), span), :] = ref[
            base : base + span, :
        ]


def read_notes(ref, base, part, heads):
    half = NOTES // 2
    rows = ref[base : base + NOTES, :].astype(jnp.float32).astype(jnp.int32)
    rows = rows[part * half : (part + 1) * half]
    lane = lax.broadcasted_iota(jnp.int32, (heads, rows.shape[1]), 1)
    return rows[:heads] + lane, rows[heads + 2 : 2 * heads + 2] + lane, rows[heads : heads + 2]


def sort_notes(notes, keeps, dests):
    shards, heads = keeps.shape[0], keeps.shape[1] // 4
    for ref, base, part, turn, flip in notes:
        place = place_of(turn, flip, shards)
        early, late, dest = read_notes(ref, base, part, heads)
        keeps[place, :heads, :] = early
        keeps[place, heads : 2 * heads, :] = late
        dests[place, :, :] = dest


def follow_lists(keeps, coded, span):
    shards, rows, cache = keeps.shape
    heads = rows // 4
    row = lax.broadcasted_iota(jnp.int32, (rows, cache), 0)
    is_early = row < heads
    state = jnp.where(row < 0, keeps[0], 0)
    own = state
    mine = lax.axis_index("ctx")
    for shard in range(shards):
        own = jnp.where(mine == shard, state, own)
        late_first = (shards + shard - (shards - 2)) * span + 1
        fresh = jnp.where(is_early[:, :LANES], shard * span + 1, late_first)
        state = look_up(state, keeps[shard], fresh)
        if shard < shards - 2:
            state = jnp.where(is_early, state, 0)
        coded[shard] = split(state)
    return own


def find_slots(early, dests, coded, owner, slots):
    shards, halves, cache = dests.shape
    heads = coded.shape[1] // 8
    cap = slots.shape[0] // shards
    upper = marks(
        lax.broadcasted_iota(jnp.int32, (LANES, LANES), 0)
        <= lax.broadcasted_iota(jnp.int32, (LANES, LANES), 1)
    )
    place = lax.broadcasted_iota(jnp.int32, (cap, cache), 0).astype(jnp.float32) + 1.0
    total = jnp.zeros((shards, 1), jnp.float32)
    ranks = []
    for half in range(halves):
        named = (dests[:, half, :] == owner).astype(jnp.float32)
        parts = []
        for chunk in range(cache // LANES):
            part = named[:, chunk * LANES : (chunk + 1) * LANES]
            upto = dot(part.astype(jnp.bfloat16), upper)
            parts.append(jnp.where(part > 0, upto + total, 0.0))
            total = total + upto[:, LANES - 1 :]
        ranks.append(jnp.concatenate(parts, axis=1))
    rank_early = jnp.where(early == 0, ranks[0], ranks[1])
    rank_late = jnp.where(early == 0, ranks[1], ranks[0])
    across = ((1,), (1,))
    for shard in range(shards):
        found = dot(marks(rank_early[shard : shard + 1] == place), coded[shard], across)
        tokens = found[:, :heads] * 128.0 + found[:, 4 * heads : 5 * heads]
        if shard >= shards - 2:
            found = dot(marks(rank_late[shard : shard + 1] == place), coded[shard], across)
            tokens += found[:, heads : 2 * heads] * 128.0 + found[:, 5 * heads : 6 * heads]
        slots[shard * cap : (shard + 1) * cap, :] = tokens.astype(jnp.int32)


def place_bands(slots, tokens, out_ref, bands, total_bands):
    rows, heads = slots.shape
    reach = tokens.shape[0]
    band = rows // total_bands
    for head in range(heads):
        lanes = slice(head * WIDTH, (head + 1) * WIDTH)
        for order, index in enumerate(bands):
            part = slots[index * band : (index + 1) * band, head : head + 1]
            found = picked(part, 1, tokens[: (index + 1) * reach // total_bands, lanes])
            out_ref[order * band : (order + 1) * band, lanes] = found.astype(jnp.bfloat16)


def add_late(slots, first, late_tokens, out_ref, base):
    band, heads = slots.shape
    for head in range(heads):
        lanes = slice(head * WIDTH, (head + 1) * WIDTH)
        found = picked(slots[:, head : head + 1], first, late_tokens[:, lanes])
        out_ref[base : base + band, lanes] += found.astype(jnp.bfloat16)


def attend_columns(q_ref, head, rows, seen, out_ref, score_ref):
    span = q_ref.shape[1]
    total = rows.shape[0]
    cache = total - span
    group = q_ref.shape[2] // (score_ref.shape[1] * HEAD)
    keys, values = rows[:, :HEAD], rows[:, HEAD:]
    flat = jnp.transpose(values.astype(jnp.float32)).astype(jnp.bfloat16)
    lane = lax.broadcasted_iota(jnp.int32, (total, HEAD), 1)
    hidden = jnp.where(seen > 0, 0.0, -1e30)
    hidden = jnp.concatenate([hidden, jnp.zeros((span, 1), jnp.float32)], axis=0)
    hidden = jnp.where(lane == 0, hidden, 0.0).astype(jnp.bfloat16)
    keys = jnp.concatenate([keys, hidden], axis=1)
    ones = jnp.ones((2 * span, HEAD), jnp.bfloat16)
    causal = lax.broadcasted_iota(jnp.int32, (span, 2 * span), 0) <= lax.rem(
        lax.broadcasted_iota(jnp.int32, (span, 2 * span), 1), span
    )
    bias = jnp.where(causal, 0.0, -1e30)
    scale = math.log2(math.e) / math.sqrt(HEAD)
    mass = None
    for pair in range(group // 2):
        first = (head * group + 2 * pair) * HEAD
        query = jnp.concatenate(
            [
                q_ref[0, :, first : first + HEAD],
                q_ref[0, :, first + HEAD : first + 2 * HEAD],
            ],
            axis=0,
        )
        scores = dot(keys, jnp.concatenate([query, ones], axis=1), ((1,), (1,)))
        near = scores[cache:] + bias
        scores = jnp.concatenate([scores[:cache], near], axis=0) * scale
        peak = jnp.max(scores, axis=0, keepdims=True)
        expo = jnp.exp2(scores - peak)
        weights = expo * (1.0 / jnp.sum(expo, axis=0, keepdims=True))
        both = weights[:, :span] + weights[:, span:]
        mass = both if mass is None else mass + both
        mixed = jnp.transpose(dot(flat, weights.astype(jnp.bfloat16)))
        for member in range(2):
            lanes = slice(first + member * HEAD, first + (member + 1) * HEAD)
            out_ref[0, :, lanes] = mixed[member * span : (member + 1) * span].astype(
                jnp.bfloat16
            )
    score_ref[0, head : head + 1, :] = jnp.sum(jnp.transpose(mass), axis=0, keepdims=True)


def late_kernel(offsets_ref, q_ref, both_ref, beside_ref, out_ref, score_ref, done_ref):
    mine, shards = lax.axis_index("ctx"), lax.axis_size("ctx")
    heads, cache = score_ref.shape[1], score_ref.shape[2] - q_ref.shape[1]
    span = q_ref.shape[1]
    done_ref[...] = jnp.zeros(done_ref.shape, jnp.float32)

    @pl.when(mine >= shards - 2)
    def _():
        _, keep, _ = read_notes(beside_ref, 2 * span, 0, heads)
        state = jnp.where(keep >= cache, keep - cache + 1, 0)
        state = jnp.where(mine == shards - 1, state, 0).astype(jnp.float32)
        state = jnp.concatenate([state, jnp.zeros((8 - heads, cache), jnp.float32)], axis=0)
        columns = jnp.transpose(state).astype(jnp.int32)
        for head in range(heads):
            lanes = slice(head * WIDTH, (head + 1) * WIDTH)
            column = columns[:, head : head + 1]
            cached = picked(column, 1, beside_ref[span : 2 * span, lanes])
            rows = jnp.concatenate(
                [cached.astype(jnp.bfloat16), both_ref[span : 2 * span, lanes]], axis=0
            )
            attend_columns(q_ref, head, rows, column, out_ref, score_ref)

    @pl.when(mine < shards - 2)
    def _():
        out_ref[...] = jnp.zeros(out_ref.shape, out_ref.dtype)
        score_ref[...] = jnp.zeros(score_ref.shape, jnp.float32)


def output_part(cache_ref, row, rows, column):
    width = cache_ref.shape[1] // lax.axis_size("kv")
    return cache_ref.at[
        pl.ds(row, rows), pl.ds(pl.multiple_of(column * width, width), width)
    ]


def fill_slots(offsets_ref, notes, keeps, dests, coded, slots_ref):
    me = lax.axis_index("ctx") * lax.axis_size("kv") + lax.axis_index("kv")
    sort_notes(notes, keeps, dests)
    own = follow_lists(keeps, coded, LANES)
    for flip in range(2):
        find_slots(early_of(offsets_ref), dests, coded, me ^ flip, slots_ref.at[flip])
    return own


def early_kernel(offsets_ref, q_ref, *rest):
    both, beside, beyond, y_own, y_beside = rest[:5]
    out_ref, score_ref, done_ref, cache_ref, top_sent, low_ref, slots_ref = rest[8:15]
    tokens, top, sem, keeps, dests, coded = rest[15:]
    done_ref[...] = jnp.zeros(done_ref.shape, jnp.float32)
    span = both.shape[0] // 2 - NOTES // 2
    column = lax.axis_index("kv")
    at = 2 * span
    notes = [(both, at, 0, 0, 0), (beside, at, 0, 1, 0), (beside, at, 1, 3, 0)]
    notes += [(beyond, at, 0, 2, 0), (beyond, at, 1, 2, 1), (y_own, at, 0, 0, 1)]
    notes += [(y_beside, at, 0, 1, 1), (y_beside, at, 1, 3, 1)]
    own = fill_slots(offsets_ref, notes, keeps, dests, coded, slots_ref)
    own = jnp.transpose(own.astype(jnp.float32)).astype(jnp.int32)
    pieces = [(both, 0, 0, 0), (beside, 0, 1, 0), (beside, span, 3, 0), (beyond, 0, 2, 0)]
    pieces += [(beyond, span, 2, 1), (y_own, 0, 0, 1), (y_beside, 0, 1, 1), (y_beside, span, 3, 1)]
    sort_tokens(pieces, tokens, span)
    bands = tuple(range(BANDS - 1))
    place_bands(slots_ref.at[0], tokens, top, bands, BANDS)
    copy = pltpu.make_async_copy(top, output_part(cache_ref, 0, top.shape[0], column), sem)
    copy.start()
    place_bands(slots_ref.at[1], tokens, top_sent, bands, BANDS)
    for flip in range(2):
        place_bands(slots_ref.at[flip], tokens, low_ref.at[flip], (BANDS - 1,), BANDS)
    for head in range(score_ref.shape[1]):
        lanes = slice(head * WIDTH, (head + 1) * WIDTH)
        chosen = own[:, head : head + 1]
        cached = picked(chosen, 1, tokens[:, lanes]).astype(jnp.bfloat16)
        rows = jnp.concatenate([cached, both[:span, lanes]], axis=0)
        attend_columns(q_ref, head, rows, chosen, out_ref, score_ref)
    copy.wait()


def far_index_kernel(offsets_ref, x_own, x_beside, d_own, d_beside, beyond, _, *rest):
    slots_ref, keeps, dests, coded = rest
    span = x_own.shape[0] - NOTES
    at = 2 * span
    notes = [(x_own, span, 0, 0, 0), (d_own, span, 0, 0, 1), (x_beside, at, 0, 1, 0)]
    notes += [(x_beside, at, 1, 3, 0), (d_beside, at, 0, 1, 1), (d_beside, at, 1, 3, 1)]
    notes += [(beyond, at + NOTES, 0, 2, 0), (beyond, at + NOTES, 1, 2, 1)]
    fill_slots(offsets_ref, notes, keeps, dests, coded, slots_ref)


def far_rows(flip, refs, far_ref, low, tokens, near_late, far_late):
    x_own, x_beside, x_end, d_own, d_beside, d_late, late, y_late, low_ref = refs[:9]
    near_slots, far_slots = refs[9:]
    span = late.shape[0]
    rows = far_slots.shape[1]
    band = rows // BANDS
    first = tokens.shape[0] + 1
    last = pl.ds(rows - band, band)
    sort_late([(late, 0), (y_late, 0)], near_late)
    sort_late([(x_end, 2 * span), (d_late, 0)], far_late)
    low[...] = low_ref[flip]
    add_late(near_slots.at[flip, last], first, near_late, low, 0)
    pieces = [(x_own, 0, 0, 0), (x_beside, 0, 1, 0), (x_beside, span, 3, 0), (x_end, 0, 2, 0)]
    pieces += [(x_end, span, 2, 1), (d_own, 0, 0, 1), (d_beside, 0, 1, 1), (d_beside, span, 3, 1)]
    sort_tokens(pieces, tokens, span)
    place_bands(far_slots.at[flip], tokens, far_ref, tuple(range(BANDS)), BANDS)
    add_late(far_slots.at[flip, last], first, far_late, far_ref, rows - band)


def far_sent_kernel(*refs):
    top_ref, sent_ref = refs[11:13]
    rows = refs[10].shape[1]
    upper = rows + top_ref.shape[0]
    sent_ref[rows:upper, :] = top_ref[...]
    far_rows(1, refs[:11], sent_ref.at[:rows], sent_ref.at[upper:], *refs[13:])


def far_kept_kernel(*refs):
    cache_ref, far, low, tokens, near_late, far_late, sems = refs[12:]
    column = lax.axis_index("kv")
    rows, band = far.shape[0], low.shape[0]
    far_rows(0, refs[:11], far, low, tokens, near_late, far_late)
    copies = [
        pltpu.make_async_copy(far, output_part(cache_ref, 0, rows, column ^ 2), sems.at[0]),
        pltpu.make_async_copy(
            low, output_part(cache_ref, rows - band, band, column), sems.at[1]
        ),
    ]
    for copy in copies:
        copy.start()
    for copy in copies:
        copy.wait()


def last_kernel(sent_ref, _, cache_ref, sems):
    column = lax.axis_index("kv")
    rows = cache_ref.shape[0]
    copies = [
        pltpu.make_async_copy(
            sent_ref.at[index * rows : (index + 1) * rows],
            output_part(cache_ref, 0, rows, column ^ place),
            sems.at[index],
        )
        for index, place in enumerate((3, 1))
    ]
    for copy in copies:
        copy.start()
    for copy in copies:
        copy.wait()


def send(value, axis, pairs):
    return lax.ppermute(value, axis, pairs)


def local_in_planes(query, kv_rows, keep, dest, offsets):
    prompts, span, qwidth = query.shape
    shards, columns = lax.axis_size("ctx"), lax.axis_size("kv")
    width = kv_rows.shape[2]
    heads = width // WIDTH
    cache = keep.shape[3]
    rows = 2 * prompts * cache // columns
    band = rows // BANDS
    vmem = pl.BlockSpec(memory_space=pltpu.VMEM)
    smem = pl.BlockSpec(memory_space=pltpu.SMEM)
    anywhere = pl.BlockSpec(memory_space=pl.ANY)
    hbm = pl.BlockSpec(memory_space=pltpu.HBM)
    params = pltpu.CompilerParams(vmem_limit_bytes=PLANE_BYTES)

    def cost(flops, moved):
        return pl.CostEstimate(flops=flops, bytes_accessed=moved, transcendentals=0)

    def piece(count):
        return jax.ShapeDtypeStruct((count, width), jnp.bfloat16)

    def along_z(value, turn):
        return send(value, "ctx", [(i, (i + 2 * turn) % shards) for i in range(shards)])

    def across_y(value):
        return send(value, "ctx", [(i, i ^ 1) for i in range(shards)])

    def across_x(value):
        return send(value, "kv", [(i, i ^ 2) for i in range(columns)])

    def across_both(value):
        pairs = [(i, i ^ columns ^ 2) for i in range(shards * columns)]
        return send(value, ("ctx", "kv"), pairs)

    def across_core(value):
        return send(value, "kv", [(i, i ^ 1) for i in range(columns)])

    both, single = pl.pallas_call(
        prepare_kernel,
        out_shape=(piece(2 * span + NOTES), piece(span + NOTES)),
        in_specs=[smem] + [hbm] * 3,
        out_specs=(vmem, vmem),
        scratch_shapes=[
            pltpu.VMEM(keep.shape, jnp.int32),
            pltpu.VMEM((1, prompts * cache), jnp.int32),
            pltpu.SemaphoreType.DMA((5,)),
        ],
        compiler_params=pltpu.CompilerParams(vmem_limit_bytes=60 * 1024 * 1024),
        cost_estimate=cost(10**9, 1),
    )(offsets, kv_rows, keep, jnp.transpose(dest))

    below, above = along_z(both, 1), along_z(single, 3)
    y_own, x_own, d_own = across_y(both), across_x(single), across_both(single)
    going = pl.pallas_call(
        going_kernel,
        out_shape=piece(2 * span + 2 * NOTES),
        in_specs=[vmem] * 4,
        out_specs=vmem,
        compiler_params=params,
        cost_estimate=cost(0, 10**6),
    )(both, y_own, x_own, d_own)
    beyond = along_z(going, 2)
    beside, relay = pl.pallas_call(
        beside_kernel,
        out_shape=(piece(2 * span + NOTES), piece(span)),
        in_specs=[vmem] * 3 + [anywhere],
        out_specs=(vmem,) * 2,
        compiler_params=params,
        cost_estimate=cost(0, 10**6),
    )(below, above, both, going)
    relayed = send(relay, "ctx", [(0, 2), (1, 3), (6, 4), (7, 5)])
    y_beside, x_beside = across_y(beside), across_x(beside)
    d_beside = across_y(x_beside)

    attention_shape = jax.ShapeDtypeStruct((prompts, span, qwidth), jnp.bfloat16)
    score_shape = jax.ShapeDtypeStruct((prompts, heads, cache + span), jnp.float32)

    def prompt_specs(late):
        def block(_, offsets_ref):
            early = early_of(offsets_ref)
            return (1 - early if late else early, 0, 0)

        return (
            pl.BlockSpec((1, span, qwidth), block),
            pl.BlockSpec((1, heads, cache + span), block),
        )

    attention, row_scores, late_done = pl.pallas_call(
        late_kernel,
        grid_spec=pltpu.PrefetchScalarGridSpec(
            num_scalar_prefetch=1,
            grid=(1,),
            in_specs=[prompt_specs(True)[0], vmem, vmem],
            out_specs=prompt_specs(True) + (vmem,),
        ),
        out_shape=(attention_shape, score_shape, jax.ShapeDtypeStruct((8, LANES), jnp.float32)),
        compiler_params=params,
        cost_estimate=cost(10**6, 1),
    )(offsets, query, both, y_own)

    late = pl.pallas_call(
        pick_late_kernel,
        out_shape=piece(span),
        in_specs=[vmem] * 2 + [anywhere],
        out_specs=vmem,
        compiler_params=params,
        cost_estimate=cost(0, 1),
    )(relay, relayed, late_done)
    y_late, d_late = across_y(late), across_both(late)
    end = pl.pallas_call(
        end_kernel,
        out_shape=piece(3 * span),
        in_specs=[vmem] * 2 + [anywhere] * 2,
        out_specs=vmem,
        compiler_params=params,
        cost_estimate=cost(0, 1),
    )(beyond, late, y_beside, x_beside)
    x_end = across_x(end)

    tokens = pltpu.VMEM((shards * span, width), jnp.bfloat16)
    late_tokens = pltpu.VMEM((2 * span, width), jnp.bfloat16)
    cache_shape = jax.ShapeDtypeStruct((rows, columns * width), jnp.bfloat16)
    slots_shape = jax.ShapeDtypeStruct((2, rows, heads), jnp.int32)
    done_shape = jax.ShapeDtypeStruct((8, LANES), jnp.float32)
    tables = [
        pltpu.VMEM((shards, 4 * heads, cache), jnp.int32),
        pltpu.VMEM((shards, prompts, cache), jnp.int32),
        pltpu.VMEM((shards, 8 * heads, cache), jnp.bfloat16),
    ]
    attention, row_scores, early_done, owner_cache, top, low, near_slots = pl.pallas_call(
        early_kernel,
        grid_spec=pltpu.PrefetchScalarGridSpec(
            num_scalar_prefetch=1,
            grid=(1,),
            in_specs=[prompt_specs(False)[0]] + [vmem] * 5 + [anywhere] * 3,
            out_specs=prompt_specs(False) + (vmem, hbm, vmem, vmem, vmem),
            scratch_shapes=[
                tokens,
                pltpu.VMEM((rows - band, width), jnp.bfloat16),
                pltpu.SemaphoreType.DMA,
            ]
            + tables,
        ),
        out_shape=(
            attention_shape,
            score_shape,
            done_shape,
            cache_shape,
            piece(rows - band),
            jax.ShapeDtypeStruct((2, band, width), jnp.bfloat16),
            slots_shape,
        ),
        input_output_aliases={8: 0, 9: 1},
        compiler_params=params,
        cost_estimate=cost(10**10, 10**7),
    )(offsets, query, both, beside, beyond, y_own, y_beside, late, attention, row_scores)
    far_slots = pl.pallas_call(
        far_index_kernel,
        out_shape=slots_shape,
        in_specs=[smem] + [vmem] * 5 + [anywhere],
        out_specs=vmem,
        scratch_shapes=tables,
        compiler_params=params,
        cost_estimate=cost(10**6, 1),
    )(offsets, x_own, x_beside, d_own, d_beside, beyond, early_done)
    far = (x_own, x_beside, x_end, d_own, d_beside, d_late, late, y_late, low)
    far += (near_slots, far_slots)
    sent = pl.pallas_call(
        far_sent_kernel,
        out_shape=piece(2 * rows),
        in_specs=[vmem] * 12,
        out_specs=vmem,
        scratch_shapes=[tokens, late_tokens, late_tokens],
        compiler_params=params,
        cost_estimate=cost(2 * 10**9, 4 * 10**6),
    )(*far, top)
    received = across_core(sent)
    owner_cache = pl.pallas_call(
        far_kept_kernel,
        out_shape=cache_shape,
        in_specs=[vmem] * 11 + [hbm],
        out_specs=hbm,
        scratch_shapes=[
            pltpu.VMEM((rows, width), jnp.bfloat16),
            pltpu.VMEM((band, width), jnp.bfloat16),
            tokens,
            late_tokens,
            late_tokens,
            pltpu.SemaphoreType.DMA((2,)),
        ],
        input_output_aliases={11: 0},
        compiler_params=params,
        cost_estimate=cost(2 * 10**9, 4 * 10**6),
    )(*far, owner_cache)
    owner_cache = pl.pallas_call(
        last_kernel,
        out_shape=cache_shape,
        in_specs=[anywhere, hbm],
        out_specs=hbm,
        scratch_shapes=[pltpu.SemaphoreType.DMA((2,))],
        input_output_aliases={1: 0},
        compiler_params=params,
        cost_estimate=cost(0, 10**6),
    )(received, owner_cache)
    return (attention, row_scores, owner_cache)


def solution(mesh):
    placed = (
        P(None, "ctx", "kv"),
        P(None, "ctx", "kv"),
        P(None, "ctx", "kv", None),
        P("ctx", None),
        P(),
    )
    in_planes = mesh.shape["ctx"] == 8 and mesh.shape["kv"] == 4
    return jax.shard_map(
        local_in_planes if in_planes else local,
        mesh=mesh,
        in_specs=placed,
        out_specs=(P(None, "ctx", "kv"), P(None, "kv", "ctx"), P(("ctx", "kv"), None)),
        check_vma=False,
    )
```

```python
import functools
import math

import jax
import jax.numpy as jnp
from jax import lax
from jax.experimental import pallas as pl
from jax.experimental.pallas import tpu as pltpu
from jax.sharding import PartitionSpec as P

HEAD = 128
WIDTH = 2 * HEAD
LANES = 128
VMEM_BYTES = 56 * 1024 * 1024
PLANE_BYTES = 28 * 1024 * 1024
NOTES = 16
BANDS = 4


def look_up(state, keep, fresh):
    tiles = state.shape[1] // LANES
    parts = []
    for tile in range(tiles):
        wanted = keep[:, tile * LANES : (tile + 1) * LANES]
        high = wanted >> 7
        low = wanted & 127
        found = jnp.where(high >= tiles, fresh + wanted - state.shape[1], 0)
        for source in range(tiles):
            held = state[:, source * LANES : (source + 1) * LANES]
            moved = jnp.take_along_axis(held, low, axis=1, mode="promise_in_bounds")
            found = jnp.where(high == source, moved, found)
        parts.append(found)
    return jnp.concatenate(parts, axis=1)


def split(state):
    both = jnp.concatenate([state >> 7, state & 127], axis=0)
    return both.astype(jnp.float32).astype(jnp.bfloat16)


def index_kernel(
    where_ref, keep_early_ref, keep_late_ref, dest_ref, slot_ref, row_ref, column_ref, coded
):
    shards, heads, cache = keep_early_ref.shape
    cap = slot_ref.shape[0] // shards
    span = LANES
    early, mine, me = where_ref[0], where_ref[1], where_ref[2]
    empty = jnp.minimum(keep_early_ref[0], 0)

    def follow(shard, carry):
        state, own = carry
        own = jnp.where(shard == mine, state, own)
        state = look_up(state, keep_early_ref[shard], shard * span + 1)
        coded[shard] = split(state)
        return state, own

    _, own_early = lax.fori_loop(0, shards, follow, (empty, empty), unroll=shards <= 8)
    base = shards * span + 1
    late_first = look_up(empty, keep_late_ref[0], base)
    late_second = look_up(late_first, keep_late_ref[1], base + span)
    own_late = jnp.where(mine == shards - 1, late_first, 0)
    for index, own in enumerate((own_early, own_late)):
        row_ref[index] = own
        column_ref[index] = jnp.transpose(own.astype(jnp.float32)).astype(jnp.int32)

    named = (dest_ref[...] == me).astype(jnp.float32)
    chunks = named.shape[1] // LANES
    upper = (
        lax.broadcasted_iota(jnp.int32, (LANES, LANES), 0)
        <= lax.broadcasted_iota(jnp.int32, (LANES, LANES), 1)
    ).astype(jnp.float32).astype(jnp.bfloat16)
    total = jnp.zeros((shards, 1), jnp.float32)
    ranks = []
    for chunk in range(chunks):
        part = named[:, chunk * LANES : (chunk + 1) * LANES]
        upto = jnp.dot(part.astype(jnp.bfloat16), upper, preferred_element_type=jnp.float32)
        ranks.append(jnp.where(part > 0, upto + total, 0.0))
        total = total + upto[:, LANES - 1 :]
    low_half = jnp.concatenate(ranks[: chunks // 2], axis=1)
    high_half = jnp.concatenate(ranks[chunks // 2 :], axis=1)
    rank_early = jnp.where(early == 0, low_half, high_half)
    rank_late = jnp.where(early == 0, high_half, low_half)
    place = lax.broadcasted_iota(jnp.int32, (cap, cache), 0).astype(jnp.float32) + 1.0
    contract = (((1,), (1,)), ((), ()))
    for shard in range(shards):
        pick = (rank_early[shard : shard + 1] == place).astype(jnp.float32).astype(jnp.bfloat16)
        found = lax.dot_general(pick, coded[shard], contract, preferred_element_type=jnp.float32)
        if shard >= shards - 2:
            state = late_first if shard == shards - 2 else late_second
            pick = (rank_late[shard : shard + 1] == place).astype(jnp.float32).astype(jnp.bfloat16)
            found += lax.dot_general(
                pick, split(state), contract, preferred_element_type=jnp.float32
            )
        tokens = found[:, :heads] * 128.0 + found[:, heads:]
        slot_ref[shard * cap : (shard + 1) * cap, :] = tokens.astype(jnp.int32)


def column_of(table, head):
    lane = lax.broadcasted_iota(jnp.int32, table.shape, 1)
    return jnp.sum(
        jnp.where(lane == head, table, 0).astype(jnp.float32), axis=1, keepdims=True
    ).astype(jnp.int32)


def picked(column, first, tokens):
    number = lax.broadcasted_iota(jnp.int32, (column.shape[0], tokens.shape[0]), 1) + first
    table = (column == number).astype(jnp.float32).astype(jnp.bfloat16)
    return jnp.dot(table, tokens, preferred_element_type=jnp.float32)


def attend(q_ref, prompt, keys, values, seen, out_ref, score_ref, head):
    span = q_ref.shape[1]
    cache = seen.shape[1]
    group = q_ref.shape[2] // HEAD
    causal = lax.broadcasted_iota(jnp.int32, (span, span), 1) <= lax.broadcasted_iota(
        jnp.int32, (span, span), 0
    )
    bias = jnp.concatenate(
        [
            jnp.broadcast_to(jnp.where(seen > 0, 0.0, -1e30), (span, cache)),
            jnp.where(causal, 0.0, -1e30),
        ],
        axis=1,
    )
    scale = math.log2(math.e) / math.sqrt(HEAD)
    mass = jnp.zeros((1, cache + span), jnp.float32)
    for member in range(group):
        query = q_ref[prompt, :, member * HEAD : (member + 1) * HEAD]
        scores = lax.dot_general(
            query, keys, (((1,), (1,)), ((), ())), preferred_element_type=jnp.float32
        )
        scores = scores + bias
        peak = jnp.max(scores, axis=1, keepdims=True)
        expo = jnp.exp2((scores - peak) * scale)
        weights = expo * (1.0 / jnp.sum(expo, axis=1, keepdims=True))
        mass = mass + jnp.sum(weights, axis=0, keepdims=True)
        mixed = jnp.dot(weights.astype(jnp.bfloat16), values, preferred_element_type=jnp.float32)
        out_ref[prompt, :, member * HEAD : (member + 1) * HEAD] = mixed.astype(jnp.bfloat16)
    score_ref[prompt, pl.ds(head, 1), :] = mass


def attention_kernel(
    where_ref, q_ref, span_ref, early_ref, late_ref, row_ref, column_ref, out_ref, score_ref
):
    early, mine, column, shards = where_ref[0], where_ref[1], where_ref[3], early_ref.shape[0]
    span = q_ref.shape[1]
    late = 1 - early
    local_head = pl.program_id(0)
    head = column * pl.num_programs(0) + local_head

    def run(which, prompt, tokens, first):
        chosen = column_of(column_ref[which], head)
        cached = picked(chosen, first, tokens).astype(jnp.bfloat16)
        rows = jnp.concatenate([cached, span_ref[prompt]], axis=0)
        seen = row_ref[which, pl.ds(head, 1), :]
        attend(
            q_ref, prompt, rows[:, :HEAD], rows[:, HEAD:], seen, out_ref, score_ref, local_head
        )

    run(0, early, early_ref[:, 0].reshape(shards * span, WIDTH), 1)

    @pl.when(mine >= shards - 2)
    def _():
        run(1, late, late_ref[0, 0], shards * span + 1)

    @pl.when(mine < shards - 2)
    def _():
        out_ref[late] = jnp.zeros(out_ref.shape[1:], out_ref.dtype)
        score_ref[late, pl.ds(local_head, 1), :] = jnp.zeros((1, score_ref.shape[2]), jnp.float32)


def owner_kernel(slot_ref, early_ref, late_ref, out_ref):
    shards, _, span, width = early_ref.shape
    rows = out_ref.shape[0]
    chosen = column_of(slot_ref[...], pl.program_id(0))
    bands = 4
    band = rows // bands
    reach = shards * span // bands
    tokens = early_ref[:, 0].reshape(shards * span, width)
    for index in range(bands):
        part = chosen[index * band : (index + 1) * band]
        found = picked(part, 1, tokens[: (index + 1) * reach])
        if index == bands - 1:
            found += picked(part, shards * span + 1, late_ref[:, 0].reshape(2 * span, width))
        out_ref[index * band : (index + 1) * band, :] = found.astype(jnp.bfloat16)


def local(query, kv_rows, keep, dest, offsets):
    prompts, span, qwidth = query.shape
    shards, columns = lax.axis_size("ctx"), lax.axis_size("kv")
    width = kv_rows.shape[2]
    heads_dev = width // WIDTH
    heads = heads_dev * columns
    cache = keep.shape[3]
    owners = shards * columns
    cap = 2 * prompts * cache // owners
    mine, column = lax.axis_index("ctx"), lax.axis_index("kv")
    early = jnp.where(offsets[0] < offsets[1], 0, 1).astype(jnp.int32)
    facts = jnp.stack([early, mine, mine * columns + column, column]).astype(jnp.int32)

    swap = early == 1
    ordered_kv = jnp.where(swap, kv_rows[::-1], kv_rows)
    ordered_keep = jnp.where(swap, keep[::-1, 0], keep[:, 0])
    digits = jnp.stack([ordered_keep >> 7, ordered_keep & 127], axis=1)
    share = dest.shape[0] // columns
    own_dest = lax.dynamic_slice_in_dim(dest[:, 0], column * share, share)
    facts_rows = jnp.concatenate([digits.reshape(-1), own_dest]).astype(jnp.bfloat16)
    used = facts_rows.shape[0]
    room = 16 * width
    facts_rows = jnp.concatenate([facts_rows, jnp.zeros((room - used,), jnp.bfloat16)])
    payload = jnp.concatenate(
        [ordered_kv.reshape(prompts * span, width), facts_rows.reshape(16, width)], axis=0
    )
    whole = lax.all_gather(payload, ("ctx", "kv")).reshape(
        shards, columns, prompts * span + 16, width
    )

    told = whole[:, :, prompts * span :, :].reshape(shards, columns, room).astype(jnp.int32)
    kept = told[:, :, : prompts * 2 * heads_dev * cache].reshape(
        shards, columns, prompts, 2, heads_dev, cache
    )
    kept = kept[:, :, :, 0] * 128 + kept[:, :, :, 1]
    kept = jnp.transpose(kept, (2, 0, 1, 3, 4)).reshape(prompts, shards, heads, cache)
    whole_dest = told[:, :, used - share : used].reshape(shards, columns * share)

    vmem = pl.BlockSpec(memory_space=pltpu.VMEM)
    smem = pl.BlockSpec(memory_space=pltpu.SMEM)
    params = pltpu.CompilerParams(vmem_limit_bytes=VMEM_BYTES)
    slots, rows, cols = pl.pallas_call(
        index_kernel,
        out_shape=(
            jax.ShapeDtypeStruct((shards * cap, heads), jnp.int32),
            jax.ShapeDtypeStruct((2, heads, cache), jnp.int32),
            jax.ShapeDtypeStruct((2, cache, heads), jnp.int32),
        ),
        in_specs=[smem, vmem, vmem, vmem],
        out_specs=(vmem, vmem, vmem),
        scratch_shapes=[pltpu.VMEM((shards, 2 * heads, cache), jnp.bfloat16)],
        compiler_params=params,
    )(facts, kept[0], kept[1, shards - 2 :], whole_dest)

    group_width = qwidth // heads_dev
    attention, row_scores = pl.pallas_call(
        attention_kernel,
        grid_spec=pltpu.PrefetchScalarGridSpec(
            num_scalar_prefetch=1,
            grid=(heads_dev,),
            in_specs=[
                pl.BlockSpec((prompts, span, group_width), lambda h, w: (0, 0, h)),
                pl.BlockSpec((prompts, span, WIDTH), lambda h, w: (0, 0, h)),
                pl.BlockSpec((shards, 1, span, WIDTH), lambda h, w: (0, w[3], 0, h)),
                pl.BlockSpec((1, 1, span, WIDTH), lambda h, w: (shards - 2, w[3], 1, h)),
                pl.BlockSpec((2, heads, cache), lambda h, w: (0, 0, 0)),
                pl.BlockSpec((2, cache, heads), lambda h, w: (0, 0, 0)),
            ],
            out_specs=(
                pl.BlockSpec((prompts, span, group_width), lambda h, w: (0, 0, h)),
                pl.BlockSpec((prompts, heads_dev, cache + span), lambda h, w: (0, 0, 0)),
            ),
        ),
        out_shape=(
            jax.ShapeDtypeStruct((prompts, span, qwidth), jnp.bfloat16),
            jax.ShapeDtypeStruct((prompts, heads_dev, cache + span), jnp.float32),
        ),
        compiler_params=params,
    )(facts, query, kv_rows, whole, whole, rows, cols)

    owner_cache = pl.pallas_call(
        owner_kernel,
        grid=(heads,),
        in_specs=[
            pl.BlockSpec((shards * cap, heads), lambda g: (0, 0)),
            pl.BlockSpec(
                (shards, 1, span, WIDTH), lambda g: (0, g // heads_dev, 0, g % heads_dev)
            ),
            pl.BlockSpec(
                (2, 1, span, WIDTH),
                lambda g: (shards // 2 - 1, g // heads_dev, 1, g % heads_dev),
            ),
        ],
        out_specs=pl.BlockSpec((shards * cap, WIDTH), lambda g: (0, g)),
        out_shape=jax.ShapeDtypeStruct((shards * cap, heads * WIDTH), jnp.bfloat16),
        compiler_params=params,
    )(slots, whole, whole)
    return (attention, row_scores, owner_cache)


def dot(a, b, dims=((1,), (0,))):
    return lax.dot_general(a, b, (dims, ((), ())), preferred_element_type=jnp.float32)


def marks(table):
    return table.astype(jnp.float32).astype(jnp.bfloat16)


def early_of(offsets_ref):
    return jnp.where(offsets_ref[0] < offsets_ref[1], 0, 1)


def prepare_kernel(
    offsets_ref, kv_ref, keep_ref, dest_ref, both_ref, single_ref, keep, dest, sems
):
    span = kv_ref.shape[1]
    heads, cache = keep_ref.shape[2], keep_ref.shape[3]
    early = early_of(offsets_ref)
    copies = [
        (keep_ref, keep),
        (dest_ref, dest),
        (kv_ref.at[early], single_ref.at[:span]),
        (kv_ref.at[early], both_ref.at[:span]),
        (kv_ref.at[1 - early], both_ref.at[span : 2 * span]),
    ]
    copies = [
        pltpu.make_async_copy(source, target, sems.at[index])
        for index, (source, target) in enumerate(copies)
    ]
    for copy in copies:
        copy.start()
    for copy in copies[:2]:
        copy.wait()
    lane = lax.broadcasted_iota(jnp.int32, (heads, cache), 1)
    rows = [
        keep[early, 0] - lane,
        dest[:, :cache],
        dest[:, cache:],
        keep[1 - early, 0] - lane,
        jnp.zeros((NOTES - 2 * heads - 2, cache), jnp.int32),
    ]
    rows = jnp.concatenate([row.astype(jnp.float32) for row in rows], axis=0)
    rows = rows.astype(jnp.bfloat16)
    single_ref[span:, :] = rows
    both_ref[2 * span :, :] = rows
    for copy in copies[2:]:
        copy.wait()


def two_notes(first, first_row, second, second_row):
    half = NOTES // 2
    return jnp.concatenate(
        [
            first[first_row : first_row + NOTES, :].astype(jnp.float32)[:half],
            second[second_row : second_row + NOTES, :].astype(jnp.float32)[:half],
        ],
        axis=0,
    ).astype(jnp.bfloat16)


def going_kernel(both, y_own, x_own, d_own, going_ref):
    span = both.shape[0] // 2 - NOTES // 2
    going_ref[:span, :] = both[:span, :]
    going_ref[span : 2 * span, :] = y_own[:span, :]
    going_ref[2 * span : 2 * span + NOTES, :] = two_notes(both, 2 * span, y_own, 2 * span)
    going_ref[2 * span + NOTES :, :] = two_notes(x_own, span, d_own, span)


def beside_kernel(below, above, both, _, beside_ref, relay_ref):
    span = relay_ref.shape[0]
    beside_ref[:span, :] = below[:span, :]
    beside_ref[span : 2 * span, :] = above[:span, :]
    beside_ref[2 * span :, :] = two_notes(below, 2 * span, above, span)
    level = lax.axis_index("ctx") // 2

    @pl.when(level == 0)
    def _():
        relay_ref[...] = below[span : 2 * span, :]

    @pl.when(level > 0)
    def _():
        relay_ref[...] = both[span : 2 * span, :]


def pick_late_kernel(relay, relayed, _, out_ref):
    level = lax.axis_index("ctx") // 2
    for ref, chosen in ((relay, (level == 0) | (level == 3)), (relayed, (level == 1) | (level == 2))):

        @pl.when(chosen)
        def _(ref=ref):
            out_ref[...] = ref[...]


def end_kernel(beyond, late, *rest):
    out_ref = rest[-1]
    span = late.shape[0]
    out_ref[: 2 * span, :] = beyond[: 2 * span, :]
    out_ref[2 * span :, :] = late[...]


def place_of(turn, flip, shards):
    mine = lax.axis_index("ctx")
    place = lax.rem(mine - 2 * turn + shards, shards)
    return place + 1 - 2 * lax.rem(mine, 2) if flip else place


def sort_tokens(pieces, tokens, span):
    shards = tokens.shape[0] // span
    for ref, base, turn, flip in pieces:
        place = place_of(turn, flip, shards)
        tokens[pl.ds(pl.multiple_of(place * span, span), span), :] = ref[base : base + span, :]


def sort_late(pieces, late_tokens):
    span = late_tokens.shape[0] // 2
    side = lax.rem(lax.axis_index("ctx"), 2)
    for flip, ref_base in enumerate(pieces):
        ref, base = ref_base
        place = side + flip - 2 * side * flip
        late_tokens[pl.ds(pl.multiple_of(place * span, span), span), :] = ref[
            base : base + span, :
        ]


def read_notes(ref, base, part, heads):
    half = NOTES // 2
    rows = ref[base : base + NOTES, :].astype(jnp.float32).astype(jnp.int32)
    rows = rows[part * half : (part + 1) * half]
    lane = lax.broadcasted_iota(jnp.int32, (heads, rows.shape[1]), 1)
    return rows[:heads] + lane, rows[heads + 2 : 2 * heads + 2] + lane, rows[heads : heads + 2]


def sort_notes(notes, keeps, dests):
    shards, heads = keeps.shape[0], keeps.shape[1] // 4
    for ref, base, part, turn, flip in notes:
        place = place_of(turn, flip, shards)
        early, late, dest = read_notes(ref, base, part, heads)
        keeps[place, :heads, :] = early
        keeps[place, heads : 2 * heads, :] = late
        dests[place, :, :] = dest


def follow_lists(keeps, coded, span):
    shards, rows, cache = keeps.shape
    heads = rows // 4
    row = lax.broadcasted_iota(jnp.int32, (rows, cache), 0)
    is_early = row < heads
    state = jnp.where(row < 0, keeps[0], 0)
    own = state
    mine = lax.axis_index("ctx")
    for shard in range(shards):
        own = jnp.where(mine == shard, state, own)
        late_first = (shards + shard - (shards - 2)) * span + 1
        fresh = jnp.where(is_early[:, :LANES], shard * span + 1, late_first)
        state = look_up(state, keeps[shard], fresh)
        if shard < shards - 2:
            state = jnp.where(is_early, state, 0)
        coded[shard] = split(state)
    return own


def fill_picks(early, dests, owner, picks):
    shards, halves, cache = dests.shape
    cap = picks.shape[1]
    upper = marks(
        lax.broadcasted_iota(jnp.int32, (LANES, LANES), 0)
        <= lax.broadcasted_iota(jnp.int32, (LANES, LANES), 1)
    )
    place = lax.broadcasted_iota(jnp.int32, (cap, cache), 0).astype(jnp.float32) + 1.0
    total = jnp.zeros((shards, 1), jnp.float32)
    ranks = []
    for half in range(halves):
        named = (dests[:, half, :] == owner).astype(jnp.float32)
        parts = []
        for chunk in range(cache // LANES):
            part = named[:, chunk * LANES : (chunk + 1) * LANES]
            upto = dot(part.astype(jnp.bfloat16), upper)
            parts.append(jnp.where(part > 0, upto + total, 0.0))
            total = total + upto[:, LANES - 1 :]
        ranks.append(jnp.concatenate(parts, axis=1))
    rank_early = jnp.where(early == 0, ranks[0], ranks[1])
    rank_late = jnp.where(early == 0, ranks[1], ranks[0])
    for shard in range(shards):
        picks[shard] = marks(rank_early[shard : shard + 1] == place)
        if shard >= shards - 2:
            picks[shard + 2] = marks(rank_late[shard : shard + 1] == place)


def find_slots(picks, coded, slots):
    shards, lists = coded.shape[0], coded.shape[1]
    heads = lists // 8
    cap = picks.shape[1]
    across = ((1,), (1,))
    for shard in range(shards):
        found = dot(picks[shard], coded[shard], across)
        tokens = found[:, :heads] * 128.0 + found[:, 4 * heads : 5 * heads]
        if shard >= shards - 2:
            found = dot(picks[shard + 2], coded[shard], across)
            tokens += found[:, heads : 2 * heads] * 128.0 + found[:, 5 * heads : 6 * heads]
        slots[shard * cap : (shard + 1) * cap, :] = tokens.astype(jnp.int32)


def place_bands(slots, tokens, out_ref, bands, total_bands):
    rows, heads = slots.shape
    reach = tokens.shape[0]
    band = rows // total_bands
    for head in range(heads):
        lanes = slice(head * WIDTH, (head + 1) * WIDTH)
        for order, index in enumerate(bands):
            part = slots[index * band : (index + 1) * band, head : head + 1]
            found = picked(part, 1, tokens[: (index + 1) * reach // total_bands, lanes])
            out_ref[order * band : (order + 1) * band, lanes] = found.astype(jnp.bfloat16)


def add_late(slots, first, late_tokens, out_ref, base):
    band, heads = slots.shape
    for head in range(heads):
        lanes = slice(head * WIDTH, (head + 1) * WIDTH)
        found = picked(slots[:, head : head + 1], first, late_tokens[:, lanes])
        out_ref[base : base + band, lanes] += found.astype(jnp.bfloat16)


def attend_columns(q_ref, head, rows, seen, out_ref, score_ref):
    span = q_ref.shape[1]
    total = rows.shape[0]
    cache = total - span
    group = q_ref.shape[2] // (score_ref.shape[1] * HEAD)
    keys, values = rows[:, :HEAD], rows[:, HEAD:]
    flat = jnp.transpose(values.astype(jnp.float32)).astype(jnp.bfloat16)
    lane = lax.broadcasted_iota(jnp.int32, (total, HEAD), 1)
    hidden = jnp.where(seen > 0, 0.0, -1e30)
    hidden = jnp.concatenate([hidden, jnp.zeros((span, 1), jnp.float32)], axis=0)
    hidden = jnp.where(lane == 0, hidden, 0.0).astype(jnp.bfloat16)
    keys = jnp.concatenate([keys, hidden], axis=1)
    ones = jnp.ones((2 * span, HEAD), jnp.bfloat16)
    causal = lax.broadcasted_iota(jnp.int32, (span, 2 * span), 0) <= lax.rem(
        lax.broadcasted_iota(jnp.int32, (span, 2 * span), 1), span
    )
    bias = jnp.where(causal, 0.0, -1e30)
    scale = math.log2(math.e) / math.sqrt(HEAD)
    mass = None
    for pair in range(group // 2):
        first = (head * group + 2 * pair) * HEAD
        query = jnp.concatenate(
            [
                q_ref[0, :, first : first + HEAD],
                q_ref[0, :, first + HEAD : first + 2 * HEAD],
            ],
            axis=0,
        )
        scores = dot(keys, jnp.concatenate([query, ones], axis=1), ((1,), (1,)))
        near = scores[cache:] + bias
        scores = jnp.concatenate([scores[:cache], near], axis=0) * scale
        peak = jnp.max(scores, axis=0, keepdims=True)
        expo = jnp.exp2(scores - peak)
        weights = expo * (1.0 / jnp.sum(expo, axis=0, keepdims=True))
        both = weights[:, :span] + weights[:, span:]
        mass = both if mass is None else mass + both
        mixed = jnp.transpose(dot(flat, weights.astype(jnp.bfloat16)))
        for member in range(2):
            lanes = slice(first + member * HEAD, first + (member + 1) * HEAD)
            out_ref[0, :, lanes] = mixed[member * span : (member + 1) * span].astype(
                jnp.bfloat16
            )
    score_ref[0, head : head + 1, :] = jnp.sum(jnp.transpose(mass), axis=0, keepdims=True)


def late_kernel(offsets_ref, q_ref, both_ref, beside_ref, out_ref, score_ref, done_ref):
    mine, shards = lax.axis_index("ctx"), lax.axis_size("ctx")
    heads, cache = score_ref.shape[1], score_ref.shape[2] - q_ref.shape[1]
    span = q_ref.shape[1]
    done_ref[...] = jnp.zeros(done_ref.shape, jnp.float32)

    @pl.when(mine >= shards - 2)
    def _():
        _, keep, _ = read_notes(beside_ref, 2 * span, 0, heads)
        state = jnp.where(keep >= cache, keep - cache + 1, 0)
        state = jnp.where(mine == shards - 1, state, 0).astype(jnp.float32)
        state = jnp.concatenate([state, jnp.zeros((8 - heads, cache), jnp.float32)], axis=0)
        columns = jnp.transpose(state).astype(jnp.int32)
        for head in range(heads):
            lanes = slice(head * WIDTH, (head + 1) * WIDTH)
            column = columns[:, head : head + 1]
            cached = picked(column, 1, beside_ref[span : 2 * span, lanes])
            rows = jnp.concatenate(
                [cached.astype(jnp.bfloat16), both_ref[span : 2 * span, lanes]], axis=0
            )
            attend_columns(q_ref, head, rows, column, out_ref, score_ref)

    @pl.when(mine < shards - 2)
    def _():
        out_ref[...] = jnp.zeros(out_ref.shape, out_ref.dtype)
        score_ref[...] = jnp.zeros(score_ref.shape, jnp.float32)


def output_part(cache_ref, row, rows, column):
    width = cache_ref.shape[1] // lax.axis_size("kv")
    return cache_ref.at[
        pl.ds(row, rows), pl.ds(pl.multiple_of(column * width, width), width)
    ]


def fill_slots(notes, keeps, dests, coded, picks_ref, slots_ref, early=None):
    sort_notes(notes, keeps, dests)
    own = follow_lists(keeps, coded, LANES)
    me = lax.axis_index("ctx") * lax.axis_size("kv") + lax.axis_index("kv")
    for flip in range(2):
        if early is not None:
            fill_picks(early, dests, me ^ flip, picks_ref.at[flip])
        find_slots(picks_ref.at[flip], coded, slots_ref.at[flip])
    return own


def early_kernel(offsets_ref, q_ref, *rest):
    both, beside, beyond, y_own, y_beside = rest[:5]
    out_ref, score_ref, done_ref, cache_ref, top_sent, low_ref, slots_ref = rest[8:15]
    picks_ref, tokens, top, sem, keeps, dests, coded = rest[15:]
    done_ref[...] = jnp.zeros(done_ref.shape, jnp.float32)
    span = both.shape[0] // 2 - NOTES // 2
    column = lax.axis_index("kv")
    at = 2 * span
    notes = [(both, at, 0, 0, 0), (beside, at, 0, 1, 0), (beside, at, 1, 3, 0)]
    notes += [(beyond, at, 0, 2, 0), (beyond, at, 1, 2, 1), (y_own, at, 0, 0, 1)]
    notes += [(y_beside, at, 0, 1, 1), (y_beside, at, 1, 3, 1)]
    early = early_of(offsets_ref)
    own = fill_slots(notes, keeps, dests, coded, picks_ref, slots_ref, early)
    own = jnp.transpose(own.astype(jnp.float32)).astype(jnp.int32)
    pieces = [(both, 0, 0, 0), (beside, 0, 1, 0), (beside, span, 3, 0), (beyond, 0, 2, 0)]
    pieces += [(beyond, span, 2, 1), (y_own, 0, 0, 1), (y_beside, 0, 1, 1), (y_beside, span, 3, 1)]
    sort_tokens(pieces, tokens, span)
    bands = tuple(range(BANDS - 1))
    place_bands(slots_ref.at[0], tokens, top, bands, BANDS)
    copy = pltpu.make_async_copy(top, output_part(cache_ref, 0, top.shape[0], column), sem)
    copy.start()
    place_bands(slots_ref.at[1], tokens, top_sent, bands, BANDS)
    for flip in range(2):
        place_bands(slots_ref.at[flip], tokens, low_ref.at[flip], (BANDS - 1,), BANDS)
    for head in range(score_ref.shape[1]):
        lanes = slice(head * WIDTH, (head + 1) * WIDTH)
        chosen = own[:, head : head + 1]
        cached = picked(chosen, 1, tokens[:, lanes]).astype(jnp.bfloat16)
        rows = jnp.concatenate([cached, both[:span, lanes]], axis=0)
        attend_columns(q_ref, head, rows, chosen, out_ref, score_ref)
    copy.wait()


def far_index_kernel(x_own, x_beside, d_own, d_beside, beyond, picks, _, *rest):
    slots_ref, keeps, dests, coded = rest
    span = x_own.shape[0] - NOTES
    at = 2 * span
    notes = [(x_own, span, 0, 0, 0), (d_own, span, 0, 0, 1), (x_beside, at, 0, 1, 0)]
    notes += [(x_beside, at, 1, 3, 0), (d_beside, at, 0, 1, 1), (d_beside, at, 1, 3, 1)]
    notes += [(beyond, at + NOTES, 0, 2, 0), (beyond, at + NOTES, 1, 2, 1)]
    fill_slots(notes, keeps, dests, coded, picks, slots_ref)


def far_rows(flip, refs, far_ref, low, tokens, near_late, far_late):
    x_own, x_beside, x_end, d_own, d_beside, d_late, late, y_late, low_ref = refs[:9]
    near_slots, far_slots = refs[9:]
    span = late.shape[0]
    rows = far_slots.shape[1]
    band = rows // BANDS
    first = tokens.shape[0] + 1
    last = pl.ds(rows - band, band)
    sort_late([(late, 0), (y_late, 0)], near_late)
    sort_late([(x_end, 2 * span), (d_late, 0)], far_late)
    low[...] = low_ref[flip]
    add_late(near_slots.at[flip, last], first, near_late, low, 0)
    pieces = [(x_own, 0, 0, 0), (x_beside, 0, 1, 0), (x_beside, span, 3, 0), (x_end, 0, 2, 0)]
    pieces += [(x_end, span, 2, 1), (d_own, 0, 0, 1), (d_beside, 0, 1, 1), (d_beside, span, 3, 1)]
    sort_tokens(pieces, tokens, span)
    place_bands(far_slots.at[flip], tokens, far_ref, tuple(range(BANDS)), BANDS)
    add_late(far_slots.at[flip, last], first, far_late, far_ref, rows - band)


def far_sent_kernel(*refs):
    top_ref, sent_ref = refs[11:13]
    rows = refs[10].shape[1]
    upper = rows + top_ref.shape[0]
    sent_ref[rows:upper, :] = top_ref[...]
    far_rows(1, refs[:11], sent_ref.at[:rows], sent_ref.at[upper:], *refs[13:])


def far_kept_kernel(*refs):
    cache_ref, far, low, tokens, near_late, far_late, sems = refs[12:]
    column = lax.axis_index("kv")
    rows, band = far.shape[0], low.shape[0]
    far_rows(0, refs[:11], far, low, tokens, near_late, far_late)
    copies = [
        pltpu.make_async_copy(far, output_part(cache_ref, 0, rows, column ^ 2), sems.at[0]),
        pltpu.make_async_copy(
            low, output_part(cache_ref, rows - band, band, column), sems.at[1]
        ),
    ]
    for copy in copies:
        copy.start()
    for copy in copies:
        copy.wait()


def last_kernel(sent_ref, _, cache_ref, sems):
    column = lax.axis_index("kv")
    rows = cache_ref.shape[0]
    copies = [
        pltpu.make_async_copy(
            sent_ref.at[index * rows : (index + 1) * rows],
            output_part(cache_ref, 0, rows, column ^ place),
            sems.at[index],
        )
        for index, place in enumerate((3, 1))
    ]
    for copy in copies:
        copy.start()
    for copy in copies:
        copy.wait()


def send(value, axis, pairs):
    return lax.ppermute(value, axis, pairs)


def local_in_planes(query, kv_rows, keep, dest, offsets):
    prompts, span, qwidth = query.shape
    shards, columns = lax.axis_size("ctx"), lax.axis_size("kv")
    width = kv_rows.shape[2]
    heads = width // WIDTH
    cache = keep.shape[3]
    rows = 2 * prompts * cache // columns
    band = rows // BANDS
    vmem = pl.BlockSpec(memory_space=pltpu.VMEM)
    smem = pl.BlockSpec(memory_space=pltpu.SMEM)
    anywhere = pl.BlockSpec(memory_space=pl.ANY)
    hbm = pl.BlockSpec(memory_space=pltpu.HBM)
    params = pltpu.CompilerParams(vmem_limit_bytes=PLANE_BYTES)

    def cost(flops, moved):
        return pl.CostEstimate(flops=flops, bytes_accessed=moved, transcendentals=0)

    def piece(count):
        return jax.ShapeDtypeStruct((count, width), jnp.bfloat16)

    def along_z(value, turn):
        return send(value, "ctx", [(i, (i + 2 * turn) % shards) for i in range(shards)])

    def across_y(value):
        return send(value, "ctx", [(i, i ^ 1) for i in range(shards)])

    def across_x(value):
        return send(value, "kv", [(i, i ^ 2) for i in range(columns)])

    def across_both(value):
        pairs = [(i, i ^ columns ^ 2) for i in range(shards * columns)]
        return send(value, ("ctx", "kv"), pairs)

    def across_core(value):
        return send(value, "kv", [(i, i ^ 1) for i in range(columns)])

    both, single = pl.pallas_call(
        prepare_kernel,
        out_shape=(piece(2 * span + NOTES), piece(span + NOTES)),
        in_specs=[smem] + [hbm] * 3,
        out_specs=(vmem, vmem),
        scratch_shapes=[
            pltpu.VMEM(keep.shape, jnp.int32),
            pltpu.VMEM((1, prompts * cache), jnp.int32),
            pltpu.SemaphoreType.DMA((5,)),
        ],
        compiler_params=pltpu.CompilerParams(vmem_limit_bytes=60 * 1024 * 1024),
        cost_estimate=cost(10**9, 1),
    )(offsets, kv_rows, keep, jnp.transpose(dest))

    below, above = along_z(both, 1), along_z(single, 3)
    y_own, x_own, d_own = across_y(both), across_x(single), across_both(single)
    going = pl.pallas_call(
        going_kernel,
        out_shape=piece(2 * span + 2 * NOTES),
        in_specs=[vmem] * 4,
        out_specs=vmem,
        compiler_params=params,
        cost_estimate=cost(0, 10**6),
    )(both, y_own, x_own, d_own)
    beyond = along_z(going, 2)
    beside, relay = pl.pallas_call(
        beside_kernel,
        out_shape=(piece(2 * span + NOTES), piece(span)),
        in_specs=[vmem] * 3 + [anywhere],
        out_specs=(vmem,) * 2,
        compiler_params=params,
        cost_estimate=cost(0, 10**6),
    )(below, above, both, going)
    relayed = send(relay, "ctx", [(0, 2), (1, 3), (6, 4), (7, 5)])
    y_beside, x_beside = across_y(beside), across_x(beside)
    d_beside = across_y(x_beside)

    attention_shape = jax.ShapeDtypeStruct((prompts, span, qwidth), jnp.bfloat16)
    score_shape = jax.ShapeDtypeStruct((prompts, heads, cache + span), jnp.float32)

    def prompt_specs(late):
        def block(_, offsets_ref):
            early = early_of(offsets_ref)
            return (1 - early if late else early, 0, 0)

        return (
            pl.BlockSpec((1, span, qwidth), block),
            pl.BlockSpec((1, heads, cache + span), block),
        )

    attention, row_scores, late_done = pl.pallas_call(
        late_kernel,
        grid_spec=pltpu.PrefetchScalarGridSpec(
            num_scalar_prefetch=1,
            grid=(1,),
            in_specs=[prompt_specs(True)[0], vmem, vmem],
            out_specs=prompt_specs(True) + (vmem,),
        ),
        out_shape=(attention_shape, score_shape, jax.ShapeDtypeStruct((8, LANES), jnp.float32)),
        compiler_params=params,
        cost_estimate=cost(10**6, 1),
    )(offsets, query, both, y_own)

    late = pl.pallas_call(
        pick_late_kernel,
        out_shape=piece(span),
        in_specs=[vmem] * 2 + [anywhere],
        out_specs=vmem,
        compiler_params=params,
        cost_estimate=cost(0, 1),
    )(relay, relayed, late_done)
    y_late, d_late = across_y(late), across_both(late)
    end = pl.pallas_call(
        end_kernel,
        out_shape=piece(3 * span),
        in_specs=[vmem] * 2 + [anywhere] * 2,
        out_specs=vmem,
        compiler_params=params,
        cost_estimate=cost(0, 1),
    )(beyond, late, y_beside, x_beside)
    x_end = across_x(end)

    tokens = pltpu.VMEM((shards * span, width), jnp.bfloat16)
    late_tokens = pltpu.VMEM((2 * span, width), jnp.bfloat16)
    cache_shape = jax.ShapeDtypeStruct((rows, columns * width), jnp.bfloat16)
    slots_shape = jax.ShapeDtypeStruct((2, rows, heads), jnp.int32)
    done_shape = jax.ShapeDtypeStruct((8, LANES), jnp.float32)
    tables = [
        pltpu.VMEM((shards, 4 * heads, cache), jnp.int32),
        pltpu.VMEM((shards, prompts, cache), jnp.int32),
        pltpu.VMEM((shards, 8 * heads, cache), jnp.bfloat16),
    ]
    (attention, row_scores, early_done, owner_cache, top, low, near_slots, picks) = pl.pallas_call(
        early_kernel,
        grid_spec=pltpu.PrefetchScalarGridSpec(
            num_scalar_prefetch=1,
            grid=(1,),
            in_specs=[prompt_specs(False)[0]] + [vmem] * 5 + [anywhere] * 3,
            out_specs=prompt_specs(False) + (vmem, hbm, vmem, vmem, vmem, vmem),
            scratch_shapes=[
                tokens,
                pltpu.VMEM((rows - band, width), jnp.bfloat16),
                pltpu.SemaphoreType.DMA,
            ]
            + tables,
        ),
        out_shape=(
            attention_shape,
            score_shape,
            done_shape,
            cache_shape,
            piece(rows - band),
            jax.ShapeDtypeStruct((2, band, width), jnp.bfloat16),
            slots_shape,
            jax.ShapeDtypeStruct((2, shards + 2, rows // shards, cache), jnp.bfloat16),
        ),
        input_output_aliases={8: 0, 9: 1},
        compiler_params=params,
        cost_estimate=cost(10**10, 10**7),
    )(offsets, query, both, beside, beyond, y_own, y_beside, late, attention, row_scores)
    far_slots = pl.pallas_call(
        far_index_kernel,
        out_shape=slots_shape,
        in_specs=[vmem] * 6 + [anywhere],
        out_specs=vmem,
        scratch_shapes=tables,
        compiler_params=params,
        cost_estimate=cost(10**6, 1),
    )(x_own, x_beside, d_own, d_beside, beyond, picks, early_done)
    far = (x_own, x_beside, x_end, d_own, d_beside, d_late, late, y_late, low)
    far += (near_slots, far_slots)
    sent = pl.pallas_call(
        far_sent_kernel,
        out_shape=piece(2 * rows),
        in_specs=[vmem] * 12,
        out_specs=vmem,
        scratch_shapes=[tokens, late_tokens, late_tokens],
        compiler_params=params,
        cost_estimate=cost(2 * 10**9, 4 * 10**6),
    )(*far, top)
    received = across_core(sent)
    owner_cache = pl.pallas_call(
        far_kept_kernel,
        out_shape=cache_shape,
        in_specs=[vmem] * 11 + [hbm],
        out_specs=hbm,
        scratch_shapes=[
            pltpu.VMEM((rows, width), jnp.bfloat16),
            pltpu.VMEM((band, width), jnp.bfloat16),
            tokens,
            late_tokens,
            late_tokens,
            pltpu.SemaphoreType.DMA((2,)),
        ],
        input_output_aliases={11: 0},
        compiler_params=params,
        cost_estimate=cost(2 * 10**9, 4 * 10**6),
    )(*far, owner_cache)
    owner_cache = pl.pallas_call(
        last_kernel,
        out_shape=cache_shape,
        in_specs=[anywhere, hbm],
        out_specs=hbm,
        scratch_shapes=[pltpu.SemaphoreType.DMA((2,))],
        input_output_aliases={1: 0},
        compiler_params=params,
        cost_estimate=cost(0, 10**6),
    )(received, owner_cache)
    return (attention, row_scores, owner_cache)


def solution(mesh):
    placed = (
        P(None, "ctx", "kv"),
        P(None, "ctx", "kv"),
        P(None, "ctx", "kv", None),
        P("ctx", None),
        P(),
    )
    in_planes = mesh.shape["ctx"] == 8 and mesh.shape["kv"] == 4
    return jax.shard_map(
        local_in_planes if in_planes else local,
        mesh=mesh,
        in_specs=placed,
        out_specs=(P(None, "ctx", "kv"), P(None, "kv", "ctx"), P(("ctx", "kv"), None)),
        check_vma=False,
    )
```

```python
import functools
import math

import jax
import jax.numpy as jnp
from jax import lax
from jax.experimental import pallas as pl
from jax.experimental.pallas import tpu as pltpu
from jax.sharding import PartitionSpec as P

HEAD = 128
WIDTH = 2 * HEAD
LANES = 128
VMEM_BYTES = 56 * 1024 * 1024
PLANE_BYTES = 28 * 1024 * 1024
NOTES = 16
BANDS = 4


def look_up(state, keep, fresh):
    tiles = state.shape[1] // LANES
    parts = []
    for tile in range(tiles):
        wanted = keep[:, tile * LANES : (tile + 1) * LANES]
        high = wanted >> 7
        low = wanted & 127
        found = jnp.where(high >= tiles, fresh + wanted - state.shape[1], 0)
        for source in range(tiles):
            held = state[:, source * LANES : (source + 1) * LANES]
            moved = jnp.take_along_axis(held, low, axis=1, mode="promise_in_bounds")
            found = jnp.where(high == source, moved, found)
        parts.append(found)
    return jnp.concatenate(parts, axis=1)


def split(state):
    both = jnp.concatenate([state >> 7, state & 127], axis=0)
    return both.astype(jnp.float32).astype(jnp.bfloat16)


def index_kernel(
    where_ref, keep_early_ref, keep_late_ref, dest_ref, slot_ref, row_ref, column_ref, coded
):
    shards, heads, cache = keep_early_ref.shape
    cap = slot_ref.shape[0] // shards
    span = LANES
    early, mine, me = where_ref[0], where_ref[1], where_ref[2]
    empty = jnp.minimum(keep_early_ref[0], 0)

    def follow(shard, carry):
        state, own = carry
        own = jnp.where(shard == mine, state, own)
        state = look_up(state, keep_early_ref[shard], shard * span + 1)
        coded[shard] = split(state)
        return state, own

    _, own_early = lax.fori_loop(0, shards, follow, (empty, empty), unroll=shards <= 8)
    base = shards * span + 1
    late_first = look_up(empty, keep_late_ref[0], base)
    late_second = look_up(late_first, keep_late_ref[1], base + span)
    own_late = jnp.where(mine == shards - 1, late_first, 0)
    for index, own in enumerate((own_early, own_late)):
        row_ref[index] = own
        column_ref[index] = jnp.transpose(own.astype(jnp.float32)).astype(jnp.int32)

    named = (dest_ref[...] == me).astype(jnp.float32)
    chunks = named.shape[1] // LANES
    upper = (
        lax.broadcasted_iota(jnp.int32, (LANES, LANES), 0)
        <= lax.broadcasted_iota(jnp.int32, (LANES, LANES), 1)
    ).astype(jnp.float32).astype(jnp.bfloat16)
    total = jnp.zeros((shards, 1), jnp.float32)
    ranks = []
    for chunk in range(chunks):
        part = named[:, chunk * LANES : (chunk + 1) * LANES]
        upto = jnp.dot(part.astype(jnp.bfloat16), upper, preferred_element_type=jnp.float32)
        ranks.append(jnp.where(part > 0, upto + total, 0.0))
        total = total + upto[:, LANES - 1 :]
    low_half = jnp.concatenate(ranks[: chunks // 2], axis=1)
    high_half = jnp.concatenate(ranks[chunks // 2 :], axis=1)
    rank_early = jnp.where(early == 0, low_half, high_half)
    rank_late = jnp.where(early == 0, high_half, low_half)
    place = lax.broadcasted_iota(jnp.int32, (cap, cache), 0).astype(jnp.float32) + 1.0
    contract = (((1,), (1,)), ((), ()))
    for shard in range(shards):
        pick = (rank_early[shard : shard + 1] == place).astype(jnp.float32).astype(jnp.bfloat16)
        found = lax.dot_general(pick, coded[shard], contract, preferred_element_type=jnp.float32)
        if shard >= shards - 2:
            state = late_first if shard == shards - 2 else late_second
            pick = (rank_late[shard : shard + 1] == place).astype(jnp.float32).astype(jnp.bfloat16)
            found += lax.dot_general(
                pick, split(state), contract, preferred_element_type=jnp.float32
            )
        tokens = found[:, :heads] * 128.0 + found[:, heads:]
        slot_ref[shard * cap : (shard + 1) * cap, :] = tokens.astype(jnp.int32)


def column_of(table, head):
    lane = lax.broadcasted_iota(jnp.int32, table.shape, 1)
    return jnp.sum(
        jnp.where(lane == head, table, 0).astype(jnp.float32), axis=1, keepdims=True
    ).astype(jnp.int32)


def picked(column, first, tokens):
    number = lax.broadcasted_iota(jnp.int32, (column.shape[0], tokens.shape[0]), 1) + first
    table = (column == number).astype(jnp.float32).astype(jnp.bfloat16)
    return jnp.dot(table, tokens, preferred_element_type=jnp.float32)


def attend(q_ref, prompt, keys, values, seen, out_ref, score_ref, head):
    span = q_ref.shape[1]
    cache = seen.shape[1]
    group = q_ref.shape[2] // HEAD
    causal = lax.broadcasted_iota(jnp.int32, (span, span), 1) <= lax.broadcasted_iota(
        jnp.int32, (span, span), 0
    )
    bias = jnp.concatenate(
        [
            jnp.broadcast_to(jnp.where(seen > 0, 0.0, -1e30), (span, cache)),
            jnp.where(causal, 0.0, -1e30),
        ],
        axis=1,
    )
    scale = math.log2(math.e) / math.sqrt(HEAD)
    mass = jnp.zeros((1, cache + span), jnp.float32)
    for member in range(group):
        query = q_ref[prompt, :, member * HEAD : (member + 1) * HEAD]
        scores = lax.dot_general(
            query, keys, (((1,), (1,)), ((), ())), preferred_element_type=jnp.float32
        )
        scores = scores + bias
        peak = jnp.max(scores, axis=1, keepdims=True)
        expo = jnp.exp2((scores - peak) * scale)
        weights = expo * (1.0 / jnp.sum(expo, axis=1, keepdims=True))
        mass = mass + jnp.sum(weights, axis=0, keepdims=True)
        mixed = jnp.dot(weights.astype(jnp.bfloat16), values, preferred_element_type=jnp.float32)
        out_ref[prompt, :, member * HEAD : (member + 1) * HEAD] = mixed.astype(jnp.bfloat16)
    score_ref[prompt, pl.ds(head, 1), :] = mass


def attention_kernel(
    where_ref, q_ref, span_ref, early_ref, late_ref, row_ref, column_ref, out_ref, score_ref
):
    early, mine, column, shards = where_ref[0], where_ref[1], where_ref[3], early_ref.shape[0]
    span = q_ref.shape[1]
    late = 1 - early
    local_head = pl.program_id(0)
    head = column * pl.num_programs(0) + local_head

    def run(which, prompt, tokens, first):
        chosen = column_of(column_ref[which], head)
        cached = picked(chosen, first, tokens).astype(jnp.bfloat16)
        rows = jnp.concatenate([cached, span_ref[prompt]], axis=0)
        seen = row_ref[which, pl.ds(head, 1), :]
        attend(
            q_ref, prompt, rows[:, :HEAD], rows[:, HEAD:], seen, out_ref, score_ref, local_head
        )

    run(0, early, early_ref[:, 0].reshape(shards * span, WIDTH), 1)

    @pl.when(mine >= shards - 2)
    def _():
        run(1, late, late_ref[0, 0], shards * span + 1)

    @pl.when(mine < shards - 2)
    def _():
        out_ref[late] = jnp.zeros(out_ref.shape[1:], out_ref.dtype)
        score_ref[late, pl.ds(local_head, 1), :] = jnp.zeros((1, score_ref.shape[2]), jnp.float32)


def owner_kernel(slot_ref, early_ref, late_ref, out_ref):
    shards, _, span, width = early_ref.shape
    rows = out_ref.shape[0]
    chosen = column_of(slot_ref[...], pl.program_id(0))
    bands = 4
    band = rows // bands
    reach = shards * span // bands
    tokens = early_ref[:, 0].reshape(shards * span, width)
    for index in range(bands):
        part = chosen[index * band : (index + 1) * band]
        found = picked(part, 1, tokens[: (index + 1) * reach])
        if index == bands - 1:
            found += picked(part, shards * span + 1, late_ref[:, 0].reshape(2 * span, width))
        out_ref[index * band : (index + 1) * band, :] = found.astype(jnp.bfloat16)


def local(query, kv_rows, keep, dest, offsets):
    prompts, span, qwidth = query.shape
    shards, columns = lax.axis_size("ctx"), lax.axis_size("kv")
    width = kv_rows.shape[2]
    heads_dev = width // WIDTH
    heads = heads_dev * columns
    cache = keep.shape[3]
    owners = shards * columns
    cap = 2 * prompts * cache // owners
    mine, column = lax.axis_index("ctx"), lax.axis_index("kv")
    early = jnp.where(offsets[0] < offsets[1], 0, 1).astype(jnp.int32)
    facts = jnp.stack([early, mine, mine * columns + column, column]).astype(jnp.int32)

    swap = early == 1
    ordered_kv = jnp.where(swap, kv_rows[::-1], kv_rows)
    ordered_keep = jnp.where(swap, keep[::-1, 0], keep[:, 0])
    digits = jnp.stack([ordered_keep >> 7, ordered_keep & 127], axis=1)
    share = dest.shape[0] // columns
    own_dest = lax.dynamic_slice_in_dim(dest[:, 0], column * share, share)
    facts_rows = jnp.concatenate([digits.reshape(-1), own_dest]).astype(jnp.bfloat16)
    used = facts_rows.shape[0]
    room = 16 * width
    facts_rows = jnp.concatenate([facts_rows, jnp.zeros((room - used,), jnp.bfloat16)])
    payload = jnp.concatenate(
        [ordered_kv.reshape(prompts * span, width), facts_rows.reshape(16, width)], axis=0
    )
    whole = lax.all_gather(payload, ("ctx", "kv")).reshape(
        shards, columns, prompts * span + 16, width
    )

    told = whole[:, :, prompts * span :, :].reshape(shards, columns, room).astype(jnp.int32)
    kept = told[:, :, : prompts * 2 * heads_dev * cache].reshape(
        shards, columns, prompts, 2, heads_dev, cache
    )
    kept = kept[:, :, :, 0] * 128 + kept[:, :, :, 1]
    kept = jnp.transpose(kept, (2, 0, 1, 3, 4)).reshape(prompts, shards, heads, cache)
    whole_dest = told[:, :, used - share : used].reshape(shards, columns * share)

    vmem = pl.BlockSpec(memory_space=pltpu.VMEM)
    smem = pl.BlockSpec(memory_space=pltpu.SMEM)
    params = pltpu.CompilerParams(vmem_limit_bytes=VMEM_BYTES)
    slots, rows, cols = pl.pallas_call(
        index_kernel,
        out_shape=(
            jax.ShapeDtypeStruct((shards * cap, heads), jnp.int32),
            jax.ShapeDtypeStruct((2, heads, cache), jnp.int32),
            jax.ShapeDtypeStruct((2, cache, heads), jnp.int32),
        ),
        in_specs=[smem, vmem, vmem, vmem],
        out_specs=(vmem, vmem, vmem),
        scratch_shapes=[pltpu.VMEM((shards, 2 * heads, cache), jnp.bfloat16)],
        compiler_params=params,
    )(facts, kept[0], kept[1, shards - 2 :], whole_dest)

    group_width = qwidth // heads_dev
    attention, row_scores = pl.pallas_call(
        attention_kernel,
        grid_spec=pltpu.PrefetchScalarGridSpec(
            num_scalar_prefetch=1,
            grid=(heads_dev,),
            in_specs=[
                pl.BlockSpec((prompts, span, group_width), lambda h, w: (0, 0, h)),
                pl.BlockSpec((prompts, span, WIDTH), lambda h, w: (0, 0, h)),
                pl.BlockSpec((shards, 1, span, WIDTH), lambda h, w: (0, w[3], 0, h)),
                pl.BlockSpec((1, 1, span, WIDTH), lambda h, w: (shards - 2, w[3], 1, h)),
                pl.BlockSpec((2, heads, cache), lambda h, w: (0, 0, 0)),
                pl.BlockSpec((2, cache, heads), lambda h, w: (0, 0, 0)),
            ],
            out_specs=(
                pl.BlockSpec((prompts, span, group_width), lambda h, w: (0, 0, h)),
                pl.BlockSpec((prompts, heads_dev, cache + span), lambda h, w: (0, 0, 0)),
            ),
        ),
        out_shape=(
            jax.ShapeDtypeStruct((prompts, span, qwidth), jnp.bfloat16),
            jax.ShapeDtypeStruct((prompts, heads_dev, cache + span), jnp.float32),
        ),
        compiler_params=params,
    )(facts, query, kv_rows, whole, whole, rows, cols)

    owner_cache = pl.pallas_call(
        owner_kernel,
        grid=(heads,),
        in_specs=[
            pl.BlockSpec((shards * cap, heads), lambda g: (0, 0)),
            pl.BlockSpec(
                (shards, 1, span, WIDTH), lambda g: (0, g // heads_dev, 0, g % heads_dev)
            ),
            pl.BlockSpec(
                (2, 1, span, WIDTH),
                lambda g: (shards // 2 - 1, g // heads_dev, 1, g % heads_dev),
            ),
        ],
        out_specs=pl.BlockSpec((shards * cap, WIDTH), lambda g: (0, g)),
        out_shape=jax.ShapeDtypeStruct((shards * cap, heads * WIDTH), jnp.bfloat16),
        compiler_params=params,
    )(slots, whole, whole)
    return (attention, row_scores, owner_cache)


def dot(a, b, dims=((1,), (0,))):
    return lax.dot_general(a, b, (dims, ((), ())), preferred_element_type=jnp.float32)


def marks(table):
    return table.astype(jnp.float32).astype(jnp.bfloat16)


def early_of(offsets_ref):
    return jnp.where(offsets_ref[0] < offsets_ref[1], 0, 1)


def prepare_kernel(
    offsets_ref, kv_ref, keep_ref, dest_ref, both_ref, single_ref, keep, dest, sems
):
    span = kv_ref.shape[1]
    heads, cache = keep_ref.shape[2], keep_ref.shape[3]
    early = early_of(offsets_ref)
    copies = [
        (keep_ref, keep),
        (dest_ref, dest),
        (kv_ref.at[early], single_ref.at[:span]),
        (kv_ref.at[early], both_ref.at[:span]),
        (kv_ref.at[1 - early], both_ref.at[span : 2 * span]),
    ]
    copies = [
        pltpu.make_async_copy(source, target, sems.at[index])
        for index, (source, target) in enumerate(copies)
    ]
    for copy in copies:
        copy.start()
    for copy in copies[:2]:
        copy.wait()
    lane = lax.broadcasted_iota(jnp.int32, (heads, cache), 1)
    rows = [
        keep[early, 0] - lane,
        dest[:, :cache],
        dest[:, cache:],
        keep[1 - early, 0] - lane,
        jnp.zeros((NOTES - 2 * heads - 2, cache), jnp.int32),
    ]
    rows = jnp.concatenate([row.astype(jnp.float32) for row in rows], axis=0)
    rows = rows.astype(jnp.bfloat16)
    single_ref[span:, :] = rows
    both_ref[2 * span :, :] = rows
    for copy in copies[2:]:
        copy.wait()


def two_notes(first, first_row, second, second_row):
    half = NOTES // 2
    return jnp.concatenate(
        [
            first[first_row : first_row + NOTES, :].astype(jnp.float32)[:half],
            second[second_row : second_row + NOTES, :].astype(jnp.float32)[:half],
        ],
        axis=0,
    ).astype(jnp.bfloat16)


def going_kernel(both, y_own, x_own, d_own, going_ref):
    span = both.shape[0] // 2 - NOTES // 2
    going_ref[:span, :] = both[:span, :]
    going_ref[span : 2 * span, :] = y_own[:span, :]
    going_ref[2 * span : 2 * span + NOTES, :] = two_notes(both, 2 * span, y_own, 2 * span)
    going_ref[2 * span + NOTES :, :] = two_notes(x_own, span, d_own, span)


def beside_kernel(below, above, both, _, beside_ref, relay_ref):
    span = relay_ref.shape[0]
    beside_ref[:span, :] = below[:span, :]
    beside_ref[span : 2 * span, :] = above[:span, :]
    beside_ref[2 * span :, :] = two_notes(below, 2 * span, above, span)
    level = lax.axis_index("ctx") // 2

    @pl.when(level == 0)
    def _():
        relay_ref[...] = below[span : 2 * span, :]

    @pl.when(level > 0)
    def _():
        relay_ref[...] = both[span : 2 * span, :]


def pick_late_kernel(relay, relayed, _, out_ref):
    level = lax.axis_index("ctx") // 2
    for ref, chosen in ((relay, (level == 0) | (level == 3)), (relayed, (level == 1) | (level == 2))):

        @pl.when(chosen)
        def _(ref=ref):
            out_ref[...] = ref[...]


def end_kernel(beyond, late, *rest):
    out_ref = rest[-1]
    span = late.shape[0]
    out_ref[: 2 * span, :] = beyond[: 2 * span, :]
    out_ref[2 * span :, :] = late[...]


def place_of(turn, flip, shards):
    mine = lax.axis_index("ctx")
    place = lax.rem(mine - 2 * turn + shards, shards)
    return place + 1 - 2 * lax.rem(mine, 2) if flip else place


def sort_tokens(pieces, tokens, span):
    shards = tokens.shape[0] // span
    for ref, base, turn, flip in pieces:
        place = place_of(turn, flip, shards)
        tokens[pl.ds(pl.multiple_of(place * span, span), span), :] = ref[base : base + span, :]


def sort_late(pieces, late_tokens):
    span = late_tokens.shape[0] // 2
    side = lax.rem(lax.axis_index("ctx"), 2)
    for flip, ref_base in enumerate(pieces):
        ref, base = ref_base
        place = side + flip - 2 * side * flip
        late_tokens[pl.ds(pl.multiple_of(place * span, span), span), :] = ref[
            base : base + span, :
        ]


def read_notes(ref, base, part, heads):
    half = NOTES // 2
    rows = ref[base : base + NOTES, :].astype(jnp.float32).astype(jnp.int32)
    rows = rows[part * half : (part + 1) * half]
    lane = lax.broadcasted_iota(jnp.int32, (heads, rows.shape[1]), 1)
    return rows[:heads] + lane, rows[heads + 2 : 2 * heads + 2] + lane, rows[heads : heads + 2]


def sort_notes(notes, keeps, dests):
    shards, heads = keeps.shape[0], keeps.shape[1] // 4
    for ref, base, part, turn, flip in notes:
        place = place_of(turn, flip, shards)
        early, late, dest = read_notes(ref, base, part, heads)
        keeps[place, :heads, :] = early
        keeps[place, heads : 2 * heads, :] = late
        dests[place, :, :] = dest


def follow_lists(keeps, coded, span):
    shards, rows, cache = keeps.shape
    heads = rows // 4
    row = lax.broadcasted_iota(jnp.int32, (rows, cache), 0)
    is_early = row < heads
    state = jnp.where(row < 0, keeps[0], 0)
    own = state
    mine = lax.axis_index("ctx")
    for shard in range(shards):
        own = jnp.where(mine == shard, state, own)
        late_first = (shards + shard - (shards - 2)) * span + 1
        fresh = jnp.where(is_early[:, :LANES], shard * span + 1, late_first)
        state = look_up(state, keeps[shard], fresh)
        if shard < shards - 2:
            state = jnp.where(is_early, state, 0)
        coded[shard] = split(state)
    return own


def fill_picks(early, dests, owner, picks):
    shards, halves, cache = dests.shape
    cap = picks.shape[1]
    upper = marks(
        lax.broadcasted_iota(jnp.int32, (LANES, LANES), 0)
        <= lax.broadcasted_iota(jnp.int32, (LANES, LANES), 1)
    )
    place = lax.broadcasted_iota(jnp.int32, (cap, cache), 0).astype(jnp.float32) + 1.0
    total = jnp.zeros((shards, 1), jnp.float32)
    ranks = []
    for half in range(halves):
        named = (dests[:, half, :] == owner).astype(jnp.float32)
        parts = []
        for chunk in range(cache // LANES):
            part = named[:, chunk * LANES : (chunk + 1) * LANES]
            upto = dot(part.astype(jnp.bfloat16), upper)
            parts.append(jnp.where(part > 0, upto + total, 0.0))
            total = total + upto[:, LANES - 1 :]
        ranks.append(jnp.concatenate(parts, axis=1))
    rank_early = jnp.where(early == 0, ranks[0], ranks[1])
    rank_late = jnp.where(early == 0, ranks[1], ranks[0])
    for shard in range(shards):
        picks[shard] = marks(rank_early[shard : shard + 1] == place)
        if shard >= shards - 2:
            picks[shard + 2] = marks(rank_late[shard : shard + 1] == place)


def find_slots(picks, coded, slots):
    shards, lists = coded.shape[0], coded.shape[1]
    heads = lists // 8
    cap = picks.shape[1]
    across = ((1,), (1,))
    for shard in range(shards):
        found = dot(picks[shard], coded[shard], across)
        tokens = found[:, :heads] * 128.0 + found[:, 4 * heads : 5 * heads]
        if shard >= shards - 2:
            found = dot(picks[shard + 2], coded[shard], across)
            tokens += found[:, heads : 2 * heads] * 128.0 + found[:, 5 * heads : 6 * heads]
        slots[shard * cap : (shard + 1) * cap, :] = tokens.astype(jnp.int32)


def place_bands(slots, tokens, out_ref, bands, total_bands):
    rows, heads = slots.shape
    reach = tokens.shape[0]
    band = rows // total_bands
    for head in range(heads):
        lanes = slice(head * WIDTH, (head + 1) * WIDTH)
        for order, index in enumerate(bands):
            part = slots[index * band : (index + 1) * band, head : head + 1]
            found = picked(part, 1, tokens[: (index + 1) * reach // total_bands, lanes])
            out_ref[order * band : (order + 1) * band, lanes] = found.astype(jnp.bfloat16)


def add_late(slots, first, late_tokens, out_ref, base):
    band, heads = slots.shape
    for head in range(heads):
        lanes = slice(head * WIDTH, (head + 1) * WIDTH)
        found = picked(slots[:, head : head + 1], first, late_tokens[:, lanes])
        out_ref[base : base + band, lanes] += found.astype(jnp.bfloat16)


def attend_columns(q_ref, head, rows, seen, out_ref, score_ref):
    span = q_ref.shape[1]
    total = rows.shape[0]
    cache = total - span
    group = q_ref.shape[2] // (score_ref.shape[1] * HEAD)
    keys, values = rows[:, :HEAD], rows[:, HEAD:]
    flat = jnp.transpose(values.astype(jnp.float32)).astype(jnp.bfloat16)
    lane = lax.broadcasted_iota(jnp.int32, (total, HEAD), 1)
    hidden = jnp.where(seen > 0, 0.0, -1e30)
    hidden = jnp.concatenate([hidden, jnp.zeros((span, 1), jnp.float32)], axis=0)
    hidden = jnp.where(lane == 0, hidden, 0.0).astype(jnp.bfloat16)
    keys = jnp.concatenate([keys, hidden], axis=1)
    ones = jnp.ones((2 * span, HEAD), jnp.bfloat16)
    causal = lax.broadcasted_iota(jnp.int32, (span, 2 * span), 0) <= lax.rem(
        lax.broadcasted_iota(jnp.int32, (span, 2 * span), 1), span
    )
    bias = jnp.where(causal, 0.0, -1e30)
    scale = math.log2(math.e) / math.sqrt(HEAD)
    mass = None
    for pair in range(group // 2):
        first = (head * group + 2 * pair) * HEAD
        query = jnp.concatenate(
            [
                q_ref[0, :, first : first + HEAD],
                q_ref[0, :, first + HEAD : first + 2 * HEAD],
            ],
            axis=0,
        )
        scores = dot(keys, jnp.concatenate([query, ones], axis=1), ((1,), (1,)))
        scores = jnp.concatenate([scores[:cache], scores[cache:] + bias], axis=0)
        peak = jnp.max(scores, axis=0, keepdims=True)
        expo = jnp.exp2((scores - peak) * scale)
        weights = expo * (1.0 / jnp.sum(expo, axis=0, keepdims=True))
        both = weights[:, :span] + weights[:, span:]
        mass = both if mass is None else mass + both
        mixed = jnp.transpose(dot(flat, weights.astype(jnp.bfloat16)))
        for member in range(2):
            lanes = slice(first + member * HEAD, first + (member + 1) * HEAD)
            out_ref[0, :, lanes] = mixed[member * span : (member + 1) * span].astype(
                jnp.bfloat16
            )
    score_ref[0, head : head + 1, :] = jnp.sum(jnp.transpose(mass), axis=0, keepdims=True)


def late_kernel(offsets_ref, q_ref, both_ref, beside_ref, out_ref, score_ref, done_ref):
    mine, shards = lax.axis_index("ctx"), lax.axis_size("ctx")
    heads, cache = score_ref.shape[1], score_ref.shape[2] - q_ref.shape[1]
    span = q_ref.shape[1]
    done_ref[...] = jnp.zeros(done_ref.shape, jnp.float32)

    @pl.when(mine >= shards - 2)
    def _():
        _, keep, _ = read_notes(beside_ref, 2 * span, 0, heads)
        state = jnp.where(keep >= cache, keep - cache + 1, 0)
        state = jnp.where(mine == shards - 1, state, 0).astype(jnp.float32)
        state = jnp.concatenate([state, jnp.zeros((8 - heads, cache), jnp.float32)], axis=0)
        columns = jnp.transpose(state).astype(jnp.int32)
        for head in range(heads):
            lanes = slice(head * WIDTH, (head + 1) * WIDTH)
            column = columns[:, head : head + 1]
            cached = picked(column, 1, beside_ref[span : 2 * span, lanes])
            rows = jnp.concatenate(
                [cached.astype(jnp.bfloat16), both_ref[span : 2 * span, lanes]], axis=0
            )
            attend_columns(q_ref, head, rows, column, out_ref, score_ref)

    @pl.when(mine < shards - 2)
    def _():
        out_ref[...] = jnp.zeros(out_ref.shape, out_ref.dtype)
        score_ref[...] = jnp.zeros(score_ref.shape, jnp.float32)


def output_part(cache_ref, row, rows, column):
    width = cache_ref.shape[1] // lax.axis_size("kv")
    return cache_ref.at[
        pl.ds(row, rows), pl.ds(pl.multiple_of(column * width, width), width)
    ]


def fill_slots(notes, keeps, dests, coded, picks_ref, slots_ref, early=None):
    sort_notes(notes, keeps, dests)
    own = follow_lists(keeps, coded, LANES)
    me = lax.axis_index("ctx") * lax.axis_size("kv") + lax.axis_index("kv")
    for flip in range(2):
        if early is not None:
            fill_picks(early, dests, me ^ flip, picks_ref.at[flip])
        find_slots(picks_ref.at[flip], coded, slots_ref.at[flip])
    return own


def early_kernel(offsets_ref, q_ref, *rest):
    both, beside, beyond, y_own, y_beside = rest[:5]
    out_ref, score_ref, done_ref, cache_ref, top_sent, low_ref, slots_ref = rest[8:15]
    picks_ref, tokens, top, sem, keeps, dests, coded = rest[15:]
    done_ref[...] = jnp.zeros(done_ref.shape, jnp.float32)
    span = both.shape[0] // 2 - NOTES // 2
    column = lax.axis_index("kv")
    at = 2 * span
    notes = [(both, at, 0, 0, 0), (beside, at, 0, 1, 0), (beside, at, 1, 3, 0)]
    notes += [(beyond, at, 0, 2, 0), (beyond, at, 1, 2, 1), (y_own, at, 0, 0, 1)]
    notes += [(y_beside, at, 0, 1, 1), (y_beside, at, 1, 3, 1)]
    early = early_of(offsets_ref)
    own = fill_slots(notes, keeps, dests, coded, picks_ref, slots_ref, early)
    own = jnp.transpose(own.astype(jnp.float32)).astype(jnp.int32)
    pieces = [(both, 0, 0, 0), (beside, 0, 1, 0), (beside, span, 3, 0), (beyond, 0, 2, 0)]
    pieces += [(beyond, span, 2, 1), (y_own, 0, 0, 1), (y_beside, 0, 1, 1), (y_beside, span, 3, 1)]
    sort_tokens(pieces, tokens, span)
    bands = tuple(range(BANDS - 1))
    place_bands(slots_ref.at[0], tokens, top, bands, BANDS)
    copy = pltpu.make_async_copy(top, output_part(cache_ref, 0, top.shape[0], column), sem)
    copy.start()
    place_bands(slots_ref.at[1], tokens, top_sent, bands, BANDS)
    for flip in range(2):
        place_bands(slots_ref.at[flip], tokens, low_ref.at[flip], (BANDS - 1,), BANDS)
    for head in range(score_ref.shape[1]):
        lanes = slice(head * WIDTH, (head + 1) * WIDTH)
        chosen = own[:, head : head + 1]
        cached = picked(chosen, 1, tokens[:, lanes]).astype(jnp.bfloat16)
        rows = jnp.concatenate([cached, both[:span, lanes]], axis=0)
        attend_columns(q_ref, head, rows, chosen, out_ref, score_ref)
    copy.wait()


def far_index_kernel(x_own, x_beside, d_own, d_beside, beyond, picks, _, *rest):
    slots_ref, keeps, dests, coded = rest
    span = x_own.shape[0] - NOTES
    at = 2 * span
    notes = [(x_own, span, 0, 0, 0), (d_own, span, 0, 0, 1), (x_beside, at, 0, 1, 0)]
    notes += [(x_beside, at, 1, 3, 0), (d_beside, at, 0, 1, 1), (d_beside, at, 1, 3, 1)]
    notes += [(beyond, at + NOTES, 0, 2, 0), (beyond, at + NOTES, 1, 2, 1)]
    fill_slots(notes, keeps, dests, coded, picks, slots_ref)


def far_rows(flip, refs, far_ref, low, tokens, near_late, far_late):
    x_own, x_beside, x_end, d_own, d_beside, d_late, late, y_late, low_ref = refs[:9]
    near_slots, far_slots = refs[9:]
    span = late.shape[0]
    rows = far_slots.shape[1]
    band = rows // BANDS
    first = tokens.shape[0] + 1
    last = pl.ds(rows - band, band)
    sort_late([(late, 0), (y_late, 0)], near_late)
    sort_late([(x_end, 2 * span), (d_late, 0)], far_late)
    low[...] = low_ref[flip]
    add_late(near_slots.at[flip, last], first, near_late, low, 0)
    pieces = [(x_own, 0, 0, 0), (x_beside, 0, 1, 0), (x_beside, span, 3, 0), (x_end, 0, 2, 0)]
    pieces += [(x_end, span, 2, 1), (d_own, 0, 0, 1), (d_beside, 0, 1, 1), (d_beside, span, 3, 1)]
    sort_tokens(pieces, tokens, span)
    place_bands(far_slots.at[flip], tokens, far_ref, tuple(range(BANDS)), BANDS)
    add_late(far_slots.at[flip, last], first, far_late, far_ref, rows - band)


def far_sent_kernel(*refs):
    top_ref, sent_ref = refs[11:13]
    rows = refs[10].shape[1]
    upper = rows + top_ref.shape[0]
    sent_ref[rows:upper, :] = top_ref[...]
    far_rows(1, refs[:11], sent_ref.at[:rows], sent_ref.at[upper:], *refs[13:])


def far_kept_kernel(*refs):
    cache_ref, far, low, tokens, near_late, far_late, sems = refs[12:]
    column = lax.axis_index("kv")
    rows, band = far.shape[0], low.shape[0]
    far_rows(0, refs[:11], far, low, tokens, near_late, far_late)
    copies = [
        pltpu.make_async_copy(far, output_part(cache_ref, 0, rows, column ^ 2), sems.at[0]),
        pltpu.make_async_copy(
            low, output_part(cache_ref, rows - band, band, column), sems.at[1]
        ),
    ]
    for copy in copies:
        copy.start()
    for copy in copies:
        copy.wait()


def last_kernel(sent_ref, _, cache_ref, sems):
    column = lax.axis_index("kv")
    rows = cache_ref.shape[0]
    copies = [
        pltpu.make_async_copy(
            sent_ref.at[index * rows : (index + 1) * rows],
            output_part(cache_ref, 0, rows, column ^ place),
            sems.at[index],
        )
        for index, place in enumerate((3, 1))
    ]
    for copy in copies:
        copy.start()
    for copy in copies:
        copy.wait()


def send(value, axis, pairs):
    return lax.ppermute(value, axis, pairs)


def local_in_planes(query, kv_rows, keep, dest, offsets):
    prompts, span, qwidth = query.shape
    shards, columns = lax.axis_size("ctx"), lax.axis_size("kv")
    width = kv_rows.shape[2]
    heads = width // WIDTH
    cache = keep.shape[3]
    rows = 2 * prompts * cache // columns
    band = rows // BANDS
    vmem = pl.BlockSpec(memory_space=pltpu.VMEM)
    smem = pl.BlockSpec(memory_space=pltpu.SMEM)
    anywhere = pl.BlockSpec(memory_space=pl.ANY)
    hbm = pl.BlockSpec(memory_space=pltpu.HBM)
    params = pltpu.CompilerParams(vmem_limit_bytes=PLANE_BYTES)

    def cost(flops, moved):
        return pl.CostEstimate(flops=flops, bytes_accessed=moved, transcendentals=0)

    def piece(count):
        return jax.ShapeDtypeStruct((count, width), jnp.bfloat16)

    def along_z(value, turn):
        return send(value, "ctx", [(i, (i + 2 * turn) % shards) for i in range(shards)])

    def across_y(value):
        return send(value, "ctx", [(i, i ^ 1) for i in range(shards)])

    def across_x(value):
        return send(value, "kv", [(i, i ^ 2) for i in range(columns)])

    def across_both(value):
        pairs = [(i, i ^ columns ^ 2) for i in range(shards * columns)]
        return send(value, ("ctx", "kv"), pairs)

    def across_core(value):
        return send(value, "kv", [(i, i ^ 1) for i in range(columns)])

    both, single = pl.pallas_call(
        prepare_kernel,
        out_shape=(piece(2 * span + NOTES), piece(span + NOTES)),
        in_specs=[smem] + [hbm] * 3,
        out_specs=(vmem, vmem),
        scratch_shapes=[
            pltpu.VMEM(keep.shape, jnp.int32),
            pltpu.VMEM((1, prompts * cache), jnp.int32),
            pltpu.SemaphoreType.DMA((5,)),
        ],
        compiler_params=pltpu.CompilerParams(vmem_limit_bytes=60 * 1024 * 1024),
        cost_estimate=cost(10**9, 1),
    )(offsets, kv_rows, keep, jnp.transpose(dest))

    below, above = along_z(both, 1), along_z(single, 3)
    y_own, x_own, d_own = across_y(both), across_x(single), across_both(single)
    going = pl.pallas_call(
        going_kernel,
        out_shape=piece(2 * span + 2 * NOTES),
        in_specs=[vmem] * 4,
        out_specs=vmem,
        compiler_params=params,
        cost_estimate=cost(0, 10**6),
    )(both, y_own, x_own, d_own)
    beyond = along_z(going, 2)
    beside, relay = pl.pallas_call(
        beside_kernel,
        out_shape=(piece(2 * span + NOTES), piece(span)),
        in_specs=[vmem] * 3 + [anywhere],
        out_specs=(vmem,) * 2,
        compiler_params=params,
        cost_estimate=cost(0, 10**6),
    )(below, above, both, going)
    relayed = send(relay, "ctx", [(0, 2), (1, 3), (6, 4), (7, 5)])
    y_beside, x_beside = across_y(beside), across_x(beside)
    d_beside = across_y(x_beside)

    attention_shape = jax.ShapeDtypeStruct((prompts, span, qwidth), jnp.bfloat16)
    score_shape = jax.ShapeDtypeStruct((prompts, heads, cache + span), jnp.float32)

    def prompt_specs(late):
        def block(_, offsets_ref):
            early = early_of(offsets_ref)
            return (1 - early if late else early, 0, 0)

        return (
            pl.BlockSpec((1, span, qwidth), block),
            pl.BlockSpec((1, heads, cache + span), block),
        )

    attention, row_scores, late_done = pl.pallas_call(
        late_kernel,
        grid_spec=pltpu.PrefetchScalarGridSpec(
            num_scalar_prefetch=1,
            grid=(1,),
            in_specs=[prompt_specs(True)[0], vmem, vmem],
            out_specs=prompt_specs(True) + (vmem,),
        ),
        out_shape=(attention_shape, score_shape, jax.ShapeDtypeStruct((8, LANES), jnp.float32)),
        compiler_params=params,
        cost_estimate=cost(10**6, 1),
    )(offsets, query, both, y_own)

    late = pl.pallas_call(
        pick_late_kernel,
        out_shape=piece(span),
        in_specs=[vmem] * 2 + [anywhere],
        out_specs=vmem,
        compiler_params=params,
        cost_estimate=cost(0, 1),
    )(relay, relayed, late_done)
    y_late, d_late = across_y(late), across_both(late)
    end = pl.pallas_call(
        end_kernel,
        out_shape=piece(3 * span),
        in_specs=[vmem] * 2 + [anywhere] * 2,
        out_specs=vmem,
        compiler_params=params,
        cost_estimate=cost(0, 1),
    )(beyond, late, y_beside, x_beside)
    x_end = across_x(end)

    tokens = pltpu.VMEM((shards * span, width), jnp.bfloat16)
    late_tokens = pltpu.VMEM((2 * span, width), jnp.bfloat16)
    cache_shape = jax.ShapeDtypeStruct((rows, columns * width), jnp.bfloat16)
    slots_shape = jax.ShapeDtypeStruct((2, rows, heads), jnp.int32)
    done_shape = jax.ShapeDtypeStruct((8, LANES), jnp.float32)
    tables = [
        pltpu.VMEM((shards, 4 * heads, cache), jnp.int32),
        pltpu.VMEM((shards, prompts, cache), jnp.int32),
        pltpu.VMEM((shards, 8 * heads, cache), jnp.bfloat16),
    ]
    (attention, row_scores, early_done, owner_cache, top, low, near_slots, picks) = pl.pallas_call(
        early_kernel,
        grid_spec=pltpu.PrefetchScalarGridSpec(
            num_scalar_prefetch=1,
            grid=(1,),
            in_specs=[prompt_specs(False)[0]] + [vmem] * 5 + [anywhere] * 3,
            out_specs=prompt_specs(False) + (vmem, hbm, vmem, vmem, vmem, vmem),
            scratch_shapes=[
                tokens,
                pltpu.VMEM((rows - band, width), jnp.bfloat16),
                pltpu.SemaphoreType.DMA,
            ]
            + tables,
        ),
        out_shape=(
            attention_shape,
            score_shape,
            done_shape,
            cache_shape,
            piece(rows - band),
            jax.ShapeDtypeStruct((2, band, width), jnp.bfloat16),
            slots_shape,
            jax.ShapeDtypeStruct((2, shards + 2, rows // shards, cache), jnp.bfloat16),
        ),
        input_output_aliases={8: 0, 9: 1},
        compiler_params=params,
        cost_estimate=cost(10**10, 10**7),
    )(offsets, query, both, beside, beyond, y_own, y_beside, late, attention, row_scores)
    far_slots = pl.pallas_call(
        far_index_kernel,
        out_shape=slots_shape,
        in_specs=[vmem] * 6 + [anywhere],
        out_specs=vmem,
        scratch_shapes=tables,
        compiler_params=params,
        cost_estimate=cost(10**6, 1),
    )(x_own, x_beside, d_own, d_beside, beyond, picks, early_done)
    far = (x_own, x_beside, x_end, d_own, d_beside, d_late, late, y_late, low)
    far += (near_slots, far_slots)
    sent = pl.pallas_call(
        far_sent_kernel,
        out_shape=piece(2 * rows),
        in_specs=[vmem] * 12,
        out_specs=vmem,
        scratch_shapes=[tokens, late_tokens, late_tokens],
        compiler_params=params,
        cost_estimate=cost(2 * 10**9, 4 * 10**6),
    )(*far, top)
    received = across_core(sent)
    owner_cache = pl.pallas_call(
        far_kept_kernel,
        out_shape=cache_shape,
        in_specs=[vmem] * 11 + [hbm],
        out_specs=hbm,
        scratch_shapes=[
            pltpu.VMEM((rows, width), jnp.bfloat16),
            pltpu.VMEM((band, width), jnp.bfloat16),
            tokens,
            late_tokens,
            late_tokens,
            pltpu.SemaphoreType.DMA((2,)),
        ],
        input_output_aliases={11: 0},
        compiler_params=params,
        cost_estimate=cost(2 * 10**9, 4 * 10**6),
    )(*far, owner_cache)
    owner_cache = pl.pallas_call(
        last_kernel,
        out_shape=cache_shape,
        in_specs=[anywhere, hbm],
        out_specs=hbm,
        scratch_shapes=[pltpu.SemaphoreType.DMA((2,))],
        input_output_aliases={1: 0},
        compiler_params=params,
        cost_estimate=cost(0, 10**6),
    )(received, owner_cache)
    return (attention, row_scores, owner_cache)


def solution(mesh):
    placed = (
        P(None, "ctx", "kv"),
        P(None, "ctx", "kv"),
        P(None, "ctx", "kv", None),
        P("ctx", None),
        P(),
    )
    in_planes = mesh.shape["ctx"] == 8 and mesh.shape["kv"] == 4
    return jax.shard_map(
        local_in_planes if in_planes else local,
        mesh=mesh,
        in_specs=placed,
        out_specs=(P(None, "ctx", "kv"), P(None, "kv", "ctx"), P(("ctx", "kv"), None)),
        check_vma=False,
    )
```
